32 devices in a mesh: tm: 4 (over x, core), space: 8 (over z, y).
Axes of the slice: x: 2, y: 2, z: 4, core: 2. Of those that a mesh axis runs over, the one named last changes fastest.
Arguments:
- pixels: bfloat16 [163840, 128], P(('tm', 'space')), may hold values from -48 to 48
- weights: bfloat16 [163840], P(('tm', 'space')), may hold values from 0.5 to 2
- tile_index: int32 [163840], P(('tm', 'space')), may hold values from 0 to 7, as said below
- tile_row: int32 [163840], P(('tm', 'space')), may hold values from 0 to 159, as said below
- granule_day: int32 [163840], P(('tm', 'space')), may hold values from 0 to 127
Outputs:
- field: bfloat16 [8, 160, 512, 128], P('space', 'tm')
- basis: bfloat16 [8, 160, 256, 128], P('space', 'tm')
- propagator: float32 [256, 256], replicated
The draws below stay inside these ranges and needn't reach their ends.
Inputs may be any that keep to these rules, and one draw needn't show every extreme that they name: `tile_index`: of the rows of one device, at most 1280 name one tile, and in every device's rows some tile is named by exactly 1280. `tile_row`: of the rows of one device, at most 320 name one tile and a grid row from k * 40 to (k + 1) * 40 - 1 for one k, and in every device's rows some tile and k reach 320.
All inputs are finite; a program needn't handle non-finite values.
Results may differ from the reference program's by a relative error of at most 0.0061.
Values may be sent and summed in bfloat16 or wider, within the bound.
No kernel may reach another device: no remote copies, remote signals or barrier semaphores. Data moves between devices by JAX's collectives and lax.ppermute only.
A program may use at most 64 MiB of HBM per device.

```python
import math
import jax
import jax.numpy as jnp
from jax import lax

PIX = 128
GR_DEV = 160
DAYS = 512
RANK = 256
ITERS = 8
DAY_DEV = 128
SW_DEV = 5120
SW_TM = 40960
SWATH = 163840
CAP = 1280
CELLS = 163840
N_TM = 4
N_SPACE = 8


def swath_layout(key):
    blocks = SWATH // SW_DEV
    rows_tm = GR_DEV // N_TM

    def one_block(block_key):
        keys = jax.random.split(block_key, 6)
        hottest = jax.random.randint(keys[0], (), 0, N_SPACE)
        second = (hottest + jax.random.randint(keys[1], (), 1, N_SPACE)) % N_SPACE
        extra = jax.random.randint(keys[2], (), 0, CAP // 2)
        places = jnp.arange(SW_DEV, dtype=jnp.int32)
        rest = jnp.maximum(places - CAP - extra, 0)
        cycled = (hottest + 1 + rest % (N_SPACE - 1)) % N_SPACE
        tiles = jnp.where(places < CAP, hottest, jnp.where(places < CAP + extra, second, cycled))
        rest_rank = rest // (N_SPACE - 1) + jnp.where(cycled == second, extra, 0)
        order_rank = jnp.where(places < CAP, places, jnp.where(places < CAP + extra, places - CAP, rest_rank))
        rows = order_rank % N_TM * rows_tm + jax.random.randint(keys[3], (SW_DEV,), 0, rows_tm)
        days = jax.random.randint(keys[4], (SW_DEV,), 0, DAYS // N_TM)
        shuffle = jax.random.permutation(keys[5], SW_DEV)
        return (tiles[shuffle], rows[shuffle], days[shuffle])
    tiles, rows, days = jax.vmap(one_block)(jax.random.split(key, blocks))
    return (tiles.reshape(-1).astype(jnp.int32), rows.reshape(-1).astype(jnp.int32), days.reshape(-1).astype(jnp.int32))


def draw_tile_index(key, part):
    return swath_layout(jax.random.fold_in(key, 7))[0]


def draw_tile_row(key, part):
    return swath_layout(jax.random.fold_in(key, 7))[1]


def draw_granule_day(key, part):
    return swath_layout(jax.random.fold_in(key, 7))[2]


def draw_pixels(key, part):
    tiles, rows, days = swath_layout(jax.random.fold_in(key, 7))
    keys = jax.random.split(jax.random.fold_in(key, 11), 6)
    grid_rows = N_SPACE * GR_DEV
    cell_row = tiles * GR_DEV + rows
    global_day = jnp.arange(SWATH, dtype=jnp.int32) // SW_TM * (DAYS // N_TM) + days
    row_scale = jnp.exp(jax.random.uniform(keys[0], (grid_rows,), jnp.float32, 0.0, math.log(10.0)))
    common = 0.7
    noise = jnp.clip(jax.random.normal(keys[1], (SWATH, PIX), jnp.float32), -6.0, 6.0)
    mode_row = jnp.clip(jax.random.normal(keys[2], (grid_rows,), jnp.float32), -4.0, 4.0)
    mode_pix = jnp.clip(jax.random.normal(keys[3], (PIX,), jnp.float32), -4.0, 4.0)
    phase = jax.random.uniform(keys[4], (), jnp.float32, -math.pi, math.pi)
    day_noise = jnp.clip(jax.random.normal(keys[5], (DAYS,), jnp.float32), -4.0, 4.0)
    day_values = jnp.cos(2.0 * math.pi * jnp.arange(DAYS, dtype=jnp.float32) / 365.0 + phase) + 0.5 * day_noise
    mode_day = day_values[global_day]
    inner = common * mode_row[cell_row][:, None] * mode_pix[None, :] * mode_day[:, None] + noise
    inner = jnp.clip(inner, -8.0, 8.0)
    rise = 1.0 + 2.0 * tiles.astype(jnp.float32) / (N_SPACE - 1)
    values = row_scale[cell_row][:, None] * rise[:, None] * inner / 5.0
    return values.astype(jnp.bfloat16)


def shard_levels(key, shape, pieces, least, top_value):
    loudness = 1.0
    for axis_at, parts in pieces:
        heights = jax.random.uniform(jax.random.fold_in(jax.random.fold_in(key, 6), axis_at), (parts,), jnp.float32, least / len(pieces), top_value / len(pieces))
        loudness = loudness * jnp.repeat(jnp.exp(heights), shape[axis_at] // parts).reshape((-1,) + (1,) * (len(shape) - 1 - axis_at))
    return loudness


def setup_inputs(seed: int = 0) -> dict:
    seeds = jax.random.split(jax.random.key(seed), 6)
    pixels = draw_pixels(jax.random.fold_in(seeds[5], 71), 0)
    weights = jnp.clip(jnp.exp(math.log(2.0) - 1.3862944 * jax.random.uniform(seeds[1], (SWATH,), jnp.float32) ** shard_levels(seeds[1], (SWATH,), ((0, 32),), -0.2, 0.2)), 0.5, 2.0).astype(jnp.bfloat16)
    tile_index = draw_tile_index(jax.random.fold_in(seeds[5], 71), 0)
    tile_row = draw_tile_row(jax.random.fold_in(seeds[5], 71), 0)
    granule_day = draw_granule_day(jax.random.fold_in(seeds[5], 71), 0)
    return {"pixels": pixels, "weights": weights, "tile_index": tile_index, "tile_row": tile_row, "granule_day": granule_day}


def reference(pixels, weights, tile_index, tile_row, granule_day):
    swath = pixels.shape[0]
    gday = jnp.arange(swath, dtype=jnp.int32) // SW_TM * DAY_DEV + granule_day
    contrib = weights.astype(jnp.float32)[:, None] * pixels.astype(jnp.float32)
    target = tile_row * DAYS + gday

    def one_tile(which):
        place = jnp.where(tile_index == which, target, GR_DEV * DAYS)
        summed = jnp.zeros((GR_DEV * DAYS, PIX), jnp.float32).at[place].add(contrib, mode='drop')
        return summed.astype(jnp.bfloat16).reshape(GR_DEV, DAYS, PIX)
    field = lax.map(one_tile, jnp.arange(N_SPACE, dtype=jnp.int32))

    def add_tile(total, piece):
        values = piece.astype(jnp.float32)
        return (total + jnp.einsum('rdp,rep->de', values, values, precision=lax.Precision.HIGHEST), None)
    gram, _ = lax.scan(add_tile, jnp.zeros((DAYS, DAYS), jnp.float32), field)
    factor = jnp.linalg.cholesky(gram).T
    cross = jnp.dot(factor[:RANK, 1:], factor[:RANK, :-1].T, precision=lax.Precision.HIGHEST)
    polar = cross / jnp.sqrt(jnp.sum(cross * cross) + 1e-06)
    for sweep in range(ITERS):
        square = jnp.dot(polar.T, polar, precision=lax.Precision.HIGHEST)
        polar = 1.5 * polar - 0.5 * jnp.dot(polar, square, precision=lax.Precision.HIGHEST)
    propagator = jnp.sqrt(jnp.float32(RANK)) * polar
    inverse = lax.linalg.triangular_solve(factor[:RANK, :RANK], jnp.eye(RANK, dtype=factor.dtype), left_side=True, lower=False)
    scaled_inverse = (jnp.sqrt(jnp.float32(CELLS)) * inverse).astype(jnp.bfloat16).astype(jnp.float32)

    def project(piece):
        values = piece[:, :RANK, :].astype(jnp.float32)
        return jnp.einsum('rdp,dk->rkp', values, scaled_inverse, precision=lax.Precision.HIGHEST).astype(jnp.bfloat16)
    basis = lax.map(project, field)
    return (field, basis, propagator)
```

```python
import functools
import math

import jax
import jax.numpy as jnp
from jax import lax
from jax.experimental import pallas as pl
from jax.experimental.pallas import tpu as pltpu
from jax.sharding import PartitionSpec as P

GR_DEV = 160
DAYS = 512
RANK = 256
ITERS = 8
LANES = 128
META_ROWS = 16
GRID_STEPS = 5
VMEM = 56 * 1024 * 1024

LAST_LAST = (((1,), (1,)), ((), ()))
FIRST_FIRST = (((0,), (0,)), ((), ()))


def round_up(value, unit):
    return -(-value // unit) * unit


def pack_kernel(dims, tile_ref, row_ref, day_ref, weight_ref, pix_ref, out_ref, pos_v, pos_s, pixf, outf, mrow, sem):
    time_count, space_count, rows_tm, slot_rows, width = dims
    dest_count = time_count * space_count
    chunks = tile_ref.shape[0]
    pieces = width // LANES

    tile = tile_ref[...]
    row = row_ref[...]
    group = jnp.zeros_like(row)
    for k in range(1, time_count):
        group = group + jnp.where(row >= k * rows_tm, 1, 0)
    dest_all = group * space_count + tile
    local_row = (row - group * rows_tm).astype(jnp.float32)
    day = day_ref[...].astype(jnp.float32)
    weight = weight_ref[...].astype(jnp.float32)

    dest_iota = lax.broadcasted_iota(jnp.int32, (dest_count, LANES), 0)
    slot_iota = lax.broadcasted_iota(jnp.int32, (width, LANES), 0)
    upper = jnp.where(
        lax.broadcasted_iota(jnp.int32, (LANES, LANES), 0) <= lax.broadcasted_iota(jnp.int32, (LANES, LANES), 1), 1.0, 0.0
    ).astype(jnp.bfloat16)
    carry = jnp.zeros((dest_count, 1), jnp.float32)
    meta = jnp.zeros((3 * dest_count, width), jnp.float32)
    for c in range(chunks):
        dest = dest_all[c : c + 1, :]
        hot = dest_iota == dest
        prefix = jnp.dot(jnp.where(hot, 1.0, 0.0).astype(jnp.bfloat16), upper, preferred_element_type=jnp.float32)
        rank = jnp.sum(jnp.where(hot, prefix + carry, 0.0), axis=0, keepdims=True).astype(jnp.int32) - 1
        carry = carry + prefix[:, LANES - 1 : LANES]
        pos_v[c : c + 1, :] = dest * slot_rows + rank
        place = jnp.where(slot_iota == rank, 1.0, 0.0).astype(jnp.bfloat16)
        values = jnp.concatenate(
            [jnp.where(hot, v[c : c + 1, :], 0.0) for v in (weight, local_row, day)], axis=0
        ).astype(jnp.bfloat16)
        meta = meta + lax.dot_general(values, place, LAST_LAST, preferred_element_type=jnp.float32)
    copy = pltpu.make_async_copy(pos_v, pos_s, sem)
    copy.start()

    mrow[...] = jnp.zeros_like(mrow)
    for v in range(3):
        for i in range(pieces):
            mrow[pl.ds(v * pieces + i, dest_count, stride=META_ROWS), :] = meta[
                v * dest_count : (v + 1) * dest_count, i * LANES : (i + 1) * LANES
            ]

    def widen(c, _):
        at = pl.ds(pl.multiple_of(c * LANES, LANES), LANES)
        pixf[at, :] = pix_ref[at, :].astype(jnp.float32)
        return 0

    lax.fori_loop(0, chunks, widen, 0)

    def clear(b, _):
        outf[pl.ds(pl.multiple_of(b * slot_rows, 16), slot_rows), :] = jnp.zeros((slot_rows, LANES), jnp.float32)
        return 0

    lax.fori_loop(0, dest_count, clear, 0)
    copy.wait()

    def move(c, _):
        base = c * LANES
        for lane in range(LANES):
            outf[pl.ds(pos_s[c, lane], 1), :] = pixf[pl.ds(base + lane, 1), :]
        return 0

    lax.fori_loop(0, chunks, move, 0)

    def narrow(b, _):
        out_ref[b, :slot_rows, :] = outf[pl.ds(pl.multiple_of(b * slot_rows, 16), slot_rows), :].astype(jnp.bfloat16)
        out_ref[b, slot_rows:, :] = mrow[pl.ds(pl.multiple_of(b * META_ROWS, 16), META_ROWS), :].astype(jnp.bfloat16)
        return 0

    lax.fori_loop(0, dest_count, narrow, 0)


def pack(pixels, weights, tile_index, tile_row, granule_day, time_count, space_count, rows_tm, slots):
    swath_rows = pixels.shape[0]
    chunks = swath_rows // LANES
    dest_count = time_count * space_count
    slot_rows = round_up(slots, 16)
    width = round_up(slots, LANES)
    shape = (chunks, LANES)
    return pl.pallas_call(
        functools.partial(pack_kernel, (time_count, space_count, rows_tm, slot_rows, width)),
        out_shape=jax.ShapeDtypeStruct((dest_count, slot_rows + META_ROWS, LANES), jnp.bfloat16),
        scratch_shapes=[
            pltpu.VMEM(shape, jnp.int32),
            pltpu.SMEM(shape, jnp.int32),
            pltpu.VMEM((swath_rows, LANES), jnp.float32),
            pltpu.VMEM((dest_count * slot_rows, LANES), jnp.float32),
            pltpu.VMEM((dest_count * META_ROWS, LANES), jnp.float32),
            pltpu.SemaphoreType.DMA,
        ],
        compiler_params=pltpu.CompilerParams(vmem_limit_bytes=VMEM),
        name="pack",
    )(
        tile_index.reshape(shape),
        tile_row.reshape(shape),
        granule_day.reshape(shape),
        weights.reshape(shape),
        pixels,
    )


def grid_kernel(dims, moved_ref, field_ref, gram_ref, pix2, onehot, pair_of):
    time_count, space_count, rows_tm, slot_rows, width = dims
    day_dev = DAYS // time_count
    pieces = width // LANES
    pairs = rows_tm // 2 // GRID_STEPS
    step = pl.program_id(0)

    @pl.when(step == 0)
    def _():
        gram_ref[...] = jnp.zeros_like(gram_ref)
        day_iota = lax.broadcasted_iota(jnp.int32, (day_dev, width), 0).astype(jnp.float32)

        def spread(b, _):
            m = b // space_count
            at = pl.ds(pl.multiple_of((b % space_count) * width, LANES), width)
            meta = moved_ref[b, slot_rows:, :].astype(jnp.float32)
            weight, local_row, day = (
                jnp.concatenate([meta[v * pieces + i : v * pieces + i + 1, :] for i in range(pieces)], axis=1)
                for v in range(3)
            )
            onehot[m, :, at] = jnp.where(day_iota == day, weight, 0.0).astype(jnp.bfloat16)
            half = jnp.floor(local_row * 0.5)
            pair_of[m, :, at] = jnp.broadcast_to(half, (8, width))
            odd = jnp.transpose(jnp.broadcast_to(local_row - 2.0 * half, (8, width)))[:slot_rows, 0:1]
            odd = jnp.broadcast_to(odd, (slot_rows, LANES)).astype(jnp.bfloat16)
            pix = moved_ref[b, :slot_rows, :]
            right = pix * odd
            rows = pl.ds(pl.multiple_of((b % space_count) * width, LANES), slot_rows)
            pix2[m, rows, :LANES] = pix - right
            pix2[m, rows, LANES:] = right
            if width > slot_rows:
                rest = pl.ds(pl.multiple_of((b % space_count) * width + slot_rows, 16), width - slot_rows)
                pix2[m, rest, :] = jnp.zeros((width - slot_rows, 2 * LANES), jnp.bfloat16)
            return 0

        lax.fori_loop(0, time_count * space_count, spread, 0)

    for m in range(time_count):
        mine = pair_of[m, 0:1, :]
        chosen = onehot[m]
        left = jnp.concatenate(
            [
                chosen * jnp.where(mine == (step * pairs + q).astype(jnp.float32), 1.0, 0.0).astype(jnp.bfloat16)
                for q in range(pairs)
            ],
            axis=0,
        )
        sums = jnp.dot(left, pix2[m], preferred_element_type=jnp.float32).astype(jnp.bfloat16)
        for q in range(pairs):
            here = sums[q * day_dev : (q + 1) * day_dev, :]
            field_ref[2 * q, m * day_dev : (m + 1) * day_dev, :] = here[:, :LANES]
            field_ref[2 * q + 1, m * day_dev : (m + 1) * day_dev, :] = here[:, LANES:]
    for q in range(pairs):
        both = jnp.concatenate([field_ref[2 * q], field_ref[2 * q + 1]], axis=1)
        part = lax.dot_general(both[:RANK], both, LAST_LAST, preferred_element_type=jnp.float32)
        for i in range(DAYS // LANES):
            gram_ref[i] += part[:, i * LANES : (i + 1) * LANES]


def grid_rows(moved, time_count, space_count, rows_tm, slots):
    slot_rows = round_up(slots, 16)
    width = round_up(slots, LANES)
    day_dev = DAYS // time_count
    depth = space_count * width
    rows_step = rows_tm // GRID_STEPS
    return pl.pallas_call(
        functools.partial(grid_kernel, (time_count, space_count, rows_tm, slot_rows, width)),
        grid=(GRID_STEPS,),
        in_specs=[pl.BlockSpec(moved.shape, lambda i: (0, 0, 0))],
        out_specs=[
            pl.BlockSpec((rows_step, DAYS, LANES), lambda i: (i, 0, 0)),
            pl.BlockSpec((DAYS // LANES, RANK, LANES), lambda i: (0, 0, 0)),
        ],
        out_shape=[
            jax.ShapeDtypeStruct((rows_tm, DAYS, LANES), jnp.bfloat16),
            jax.ShapeDtypeStruct((DAYS // LANES, RANK, LANES), jnp.float32),
        ],
        scratch_shapes=[
            pltpu.VMEM((time_count, depth, 2 * LANES), jnp.bfloat16),
            pltpu.VMEM((time_count, day_dev, depth), jnp.bfloat16),
            pltpu.VMEM((time_count, 8, depth), jnp.float32),
        ],
        compiler_params=pltpu.CompilerParams(vmem_limit_bytes=VMEM),
        name="grid_and_gram",
    )(moved)


def dot_f32(a, b, dims=(((1,), (0,)), ((), ()))):
    return lax.dot_general(a, b, dims, precision=lax.Precision.HIGHEST, preferred_element_type=jnp.float32)


def lower_inverse(a):
    n = a.shape[0]
    tiles = [a[8 * i : 8 * i + 8, :] for i in range(n // 8)]
    lane = lax.broadcasted_iota(jnp.int32, (8, n), 1)
    below = lax.broadcasted_iota(jnp.int32, (8, n), 0)
    lane_row = lax.broadcasted_iota(jnp.int32, (1, n), 1)
    for k in range(n):
        at, sub = divmod(k, 8)
        row = tiles[at][sub : sub + 1, :]
        scaled = jnp.where(lane_row == k, 1.0, row) * (1.0 / row[:, k : k + 1])
        for i in range(at, n // 8):
            col = jnp.broadcast_to(tiles[i][:, k : k + 1], (8, n))
            if i == at:
                col = jnp.where(below > sub, col, 0.0)
                base = jnp.where((lane == k) & (below > sub), 0.0, tiles[i])
            else:
                base = jnp.where(lane == k, 0.0, tiles[i])
            tiles[i] = base - col * scaled
    out = []
    for i, t in enumerate(tiles):
        diag = below + 8 * i
        pivot = jnp.sum(jnp.where(lane == diag, t, 0.0), axis=1, keepdims=True)
        out.append(jnp.where(lane < diag, t, jnp.where(lane == diag, 1.0, 0.0)) * lax.rsqrt(pivot))
    return jnp.concatenate(out, axis=0)


def solve_kernel(scale, gram_ref, basis_ref, prop_ref):
    h = LANES
    pieces = DAYS // h
    corner = gram_ref[1, :h, :]
    x1 = lower_inverse(gram_ref[0, :h, :])
    r12 = dot_f32(x1, corner)
    x2 = lower_inverse(gram_ref[1, h:, :] - dot_f32(r12, r12, FIRST_FIRST))
    mixed = -dot_f32(x2, dot_f32(r12, x1, FIRST_FIRST))
    lower = jnp.concatenate(
        [
            jnp.concatenate([x1, jnp.zeros((h, h), jnp.float32)], axis=1),
            jnp.concatenate([mixed, x2], axis=1),
        ],
        axis=0,
    )
    basis_ref[...] = (scale * lower).astype(jnp.bfloat16)

    down = lax.broadcasted_iota(jnp.int32, (RANK, DAYS), 0)
    across = lax.broadcasted_iota(jnp.int32, (RANK, DAYS), 1)
    gram = jnp.concatenate([gram_ref[i] for i in range(pieces)], axis=1)
    factor = jnp.where(across >= down, dot_f32(lower, gram), 0.0)
    ahead = jnp.where(across < DAYS - 1, pltpu.roll(factor, DAYS - 1, 1), 0.0)
    cross = dot_f32(ahead, factor, LAST_LAST)
    polar = cross / jnp.sqrt(jnp.sum(cross * cross) + 1e-06)
    for _ in range(ITERS):
        square = dot_f32(polar, polar, LAST_LAST)
        polar = 1.5 * polar - 0.5 * dot_f32(square, polar)
    prop_ref[...] = math.sqrt(RANK) * polar


def solve(gram, cell_total):
    return pl.pallas_call(
        functools.partial(solve_kernel, math.sqrt(cell_total)),
        out_shape=[
            jax.ShapeDtypeStruct((RANK, RANK), jnp.bfloat16),
            jax.ShapeDtypeStruct((RANK, RANK), jnp.float32),
        ],
        compiler_params=pltpu.CompilerParams(vmem_limit_bytes=VMEM),
        name="factor_and_polar",
    )(gram)


def body(pixels, weights, tile_index, tile_row, granule_day):
    swath_rows = pixels.shape[0]
    width = pixels.shape[1]
    space_count = lax.axis_size("space")
    time_count = lax.axis_size("tm")
    dest_count = time_count * space_count
    rows_tm = GR_DEV // time_count
    slots = 2 * swath_rows // space_count // time_count
    axes = ("tm", "space")
    packed = pack(pixels, weights, tile_index, tile_row, granule_day, time_count, space_count, rows_tm, slots)
    moved = lax.all_to_all(packed, axes, split_axis=0, concat_axis=0, tiled=True)
    field, partial_gram = grid_rows(moved, time_count, space_count, rows_tm, slots)
    pieces = partial_gram.reshape(dest_count, -1, LANES)
    pieces = lax.all_to_all(pieces, axes, split_axis=0, concat_axis=0, tiled=True)
    mine = jnp.sum(pieces, axis=0, keepdims=True)
    gram = lax.all_to_all(jnp.broadcast_to(mine, pieces.shape), axes, split_axis=0, concat_axis=0, tiled=True)
    cell_total = space_count * GR_DEV * width
    scaled_lower, propagator = solve(gram.reshape(partial_gram.shape), cell_total)
    basis = jnp.einsum("kd,rdp->rkp", scaled_lower, field[:, :RANK, :], preferred_element_type=jnp.float32)
    return (field[None], basis.astype(jnp.bfloat16)[None], propagator)


def solution(mesh):
    placed = (
        P(("tm", "space"), None),
        P(("tm", "space")),
        P(("tm", "space")),
        P(("tm", "space")),
        P(("tm", "space")),
    )
    return jax.shard_map(
        body,
        mesh=mesh,
        in_specs=placed,
        out_specs=(P("space", "tm", None, None), P("space", "tm", None, None), P()),
        check_vma=False,
    )
```

```python
import functools
import math

import jax
import jax.numpy as jnp
from jax import lax
from jax.experimental import pallas as pl
from jax.experimental.pallas import tpu as pltpu
from jax.sharding import PartitionSpec as P

GR_DEV = 160
DAYS = 512
RANK = 256
ITERS = 8
LANES = 128
META_ROWS = 16
VMEM = 56 * 1024 * 1024

LAST_LAST = (((1,), (1,)), ((), ()))
FIRST_FIRST = (((0,), (0,)), ((), ()))


def round_up(value, unit):
    return -(-value // unit) * unit


def pack_kernel(dims, tile_ref, row_ref, day_ref, weight_ref, pix_ref, out_ref, pos_v, pos_s, pixf, outf, mrow, sem):
    time_count, space_count, rows_tm, slot_rows, width = dims
    dest_count = time_count * space_count
    chunks = tile_ref.shape[0]
    pieces = width // LANES

    tile = tile_ref[...]
    row = row_ref[...]
    group = jnp.zeros_like(row)
    for k in range(1, time_count):
        group = group + jnp.where(row >= k * rows_tm, 1, 0)
    dest_all = group * space_count + tile
    local_row = (row - group * rows_tm).astype(jnp.float32)
    day = day_ref[...].astype(jnp.float32)
    weight = weight_ref[...].astype(jnp.float32)

    dest_iota = lax.broadcasted_iota(jnp.int32, (dest_count, LANES), 0)
    slot_iota = lax.broadcasted_iota(jnp.int32, (width, LANES), 0)
    upper = jnp.where(
        lax.broadcasted_iota(jnp.int32, (LANES, LANES), 0) <= lax.broadcasted_iota(jnp.int32, (LANES, LANES), 1), 1.0, 0.0
    ).astype(jnp.bfloat16)
    carry = jnp.zeros((dest_count, 1), jnp.float32)
    meta = jnp.zeros((3 * dest_count, width), jnp.float32)
    for c in range(chunks):
        dest = dest_all[c : c + 1, :]
        hot = dest_iota == dest
        prefix = jnp.dot(jnp.where(hot, 1.0, 0.0).astype(jnp.bfloat16), upper, preferred_element_type=jnp.float32)
        rank = jnp.sum(jnp.where(hot, prefix + carry, 0.0), axis=0, keepdims=True).astype(jnp.int32) - 1
        carry = carry + prefix[:, LANES - 1 : LANES]
        pos_v[c : c + 1, :] = dest * slot_rows + rank
        place = jnp.where(slot_iota == rank, 1.0, 0.0).astype(jnp.bfloat16)
        values = jnp.concatenate(
            [jnp.where(hot, v[c : c + 1, :], 0.0) for v in (weight, local_row, day)], axis=0
        ).astype(jnp.bfloat16)
        meta = meta + lax.dot_general(values, place, LAST_LAST, preferred_element_type=jnp.float32)
    copy = pltpu.make_async_copy(pos_v, pos_s, sem)
    copy.start()

    mrow[...] = jnp.zeros_like(mrow)
    for v in range(3):
        for i in range(pieces):
            mrow[pl.ds(v * pieces + i, dest_count, stride=META_ROWS), :] = meta[
                v * dest_count : (v + 1) * dest_count, i * LANES : (i + 1) * LANES
            ]

    def widen(c, _):
        at = pl.ds(pl.multiple_of(c * LANES, LANES), LANES)
        pixf[at, :] = pix_ref[at, :].astype(jnp.float32)
        return 0

    lax.fori_loop(0, chunks, widen, 0)

    def clear(b, _):
        outf[pl.ds(pl.multiple_of(b * slot_rows, 16), slot_rows), :] = jnp.zeros((slot_rows, LANES), jnp.float32)
        return 0

    lax.fori_loop(0, dest_count, clear, 0)
    copy.wait()

    def move(c, _):
        base = c * LANES
        for lane in range(LANES):
            outf[pl.ds(pos_s[c, lane], 1), :] = pixf[pl.ds(base + lane, 1), :]
        return 0

    lax.fori_loop(0, chunks, move, 0)

    def narrow(b, _):
        out_ref[b, :slot_rows, :] = outf[pl.ds(pl.multiple_of(b * slot_rows, 16), slot_rows), :].astype(jnp.bfloat16)
        out_ref[b, slot_rows:, :] = mrow[pl.ds(pl.multiple_of(b * META_ROWS, 16), META_ROWS), :].astype(jnp.bfloat16)
        return 0

    lax.fori_loop(0, dest_count, narrow, 0)


def pack(pixels, weights, tile_index, tile_row, granule_day, time_count, space_count, rows_tm, slots):
    swath_rows = pixels.shape[0]
    chunks = swath_rows // LANES
    dest_count = time_count * space_count
    slot_rows = round_up(slots, 16)
    width = round_up(slots, LANES)
    shape = (chunks, LANES)
    return pl.pallas_call(
        functools.partial(pack_kernel, (time_count, space_count, rows_tm, slot_rows, width)),
        out_shape=jax.ShapeDtypeStruct((dest_count, slot_rows + META_ROWS, LANES), jnp.bfloat16),
        scratch_shapes=[
            pltpu.VMEM(shape, jnp.int32),
            pltpu.SMEM(shape, jnp.int32),
            pltpu.VMEM((swath_rows, LANES), jnp.float32),
            pltpu.VMEM((dest_count * slot_rows, LANES), jnp.float32),
            pltpu.VMEM((dest_count * META_ROWS, LANES), jnp.float32),
            pltpu.SemaphoreType.DMA,
        ],
        compiler_params=pltpu.CompilerParams(vmem_limit_bytes=VMEM),
        name="pack",
    )(
        tile_index.reshape(shape),
        tile_row.reshape(shape),
        granule_day.reshape(shape),
        weights.reshape(shape),
        pixels,
    )


def grid_kernel(dims, moved_ref, field_ref, gram_ref, pixf, code_v, code_s, count_v, count_s, field_v, sems, *sums):
    time_count, space_count, rows_tm, slot_rows, width = dims
    day_dev = DAYS // time_count
    pieces = width // LANES
    spare = rows_tm * day_dev
    group = 4

    def spread(b, _):
        meta = moved_ref[b, slot_rows:, :].astype(jnp.float32)
        weight, local_row, day = (
            jnp.concatenate([meta[v * pieces + i : v * pieces + i + 1, :] for i in range(pieces)], axis=1)
            for v in range(3)
        )
        used = weight > 0.0
        code = jnp.where(used, local_row * day_dev + day, float(spare)).astype(jnp.int32)
        for i in range(pieces):
            code_v[pl.ds(b * pieces + i, 1), :] = code[:, i * LANES : (i + 1) * LANES]
        count = jnp.sum(jnp.where(used, 1.0, 0.0), axis=1, keepdims=True)
        count_v[pl.ds(b, 1), :] = jnp.broadcast_to(count, (1, LANES)).astype(jnp.int32)
        column = jnp.transpose(jnp.broadcast_to(weight, (8, width)))[:slot_rows, 0:1]
        at = pl.ds(pl.multiple_of(b * slot_rows, 16), slot_rows)
        pixf[at, :] = moved_ref[b, :slot_rows, :].astype(jnp.float32) * column
        return 0

    lax.fori_loop(0, time_count * space_count, spread, 0)
    code_copy = pltpu.make_async_copy(code_v, code_s, sems.at[0])
    count_copy = pltpu.make_async_copy(count_v, count_s, sems.at[1])
    code_copy.start()
    count_copy.start()
    gram_ref[...] = jnp.zeros_like(gram_ref)

    def clear(i, _):
        for total in sums:
            total[pl.ds(pl.multiple_of(i * day_dev, day_dev), day_dev), :] = jnp.zeros((day_dev, LANES), jnp.float32)
        return 0

    lax.fori_loop(0, rows_tm, clear, 0)
    for total in sums:
        total[spare:, :] = jnp.zeros((8, LANES), jnp.float32)
    code_copy.wait()
    count_copy.wait()

    def source(s, _):
        most = count_s[s, 0]
        for m in range(1, time_count):
            most = jnp.maximum(most, count_s[m * space_count + s, 0])

        def add(j, _):
            piece, lane = j // 16, (j % 16) * 8
            for u in range(0, 8, 2):
                held = []
                for m, total in enumerate(sums):
                    b = m * space_count + s
                    one = code_s[b * pieces + piece, lane + u]
                    two = code_s[b * pieces + piece, lane + u + 1]
                    at = b * slot_rows + j * 8 + u
                    first, second = pixf[pl.ds(at, 1), :], pixf[pl.ds(at + 1, 1), :]
                    same = jnp.where(one == two, 1.0, 0.0)
                    held.append(
                        (one, total[pl.ds(one, 1), :] + first, two, total[pl.ds(two, 1), :] + (second + same * first))
                    )
                for total, (one, first, two, second) in zip(sums, held):
                    total[pl.ds(one, 1), :] = first
                    total[pl.ds(two, 1), :] = second
            return 0

        lax.fori_loop(0, (most + 7) // 8, add, 0)
        return 0

    lax.fori_loop(0, space_count, source, 0)

    def send(i):
        at = pl.ds(i * group, group)
        return pltpu.make_async_copy(field_v.at[at], field_ref.at[at], sems.at[2])

    def finish(i, _):
        for q in range(group):
            for m, total in enumerate(sums):
                at = pl.ds(pl.multiple_of((i * group + q) * day_dev, day_dev), day_dev)
                field_v[i * group + q, m * day_dev : (m + 1) * day_dev, :] = total[at, :].astype(jnp.bfloat16)
        send(i).start()
        both = jnp.concatenate([field_v[i * group + q] for q in range(group)], axis=1)
        part = lax.dot_general(both[:RANK], both, LAST_LAST, preferred_element_type=jnp.float32)
        for c in range(DAYS // LANES):
            gram_ref[c] += part[:, c * LANES : (c + 1) * LANES]
        return 0

    lax.fori_loop(0, rows_tm // group, finish, 0)
    pltpu.make_async_copy(field_v, field_ref, sems.at[2]).wait()


def grid_rows(moved, time_count, space_count, rows_tm, slots):
    slot_rows = round_up(slots, 16)
    width = round_up(slots, LANES)
    day_dev = DAYS // time_count
    blocks = time_count * space_count
    codes = (blocks * width // LANES, LANES)
    return pl.pallas_call(
        functools.partial(grid_kernel, (time_count, space_count, rows_tm, slot_rows, width)),
        out_specs=[pl.BlockSpec(memory_space=pl.ANY), pl.BlockSpec(memory_space=pltpu.VMEM)],
        out_shape=[
            jax.ShapeDtypeStruct((rows_tm, DAYS, LANES), jnp.bfloat16),
            jax.ShapeDtypeStruct((DAYS // LANES, RANK, LANES), jnp.float32),
        ],
        scratch_shapes=[
            pltpu.VMEM((blocks * slot_rows, LANES), jnp.float32),
            pltpu.VMEM(codes, jnp.int32),
            pltpu.SMEM(codes, jnp.int32),
            pltpu.VMEM((blocks, LANES), jnp.int32),
            pltpu.SMEM((blocks, LANES), jnp.int32),
            pltpu.VMEM((rows_tm, DAYS, LANES), jnp.bfloat16),
            pltpu.SemaphoreType.DMA((3,)),
        ]
        + [pltpu.VMEM((rows_tm * day_dev + 8, LANES), jnp.float32)] * time_count,
        compiler_params=pltpu.CompilerParams(vmem_limit_bytes=VMEM),
        name="grid_and_gram",
    )(moved)


def dot_f32(a, b, dims=(((1,), (0,)), ((), ()))):
    return lax.dot_general(a, b, dims, precision=lax.Precision.HIGHEST, preferred_element_type=jnp.float32)


def dot_three(a, b, dims=(((1,), (0,)), ((), ()))):
    a_high, b_high = a.astype(jnp.bfloat16), b.astype(jnp.bfloat16)
    a_low = (a - a_high.astype(jnp.float32)).astype(jnp.bfloat16)
    b_low = (b - b_high.astype(jnp.float32)).astype(jnp.bfloat16)
    dot = functools.partial(lax.dot_general, dimension_numbers=dims, preferred_element_type=jnp.float32)
    return dot(a_high, b_high) + (dot(a_high, b_low) + dot(a_low, b_high))


def invert(x):
    guess = pl.reciprocal(x, approx=True)
    guess = guess * (2.0 - x * guess)
    return guess * (2.0 - x * guess)


def lower_inverse(a):
    n = a.shape[0]
    full = (8, n)
    tiles = [a[8 * i : 8 * i + 8, :] for i in range(n // 8)]
    lane = lax.broadcasted_iota(jnp.int32, full, 1)
    down = lax.broadcasted_iota(jnp.int32, full, 0)
    out = []
    for t in range(n // 8):
        k = 8 * t
        block = (lane >= k) & (lane < k + 8)
        panel = tiles[t]
        cols = [jnp.broadcast_to(panel[:, k + c : k + c + 1], full) for c in range(8)]
        e = {(i, c): jnp.broadcast_to(cols[c][i : i + 1, :], full) for c in range(8) for i in range(c, 8)}
        start = jnp.where(block, jnp.where(lane == k + down, 1.0, 0.0), panel)
        rows = [jnp.broadcast_to(start[i : i + 1, :], full) for i in range(8)]
        held = []
        for s in range(0, 8, 2):
            p, q, r = e[s, s], e[s + 1, s], e[s + 1, s + 1]
            det = p * r - q * q
            inv = invert(det)
            factors = {}
            for i in range(s + 2, 8):
                x, y = e[i, s], e[i, s + 1]
                factors[i] = (r * x - q * y, p * y - q * x)
            for i in range(s + 2, 8):
                u, v = factors[i]
                for c in range(s + 2, i + 1):
                    e[i, c] = e[i, c] - (u * e[c, s] + v * e[c, s + 1]) * inv
                rows[i] = rows[i] - (u * rows[s] + v * rows[s + 1]) * inv
            held.append((p, q, r, det, inv, factors))
        done = jnp.zeros(full, jnp.float32)
        solved = [None] * 8
        for s in (6, 4, 2, 0):
            p, q, r, det, inv, factors = held[s // 2]
            root = lax.rsqrt(p)
            done = jnp.where(down == s, rows[s] * root, done)
            done = jnp.where(down == s + 1, (rows[s + 1] * p - q * rows[s]) * (root * lax.rsqrt(det)), done)
            first, second = r * rows[s] - q * rows[s + 1], p * rows[s + 1] - q * rows[s]
            for i in range(s + 2, 8):
                u, v = factors[i]
                first, second = first - u * solved[i], second - v * solved[i]
            solved[s], solved[s + 1] = first * inv, second * inv
        out.append(jnp.where(lane < k + 8, done, 0.0))
        for i in range(t + 1, n // 8):
            terms = [jnp.broadcast_to(tiles[i][:, k + c : k + c + 1], full) * solved[c] for c in range(8)]
            while len(terms) > 1:
                terms = [terms[j] + terms[j + 1] for j in range(0, len(terms), 2)]
            tiles[i] = jnp.where(block, 0.0, tiles[i]) - terms[0]
    return jnp.concatenate(out, axis=0)


def solve_kernel(scale, gram_ref, field_ref, basis_ref, prop_ref, field_v, basis_v, sems):
    h = LANES
    pieces = DAYS // h
    grid_rows_here = field_v.shape[0]
    load = pltpu.make_async_copy(field_ref.at[:, pl.ds(0, RANK), :], field_v, sems.at[0])
    load.start()

    eye = lax.broadcasted_iota(jnp.int32, (h, h), 0) == lax.broadcasted_iota(jnp.int32, (h, h), 1)
    a11, a12, a22 = gram_ref[0, :h, :], gram_ref[1, :h, :], gram_ref[1, h:, :]
    size_col, size_row = [], []
    for part in (a11, a22):
        diag = jnp.where(eye, part, 0.0)
        size_col.append(lax.rsqrt(jnp.sum(diag, axis=1, keepdims=True)))
        size_row.append(lax.rsqrt(jnp.sum(diag, axis=0, keepdims=True)))
    x1 = lower_inverse(a11 * size_col[0] * size_row[0])
    r12 = dot_f32(x1, a12 * size_col[0] * size_row[1])
    x2 = lower_inverse(a22 * size_col[1] * size_row[1] - dot_f32(r12, r12, FIRST_FIRST))
    mixed = -dot_f32(x2, dot_f32(r12, x1, FIRST_FIRST))
    lower = jnp.concatenate(
        [
            jnp.concatenate([x1 * size_row[0], jnp.zeros((h, h), jnp.float32)], axis=1),
            jnp.concatenate([mixed * size_row[0], x2 * size_row[1]], axis=1),
        ],
        axis=0,
    )
    inverse = (scale * lower).astype(jnp.bfloat16)
    load.wait()

    def project(i, _):
        both = jnp.concatenate([field_v[2 * i], field_v[2 * i + 1]], axis=1)
        made = jnp.dot(inverse, both, preferred_element_type=jnp.float32).astype(jnp.bfloat16)
        basis_v[2 * i] = made[:, :h]
        basis_v[2 * i + 1] = made[:, h:]
        return 0

    lax.fori_loop(0, grid_rows_here // 2, project, 0)
    store = pltpu.make_async_copy(basis_v, basis_ref, sems.at[1])
    store.start()

    down = lax.broadcasted_iota(jnp.int32, (RANK, DAYS), 0)
    across = lax.broadcasted_iota(jnp.int32, (RANK, DAYS), 1)
    gram = jnp.concatenate([gram_ref[i] for i in range(pieces)], axis=1)
    factor = jnp.where(across >= down, dot_f32(lower, gram), 0.0)
    ahead = jnp.where(across < DAYS - 1, pltpu.roll(factor, DAYS - 1, 1), 0.0)
    cross = dot_three(ahead, factor, LAST_LAST)
    polar = cross / jnp.sqrt(jnp.sum(cross * cross) + 1e-06)
    for _ in range(ITERS):
        square = dot_three(polar, polar, LAST_LAST)
        polar = 1.5 * polar - 0.5 * dot_three(square, polar)
    prop_ref[...] = math.sqrt(RANK) * polar
    store.wait()


def solve(gram, field, cell_total):
    rows_tm = field.shape[0]
    part = (rows_tm, RANK, LANES)
    return pl.pallas_call(
        functools.partial(solve_kernel, math.sqrt(cell_total)),
        in_specs=[pl.BlockSpec(memory_space=pltpu.VMEM), pl.BlockSpec(memory_space=pl.ANY)],
        out_specs=[pl.BlockSpec(memory_space=pl.ANY), pl.BlockSpec(memory_space=pltpu.VMEM)],
        out_shape=[
            jax.ShapeDtypeStruct(part, jnp.bfloat16),
            jax.ShapeDtypeStruct((RANK, RANK), jnp.float32),
        ],
        scratch_shapes=[
            pltpu.VMEM(part, jnp.bfloat16),
            pltpu.VMEM(part, jnp.bfloat16),
            pltpu.SemaphoreType.DMA((2,)),
        ],
        compiler_params=pltpu.CompilerParams(vmem_limit_bytes=VMEM),
        name="factor_basis_and_polar",
    )(gram, field)


def body(pixels, weights, tile_index, tile_row, granule_day):
    swath_rows = pixels.shape[0]
    width = pixels.shape[1]
    space_count = lax.axis_size("space")
    time_count = lax.axis_size("tm")
    dest_count = time_count * space_count
    rows_tm = GR_DEV // time_count
    slots = 2 * swath_rows // space_count // time_count
    axes = ("tm", "space")
    packed = pack(pixels, weights, tile_index, tile_row, granule_day, time_count, space_count, rows_tm, slots)
    moved = lax.all_to_all(packed, axes, split_axis=0, concat_axis=0, tiled=True)
    field, partial_gram = grid_rows(moved, time_count, space_count, rows_tm, slots)
    pieces = partial_gram.reshape(dest_count, -1, LANES)
    pieces = lax.all_to_all(pieces, axes, split_axis=0, concat_axis=0, tiled=True)
    mine = jnp.sum(pieces, axis=0, keepdims=True)
    gram = lax.all_to_all(jnp.broadcast_to(mine, pieces.shape), axes, split_axis=0, concat_axis=0, tiled=True)
    cell_total = space_count * GR_DEV * width
    basis, propagator = solve(gram.reshape(partial_gram.shape), field, cell_total)
    return (field[None], basis[None], propagator)


def solution(mesh):
    placed = (
        P(("tm", "space"), None),
        P(("tm", "space")),
        P(("tm", "space")),
        P(("tm", "space")),
        P(("tm", "space")),
    )
    return jax.shard_map(
        body,
        mesh=mesh,
        in_specs=placed,
        out_specs=(P("space", "tm", None, None), P("space", "tm", None, None), P()),
        check_vma=False,
    )
```

```python
import functools
import math

import jax
import jax.numpy as jnp
from jax import lax
from jax.experimental import pallas as pl
from jax.experimental.pallas import tpu as pltpu
from jax.sharding import PartitionSpec as P

GR_DEV = 160
DAYS = 512
RANK = 256
ITERS = 8
LANES = 128
META_ROWS = 16
GROUP = 16
CLASH = 1 << 20
VMEM = 56 * 1024 * 1024

LAST_LAST = (((1,), (1,)), ((), ()))
FIRST_FIRST = (((0,), (0,)), ((), ()))


def round_up(value, unit):
    return -(-value // unit) * unit


def split_rows(slots):
    rows = round_up(slots, 16)
    return rows, round_up(rows * 3 // 5, 16)


def pack_kernel(
    dims, tile_ref, row_ref, day_ref, weight_ref, pix_ref, first_ref, last_ref, pos_v, pos_s, rows_v, meta_v, pixf, outf, mrow, sem
):
    time_count, space_count, rows_tm, slot_rows, first_rows, width = dims
    dest_count = time_count * space_count
    chunks = tile_ref.shape[0]
    pieces = width // LANES

    tile = tile_ref[...]
    row = row_ref[...]
    group = jnp.zeros_like(row)
    for k in range(1, time_count):
        group = group + jnp.where(row >= k * rows_tm, 1, 0)
    dest_all = group * space_count + tile
    rows_v[0] = dest_all.astype(jnp.float32)
    rows_v[2] = weight_ref[...].astype(jnp.float32)
    rows_v[3] = (row - group * rows_tm).astype(jnp.float32)
    rows_v[4] = day_ref[...].astype(jnp.float32)

    dest_iota = lax.broadcasted_iota(jnp.int32, (dest_count, LANES), 0)
    upper = jnp.where(
        lax.broadcasted_iota(jnp.int32, (LANES, LANES), 0) <= lax.broadcasted_iota(jnp.int32, (LANES, LANES), 1), 1.0, 0.0
    ).astype(jnp.bfloat16)
    carry = jnp.zeros((dest_count, 1), jnp.float32)
    for c in range(chunks):
        hot = dest_iota == dest_all[c : c + 1, :]
        prefix = jnp.dot(jnp.where(hot, 1.0, 0.0).astype(jnp.bfloat16), upper, preferred_element_type=jnp.float32)
        rows_v[1, c : c + 1, :] = jnp.sum(jnp.where(hot, prefix + carry, 0.0), axis=0, keepdims=True) - 1.0
        carry = carry + prefix[:, LANES - 1 : LANES]
    pos_v[...] = dest_all * slot_rows + rows_v[1].astype(jnp.int32)
    copy = pltpu.make_async_copy(pos_v, pos_s, sem)
    copy.start()
    meta_v[...] = jnp.zeros_like(meta_v)
    mrow[...] = jnp.zeros_like(mrow)

    def clear(b, _):
        outf[pl.ds(pl.multiple_of(b * slot_rows, 16), slot_rows), :] = jnp.zeros((slot_rows, LANES), jnp.float32)
        return 0

    lax.fori_loop(0, dest_count, clear, 0)
    copy.wait()
    dest_number = dest_iota.astype(jnp.float32)
    slot_number = lax.broadcasted_iota(jnp.int32, (width, LANES), 0).astype(jnp.float32)

    def move(c, _):
        base = pl.multiple_of(c * LANES, LANES)
        pixf[pl.ds(base, LANES), :] = pix_ref[pl.ds(base, LANES), :].astype(jnp.float32)
        dest, rank, weight, local_row, day = (rows_v[v, pl.ds(c, 1), :] for v in range(5))
        hot = dest_number == dest
        place = jnp.where(slot_number == rank, 1.0, 0.0).astype(jnp.bfloat16)
        values = jnp.concatenate([jnp.where(hot, v, 0.0) for v in (weight, local_row, day)], axis=0).astype(jnp.bfloat16)
        meta_v[...] += lax.dot_general(values, place, LAST_LAST, preferred_element_type=jnp.float32)
        for lane in range(LANES):
            outf[pl.ds(pos_s[c, lane], 1), :] = pixf[pl.ds(base + lane, 1), :]
        return 0

    lax.fori_loop(0, chunks, move, 0)
    for v in range(3):
        for i in range(pieces):
            mrow[pl.ds(v * pieces + i, dest_count, stride=META_ROWS), :] = meta_v[
                v * dest_count : (v + 1) * dest_count, i * LANES : (i + 1) * LANES
            ]

    def narrow(b, _):
        at = pl.multiple_of(b * slot_rows, 16)
        first_ref[b, :first_rows, :] = outf[pl.ds(at, first_rows), :].astype(jnp.bfloat16)
        first_ref[b, first_rows:, :] = mrow[pl.ds(pl.multiple_of(b * META_ROWS, 16), META_ROWS), :].astype(jnp.bfloat16)
        last_ref[b] = outf[pl.ds(at + first_rows, slot_rows - first_rows), :].astype(jnp.bfloat16)
        return 0

    lax.fori_loop(0, dest_count, narrow, 0)


def pack(pixels, weights, tile_index, tile_row, granule_day, time_count, space_count, rows_tm, slots):
    swath_rows = pixels.shape[0]
    chunks = swath_rows // LANES
    dest_count = time_count * space_count
    slot_rows, first_rows = split_rows(slots)
    width = round_up(slots, LANES)
    shape = (chunks, LANES)
    return pl.pallas_call(
        functools.partial(pack_kernel, (time_count, space_count, rows_tm, slot_rows, first_rows, width)),
        out_shape=[
            jax.ShapeDtypeStruct((dest_count, first_rows + META_ROWS, LANES), jnp.bfloat16),
            jax.ShapeDtypeStruct((dest_count, slot_rows - first_rows, LANES), jnp.bfloat16),
        ],
        scratch_shapes=[
            pltpu.VMEM(shape, jnp.int32),
            pltpu.SMEM(shape, jnp.int32),
            pltpu.VMEM((5,) + shape, jnp.float32),
            pltpu.VMEM((3 * dest_count, width), jnp.float32),
            pltpu.VMEM((swath_rows, LANES), jnp.float32),
            pltpu.VMEM((dest_count * slot_rows, LANES), jnp.float32),
            pltpu.VMEM((dest_count * META_ROWS, LANES), jnp.float32),
            pltpu.SemaphoreType.DMA,
        ],
        compiler_params=pltpu.CompilerParams(vmem_limit_bytes=VMEM),
        name="pack",
    )(
        tile_index.reshape(shape),
        tile_row.reshape(shape),
        granule_day.reshape(shape),
        weights.reshape(shape),
        pixels,
    )


def meta_lanes(meta, which, pieces):
    return jnp.concatenate([meta[which * pieces + i : which * pieces + i + 1, :] for i in range(pieces)], axis=1)


def weight_column(meta, pieces):
    weight = meta_lanes(meta, 0, pieces)
    return jnp.transpose(jnp.broadcast_to(weight, (8, weight.shape[1])))[:, 0:1]


def add_rows(total, pixf, code_s, block, pieces, first_slot, pix_at, count):
    def group(g, _):
        slot = first_slot + g * GROUP
        code_row, lane = block * pieces + slot // LANES, slot % LANES
        at = pix_at + g * GROUP
        head = code_s[code_row, lane]
        clash = head >= CLASH
        places = [jnp.where(clash, head - CLASH, head)] + [code_s[code_row, lane + u] for u in range(1, GROUP)]

        @pl.when(jnp.logical_not(clash))
        def _():
            made = [total[pl.ds(p, 1), :] + pixf[pl.ds(at + u, 1), :] for u, p in enumerate(places)]
            for p, value in zip(places, made):
                total[pl.ds(p, 1), :] = value

        @pl.when(clash)
        def _():
            for u, p in enumerate(places):
                total[pl.ds(p, 1), :] = total[pl.ds(p, 1), :] + pixf[pl.ds(at + u, 1), :]

        return 0

    lax.fori_loop(0, (count + GROUP - 1) // GROUP, group, 0)


def grid_first_kernel(dims, moved_ref, total_ref, code_ref, count_ref, pixf, code_s, count_s, sems):
    time_count, space_count, rows_tm, slot_rows, first_rows, width = dims
    day_dev = DAYS // time_count
    blocks = time_count * space_count
    pieces = width // LANES
    spare = rows_tm * DAYS

    def targets(b, _):
        meta = moved_ref[b, first_rows:, :].astype(jnp.float32)
        weight, local_row, day = (meta_lanes(meta, v, pieces) for v in range(3))
        used = weight > 0.0
        offset = ((b // space_count) * day_dev).astype(jnp.float32)
        code = jnp.where(used, local_row * DAYS + (day + offset), float(spare)).astype(jnp.int32)
        for i in range(pieces):
            code_ref[pl.ds(b * pieces + i, 1), :] = code[:, i * LANES : (i + 1) * LANES]
        count = jnp.sum(jnp.where(used, 1.0, 0.0), axis=1, keepdims=True)
        count_ref[pl.ds(b, 1), :] = jnp.broadcast_to(count, (1, LANES)).astype(jnp.int32)
        return 0

    lax.fori_loop(0, blocks, targets, 0)
    code = code_ref[...]
    within = lax.broadcasted_iota(jnp.int32, code.shape, 1) % GROUP
    clash = jnp.zeros(code.shape, jnp.int32)
    for k in range(1, GROUP):
        ahead = pltpu.roll(code, LANES - k, 1)
        clash = jnp.where((ahead == code) & (within + k < GROUP) & (code < spare), 1, clash)
    k = 1
    while k < GROUP:
        ahead = pltpu.roll(clash, LANES - k, 1)
        clash = jnp.where(within + k < GROUP, jnp.maximum(clash, ahead), clash)
        k *= 2
    code_ref[...] = jnp.where((within == 0) & (clash > 0), code + CLASH, code)
    code_copy = pltpu.make_async_copy(code_ref, code_s, sems.at[0])
    count_copy = pltpu.make_async_copy(count_ref, count_s, sems.at[1])
    code_copy.start()
    count_copy.start()

    def weigh(b, _):
        column = weight_column(moved_ref[b, first_rows:, :].astype(jnp.float32), pieces)[:first_rows]
        at = pl.ds(pl.multiple_of(b * first_rows, 16), first_rows)
        pixf[at, :] = moved_ref[b, :first_rows, :].astype(jnp.float32) * column
        return 0

    lax.fori_loop(0, blocks, weigh, 0)

    def clear(i, _):
        total_ref[pl.ds(pl.multiple_of(i * DAYS, DAYS), DAYS), :] = jnp.zeros((DAYS, LANES), jnp.float32)
        return 0

    lax.fori_loop(0, rows_tm, clear, 0)
    total_ref[spare:, :] = jnp.zeros((8, LANES), jnp.float32)
    code_copy.wait()
    count_copy.wait()

    def add(b, _):
        add_rows(total_ref, pixf, code_s, b, pieces, 0, b * first_rows, jnp.minimum(count_s[b, 0], first_rows))
        return 0

    lax.fori_loop(0, blocks, add, 0)


def grid_last_kernel(
    dims, code_s, count_s, meta_ref, moved_ref, total_in, field_ref, gram_ref, total, pixf, field_v, sems
):
    time_count, space_count, rows_tm, slot_rows, first_rows, width = dims
    blocks = time_count * space_count
    pieces = width // LANES
    last_rows = slot_rows - first_rows
    group = 4
    load = pltpu.make_async_copy(total_in, total, sems.at[0])
    load.start()
    gram_ref[...] = jnp.zeros_like(gram_ref)

    def weigh(b, _):
        @pl.when(count_s[b, 0] > first_rows)
        def _():
            column = weight_column(meta_ref[b].astype(jnp.float32), pieces)[first_rows:slot_rows]
            at = pl.ds(pl.multiple_of(b * last_rows, 16), last_rows)
            pixf[at, :] = moved_ref[b].astype(jnp.float32) * column

        return 0

    lax.fori_loop(0, blocks, weigh, 0)
    load.wait()

    def add(b, _):
        rest = jnp.maximum(count_s[b, 0] - first_rows, 0)
        add_rows(total, pixf, code_s, b, pieces, first_rows, b * last_rows, rest)
        return 0

    lax.fori_loop(0, blocks, add, 0)

    def send(i):
        at = pl.ds(i * group, group)
        return pltpu.make_async_copy(field_v.at[at], field_ref.at[at], sems.at[1])

    def finish(i, _):
        for q in range(group):
            at = pl.ds(pl.multiple_of((i * group + q) * DAYS, DAYS), DAYS)
            field_v[i * group + q] = total[at, :].astype(jnp.bfloat16)
        send(i).start()
        both = jnp.concatenate([field_v[i * group + q] for q in range(group)], axis=1)
        part = lax.dot_general(both[:RANK], both, LAST_LAST, preferred_element_type=jnp.float32)
        for c in range(DAYS // LANES):
            gram_ref[c] += part[:, c * LANES : (c + 1) * LANES]
        return 0

    lax.fori_loop(0, rows_tm // group, finish, 0)
    pltpu.make_async_copy(field_v, field_ref, sems.at[1]).wait()


def grid_rows(moved_first, moved_last, time_count, space_count, rows_tm, slots):
    slot_rows, first_rows = split_rows(slots)
    last_rows = slot_rows - first_rows
    width = round_up(slots, LANES)
    blocks = time_count * space_count
    dims = (time_count, space_count, rows_tm, slot_rows, first_rows, width)
    codes = (blocks * width // LANES, LANES)
    counts = (blocks, LANES)
    sums = (rows_tm * DAYS + 8, LANES)
    params = pltpu.CompilerParams(vmem_limit_bytes=VMEM)
    total, code, count = pl.pallas_call(
        functools.partial(grid_first_kernel, dims),
        out_shape=[
            jax.ShapeDtypeStruct(sums, jnp.float32),
            jax.ShapeDtypeStruct(codes, jnp.int32),
            jax.ShapeDtypeStruct(counts, jnp.int32),
        ],
        scratch_shapes=[
            pltpu.VMEM((blocks * first_rows, LANES), jnp.float32),
            pltpu.SMEM(codes, jnp.int32),
            pltpu.SMEM(counts, jnp.int32),
            pltpu.SemaphoreType.DMA((2,)),
        ],
        compiler_params=params,
        cost_estimate=pl.CostEstimate(flops=0, bytes_accessed=60_000_000, transcendentals=0),
        name="grid_first",
    )(moved_first)
    return pl.pallas_call(
        functools.partial(grid_last_kernel, dims),
        grid=(1,),
        in_specs=[
            pl.BlockSpec(memory_space=pltpu.SMEM),
            pl.BlockSpec(memory_space=pltpu.SMEM),
            pl.BlockSpec((blocks, META_ROWS, LANES), lambda i: (0, first_rows // META_ROWS, 0)),
            pl.BlockSpec((blocks, last_rows, LANES), lambda i: (0, 0, 0)),
            pl.BlockSpec(memory_space=pl.ANY),
        ],
        out_specs=[
            pl.BlockSpec(memory_space=pl.ANY),
            pl.BlockSpec((DAYS // LANES, RANK, LANES), lambda i: (0, 0, 0)),
        ],
        out_shape=[
            jax.ShapeDtypeStruct((rows_tm, DAYS, LANES), jnp.bfloat16),
            jax.ShapeDtypeStruct((DAYS // LANES, RANK, LANES), jnp.float32),
        ],
        scratch_shapes=[
            pltpu.VMEM(sums, jnp.float32),
            pltpu.VMEM((blocks * last_rows, LANES), jnp.float32),
            pltpu.VMEM((rows_tm, DAYS, LANES), jnp.bfloat16),
            pltpu.SemaphoreType.DMA((2,)),
        ],
        compiler_params=params,
        name="grid_last_and_gram",
    )(code, count, moved_first, moved_last, total)


def dot_f32(a, b, dims=(((1,), (0,)), ((), ()))):
    return lax.dot_general(a, b, dims, precision=lax.Precision.HIGHEST, preferred_element_type=jnp.float32)


def dot_three(a, b, dims=(((1,), (0,)), ((), ()))):
    a_high, b_high = a.astype(jnp.bfloat16), b.astype(jnp.bfloat16)
    a_low = (a - a_high.astype(jnp.float32)).astype(jnp.bfloat16)
    b_low = (b - b_high.astype(jnp.float32)).astype(jnp.bfloat16)
    dot = functools.partial(lax.dot_general, dimension_numbers=dims, preferred_element_type=jnp.float32)
    return dot(a_high, b_high) + (dot(a_high, b_low) + dot(a_low, b_high))


def invert(x):
    guess = pl.reciprocal(x, approx=True)
    guess = guess * (2.0 - x * guess)
    return guess * (2.0 - x * guess)


def lower_inverse(a):
    n = a.shape[0]
    full = (8, n)
    tiles = [a[8 * i : 8 * i + 8, :] for i in range(n // 8)]
    lane = lax.broadcasted_iota(jnp.int32, full, 1)
    down = lax.broadcasted_iota(jnp.int32, full, 0)
    out = []
    for t in range(n // 8):
        k = 8 * t
        block = (lane >= k) & (lane < k + 8)
        panel = tiles[t]
        cols = [jnp.broadcast_to(panel[:, k + c : k + c + 1], full) for c in range(8)]
        e = {(i, c): jnp.broadcast_to(cols[c][i : i + 1, :], full) for c in range(8) for i in range(c, 8)}
        start = jnp.where(block, jnp.where(lane == k + down, 1.0, 0.0), panel)
        rows = [jnp.broadcast_to(start[i : i + 1, :], full) for i in range(8)]
        held = []
        for s in range(0, 8, 2):
            p, q, r = e[s, s], e[s + 1, s], e[s + 1, s + 1]
            det = p * r - q * q
            inv = invert(det)
            factors = {}
            for i in range(s + 2, 8):
                x, y = e[i, s], e[i, s + 1]
                factors[i] = (r * x - q * y, p * y - q * x)
            for i in range(s + 2, 8):
                u, v = factors[i]
                for c in range(s + 2, i + 1):
                    e[i, c] = e[i, c] - (u * e[c, s] + v * e[c, s + 1]) * inv
                rows[i] = rows[i] - (u * rows[s] + v * rows[s + 1]) * inv
            held.append((p, q, r, det, inv, factors))
        done = jnp.zeros(full, jnp.float32)
        solved = [None] * 8
        for s in (6, 4, 2, 0):
            p, q, r, det, inv, factors = held[s // 2]
            root = lax.rsqrt(p)
            done = jnp.where(down == s, rows[s] * root, done)
            done = jnp.where(down == s + 1, (rows[s + 1] * p - q * rows[s]) * (root * lax.rsqrt(det)), done)
            first, second = r * rows[s] - q * rows[s + 1], p * rows[s + 1] - q * rows[s]
            for i in range(s + 2, 8):
                u, v = factors[i]
                first, second = first - u * solved[i], second - v * solved[i]
            solved[s], solved[s + 1] = first * inv, second * inv
        out.append(jnp.where(lane < k + 8, done, 0.0))
        for i in range(t + 1, n // 8):
            terms = [jnp.broadcast_to(tiles[i][:, k + c : k + c + 1], full) * solved[c] for c in range(8)]
            while len(terms) > 1:
                terms = [terms[j] + terms[j + 1] for j in range(0, len(terms), 2)]
            tiles[i] = jnp.where(block, 0.0, tiles[i]) - terms[0]
    return jnp.concatenate(out, axis=0)


def solve_kernel(scale, gram_ref, field_ref, basis_ref, prop_ref, field_v, basis_v, sems):
    h = LANES
    pieces = DAYS // h
    grid_rows_here = field_v.shape[0]
    load = pltpu.make_async_copy(field_ref.at[:, pl.ds(0, RANK), :], field_v, sems.at[0])
    load.start()

    eye = lax.broadcasted_iota(jnp.int32, (h, h), 0) == lax.broadcasted_iota(jnp.int32, (h, h), 1)
    a11, a12, a22 = gram_ref[0, :h, :], gram_ref[1, :h, :], gram_ref[1, h:, :]
    size_col, size_row = [], []
    for part in (a11, a22):
        diag = jnp.where(eye, part, 0.0)
        size_col.append(lax.rsqrt(jnp.sum(diag, axis=1, keepdims=True)))
        size_row.append(lax.rsqrt(jnp.sum(diag, axis=0, keepdims=True)))
    x1 = lower_inverse(a11 * size_col[0] * size_row[0])
    r12 = dot_f32(x1, a12 * size_col[0] * size_row[1])
    x2 = lower_inverse(a22 * size_col[1] * size_row[1] - dot_f32(r12, r12, FIRST_FIRST))
    mixed = -dot_f32(x2, dot_f32(r12, x1, FIRST_FIRST))
    lower = jnp.concatenate(
        [
            jnp.concatenate([x1 * size_row[0], jnp.zeros((h, h), jnp.float32)], axis=1),
            jnp.concatenate([mixed * size_row[0], x2 * size_row[1]], axis=1),
        ],
        axis=0,
    )
    inverse = (scale * lower).astype(jnp.bfloat16)
    load.wait()

    def project(i, _):
        both = jnp.concatenate([field_v[2 * i], field_v[2 * i + 1]], axis=1)
        made = jnp.dot(inverse, both, preferred_element_type=jnp.float32).astype(jnp.bfloat16)
        basis_v[2 * i] = made[:, :h]
        basis_v[2 * i + 1] = made[:, h:]
        return 0

    lax.fori_loop(0, grid_rows_here // 2, project, 0)
    store = pltpu.make_async_copy(basis_v, basis_ref, sems.at[1])
    store.start()

    down = lax.broadcasted_iota(jnp.int32, (RANK, DAYS), 0)
    across = lax.broadcasted_iota(jnp.int32, (RANK, DAYS), 1)
    gram = jnp.concatenate([gram_ref[i] for i in range(pieces)], axis=1)
    factor = jnp.where(across >= down, dot_f32(lower, gram), 0.0)
    ahead = jnp.where(across < DAYS - 1, pltpu.roll(factor, DAYS - 1, 1), 0.0)
    cross = dot_three(ahead, factor, LAST_LAST)
    polar = cross / jnp.sqrt(jnp.sum(cross * cross) + 1e-06)
    for _ in range(ITERS):
        square = dot_three(polar, polar, LAST_LAST)
        polar = 1.5 * polar - 0.5 * dot_three(square, polar)
    prop_ref[...] = math.sqrt(RANK) * polar
    store.wait()


def solve(gram, field, cell_total):
    rows_tm = field.shape[0]
    part = (rows_tm, RANK, LANES)
    return pl.pallas_call(
        functools.partial(solve_kernel, math.sqrt(cell_total)),
        in_specs=[pl.BlockSpec(memory_space=pltpu.VMEM), pl.BlockSpec(memory_space=pl.ANY)],
        out_specs=[pl.BlockSpec(memory_space=pl.ANY), pl.BlockSpec(memory_space=pltpu.VMEM)],
        out_shape=[
            jax.ShapeDtypeStruct(part, jnp.bfloat16),
            jax.ShapeDtypeStruct((RANK, RANK), jnp.float32),
        ],
        scratch_shapes=[
            pltpu.VMEM(part, jnp.bfloat16),
            pltpu.VMEM(part, jnp.bfloat16),
            pltpu.SemaphoreType.DMA((2,)),
        ],
        compiler_params=pltpu.CompilerParams(vmem_limit_bytes=VMEM),
        name="factor_basis_and_polar",
    )(gram, field)


def body(pixels, weights, tile_index, tile_row, granule_day):
    swath_rows = pixels.shape[0]
    width = pixels.shape[1]
    space_count = lax.axis_size("space")
    time_count = lax.axis_size("tm")
    dest_count = time_count * space_count
    rows_tm = GR_DEV // time_count
    slots = 2 * swath_rows // space_count // time_count
    axes = ("tm", "space")
    first, last = pack(pixels, weights, tile_index, tile_row, granule_day, time_count, space_count, rows_tm, slots)
    first = lax.all_to_all(first, axes, split_axis=0, concat_axis=0, tiled=True)
    last = lax.all_to_all(last, axes, split_axis=0, concat_axis=0, tiled=True)
    field, partial_gram = grid_rows(first, last, time_count, space_count, rows_tm, slots)
    pieces = partial_gram.reshape(dest_count, -1, LANES)
    pieces = lax.all_to_all(pieces, axes, split_axis=0, concat_axis=0, tiled=True)
    mine = jnp.sum(pieces, axis=0, keepdims=True)
    gram = lax.all_to_all(jnp.broadcast_to(mine, pieces.shape), axes, split_axis=0, concat_axis=0, tiled=True)
    cell_total = space_count * GR_DEV * width
    basis, propagator = solve(gram.reshape(partial_gram.shape), field, cell_total)
    return (field[None], basis[None], propagator)


def solution(mesh):
    placed = (
        P(("tm", "space"), None),
        P(("tm", "space")),
        P(("tm", "space")),
        P(("tm", "space")),
        P(("tm", "space")),
    )
    return jax.shard_map(
        body,
        mesh=mesh,
        in_specs=placed,
        out_specs=(P("space", "tm", None, None), P("space", "tm", None, None), P()),
        check_vma=False,
    )
```

```python
import functools
import math

import jax
import jax.numpy as jnp
from jax import lax
from jax.experimental import pallas as pl
from jax.experimental.pallas import tpu as pltpu
from jax.sharding import PartitionSpec as P

GR_DEV = 160
DAYS = 512
RANK = 256
ITERS = 8
LANES = 128
META_ROWS = 16
GROUP = 16
CLASH = 1 << 20
STEPS = 5
VMEM = 56 * 1024 * 1024

LAST_LAST = (((1,), (1,)), ((), ()))
FIRST_FIRST = (((0,), (0,)), ((), ()))


def round_up(value, unit):
    return -(-value // unit) * unit


def split_rows(slots):
    rows = round_up(slots, 16)
    return rows, round_up(rows * 3 // 5, 16)


def pack_kernel(
    dims, tile_ref, row_ref, day_ref, weight_ref, pix_ref, first_ref, last_ref, pos_v, pos_s, rows_v, meta_v, pixf, outf, mrow, sem
):
    time_count, space_count, rows_tm, slot_rows, first_rows, width = dims
    dest_count = time_count * space_count
    chunks = tile_ref.shape[0]
    pieces = width // LANES

    tile = tile_ref[...]
    row = row_ref[...]
    group = jnp.zeros_like(row)
    for k in range(1, time_count):
        group = group + jnp.where(row >= k * rows_tm, 1, 0)
    dest_all = group * space_count + tile
    rows_v[0] = dest_all.astype(jnp.float32)
    rows_v[2] = weight_ref[...].astype(jnp.float32)
    rows_v[3] = (row - group * rows_tm).astype(jnp.float32)
    rows_v[4] = day_ref[...].astype(jnp.float32)

    dest_iota = lax.broadcasted_iota(jnp.int32, (dest_count, LANES), 0)
    upper = jnp.where(
        lax.broadcasted_iota(jnp.int32, (LANES, LANES), 0) <= lax.broadcasted_iota(jnp.int32, (LANES, LANES), 1), 1.0, 0.0
    ).astype(jnp.bfloat16)
    carry = jnp.zeros((dest_count, 1), jnp.float32)
    for c in range(chunks):
        hot = dest_iota == dest_all[c : c + 1, :]
        prefix = jnp.dot(jnp.where(hot, 1.0, 0.0).astype(jnp.bfloat16), upper, preferred_element_type=jnp.float32)
        rows_v[1, c : c + 1, :] = jnp.sum(jnp.where(hot, prefix + carry, 0.0), axis=0, keepdims=True) - 1.0
        carry = carry + prefix[:, LANES - 1 : LANES]
    pos_v[...] = dest_all * slot_rows + rows_v[1].astype(jnp.int32)
    copy = pltpu.make_async_copy(pos_v, pos_s, sem)
    copy.start()
    meta_v[...] = jnp.zeros_like(meta_v)
    mrow[...] = jnp.zeros_like(mrow)

    def clear(b, _):
        outf[pl.ds(pl.multiple_of(b * slot_rows, 16), slot_rows), :] = jnp.zeros((slot_rows, LANES), jnp.float32)
        return 0

    lax.fori_loop(0, dest_count, clear, 0)
    copy.wait()
    dest_number = dest_iota.astype(jnp.float32)
    slot_number = lax.broadcasted_iota(jnp.int32, (width, LANES), 0).astype(jnp.float32)

    def move(c, _):
        base = pl.multiple_of(c * LANES, LANES)
        pixf[pl.ds(base, LANES), :] = pix_ref[pl.ds(base, LANES), :].astype(jnp.float32)
        dest, rank, weight, local_row, day = (rows_v[v, pl.ds(c, 1), :] for v in range(5))
        hot = dest_number == dest
        place = jnp.where(slot_number == rank, 1.0, 0.0).astype(jnp.bfloat16)
        values = jnp.concatenate([jnp.where(hot, v, 0.0) for v in (weight, local_row, day)], axis=0).astype(jnp.bfloat16)
        meta_v[...] += lax.dot_general(values, place, LAST_LAST, preferred_element_type=jnp.float32)
        for lane in range(LANES):
            outf[pl.ds(pos_s[c, lane], 1), :] = pixf[pl.ds(base + lane, 1), :]
        return 0

    lax.fori_loop(0, chunks, move, 0)
    for v in range(3):
        for i in range(pieces):
            mrow[pl.ds(v * pieces + i, dest_count, stride=META_ROWS), :] = meta_v[
                v * dest_count : (v + 1) * dest_count, i * LANES : (i + 1) * LANES
            ]

    def narrow(b, _):
        at = pl.multiple_of(b * slot_rows, 16)
        first_ref[b, :first_rows, :] = outf[pl.ds(at, first_rows), :].astype(jnp.bfloat16)
        first_ref[b, first_rows:, :] = mrow[pl.ds(pl.multiple_of(b * META_ROWS, 16), META_ROWS), :].astype(jnp.bfloat16)
        last_ref[b] = outf[pl.ds(at + first_rows, slot_rows - first_rows), :].astype(jnp.bfloat16)
        return 0

    lax.fori_loop(0, dest_count, narrow, 0)


def pack(pixels, weights, tile_index, tile_row, granule_day, time_count, space_count, rows_tm, slots):
    swath_rows = pixels.shape[0]
    chunks = swath_rows // LANES
    dest_count = time_count * space_count
    slot_rows, first_rows = split_rows(slots)
    width = round_up(slots, LANES)
    shape = (chunks, LANES)
    return pl.pallas_call(
        functools.partial(pack_kernel, (time_count, space_count, rows_tm, slot_rows, first_rows, width)),
        out_shape=[
            jax.ShapeDtypeStruct((dest_count, first_rows + META_ROWS, LANES), jnp.bfloat16),
            jax.ShapeDtypeStruct((dest_count, slot_rows - first_rows, LANES), jnp.bfloat16),
        ],
        scratch_shapes=[
            pltpu.VMEM(shape, jnp.int32),
            pltpu.SMEM(shape, jnp.int32),
            pltpu.VMEM((5,) + shape, jnp.float32),
            pltpu.VMEM((3 * dest_count, width), jnp.float32),
            pltpu.VMEM((swath_rows, LANES), jnp.float32),
            pltpu.VMEM((dest_count * slot_rows, LANES), jnp.float32),
            pltpu.VMEM((dest_count * META_ROWS, LANES), jnp.float32),
            pltpu.SemaphoreType.DMA,
        ],
        compiler_params=pltpu.CompilerParams(vmem_limit_bytes=VMEM),
        name="pack",
    )(
        tile_index.reshape(shape),
        tile_row.reshape(shape),
        granule_day.reshape(shape),
        weights.reshape(shape),
        pixels,
    )


def chunk_of(rows):
    return max(c for c in (32, 16) if rows % c == 0)


def add_rows(total, pixf, code_s, code_row, first_slot, rows, pix_at, count):
    chunk = chunk_of(rows)

    def add_group(row, lane, at):
        places = [code_s[row, lane + u] for u in range(GROUP)]
        made = [total[pl.ds(p, 1), :] + pixf[pl.ds(at + u, 1), :] for u, p in enumerate(places)]
        for p, value in zip(places, made):
            total[pl.ds(p, 1), :] = value

    def add_singly(row, lane, at):
        def one(u, _):
            p = code_s[row, lane + u]
            p = jnp.where(p >= CLASH, p - CLASH, p)
            total[pl.ds(p, 1), :] = total[pl.ds(p, 1), :] + pixf[pl.ds(at + u, 1), :]
            return 0

        lax.fori_loop(0, GROUP, one, 0)

    for start in range(0, rows, chunk):
        slot = first_slot + start
        row, lane = code_row(slot // LANES), slot % LANES
        at = pix_at + start
        heads = [code_s[row, lane + g] for g in range(0, chunk, GROUP)]
        clash = functools.reduce(jnp.maximum, heads) >= CLASH

        @pl.when((count > start) & jnp.logical_not(clash))
        def _():
            for g in range(0, chunk, GROUP):
                add_group(row, lane + g, at + g)

        @pl.when((count > start) & clash)
        def _():
            for g, head in zip(range(0, chunk, GROUP), heads):
                pl.when(head < CLASH)(functools.partial(add_group, row, lane + g, at + g))
                pl.when(head >= CLASH)(functools.partial(add_singly, row, lane + g, at + g))


def grid_first_kernel(
    dims, moved_ref, total_ref, code_ref, count_ref, column_ref, meta_v, pixf, code_s, count_s, sems
):
    time_count, space_count, rows_tm, slot_rows, first_rows, width = dims
    day_dev = DAYS // time_count
    blocks = time_count * space_count
    pieces = width // LANES
    spare = rows_tm * DAYS

    meta_v[...] = moved_ref[:, first_rows:, :].astype(jnp.float32).reshape(blocks * META_ROWS, LANES)
    block = lax.broadcasted_iota(jnp.int32, (blocks, LANES), 0)
    offset = jnp.zeros((blocks, LANES), jnp.float32)
    for m in range(1, time_count):
        offset = offset + jnp.where(block >= m * space_count, float(day_dev), 0.0)
    within = lax.broadcasted_iota(jnp.int32, (blocks, LANES), 1) % GROUP
    count = jnp.zeros((blocks, 1), jnp.float32)
    for i in range(pieces):
        weight, local_row, day = (meta_v[pl.ds(v * pieces + i, blocks, stride=META_ROWS), :] for v in range(3))
        used = weight > 0.0
        count = count + jnp.sum(jnp.where(used, 1.0, 0.0), axis=1, keepdims=True)
        column_ref[i * LANES : (i + 1) * LANES, :] = jnp.transpose(weight)
        code = jnp.where(used, local_row * DAYS + (day + offset), float(spare)).astype(jnp.int32)
        clash = jnp.zeros(code.shape, jnp.int32)
        for k in range(1, GROUP):
            ahead = pltpu.roll(code, LANES - k, 1)
            clash = jnp.where((ahead == code) & (within + k < GROUP) & (code < spare), 1, clash)
        k = 1
        while k < GROUP:
            ahead = pltpu.roll(clash, LANES - k, 1)
            clash = jnp.where(within + k < GROUP, jnp.maximum(clash, ahead), clash)
            k *= 2
        code_ref[i * blocks : (i + 1) * blocks, :] = jnp.where((within == 0) & (clash > 0), code + CLASH, code)
    count_ref[...] = jnp.broadcast_to(count, (blocks, LANES)).astype(jnp.int32)
    code_copy = pltpu.make_async_copy(code_ref, code_s, sems.at[0])
    count_copy = pltpu.make_async_copy(count_ref, count_s, sems.at[1])
    code_copy.start()
    count_copy.start()

    for b in range(blocks):
        column = column_ref[:first_rows, b : b + 1]
        pixf[b * first_rows : (b + 1) * first_rows, :] = moved_ref[b, :first_rows, :].astype(jnp.float32) * column

    def clear(i, _):
        total_ref[pl.ds(pl.multiple_of(i * DAYS, DAYS), DAYS), :] = jnp.zeros((DAYS, LANES), jnp.float32)
        return 0

    lax.fori_loop(0, rows_tm, clear, 0)
    total_ref[spare:, :] = jnp.zeros((8, LANES), jnp.float32)
    code_copy.wait()
    count_copy.wait()

    def add(b, _):
        add_rows(total_ref, pixf, code_s, lambda i: i * blocks + b, 0, first_rows, b * first_rows, count_s[b, 0])
        return 0

    lax.fori_loop(0, blocks, add, 0)


def grid_last_kernel(
    dims, code_s, count_s, column_ref, moved_ref, total_in, field_ref, gram_ref, total, pixf, field_v, sems
):
    time_count, space_count, rows_tm, slot_rows, first_rows, width = dims
    blocks = time_count * space_count
    last_rows = slot_rows - first_rows
    group = rows_tm // STEPS
    load = pltpu.make_async_copy(total_in, total, sems.at[0])
    load.start()
    gram_ref[...] = jnp.zeros_like(gram_ref)

    for b in range(blocks):

        @pl.when(count_s[b, 0] > first_rows)
        def _():
            column = column_ref[first_rows:slot_rows, b : b + 1]
            pixf[b * last_rows : (b + 1) * last_rows, :] = moved_ref[b].astype(jnp.float32) * column

    load.wait()

    def add(b, _):
        rest = count_s[b, 0] - first_rows

        @pl.when(rest > 0)
        def _():
            add_rows(total, pixf, code_s, lambda i: i * blocks + b, first_rows, last_rows, b * last_rows, rest)

        return 0

    lax.fori_loop(0, blocks, add, 0)

    def send(i):
        at = pl.ds(i * group, group)
        return pltpu.make_async_copy(field_v.at[at], field_ref.at[at], sems.at[1])

    def finish(i, _):
        for q in range(group):
            at = pl.ds(pl.multiple_of((i * group + q) * DAYS, DAYS), DAYS)
            field_v[i * group + q] = total[at, :].astype(jnp.bfloat16)
        send(i).start()
        both = jnp.concatenate([field_v[i * group + q] for q in range(group)], axis=1)
        part = lax.dot_general(both[:RANK], both, LAST_LAST, preferred_element_type=jnp.float32)
        for c in range(DAYS // LANES):
            gram_ref[c] += part[:, c * LANES : (c + 1) * LANES]
        return 0

    lax.fori_loop(0, STEPS, finish, 0)
    pltpu.make_async_copy(field_v, field_ref, sems.at[1]).wait()


def grid_rows(moved_first, moved_last, time_count, space_count, rows_tm, slots):
    slot_rows, first_rows = split_rows(slots)
    last_rows = slot_rows - first_rows
    width = round_up(slots, LANES)
    blocks = time_count * space_count
    dims = (time_count, space_count, rows_tm, slot_rows, first_rows, width)
    codes = (blocks * width // LANES, LANES)
    counts = (blocks, LANES)
    sums = (rows_tm * DAYS + 8, LANES)
    params = pltpu.CompilerParams(vmem_limit_bytes=VMEM)
    columns = (width, blocks)
    total, code, count, column = pl.pallas_call(
        functools.partial(grid_first_kernel, dims),
        out_shape=[
            jax.ShapeDtypeStruct(sums, jnp.float32),
            jax.ShapeDtypeStruct(codes, jnp.int32),
            jax.ShapeDtypeStruct(counts, jnp.int32),
            jax.ShapeDtypeStruct(columns, jnp.float32),
        ],
        scratch_shapes=[
            pltpu.VMEM((blocks * META_ROWS, LANES), jnp.float32),
            pltpu.VMEM((blocks * first_rows, LANES), jnp.float32),
            pltpu.SMEM(codes, jnp.int32),
            pltpu.SMEM(counts, jnp.int32),
            pltpu.SemaphoreType.DMA((2,)),
        ],
        compiler_params=params,
        cost_estimate=pl.CostEstimate(flops=0, bytes_accessed=60_000_000, transcendentals=0),
        name="grid_first",
    )(moved_first)
    return pl.pallas_call(
        functools.partial(grid_last_kernel, dims),
        in_specs=[
            pl.BlockSpec(memory_space=pltpu.SMEM),
            pl.BlockSpec(memory_space=pltpu.SMEM),
            pl.BlockSpec(memory_space=pltpu.VMEM),
            pl.BlockSpec(memory_space=pltpu.VMEM),
            pl.BlockSpec(memory_space=pl.ANY),
        ],
        out_specs=[
            pl.BlockSpec(memory_space=pl.ANY),
            pl.BlockSpec(memory_space=pltpu.VMEM),
        ],
        out_shape=[
            jax.ShapeDtypeStruct((rows_tm, DAYS, LANES), jnp.bfloat16),
            jax.ShapeDtypeStruct((DAYS // LANES, RANK, LANES), jnp.float32),
        ],
        scratch_shapes=[
            pltpu.VMEM(sums, jnp.float32),
            pltpu.VMEM((blocks * last_rows, LANES), jnp.float32),
            pltpu.VMEM((rows_tm, DAYS, LANES), jnp.bfloat16),
            pltpu.SemaphoreType.DMA((2,)),
        ],
        compiler_params=params,
        name="grid_last_and_gram",
    )(code, count, column, moved_last, total)


def dot_f32(a, b, dims=(((1,), (0,)), ((), ()))):
    return lax.dot_general(a, b, dims, precision=lax.Precision.HIGHEST, preferred_element_type=jnp.float32)


def dot_three(a, b, dims=(((1,), (0,)), ((), ()))):
    a_high, b_high = a.astype(jnp.bfloat16), b.astype(jnp.bfloat16)
    a_low = (a - a_high.astype(jnp.float32)).astype(jnp.bfloat16)
    b_low = (b - b_high.astype(jnp.float32)).astype(jnp.bfloat16)
    left, right = dims[0][0][0], dims[0][1][0]
    a_all = jnp.concatenate([a_high, a_high, a_low], axis=left)
    b_all = jnp.concatenate([b_high, b_low, b_high], axis=right)
    return lax.dot_general(a_all, b_all, dims, preferred_element_type=jnp.float32)


def invert(x):
    guess = pl.reciprocal(x, approx=True)
    guess = guess * (2.0 - x * guess)
    return guess * (2.0 - x * guess)


def lower_inverse(a):
    n = a.shape[0]
    full = (8, n)
    tiles = [a[8 * i : 8 * i + 8, :] for i in range(n // 8)]
    lane = lax.broadcasted_iota(jnp.int32, full, 1)
    down = lax.broadcasted_iota(jnp.int32, full, 0)
    out = []
    for t in range(n // 8):
        k = 8 * t
        block = (lane >= k) & (lane < k + 8)
        panel = tiles[t]
        cols = [jnp.broadcast_to(panel[:, k + c : k + c + 1], full) for c in range(8)]
        e = {(i, c): jnp.broadcast_to(cols[c][i : i + 1, :], full) for c in range(8) for i in range(c, 8)}
        start = jnp.where(block, jnp.where(lane == k + down, 1.0, 0.0), panel)
        rows = [jnp.broadcast_to(start[i : i + 1, :], full) for i in range(8)]
        held = []
        for s in range(0, 8, 2):
            p, q, r = e[s, s], e[s + 1, s], e[s + 1, s + 1]
            det = p * r - q * q
            inv = invert(det)
            factors = {}
            for i in range(s + 2, 8):
                x, y = e[i, s], e[i, s + 1]
                factors[i] = (r * x - q * y, p * y - q * x)
            for i in range(s + 2, 8):
                u, v = factors[i]
                for c in range(s + 2, i + 1):
                    e[i, c] = e[i, c] - (u * e[c, s] + v * e[c, s + 1]) * inv
                rows[i] = rows[i] - (u * rows[s] + v * rows[s + 1]) * inv
            held.append((p, q, r, det, inv, factors))
        done = jnp.zeros(full, jnp.float32)
        solved = [None] * 8
        for s in (6, 4, 2, 0):
            p, q, r, det, inv, factors = held[s // 2]
            root = lax.rsqrt(p)
            done = jnp.where(down == s, rows[s] * root, done)
            done = jnp.where(down == s + 1, (rows[s + 1] * p - q * rows[s]) * (root * lax.rsqrt(det)), done)
            first, second = r * rows[s] - q * rows[s + 1], p * rows[s + 1] - q * rows[s]
            for i in range(s + 2, 8):
                u, v = factors[i]
                first, second = first - u * solved[i], second - v * solved[i]
            solved[s], solved[s + 1] = first * inv, second * inv
        out.append(jnp.where(lane < k + 8, done, 0.0))
        for i in range(t + 1, n // 8):
            terms = [jnp.broadcast_to(tiles[i][:, k + c : k + c + 1], full) * solved[c] for c in range(8)]
            while len(terms) > 1:
                terms = [terms[j] + terms[j + 1] for j in range(0, len(terms), 2)]
            tiles[i] = jnp.where(block, 0.0, tiles[i]) - terms[0]
    return jnp.concatenate(out, axis=0)


def solve_kernel(scale, gram_ref, field_ref, basis_ref, prop_ref, field_v, basis_v, sems):
    h = LANES
    pieces = DAYS // h
    group = field_v.shape[0] // STEPS
    load = pltpu.make_async_copy(field_ref.at[:, pl.ds(0, RANK), :], field_v, sems.at[0])
    load.start()

    eye = lax.broadcasted_iota(jnp.int32, (h, h), 0) == lax.broadcasted_iota(jnp.int32, (h, h), 1)
    a11, a12, a22 = gram_ref[0, :h, :], gram_ref[1, :h, :], gram_ref[1, h:, :]
    size_col, size_row = [], []
    for part in (a11, a22):
        diag = jnp.where(eye, part, 0.0)
        size_col.append(lax.rsqrt(jnp.sum(diag, axis=1, keepdims=True)))
        size_row.append(lax.rsqrt(jnp.sum(diag, axis=0, keepdims=True)))
    x1 = lower_inverse(a11 * size_col[0] * size_row[0])
    r12 = dot_f32(x1, a12 * size_col[0] * size_row[1])
    x2 = lower_inverse(a22 * size_col[1] * size_row[1] - dot_f32(r12, r12, FIRST_FIRST))
    mixed = -dot_f32(x2, dot_f32(r12, x1, FIRST_FIRST))
    lower = jnp.concatenate(
        [
            jnp.concatenate([x1 * size_row[0], jnp.zeros((h, h), jnp.float32)], axis=1),
            jnp.concatenate([mixed * size_row[0], x2 * size_row[1]], axis=1),
        ],
        axis=0,
    )
    inverse = (scale * lower).astype(jnp.bfloat16)
    load.wait()

    def project(i, _):
        both = jnp.concatenate([field_v[i * group + q] for q in range(group)], axis=1)
        made = jnp.dot(inverse, both, preferred_element_type=jnp.float32).astype(jnp.bfloat16)
        for q in range(group):
            basis_v[i * group + q] = made[:, q * h : (q + 1) * h]
        return 0

    lax.fori_loop(0, STEPS, project, 0)
    store = pltpu.make_async_copy(basis_v, basis_ref, sems.at[1])
    store.start()

    down = lax.broadcasted_iota(jnp.int32, (RANK, DAYS), 0)
    across = lax.broadcasted_iota(jnp.int32, (RANK, DAYS), 1)
    gram = jnp.concatenate([gram_ref[i] for i in range(pieces)], axis=1)
    factor = jnp.where(across >= down, dot_f32(lower, gram), 0.0)
    ahead = jnp.where(across < DAYS - 1, pltpu.roll(factor, DAYS - 1, 1), 0.0)
    cross = dot_three(ahead, factor, LAST_LAST)
    polar = cross / jnp.sqrt(jnp.sum(cross * cross) + 1e-06)
    for _ in range(ITERS):
        square = dot_three(polar, polar, LAST_LAST)
        polar = 1.5 * polar - 0.5 * dot_three(square, polar)
    prop_ref[...] = math.sqrt(RANK) * polar
    store.wait()


def solve(gram, field, cell_total):
    rows_tm = field.shape[0]
    part = (rows_tm, RANK, LANES)
    return pl.pallas_call(
        functools.partial(solve_kernel, math.sqrt(cell_total)),
        in_specs=[pl.BlockSpec(memory_space=pltpu.VMEM), pl.BlockSpec(memory_space=pl.ANY)],
        out_specs=[pl.BlockSpec(memory_space=pl.ANY), pl.BlockSpec(memory_space=pltpu.VMEM)],
        out_shape=[
            jax.ShapeDtypeStruct(part, jnp.bfloat16),
            jax.ShapeDtypeStruct((RANK, RANK), jnp.float32),
        ],
        scratch_shapes=[
            pltpu.VMEM(part, jnp.bfloat16),
            pltpu.VMEM(part, jnp.bfloat16),
            pltpu.SemaphoreType.DMA((2,)),
        ],
        compiler_params=pltpu.CompilerParams(vmem_limit_bytes=VMEM),
        name="factor_basis_and_polar",
    )(gram, field)


def body(pixels, weights, tile_index, tile_row, granule_day):
    swath_rows = pixels.shape[0]
    width = pixels.shape[1]
    space_count = lax.axis_size("space")
    time_count = lax.axis_size("tm")
    dest_count = time_count * space_count
    rows_tm = GR_DEV // time_count
    slots = 2 * swath_rows // space_count // time_count
    axes = ("tm", "space")
    first, last = pack(pixels, weights, tile_index, tile_row, granule_day, time_count, space_count, rows_tm, slots)
    first = lax.all_to_all(first, axes, split_axis=0, concat_axis=0, tiled=True)
    last = lax.all_to_all(last, axes, split_axis=0, concat_axis=0, tiled=True)
    field, partial_gram = grid_rows(first, last, time_count, space_count, rows_tm, slots)
    pieces = partial_gram.reshape(dest_count, -1, LANES)
    pieces = lax.all_to_all(pieces, axes, split_axis=0, concat_axis=0, tiled=True)
    mine = jnp.sum(pieces, axis=0, keepdims=True)
    gram = lax.all_to_all(jnp.broadcast_to(mine, pieces.shape), axes, split_axis=0, concat_axis=0, tiled=True)
    cell_total = space_count * GR_DEV * width
    basis, propagator = solve(gram.reshape(partial_gram.shape), field, cell_total)
    return (field[None], basis[None], propagator)


def solution(mesh):
    placed = (
        P(("tm", "space"), None),
        P(("tm", "space")),
        P(("tm", "space")),
        P(("tm", "space")),
        P(("tm", "space")),
    )
    return jax.shard_map(
        body,
        mesh=mesh,
        in_specs=placed,
        out_specs=(P("space", "tm", None, None), P("space", "tm", None, None), P()),
        check_vma=False,
    )
```

```python
import functools
import math

import jax
import jax.numpy as jnp
from jax import lax
from jax.experimental import pallas as pl
from jax.experimental.pallas import tpu as pltpu
from jax.sharding import PartitionSpec as P

GR_DEV = 160
DAYS = 512
RANK = 256
ITERS = 8
LANES = 128
META_ROWS = 16
GROUP = 16
CLASH = 1 << 20
STEPS = 5
VMEM = 56 * 1024 * 1024

LAST_LAST = (((1,), (1,)), ((), ()))
FIRST_FIRST = (((0,), (0,)), ((), ()))


def round_up(value, unit):
    return -(-value // unit) * unit


def split_rows(slots):
    rows = round_up(slots, 16)
    return rows, round_up(rows * 3 // 5, 16)


def pack_kernel(
    dims, tile_ref, row_ref, day_ref, weight_ref, pix_ref, first_ref, last_ref, pos_v, pos_s, rows_v, meta_v, pixf, outf, mrow,
    first_v, last_v, sems
):
    time_count, space_count, rows_tm, slot_rows, first_rows, width = dims
    dest_count = time_count * space_count
    chunks = tile_ref.shape[0]
    pieces = width // LANES

    tile = tile_ref[...]
    row = row_ref[...]
    group = jnp.zeros_like(row)
    for k in range(1, time_count):
        group = group + jnp.where(row >= k * rows_tm, 1, 0)
    dest_all = group * space_count + tile
    rows_v[0] = dest_all.astype(jnp.float32)
    rows_v[2] = weight_ref[...].astype(jnp.float32)
    rows_v[3] = (row - group * rows_tm).astype(jnp.float32)
    rows_v[4] = day_ref[...].astype(jnp.float32)

    dest_iota = lax.broadcasted_iota(jnp.int32, (dest_count, LANES), 0)
    upper = jnp.where(
        lax.broadcasted_iota(jnp.int32, (LANES, LANES), 0) <= lax.broadcasted_iota(jnp.int32, (LANES, LANES), 1), 1.0, 0.0
    ).astype(jnp.bfloat16)
    carry = jnp.zeros((dest_count, 1), jnp.float32)
    for c in range(chunks):
        hot = dest_iota == dest_all[c : c + 1, :]
        prefix = jnp.dot(jnp.where(hot, 1.0, 0.0).astype(jnp.bfloat16), upper, preferred_element_type=jnp.float32)
        rows_v[1, c : c + 1, :] = jnp.sum(jnp.where(hot, prefix + carry, 0.0), axis=0, keepdims=True) - 1.0
        carry = carry + prefix[:, LANES - 1 : LANES]
    pos_v[...] = dest_all * slot_rows + rows_v[1].astype(jnp.int32)
    copy = pltpu.make_async_copy(pos_v, pos_s, sems.at[0])
    copy.start()
    meta_v[...] = jnp.zeros_like(meta_v)
    mrow[...] = jnp.zeros_like(mrow)

    def clear(b, _):
        outf[pl.ds(pl.multiple_of(b * slot_rows, 16), slot_rows), :] = jnp.zeros((slot_rows, LANES), jnp.float32)
        return 0

    lax.fori_loop(0, dest_count, clear, 0)
    copy.wait()
    dest_number = dest_iota.astype(jnp.float32)
    slot_number = lax.broadcasted_iota(jnp.int32, (width, LANES), 0).astype(jnp.float32)

    def move(c, _):
        base = pl.multiple_of(c * LANES, LANES)
        pixf[pl.ds(base, LANES), :] = pix_ref[pl.ds(base, LANES), :].astype(jnp.float32)
        dest, rank, weight, local_row, day = (rows_v[v, pl.ds(c, 1), :] for v in range(5))
        hot = dest_number == dest
        place = jnp.where(slot_number == rank, 1.0, 0.0).astype(jnp.bfloat16)
        values = jnp.concatenate([jnp.where(hot, v, 0.0) for v in (weight, local_row, day)], axis=0).astype(jnp.bfloat16)
        meta_v[...] += lax.dot_general(values, place, LAST_LAST, preferred_element_type=jnp.float32)
        for lane in range(LANES):
            outf[pl.ds(pos_s[c, lane], 1), :] = pixf[pl.ds(base + lane, 1), :]
        return 0

    lax.fori_loop(0, chunks, move, 0)
    for v in range(3):
        for i in range(pieces):
            mrow[pl.ds(v * pieces + i, dest_count, stride=META_ROWS), :] = meta_v[
                v * dest_count : (v + 1) * dest_count, i * LANES : (i + 1) * LANES
            ]

    together = 8

    def narrow(i, _):
        for q in range(together):
            b = i * together + q
            at = pl.multiple_of(b * slot_rows, 16)
            first_v[b, :first_rows, :] = outf[pl.ds(at, first_rows), :].astype(jnp.bfloat16)
            first_v[b, first_rows:, :] = mrow[pl.ds(pl.multiple_of(b * META_ROWS, 16), META_ROWS), :].astype(jnp.bfloat16)
            last_v[b] = outf[pl.ds(at + first_rows, slot_rows - first_rows), :].astype(jnp.bfloat16)
        some = pl.ds(i * together, together)
        pltpu.make_async_copy(first_v.at[some], first_ref.at[some], sems.at[1]).start()
        pltpu.make_async_copy(last_v.at[some], last_ref.at[some], sems.at[2]).start()
        return 0

    lax.fori_loop(0, dest_count // together, narrow, 0)
    pltpu.make_async_copy(first_v, first_ref, sems.at[1]).wait()
    pltpu.make_async_copy(last_v, last_ref, sems.at[2]).wait()


def pack(pixels, weights, tile_index, tile_row, granule_day, time_count, space_count, rows_tm, slots):
    swath_rows = pixels.shape[0]
    chunks = swath_rows // LANES
    dest_count = time_count * space_count
    slot_rows, first_rows = split_rows(slots)
    width = round_up(slots, LANES)
    shape = (chunks, LANES)
    first_shape = (dest_count, first_rows + META_ROWS, LANES)
    last_shape = (dest_count, slot_rows - first_rows, LANES)
    return pl.pallas_call(
        functools.partial(pack_kernel, (time_count, space_count, rows_tm, slot_rows, first_rows, width)),
        out_specs=[pl.BlockSpec(memory_space=pl.ANY)] * 2,
        out_shape=[jax.ShapeDtypeStruct(first_shape, jnp.bfloat16), jax.ShapeDtypeStruct(last_shape, jnp.bfloat16)],
        scratch_shapes=[
            pltpu.VMEM(shape, jnp.int32),
            pltpu.SMEM(shape, jnp.int32),
            pltpu.VMEM((5,) + shape, jnp.float32),
            pltpu.VMEM((3 * dest_count, width), jnp.float32),
            pltpu.VMEM((swath_rows, LANES), jnp.float32),
            pltpu.VMEM((dest_count * slot_rows, LANES), jnp.float32),
            pltpu.VMEM((dest_count * META_ROWS, LANES), jnp.float32),
            pltpu.VMEM(first_shape, jnp.bfloat16),
            pltpu.VMEM(last_shape, jnp.bfloat16),
            pltpu.SemaphoreType.DMA((3,)),
        ],
        compiler_params=pltpu.CompilerParams(vmem_limit_bytes=VMEM),
        name="pack",
    )(
        tile_index.reshape(shape),
        tile_row.reshape(shape),
        granule_day.reshape(shape),
        weights.reshape(shape),
        pixels,
    )


def chunk_of(rows):
    return max(c for c in (32, 16) if rows % c == 0)


def add_rows(total, pixf, code_s, code_row, first_slot, rows, pix_at, count):
    chunk = chunk_of(rows)

    def add_group(row, lane, at):
        places = [code_s[row, lane + u] for u in range(GROUP)]
        made = [total[pl.ds(p, 1), :] + pixf[pl.ds(at + u, 1), :] for u, p in enumerate(places)]
        for p, value in zip(places, made):
            total[pl.ds(p, 1), :] = value

    def add_singly(row, lane, at):
        def one(u, _):
            p = code_s[row, lane + u]
            p = jnp.where(p >= CLASH, p - CLASH, p)
            total[pl.ds(p, 1), :] = total[pl.ds(p, 1), :] + pixf[pl.ds(at + u, 1), :]
            return 0

        lax.fori_loop(0, GROUP, one, 0)

    for start in range(0, rows, chunk):
        slot = first_slot + start
        row, lane = code_row(slot // LANES), slot % LANES
        at = pix_at + start
        heads = [code_s[row, lane + g] for g in range(0, chunk, GROUP)]
        clash = functools.reduce(jnp.maximum, heads) >= CLASH

        @pl.when((count > start) & jnp.logical_not(clash))
        def _():
            for g in range(0, chunk, GROUP):
                add_group(row, lane + g, at + g)

        @pl.when((count > start) & clash)
        def _():
            for g, head in zip(range(0, chunk, GROUP), heads):
                pl.when(head < CLASH)(functools.partial(add_group, row, lane + g, at + g))
                pl.when(head >= CLASH)(functools.partial(add_singly, row, lane + g, at + g))


def grid_first_kernel(
    dims, moved_ref, total_ref, code_ref, count_ref, column_ref, meta_v, pixf, code_s, count_s, sems
):
    time_count, space_count, rows_tm, slot_rows, first_rows, width = dims
    day_dev = DAYS // time_count
    blocks = time_count * space_count
    pieces = width // LANES
    spare = rows_tm * DAYS

    meta_v[...] = moved_ref[:, first_rows:, :].astype(jnp.float32).reshape(blocks * META_ROWS, LANES)
    block = lax.broadcasted_iota(jnp.int32, (blocks, LANES), 0)
    offset = jnp.zeros((blocks, LANES), jnp.float32)
    for m in range(1, time_count):
        offset = offset + jnp.where(block >= m * space_count, float(day_dev), 0.0)
    within = lax.broadcasted_iota(jnp.int32, (blocks, LANES), 1) % GROUP
    count = jnp.zeros((blocks, 1), jnp.float32)
    for i in range(pieces):
        weight, local_row, day = (meta_v[pl.ds(v * pieces + i, blocks, stride=META_ROWS), :] for v in range(3))
        used = weight > 0.0
        count = count + jnp.sum(jnp.where(used, 1.0, 0.0), axis=1, keepdims=True)
        column_ref[i * LANES : (i + 1) * LANES, :] = jnp.transpose(weight)
        code = jnp.where(used, local_row * DAYS + (day + offset), float(spare)).astype(jnp.int32)
        clash = jnp.zeros(code.shape, jnp.int32)
        for k in range(1, GROUP):
            ahead = pltpu.roll(code, LANES - k, 1)
            clash = jnp.where((ahead == code) & (within + k < GROUP) & (code < spare), 1, clash)
        k = 1
        while k < GROUP:
            ahead = pltpu.roll(clash, LANES - k, 1)
            clash = jnp.where(within + k < GROUP, jnp.maximum(clash, ahead), clash)
            k *= 2
        code_ref[i * blocks : (i + 1) * blocks, :] = jnp.where((within == 0) & (clash > 0), code + CLASH, code)
    count_ref[...] = jnp.broadcast_to(count, (blocks, LANES)).astype(jnp.int32)
    code_copy = pltpu.make_async_copy(code_ref, code_s, sems.at[0])
    count_copy = pltpu.make_async_copy(count_ref, count_s, sems.at[1])
    code_copy.start()
    count_copy.start()

    for b in range(blocks):
        column = column_ref[:first_rows, b : b + 1]
        pixf[b * first_rows : (b + 1) * first_rows, :] = moved_ref[b, :first_rows, :].astype(jnp.float32) * column

    def clear(i, _):
        total_ref[pl.ds(pl.multiple_of(i * DAYS, DAYS), DAYS), :] = jnp.zeros((DAYS, LANES), jnp.float32)
        return 0

    lax.fori_loop(0, rows_tm, clear, 0)
    total_ref[spare:, :] = jnp.zeros((8, LANES), jnp.float32)
    code_copy.wait()
    count_copy.wait()

    def add(b, _):
        add_rows(total_ref, pixf, code_s, lambda i: i * blocks + b, 0, first_rows, b * first_rows, count_s[b, 0])
        return 0

    lax.fori_loop(0, blocks, add, 0)


def grid_last_kernel(
    dims, code_s, count_s, column_ref, moved_ref, total_in, field_ref, gram_ref, total, pixf, field_v, sems
):
    time_count, space_count, rows_tm, slot_rows, first_rows, width = dims
    blocks = time_count * space_count
    last_rows = slot_rows - first_rows
    group = rows_tm // STEPS
    load = pltpu.make_async_copy(total_in, total, sems.at[0])
    load.start()
    gram_ref[...] = jnp.zeros_like(gram_ref)

    for b in range(blocks):

        @pl.when(count_s[b, 0] > first_rows)
        def _():
            column = column_ref[first_rows:slot_rows, b : b + 1]
            pixf[b * last_rows : (b + 1) * last_rows, :] = moved_ref[b].astype(jnp.float32) * column

    load.wait()

    def add(b, _):
        rest = count_s[b, 0] - first_rows

        @pl.when(rest > 0)
        def _():
            add_rows(total, pixf, code_s, lambda i: i * blocks + b, first_rows, last_rows, b * last_rows, rest)

        return 0

    lax.fori_loop(0, blocks, add, 0)

    def send(i):
        at = pl.ds(i * group, group)
        return pltpu.make_async_copy(field_v.at[at], field_ref.at[at], sems.at[1])

    def finish(i, _):
        for q in range(group):
            at = pl.ds(pl.multiple_of((i * group + q) * DAYS, DAYS), DAYS)
            field_v[i * group + q] = total[at, :].astype(jnp.bfloat16)
        send(i).start()
        both = jnp.concatenate([field_v[i * group + q] for q in range(group)], axis=1)
        part = lax.dot_general(both[:RANK], both, LAST_LAST, preferred_element_type=jnp.float32)
        for c in range(DAYS // LANES):
            gram_ref[c] += part[:, c * LANES : (c + 1) * LANES]
        return 0

    lax.fori_loop(0, STEPS, finish, 0)
    pltpu.make_async_copy(field_v, field_ref, sems.at[1]).wait()


def grid_rows(moved_first, moved_last, time_count, space_count, rows_tm, slots):
    slot_rows, first_rows = split_rows(slots)
    last_rows = slot_rows - first_rows
    width = round_up(slots, LANES)
    blocks = time_count * space_count
    dims = (time_count, space_count, rows_tm, slot_rows, first_rows, width)
    codes = (blocks * width // LANES, LANES)
    counts = (blocks, LANES)
    sums = (rows_tm * DAYS + 8, LANES)
    params = pltpu.CompilerParams(vmem_limit_bytes=VMEM)
    columns = (width, blocks)
    total, code, count, column = pl.pallas_call(
        functools.partial(grid_first_kernel, dims),
        out_shape=[
            jax.ShapeDtypeStruct(sums, jnp.float32),
            jax.ShapeDtypeStruct(codes, jnp.int32),
            jax.ShapeDtypeStruct(counts, jnp.int32),
            jax.ShapeDtypeStruct(columns, jnp.float32),
        ],
        scratch_shapes=[
            pltpu.VMEM((blocks * META_ROWS, LANES), jnp.float32),
            pltpu.VMEM((blocks * first_rows, LANES), jnp.float32),
            pltpu.SMEM(codes, jnp.int32),
            pltpu.SMEM(counts, jnp.int32),
            pltpu.SemaphoreType.DMA((2,)),
        ],
        compiler_params=params,
        cost_estimate=pl.CostEstimate(flops=0, bytes_accessed=60_000_000, transcendentals=0),
        name="grid_first",
    )(moved_first)
    return pl.pallas_call(
        functools.partial(grid_last_kernel, dims),
        in_specs=[
            pl.BlockSpec(memory_space=pltpu.SMEM),
            pl.BlockSpec(memory_space=pltpu.SMEM),
            pl.BlockSpec(memory_space=pltpu.VMEM),
            pl.BlockSpec(memory_space=pltpu.VMEM),
            pl.BlockSpec(memory_space=pl.ANY),
        ],
        out_specs=[
            pl.BlockSpec(memory_space=pl.ANY),
            pl.BlockSpec(memory_space=pltpu.VMEM),
        ],
        out_shape=[
            jax.ShapeDtypeStruct((rows_tm, DAYS, LANES), jnp.bfloat16),
            jax.ShapeDtypeStruct((DAYS // LANES, RANK, LANES), jnp.float32),
        ],
        scratch_shapes=[
            pltpu.VMEM(sums, jnp.float32),
            pltpu.VMEM((blocks * last_rows, LANES), jnp.float32),
            pltpu.VMEM((rows_tm, DAYS, LANES), jnp.bfloat16),
            pltpu.SemaphoreType.DMA((2,)),
        ],
        compiler_params=params,
        name="grid_last_and_gram",
    )(code, count, column, moved_last, total)


def dot_f32(a, b, dims=(((1,), (0,)), ((), ()))):
    return lax.dot_general(a, b, dims, precision=lax.Precision.HIGHEST, preferred_element_type=jnp.float32)


def dot_three(a, b, dims=(((1,), (0,)), ((), ()))):
    a_high, b_high = a.astype(jnp.bfloat16), b.astype(jnp.bfloat16)
    a_low = (a - a_high.astype(jnp.float32)).astype(jnp.bfloat16)
    b_low = (b - b_high.astype(jnp.float32)).astype(jnp.bfloat16)
    left, right = dims[0][0][0], dims[0][1][0]
    a_all = jnp.concatenate([a_high, a_high, a_low], axis=left)
    b_all = jnp.concatenate([b_high, b_low, b_high], axis=right)
    return lax.dot_general(a_all, b_all, dims, preferred_element_type=jnp.float32)


def invert(x):
    guess = pl.reciprocal(x, approx=True)
    guess = guess * (2.0 - x * guess)
    return guess * (2.0 - x * guess)


def lower_inverse(a):
    n = a.shape[0]
    full = (8, n)
    tiles = [a[8 * i : 8 * i + 8, :] for i in range(n // 8)]
    lane = lax.broadcasted_iota(jnp.int32, full, 1)
    down = lax.broadcasted_iota(jnp.int32, full, 0)
    out = []
    for t in range(n // 8):
        k = 8 * t
        block = (lane >= k) & (lane < k + 8)
        panel = tiles[t]
        cols = [jnp.broadcast_to(panel[:, k + c : k + c + 1], full) for c in range(8)]
        e = {(i, c): jnp.broadcast_to(cols[c][i : i + 1, :], full) for c in range(8) for i in range(c, 8)}
        start = jnp.where(block, jnp.where(lane == k + down, 1.0, 0.0), panel)
        rows = [jnp.broadcast_to(start[i : i + 1, :], full) for i in range(8)]
        held = []
        for s in range(0, 8, 2):
            p, q, r = e[s, s], e[s + 1, s], e[s + 1, s + 1]
            det = p * r - q * q
            inv = invert(det)
            factors = {}
            for i in range(s + 2, 8):
                x, y = e[i, s], e[i, s + 1]
                factors[i] = (r * x - q * y, p * y - q * x)
            for i in range(s + 2, 8):
                u, v = factors[i]
                for c in range(s + 2, i + 1):
                    e[i, c] = e[i, c] - (u * e[c, s] + v * e[c, s + 1]) * inv
                rows[i] = rows[i] - (u * rows[s] + v * rows[s + 1]) * inv
            held.append((p, q, r, det, inv, factors))
        done = jnp.zeros(full, jnp.float32)
        solved = [None] * 8
        for s in (6, 4, 2, 0):
            p, q, r, det, inv, factors = held[s // 2]
            root = lax.rsqrt(p)
            done = jnp.where(down == s, rows[s] * root, done)
            done = jnp.where(down == s + 1, (rows[s + 1] * p - q * rows[s]) * (root * lax.rsqrt(det)), done)
            first, second = r * rows[s] - q * rows[s + 1], p * rows[s + 1] - q * rows[s]
            for i in range(7, s + 1, -1):
                u, v = factors[i]
                first, second = first - u * solved[i], second - v * solved[i]
            solved[s], solved[s + 1] = first * inv, second * inv
        out.append(jnp.where(lane < k + 8, done, 0.0))
        for i in range(t + 1, n // 8):
            terms = [jnp.broadcast_to(tiles[i][:, k + c : k + c + 1], full) * solved[c] for c in range(8)]
            while len(terms) > 1:
                terms = [terms[j] + terms[j + 1] for j in range(0, len(terms), 2)]
            tiles[i] = jnp.where(block, 0.0, tiles[i]) - terms[0]
    return jnp.concatenate(out, axis=0)


def solve_kernel(scale, gram_ref, field_ref, basis_ref, prop_ref, field_v, basis_v, sems):
    h = LANES
    pieces = DAYS // h
    group = field_v.shape[0] // STEPS
    load = pltpu.make_async_copy(field_ref.at[:, pl.ds(0, RANK), :], field_v, sems.at[0])
    load.start()

    eye = lax.broadcasted_iota(jnp.int32, (h, h), 0) == lax.broadcasted_iota(jnp.int32, (h, h), 1)
    a11, a12, a22 = gram_ref[0, :h, :], gram_ref[1, :h, :], gram_ref[1, h:, :]
    size_col, size_row = [], []
    for part in (a11, a22):
        diag = jnp.where(eye, part, 0.0)
        size_col.append(lax.rsqrt(jnp.sum(diag, axis=1, keepdims=True)))
        size_row.append(lax.rsqrt(jnp.sum(diag, axis=0, keepdims=True)))
    x1 = lower_inverse(a11 * size_col[0] * size_row[0])
    r12 = dot_f32(x1, a12 * size_col[0] * size_row[1])
    x2 = lower_inverse(a22 * size_col[1] * size_row[1] - dot_f32(r12, r12, FIRST_FIRST))
    mixed = -dot_f32(x2, dot_f32(r12, x1, FIRST_FIRST))
    lower = jnp.concatenate(
        [
            jnp.concatenate([x1 * size_row[0], jnp.zeros((h, h), jnp.float32)], axis=1),
            jnp.concatenate([mixed * size_row[0], x2 * size_row[1]], axis=1),
        ],
        axis=0,
    )
    inverse = (scale * lower).astype(jnp.bfloat16)
    load.wait()

    def project(i, _):
        both = jnp.concatenate([field_v[i * group + q] for q in range(group)], axis=1)
        made = jnp.dot(inverse, both, preferred_element_type=jnp.float32).astype(jnp.bfloat16)
        for q in range(group):
            basis_v[i * group + q] = made[:, q * h : (q + 1) * h]
        return 0

    lax.fori_loop(0, STEPS, project, 0)
    store = pltpu.make_async_copy(basis_v, basis_ref, sems.at[1])
    store.start()

    down = lax.broadcasted_iota(jnp.int32, (RANK, DAYS), 0)
    across = lax.broadcasted_iota(jnp.int32, (RANK, DAYS), 1)
    gram = jnp.concatenate([gram_ref[i] for i in range(pieces)], axis=1)
    factor = jnp.where(across >= down, dot_f32(lower, gram), 0.0)
    ahead = jnp.where(across < DAYS - 1, pltpu.roll(factor, DAYS - 1, 1), 0.0)
    cross = dot_three(ahead, factor, LAST_LAST)
    polar = cross / jnp.sqrt(jnp.sum(cross * cross) + 1e-06)
    for _ in range(ITERS):
        square = dot_three(polar, polar, LAST_LAST)
        polar = 1.5 * polar - 0.5 * dot_three(square, polar)
    prop_ref[...] = math.sqrt(RANK) * polar
    store.wait()


def solve(gram, field, cell_total):
    rows_tm = field.shape[0]
    part = (rows_tm, RANK, LANES)
    return pl.pallas_call(
        functools.partial(solve_kernel, math.sqrt(cell_total)),
        in_specs=[pl.BlockSpec(memory_space=pltpu.VMEM), pl.BlockSpec(memory_space=pl.ANY)],
        out_specs=[pl.BlockSpec(memory_space=pl.ANY), pl.BlockSpec(memory_space=pltpu.VMEM)],
        out_shape=[
            jax.ShapeDtypeStruct(part, jnp.bfloat16),
            jax.ShapeDtypeStruct((RANK, RANK), jnp.float32),
        ],
        scratch_shapes=[
            pltpu.VMEM(part, jnp.bfloat16),
            pltpu.VMEM(part, jnp.bfloat16),
            pltpu.SemaphoreType.DMA((2,)),
        ],
        compiler_params=pltpu.CompilerParams(vmem_limit_bytes=VMEM),
        name="factor_basis_and_polar",
    )(gram, field)


def body(pixels, weights, tile_index, tile_row, granule_day):
    swath_rows = pixels.shape[0]
    width = pixels.shape[1]
    space_count = lax.axis_size("space")
    time_count = lax.axis_size("tm")
    dest_count = time_count * space_count
    rows_tm = GR_DEV // time_count
    slots = 2 * swath_rows // space_count // time_count
    axes = ("tm", "space")
    first, last = pack(pixels, weights, tile_index, tile_row, granule_day, time_count, space_count, rows_tm, slots)
    first = lax.all_to_all(first, axes, split_axis=0, concat_axis=0, tiled=True)
    last = lax.all_to_all(last, axes, split_axis=0, concat_axis=0, tiled=True)
    field, partial_gram = grid_rows(first, last, time_count, space_count, rows_tm, slots)
    pieces = partial_gram.reshape(dest_count, -1, LANES)
    pieces = lax.all_to_all(pieces, axes, split_axis=0, concat_axis=0, tiled=True)
    mine = jnp.sum(pieces, axis=0, keepdims=True)
    gram = lax.all_gather(mine, axes, axis=0, tiled=True)
    cell_total = space_count * GR_DEV * width
    basis, propagator = solve(gram.reshape(partial_gram.shape), field, cell_total)
    return (field[None], basis[None], propagator)


def solution(mesh):
    placed = (
        P(("tm", "space"), None),
        P(("tm", "space")),
        P(("tm", "space")),
        P(("tm", "space")),
        P(("tm", "space")),
    )
    return jax.shard_map(
        body,
        mesh=mesh,
        in_specs=placed,
        out_specs=(P("space", "tm", None, None), P("space", "tm", None, None), P()),
        check_vma=False,
    )
```

```python
import functools
import math

import jax
import jax.numpy as jnp
from jax import lax
from jax.experimental import pallas as pl
from jax.experimental.pallas import tpu as pltpu
from jax.sharding import PartitionSpec as P

GR_DEV = 160
DAYS = 512
RANK = 256
ITERS = 8
LANES = 128
META_ROWS = 16
GROUP = 16
CLASH = 1 << 20
STEPS = 5
VMEM = 56 * 1024 * 1024

LAST_LAST = (((1,), (1,)), ((), ()))
FIRST_FIRST = (((0,), (0,)), ((), ()))


def round_up(value, unit):
    return -(-value // unit) * unit


def split_rows(slots):
    rows = round_up(slots, 16)
    return rows, rows * 7 // 10 // 16 * 16


def pack_kernel(
    dims, tile_ref, row_ref, day_ref, weight_ref, pix_ref, first_ref, last_ref, pos_v, pos_s, rows_v, meta_v, pixf, outf, mrow,
    first_v, last_v, sems
):
    time_count, space_count, rows_tm, slot_rows, first_rows, width = dims
    dest_count = time_count * space_count
    chunks = tile_ref.shape[0]
    pieces = width // LANES

    tile = tile_ref[...]
    row = row_ref[...]
    group = jnp.zeros_like(row)
    for k in range(1, time_count):
        group = group + jnp.where(row >= k * rows_tm, 1, 0)
    dest_all = group * space_count + tile
    rows_v[0] = dest_all.astype(jnp.float32)
    rows_v[2] = weight_ref[...].astype(jnp.float32)
    rows_v[3] = (row - group * rows_tm).astype(jnp.float32)
    rows_v[4] = day_ref[...].astype(jnp.float32)

    dest_iota = lax.broadcasted_iota(jnp.int32, (dest_count, LANES), 0)
    upper = jnp.where(
        lax.broadcasted_iota(jnp.int32, (LANES, LANES), 0) <= lax.broadcasted_iota(jnp.int32, (LANES, LANES), 1), 1.0, 0.0
    ).astype(jnp.bfloat16)
    carry = jnp.zeros((dest_count, 1), jnp.float32)
    for c in range(chunks):
        hot = dest_iota == dest_all[c : c + 1, :]
        prefix = jnp.dot(jnp.where(hot, 1.0, 0.0).astype(jnp.bfloat16), upper, preferred_element_type=jnp.float32)
        rows_v[1, c : c + 1, :] = jnp.sum(jnp.where(hot, prefix + carry, 0.0), axis=0, keepdims=True) - 1.0
        carry = carry + prefix[:, LANES - 1 : LANES]
    pos_v[...] = dest_all * slot_rows + rows_v[1].astype(jnp.int32)
    copy = pltpu.make_async_copy(pos_v, pos_s, sems.at[0])
    copy.start()
    meta_v[...] = jnp.zeros_like(meta_v)
    mrow[...] = jnp.zeros_like(mrow)

    def clear(b, _):
        outf[pl.ds(pl.multiple_of(b * slot_rows, 16), slot_rows), :] = jnp.zeros((slot_rows, LANES), jnp.float32)
        return 0

    lax.fori_loop(0, dest_count, clear, 0)
    copy.wait()
    dest_number = dest_iota.astype(jnp.float32)
    slot_number = lax.broadcasted_iota(jnp.int32, (width, LANES), 0).astype(jnp.float32)

    def move(c, _):
        base = pl.multiple_of(c * LANES, LANES)
        pixf[pl.ds(base, LANES), :] = pix_ref[pl.ds(base, LANES), :].astype(jnp.float32)
        dest, rank, weight, local_row, day = (rows_v[v, pl.ds(c, 1), :] for v in range(5))
        hot = dest_number == dest
        place = jnp.where(slot_number == rank, 1.0, 0.0).astype(jnp.bfloat16)
        values = jnp.concatenate([jnp.where(hot, v, 0.0) for v in (weight, local_row, day)], axis=0).astype(jnp.bfloat16)
        meta_v[...] += lax.dot_general(values, place, LAST_LAST, preferred_element_type=jnp.float32)
        for lane in range(LANES):
            outf[pl.ds(pos_s[c, lane], 1), :] = pixf[pl.ds(base + lane, 1), :]
        return 0

    lax.fori_loop(0, chunks, move, 0)
    for v in range(3):
        for i in range(pieces):
            mrow[pl.ds(v * pieces + i, dest_count, stride=META_ROWS), :] = meta_v[
                v * dest_count : (v + 1) * dest_count, i * LANES : (i + 1) * LANES
            ]

    together = 8

    def narrow(i, _):
        for q in range(together):
            b = i * together + q
            at = pl.multiple_of(b * slot_rows, 16)
            first_v[b, :first_rows, :] = outf[pl.ds(at, first_rows), :].astype(jnp.bfloat16)
            first_v[b, first_rows:, :] = mrow[pl.ds(pl.multiple_of(b * META_ROWS, 16), META_ROWS), :].astype(jnp.bfloat16)
            last_v[b] = outf[pl.ds(at + first_rows, slot_rows - first_rows), :].astype(jnp.bfloat16)
        some = pl.ds(i * together, together)
        pltpu.make_async_copy(first_v.at[some], first_ref.at[some], sems.at[1]).start()
        pltpu.make_async_copy(last_v.at[some], last_ref.at[some], sems.at[2]).start()
        return 0

    lax.fori_loop(0, dest_count // together, narrow, 0)
    pltpu.make_async_copy(first_v, first_ref, sems.at[1]).wait()
    pltpu.make_async_copy(last_v, last_ref, sems.at[2]).wait()


def pack(pixels, weights, tile_index, tile_row, granule_day, time_count, space_count, rows_tm, slots):
    swath_rows = pixels.shape[0]
    chunks = swath_rows // LANES
    dest_count = time_count * space_count
    slot_rows, first_rows = split_rows(slots)
    width = round_up(slots, LANES)
    shape = (chunks, LANES)
    first_shape = (dest_count, first_rows + META_ROWS, LANES)
    last_shape = (dest_count, slot_rows - first_rows, LANES)
    return pl.pallas_call(
        functools.partial(pack_kernel, (time_count, space_count, rows_tm, slot_rows, first_rows, width)),
        out_specs=[pl.BlockSpec(memory_space=pl.ANY)] * 2,
        out_shape=[jax.ShapeDtypeStruct(first_shape, jnp.bfloat16), jax.ShapeDtypeStruct(last_shape, jnp.bfloat16)],
        scratch_shapes=[
            pltpu.VMEM(shape, jnp.int32),
            pltpu.SMEM(shape, jnp.int32),
            pltpu.VMEM((5,) + shape, jnp.float32),
            pltpu.VMEM((3 * dest_count, width), jnp.float32),
            pltpu.VMEM((swath_rows, LANES), jnp.float32),
            pltpu.VMEM((dest_count * slot_rows, LANES), jnp.float32),
            pltpu.VMEM((dest_count * META_ROWS, LANES), jnp.float32),
            pltpu.VMEM(first_shape, jnp.bfloat16),
            pltpu.VMEM(last_shape, jnp.bfloat16),
            pltpu.SemaphoreType.DMA((3,)),
        ],
        compiler_params=pltpu.CompilerParams(vmem_limit_bytes=VMEM),
        name="pack",
    )(
        tile_index.reshape(shape),
        tile_row.reshape(shape),
        granule_day.reshape(shape),
        weights.reshape(shape),
        pixels,
    )


def chunk_of(rows):
    return max(c for c in (32, 16) if rows % c == 0)


def add_rows(total, pixf, code_s, code_row, first_slot, rows, pix_at, count):
    chunk = chunk_of(rows)

    def add_group(row, lane, at):
        places = [code_s[row, lane + u] for u in range(GROUP)]
        made = [total[pl.ds(p, 1), :] + pixf[pl.ds(at + u, 1), :] for u, p in enumerate(places)]
        for p, value in zip(places, made):
            total[pl.ds(p, 1), :] = value

    def add_singly(row, lane, at):
        def one(u, _):
            p = code_s[row, lane + u]
            p = jnp.where(p >= CLASH, p - CLASH, p)
            total[pl.ds(p, 1), :] = total[pl.ds(p, 1), :] + pixf[pl.ds(at + u, 1), :]
            return 0

        lax.fori_loop(0, GROUP, one, 0)

    for start in range(0, rows, chunk):
        slot = first_slot + start
        row, lane = code_row(slot // LANES), slot % LANES
        at = pix_at + start
        heads = [code_s[row, lane + g] for g in range(0, chunk, GROUP)]
        clash = functools.reduce(jnp.maximum, heads) >= CLASH

        @pl.when((count > start) & jnp.logical_not(clash))
        def _():
            for g in range(0, chunk, GROUP):
                add_group(row, lane + g, at + g)

        @pl.when((count > start) & clash)
        def _():
            for g, head in zip(range(0, chunk, GROUP), heads):
                pl.when(head < CLASH)(functools.partial(add_group, row, lane + g, at + g))
                pl.when(head >= CLASH)(functools.partial(add_singly, row, lane + g, at + g))


def grid_first_kernel(
    dims, moved_ref, total_ref, code_ref, rest_ref, count_ref, column_ref, meta_v, pixf, code_s, count_s, sems
):
    time_count, space_count, rows_tm, slot_rows, first_rows, width = dims
    day_dev = DAYS // time_count
    blocks = time_count * space_count
    pieces = width // LANES
    spare = rows_tm * DAYS

    meta_v[...] = moved_ref[:, first_rows:, :].astype(jnp.float32).reshape(blocks * META_ROWS, LANES)
    block = lax.broadcasted_iota(jnp.int32, (blocks, LANES), 0)
    offset = jnp.zeros((blocks, LANES), jnp.float32)
    for m in range(1, time_count):
        offset = offset + jnp.where(block >= m * space_count, float(day_dev), 0.0)
    within = lax.broadcasted_iota(jnp.int32, (blocks, LANES), 1) % GROUP
    count = jnp.zeros((blocks, 1), jnp.float32)
    for i in range(pieces):
        weight, local_row, day = (meta_v[pl.ds(v * pieces + i, blocks, stride=META_ROWS), :] for v in range(3))
        used = weight > 0.0
        count = count + jnp.sum(jnp.where(used, 1.0, 0.0), axis=1, keepdims=True)
        column_ref[i * LANES : (i + 1) * LANES, :] = jnp.transpose(weight)
        code = jnp.where(used, local_row * DAYS + (day + offset), float(spare)).astype(jnp.int32)
        clash = jnp.zeros(code.shape, jnp.int32)
        for k in range(1, GROUP):
            ahead = pltpu.roll(code, LANES - k, 1)
            clash = jnp.where((ahead == code) & (within + k < GROUP) & (code < spare), 1, clash)
        k = 1
        while k < GROUP:
            ahead = pltpu.roll(clash, LANES - k, 1)
            clash = jnp.where(within + k < GROUP, jnp.maximum(clash, ahead), clash)
            k *= 2
        code_ref[i * blocks : (i + 1) * blocks, :] = jnp.where((within == 0) & (clash > 0), code + CLASH, code)
    rest_ref[...] = code_ref[first_rows // LANES * blocks :, :]
    count_ref[...] = jnp.broadcast_to(count, (blocks, LANES)).astype(jnp.int32)
    code_copy = pltpu.make_async_copy(code_ref, code_s, sems.at[0])
    count_copy = pltpu.make_async_copy(count_ref, count_s, sems.at[1])
    code_copy.start()
    count_copy.start()

    for b in range(blocks):
        column = column_ref[:first_rows, b : b + 1]
        pixf[b * first_rows : (b + 1) * first_rows, :] = moved_ref[b, :first_rows, :].astype(jnp.float32) * column

    def clear(i, _):
        total_ref[pl.ds(pl.multiple_of(i * DAYS, DAYS), DAYS), :] = jnp.zeros((DAYS, LANES), jnp.float32)
        return 0

    lax.fori_loop(0, rows_tm, clear, 0)
    total_ref[spare:, :] = jnp.zeros((8, LANES), jnp.float32)
    code_copy.wait()
    count_copy.wait()

    def add(b, _):
        add_rows(total_ref, pixf, code_s, lambda i: i * blocks + b, 0, first_rows, b * first_rows, count_s[b, 0])
        return 0

    lax.fori_loop(0, blocks, add, 0)


def grid_last_kernel(
    dims, code_s, count_s, column_ref, moved_ref, first_ref, field_ref, keep_ref, give_ref,
    total, first_v, moved_v, pixf, field_v, gram_v, first_sems, block_sems, out_sem
):
    time_count, space_count, rows_tm, slot_rows, first_rows, width = dims
    blocks = time_count * space_count
    last_rows = slot_rows - first_rows
    group = rows_tm // STEPS
    skipped = first_rows // LANES

    def load(i):
        at = pl.ds(pl.multiple_of(i * group * DAYS, DAYS), group * DAYS)
        return pltpu.make_async_copy(first_ref.at[at], first_v.at[at], first_sems.at[i])

    def fetch(b):
        return pltpu.make_async_copy(moved_ref.at[b], moved_v.at[b], block_sems.at[b])

    for b in range(blocks):
        pl.when(count_s[b, 0] > first_rows)(fetch(b).start)
    for i in range(STEPS):
        load(i).start()
    gram_v[...] = jnp.zeros_like(gram_v)

    def clear(i, _):
        total[pl.ds(pl.multiple_of(i * DAYS, DAYS), DAYS), :] = jnp.zeros((DAYS, LANES), jnp.float32)
        return 0

    lax.fori_loop(0, rows_tm, clear, 0)
    total[rows_tm * DAYS :, :] = jnp.zeros((8, LANES), jnp.float32)
    for b in range(blocks):

        @pl.when(count_s[b, 0] > first_rows)
        def _():
            fetch(b).wait()
            column = column_ref[first_rows:slot_rows, b : b + 1]
            pixf[b * last_rows : (b + 1) * last_rows, :] = moved_v[b].astype(jnp.float32) * column

    def add(b, _):
        rest = count_s[b, 0] - first_rows

        @pl.when(rest > 0)
        def _():
            add_rows(
                total, pixf, code_s, lambda i: (i - skipped) * blocks + b, first_rows, last_rows, b * last_rows, rest
            )

        return 0

    lax.fori_loop(0, blocks, add, 0)

    def send(i):
        at = pl.ds(i * group, group)
        return pltpu.make_async_copy(field_v.at[at], field_ref.at[at], out_sem)

    def finish(i, _):
        load(i).wait()
        for q in range(group):
            at = pl.ds(pl.multiple_of((i * group + q) * DAYS, DAYS), DAYS)
            field_v[i * group + q] = (first_v[at, :] + total[at, :]).astype(jnp.bfloat16)
        send(i).start()
        both = jnp.concatenate([field_v[i * group + q] for q in range(group)], axis=1)
        part = lax.dot_general(both[:RANK], both, LAST_LAST, preferred_element_type=jnp.float32)
        for c in range(DAYS // LANES):
            gram_v[c] += part[:, c * LANES : (c + 1) * LANES]
        return 0

    lax.fori_loop(0, STEPS, finish, 0)
    odd = lax.axis_index("tm") % 2
    half = DAYS // LANES // 2
    for c in range(half):
        keep_ref[c] = gram_v[odd * half + c]
        give_ref[c] = gram_v[(1 - odd) * half + c]
    pltpu.make_async_copy(field_v, field_ref, out_sem).wait()


def grid_rows(moved_first, moved_last, time_count, space_count, rows_tm, slots):
    slot_rows, first_rows = split_rows(slots)
    last_rows = slot_rows - first_rows
    width = round_up(slots, LANES)
    blocks = time_count * space_count
    dims = (time_count, space_count, rows_tm, slot_rows, first_rows, width)
    codes = (blocks * width // LANES, LANES)
    rest = (codes[0] - first_rows // LANES * blocks, LANES)
    counts = (blocks, LANES)
    columns = (width, blocks)
    sums = (rows_tm * DAYS + 8, LANES)
    half = (DAYS // LANES // 2, RANK, LANES)
    params = pltpu.CompilerParams(vmem_limit_bytes=VMEM)
    total, _, code, count, column = pl.pallas_call(
        functools.partial(grid_first_kernel, dims),
        out_shape=[
            jax.ShapeDtypeStruct(sums, jnp.float32),
            jax.ShapeDtypeStruct(codes, jnp.int32),
            jax.ShapeDtypeStruct(rest, jnp.int32),
            jax.ShapeDtypeStruct(counts, jnp.int32),
            jax.ShapeDtypeStruct(columns, jnp.float32),
        ],
        scratch_shapes=[
            pltpu.VMEM((blocks * META_ROWS, LANES), jnp.float32),
            pltpu.VMEM((blocks * first_rows, LANES), jnp.float32),
            pltpu.SMEM(codes, jnp.int32),
            pltpu.SMEM(counts, jnp.int32),
            pltpu.SemaphoreType.DMA((2,)),
        ],
        compiler_params=params,
        cost_estimate=pl.CostEstimate(flops=0, bytes_accessed=60_000_000, transcendentals=0),
        name="grid_first",
    )(moved_first)
    whole = pl.BlockSpec(memory_space=pltpu.VMEM)
    return pl.pallas_call(
        functools.partial(grid_last_kernel, dims),
        in_specs=[
            pl.BlockSpec(memory_space=pltpu.SMEM),
            pl.BlockSpec(memory_space=pltpu.SMEM),
            whole,
            pl.BlockSpec(memory_space=pl.ANY),
            pl.BlockSpec(memory_space=pl.ANY),
        ],
        out_specs=[pl.BlockSpec(memory_space=pl.ANY), whole, whole],
        out_shape=[
            jax.ShapeDtypeStruct((rows_tm, DAYS, LANES), jnp.bfloat16),
            jax.ShapeDtypeStruct(half, jnp.float32),
            jax.ShapeDtypeStruct(half, jnp.float32),
        ],
        scratch_shapes=[
            pltpu.VMEM(sums, jnp.float32),
            pltpu.VMEM((rows_tm * DAYS, LANES), jnp.float32),
            pltpu.VMEM((blocks, last_rows, LANES), jnp.bfloat16),
            pltpu.VMEM((blocks * last_rows, LANES), jnp.float32),
            pltpu.VMEM((rows_tm, DAYS, LANES), jnp.bfloat16),
            pltpu.VMEM((DAYS // LANES, RANK, LANES), jnp.float32),
            pltpu.SemaphoreType.DMA((STEPS,)),
            pltpu.SemaphoreType.DMA((blocks,)),
            pltpu.SemaphoreType.DMA,
        ],
        compiler_params=params,
        name="grid_last_and_gram",
    )(code, count, column, moved_last, total)


def dot_f32(a, b, dims=(((1,), (0,)), ((), ()))):
    return lax.dot_general(a, b, dims, precision=lax.Precision.HIGHEST, preferred_element_type=jnp.float32)


def dot_three(a, b, dims=(((1,), (0,)), ((), ()))):
    a_high, b_high = a.astype(jnp.bfloat16), b.astype(jnp.bfloat16)
    a_low = (a - a_high.astype(jnp.float32)).astype(jnp.bfloat16)
    b_low = (b - b_high.astype(jnp.float32)).astype(jnp.bfloat16)
    left, right = dims[0][0][0], dims[0][1][0]
    a_all = jnp.concatenate([a_high, a_high, a_low], axis=left)
    b_all = jnp.concatenate([b_high, b_low, b_high], axis=right)
    return lax.dot_general(a_all, b_all, dims, preferred_element_type=jnp.float32)


def invert(x):
    guess = pl.reciprocal(x, approx=True)
    guess = guess * (2.0 - x * guess)
    return guess * (2.0 - x * guess)


def lower_inverse(a):
    n = a.shape[0]
    full = (8, n)
    tiles = [a[8 * i : 8 * i + 8, :] for i in range(n // 8)]
    lane = lax.broadcasted_iota(jnp.int32, full, 1)
    down = lax.broadcasted_iota(jnp.int32, full, 0)
    out = []
    for t in range(n // 8):
        k = 8 * t
        block = (lane >= k) & (lane < k + 8)
        panel = tiles[t]
        cols = [jnp.broadcast_to(panel[:, k + c : k + c + 1], full) for c in range(8)]
        e = {(i, c): jnp.broadcast_to(cols[c][i : i + 1, :], full) for c in range(8) for i in range(c, 8)}
        start = jnp.where(block, jnp.where(lane == k + down, 1.0, 0.0), panel)
        rows = [jnp.broadcast_to(start[i : i + 1, :], full) for i in range(8)]
        held = []
        for s in range(0, 8, 2):
            p, q, r = e[s, s], e[s + 1, s], e[s + 1, s + 1]
            det = p * r - q * q
            inv = invert(det)
            factors = {}
            for i in range(s + 2, 8):
                x, y = e[i, s], e[i, s + 1]
                factors[i] = (r * x - q * y, p * y - q * x)
            for i in range(s + 2, 8):
                u, v = factors[i]
                for c in range(s + 2, i + 1):
                    e[i, c] = e[i, c] - (u * e[c, s] + v * e[c, s + 1]) * inv
                rows[i] = rows[i] - (u * rows[s] + v * rows[s + 1]) * inv
            held.append((p, q, r, det, inv, factors))
        done = jnp.zeros(full, jnp.float32)
        solved = [None] * 8
        for s in (6, 4, 2, 0):
            p, q, r, det, inv, factors = held[s // 2]
            root = lax.rsqrt(p)
            done = jnp.where(down == s, rows[s] * root, done)
            done = jnp.where(down == s + 1, (rows[s + 1] * p - q * rows[s]) * (root * lax.rsqrt(det)), done)
            first, second = r * rows[s] - q * rows[s + 1], p * rows[s + 1] - q * rows[s]
            for i in range(7, s + 1, -1):
                u, v = factors[i]
                first, second = first - u * solved[i], second - v * solved[i]
            solved[s], solved[s + 1] = first * inv, second * inv
        out.append(jnp.where(lane < k + 8, done, 0.0))
        for i in range(t + 1, n // 8):
            terms = [jnp.broadcast_to(tiles[i][:, k + c : k + c + 1], full) * solved[c] for c in range(8)]
            while len(terms) > 1:
                terms = [terms[j] + terms[j + 1] for j in range(0, len(terms), 2)]
            tiles[i] = jnp.where(block, 0.0, tiles[i]) - terms[0]
    return jnp.concatenate(out, axis=0)


def solve_kernel(scale, own_ref, other_ref, field_ref, basis_ref, prop_ref, gram_v, field_v, basis_v, sems):
    h = LANES
    pieces = DAYS // h
    rows_here = field_v.shape[0]
    load = pltpu.make_async_copy(field_ref.at[:, pl.ds(0, RANK), :], field_v, sems.at[0])
    load.start()
    odd = lax.axis_index("tm") % 2
    for c in range(pieces // 2):
        gram_v[odd * (pieces // 2) + c] = own_ref[c]
        gram_v[(1 - odd) * (pieces // 2) + c] = other_ref[c]

    eye = lax.broadcasted_iota(jnp.int32, (h, h), 0) == lax.broadcasted_iota(jnp.int32, (h, h), 1)
    a11, a12, a22 = gram_v[0, :h, :], gram_v[1, :h, :], gram_v[1, h:, :]
    size_col, size_row = [], []
    for part in (a11, a22):
        diag = jnp.where(eye, part, 0.0)
        size_col.append(lax.rsqrt(jnp.sum(diag, axis=1, keepdims=True)))
        size_row.append(lax.rsqrt(jnp.sum(diag, axis=0, keepdims=True)))
    x1 = lower_inverse(a11 * size_col[0] * size_row[0])
    r12 = dot_f32(x1, a12 * size_col[0] * size_row[1])
    x2 = lower_inverse(a22 * size_col[1] * size_row[1] - dot_f32(r12, r12, FIRST_FIRST))
    mixed = -dot_f32(x2, dot_f32(r12, x1, FIRST_FIRST))
    lower = jnp.concatenate(
        [
            jnp.concatenate([x1 * size_row[0], jnp.zeros((h, h), jnp.float32)], axis=1),
            jnp.concatenate([mixed * size_row[0], x2 * size_row[1]], axis=1),
        ],
        axis=0,
    )
    inverse = (scale * lower).astype(jnp.bfloat16)
    load.wait()

    def project(i):
        both = jnp.concatenate([field_v[2 * i], field_v[2 * i + 1]], axis=1)
        made = jnp.dot(inverse, both, preferred_element_type=jnp.float32).astype(jnp.bfloat16)
        basis_v[2 * i] = made[:, :h]
        basis_v[2 * i + 1] = made[:, h:]

    down = lax.broadcasted_iota(jnp.int32, (RANK, DAYS), 0)
    across = lax.broadcasted_iota(jnp.int32, (RANK, DAYS), 1)
    gram = jnp.concatenate([gram_v[i] for i in range(pieces)], axis=1)
    factor = jnp.where(across >= down, dot_f32(lower, gram), 0.0)
    ahead = jnp.where(across < DAYS - 1, pltpu.roll(factor, DAYS - 1, 1), 0.0)
    cross = dot_three(ahead, factor, LAST_LAST)
    polar = cross / jnp.sqrt(jnp.sum(cross * cross) + 1e-06)
    todo = list(range(rows_here // 2))
    share = -(-len(todo) // (ITERS - 1))
    store = pltpu.make_async_copy(basis_v, basis_ref, sems.at[1])
    for n in range(ITERS):
        square = dot_three(polar, polar, LAST_LAST)
        for i in todo[n * share : (n + 1) * share]:
            project(i)
        if n == ITERS - 2:
            store.start()
        polar = 1.5 * polar - 0.5 * dot_three(square, polar)
    prop_ref[...] = math.sqrt(RANK) * polar
    store.wait()


def solve(own, other, field, cell_total):
    rows_tm = field.shape[0]
    part = (rows_tm, RANK, LANES)
    whole = pl.BlockSpec(memory_space=pltpu.VMEM)
    return pl.pallas_call(
        functools.partial(solve_kernel, math.sqrt(cell_total)),
        in_specs=[whole, whole, pl.BlockSpec(memory_space=pl.ANY)],
        out_specs=[pl.BlockSpec(memory_space=pl.ANY), whole],
        out_shape=[
            jax.ShapeDtypeStruct(part, jnp.bfloat16),
            jax.ShapeDtypeStruct((RANK, RANK), jnp.float32),
        ],
        scratch_shapes=[
            pltpu.VMEM((DAYS // LANES, RANK, LANES), jnp.float32),
            pltpu.VMEM(part, jnp.bfloat16),
            pltpu.VMEM(part, jnp.bfloat16),
            pltpu.SemaphoreType.DMA((2,)),
        ],
        compiler_params=pltpu.CompilerParams(vmem_limit_bytes=VMEM),
        name="factor_basis_and_polar",
    )(own, other, field)


def body(pixels, weights, tile_index, tile_row, granule_day):
    swath_rows = pixels.shape[0]
    width = pixels.shape[1]
    space_count = lax.axis_size("space")
    time_count = lax.axis_size("tm")
    dest_count = time_count * space_count
    rows_tm = GR_DEV // time_count
    slots = 2 * swath_rows // space_count // time_count
    axes = ("tm", "space")
    first, last = pack(pixels, weights, tile_index, tile_row, granule_day, time_count, space_count, rows_tm, slots)
    first = lax.all_to_all(first, axes, split_axis=0, concat_axis=0, tiled=True)
    last = lax.all_to_all(last, axes, split_axis=0, concat_axis=0, tiled=True)
    field, keep, give = grid_rows(first, last, time_count, space_count, rows_tm, slots)

    swap = [(t, t ^ 1) for t in range(time_count)]
    peers = [[t * space_count + s for t in range(core, time_count, 2) for s in range(space_count)] for core in (0, 1)]
    among = functools.partial(
        lax.all_to_all, axis_name=axes, split_axis=0, concat_axis=0, axis_index_groups=peers, tiled=True
    )
    pieces = (keep + lax.ppermute(give, "tm", swap)).reshape(dest_count // 2, -1, LANES)
    mine = jnp.sum(among(pieces), axis=0, keepdims=True)
    own = among(jnp.broadcast_to(mine, pieces.shape)).reshape(keep.shape)
    other = lax.ppermute(own, "tm", swap)
    cell_total = space_count * GR_DEV * width
    basis, propagator = solve(own, other, field, cell_total)
    return (field[None], basis[None], propagator)


def solution(mesh):
    placed = (
        P(("tm", "space"), None),
        P(("tm", "space")),
        P(("tm", "space")),
        P(("tm", "space")),
        P(("tm", "space")),
    )
    return jax.shard_map(
        body,
        mesh=mesh,
        in_specs=placed,
        out_specs=(P("space", "tm", None, None), P("space", "tm", None, None), P()),
        check_vma=False,
    )
```

```python
import functools
import math

import jax
import jax.numpy as jnp
from jax import lax
from jax.experimental import pallas as pl
from jax.experimental.pallas import tpu as pltpu
from jax.sharding import PartitionSpec as P

GR_DEV = 160
DAYS = 512
RANK = 256
ITERS = 8
LANES = 128
META_ROWS = 16
GROUP = 16
CLASH = 1 << 20
STEPS = 5
VMEM = 56 * 1024 * 1024

LAST_LAST = (((1,), (1,)), ((), ()))
FIRST_FIRST = (((0,), (0,)), ((), ()))


def round_up(value, unit):
    return -(-value // unit) * unit


def split_rows(slots):
    rows = round_up(slots, 16)
    return rows, rows * 7 // 10 // 16 * 16


def pack_kernel(
    dims, tile_ref, row_ref, day_ref, weight_ref, pix_ref, first_ref, last_ref, pos_v, pos_s, rows_v, meta_v, pixf, outf, mrow,
    first_v, last_v, pix_v, hot_v, prefix_v, sems
):
    time_count, space_count, rows_tm, slot_rows, first_rows, width = dims
    dest_count = time_count * space_count
    chunks = tile_ref.shape[0]
    pieces = width // LANES

    fetch = pltpu.make_async_copy(pix_ref, pix_v, sems.at[3])
    fetch.start()
    tile = tile_ref[...]
    row = row_ref[...]
    group = jnp.zeros_like(row)
    for k in range(1, time_count):
        group = group + jnp.where(row >= k * rows_tm, 1, 0)
    dest_all = group * space_count + tile
    rows_v[0] = dest_all.astype(jnp.float32)
    rows_v[2] = weight_ref[...].astype(jnp.float32)
    rows_v[3] = (row - group * rows_tm).astype(jnp.float32)
    rows_v[4] = day_ref[...].astype(jnp.float32)

    dest_iota = lax.broadcasted_iota(jnp.int32, (dest_count, LANES), 0)
    upper = jnp.where(
        lax.broadcasted_iota(jnp.int32, (LANES, LANES), 0) <= lax.broadcasted_iota(jnp.int32, (LANES, LANES), 1), 1.0, 0.0
    ).astype(jnp.bfloat16)
    for c in range(chunks):
        hot = dest_iota == dest_all[c : c + 1, :]
        hot_v[c * dest_count : (c + 1) * dest_count, :] = jnp.where(hot, 1.0, 0.0).astype(jnp.bfloat16)
    prefix_v[...] = jnp.dot(hot_v[...], upper, preferred_element_type=jnp.float32)
    carry = jnp.zeros((dest_count, 1), jnp.float32)
    for c in range(chunks):
        prefix = prefix_v[c * dest_count : (c + 1) * dest_count, :]
        hot = dest_iota == dest_all[c : c + 1, :]
        rows_v[1, c : c + 1, :] = jnp.sum(jnp.where(hot, prefix + carry, 0.0), axis=0, keepdims=True) - 1.0
        carry = carry + prefix[:, LANES - 1 : LANES]
    pos_v[...] = dest_all * slot_rows + rows_v[1].astype(jnp.int32)
    copy = pltpu.make_async_copy(pos_v, pos_s, sems.at[0])
    copy.start()
    meta_v[...] = jnp.zeros_like(meta_v)
    mrow[...] = jnp.zeros_like(mrow)

    def clear(b, _):
        outf[pl.ds(pl.multiple_of(b * slot_rows, 16), slot_rows), :] = jnp.zeros((slot_rows, LANES), jnp.float32)
        return 0

    lax.fori_loop(0, dest_count, clear, 0)
    fetch.wait()
    copy.wait()
    dest_number = dest_iota.astype(jnp.float32)
    slot_number = lax.broadcasted_iota(jnp.int32, (width, LANES), 0).astype(jnp.float32)

    def move(c, _):
        base = pl.multiple_of(c * LANES, LANES)
        pixf[pl.ds(base, LANES), :] = pix_v[pl.ds(base, LANES), :].astype(jnp.float32)
        dest, rank, weight, local_row, day = (rows_v[v, pl.ds(c, 1), :] for v in range(5))
        hot = dest_number == dest
        place = jnp.where(slot_number == rank, 1.0, 0.0).astype(jnp.bfloat16)
        values = jnp.concatenate([jnp.where(hot, v, 0.0) for v in (weight, local_row, day)], axis=0).astype(jnp.bfloat16)
        meta_v[...] += lax.dot_general(values, place, LAST_LAST, preferred_element_type=jnp.float32)
        for lane in range(LANES):
            outf[pl.ds(pos_s[c, lane], 1), :] = pixf[pl.ds(base + lane, 1), :]
        return 0

    lax.fori_loop(0, chunks, move, 0)
    for v in range(3):
        for i in range(pieces):
            mrow[pl.ds(v * pieces + i, dest_count, stride=META_ROWS), :] = meta_v[
                v * dest_count : (v + 1) * dest_count, i * LANES : (i + 1) * LANES
            ]

    together = 8

    def narrow(i, _):
        for q in range(together):
            b = i * together + q
            at = pl.multiple_of(b * slot_rows, 16)
            first_v[b, :first_rows, :] = outf[pl.ds(at, first_rows), :].astype(jnp.bfloat16)
            first_v[b, first_rows:, :] = mrow[pl.ds(pl.multiple_of(b * META_ROWS, 16), META_ROWS), :].astype(jnp.bfloat16)
            last_v[b] = outf[pl.ds(at + first_rows, slot_rows - first_rows), :].astype(jnp.bfloat16)
        some = pl.ds(i * together, together)
        pltpu.make_async_copy(first_v.at[some], first_ref.at[some], sems.at[1]).start()
        pltpu.make_async_copy(last_v.at[some], last_ref.at[some], sems.at[2]).start()
        return 0

    lax.fori_loop(0, dest_count // together, narrow, 0)
    pltpu.make_async_copy(first_v, first_ref, sems.at[1]).wait()
    pltpu.make_async_copy(last_v, last_ref, sems.at[2]).wait()


def pack(pixels, weights, tile_index, tile_row, granule_day, time_count, space_count, rows_tm, slots):
    swath_rows = pixels.shape[0]
    chunks = swath_rows // LANES
    dest_count = time_count * space_count
    slot_rows, first_rows = split_rows(slots)
    width = round_up(slots, LANES)
    shape = (chunks, LANES)
    first_shape = (dest_count, first_rows + META_ROWS, LANES)
    last_shape = (dest_count, slot_rows - first_rows, LANES)
    return pl.pallas_call(
        functools.partial(pack_kernel, (time_count, space_count, rows_tm, slot_rows, first_rows, width)),
        in_specs=[pl.BlockSpec(memory_space=pltpu.VMEM)] * 4 + [pl.BlockSpec(memory_space=pl.ANY)],
        out_specs=[pl.BlockSpec(memory_space=pl.ANY)] * 2,
        out_shape=[jax.ShapeDtypeStruct(first_shape, jnp.bfloat16), jax.ShapeDtypeStruct(last_shape, jnp.bfloat16)],
        scratch_shapes=[
            pltpu.VMEM(shape, jnp.int32),
            pltpu.SMEM(shape, jnp.int32),
            pltpu.VMEM((5,) + shape, jnp.float32),
            pltpu.VMEM((3 * dest_count, width), jnp.float32),
            pltpu.VMEM((swath_rows, LANES), jnp.float32),
            pltpu.VMEM((dest_count * slot_rows, LANES), jnp.float32),
            pltpu.VMEM((dest_count * META_ROWS, LANES), jnp.float32),
            pltpu.VMEM(first_shape, jnp.bfloat16),
            pltpu.VMEM(last_shape, jnp.bfloat16),
            pltpu.VMEM((swath_rows, LANES), jnp.bfloat16),
            pltpu.VMEM((chunks * dest_count, LANES), jnp.bfloat16),
            pltpu.VMEM((chunks * dest_count, LANES), jnp.float32),
            pltpu.SemaphoreType.DMA((4,)),
        ],
        compiler_params=pltpu.CompilerParams(vmem_limit_bytes=VMEM),
        name="pack",
    )(
        tile_index.reshape(shape),
        tile_row.reshape(shape),
        granule_day.reshape(shape),
        weights.reshape(shape),
        pixels,
    )


def chunk_of(rows):
    return max(c for c in (32, 16) if rows % c == 0)


def add_rows(total, pixf, code_s, code_row, first_slot, rows, pix_at, count):
    chunk = chunk_of(rows)

    def add_group(row, lane, at):
        places = [code_s[row, lane + u] for u in range(GROUP)]
        made = [total[pl.ds(p, 1), :] + pixf[pl.ds(at + u, 1), :] for u, p in enumerate(places)]
        for p, value in zip(places, made):
            total[pl.ds(p, 1), :] = value

    def add_singly(row, lane, at):
        def one(u, _):
            p = code_s[row, lane + u]
            p = jnp.where(p >= CLASH, p - CLASH, p)
            total[pl.ds(p, 1), :] = total[pl.ds(p, 1), :] + pixf[pl.ds(at + u, 1), :]
            return 0

        lax.fori_loop(0, GROUP, one, 0)

    for start in range(0, rows, chunk):
        slot = first_slot + start
        row, lane = code_row(slot // LANES), slot % LANES
        at = pix_at + start
        heads = [code_s[row, lane + g] for g in range(0, chunk, GROUP)]
        clash = functools.reduce(jnp.maximum, heads) >= CLASH

        @pl.when((count > start) & jnp.logical_not(clash))
        def _():
            for g in range(0, chunk, GROUP):
                add_group(row, lane + g, at + g)

        @pl.when((count > start) & clash)
        def _():
            for g, head in zip(range(0, chunk, GROUP), heads):
                pl.when(head < CLASH)(functools.partial(add_group, row, lane + g, at + g))
                pl.when(head >= CLASH)(functools.partial(add_singly, row, lane + g, at + g))


def grid_first_kernel(
    dims, moved_ref, total_ref, code_ref, rest_ref, count_ref, column_ref, meta_v, pixf, code_s, count_s, sems
):
    time_count, space_count, rows_tm, slot_rows, first_rows, width = dims
    day_dev = DAYS // time_count
    blocks = time_count * space_count
    pieces = width // LANES
    spare = rows_tm * DAYS

    meta_v[...] = moved_ref[:, first_rows:, :].astype(jnp.float32).reshape(blocks * META_ROWS, LANES)
    block = lax.broadcasted_iota(jnp.int32, (blocks, LANES), 0)
    offset = jnp.zeros((blocks, LANES), jnp.float32)
    for m in range(1, time_count):
        offset = offset + jnp.where(block >= m * space_count, float(day_dev), 0.0)
    within = lax.broadcasted_iota(jnp.int32, (blocks, LANES), 1) % GROUP
    count = jnp.zeros((blocks, 1), jnp.float32)
    for i in range(pieces):
        weight, local_row, day = (meta_v[pl.ds(v * pieces + i, blocks, stride=META_ROWS), :] for v in range(3))
        used = weight > 0.0
        count = count + jnp.sum(jnp.where(used, 1.0, 0.0), axis=1, keepdims=True)
        column_ref[i * LANES : (i + 1) * LANES, :] = jnp.transpose(weight)
        code = jnp.where(used, local_row * DAYS + (day + offset), float(spare)).astype(jnp.int32)
        clash = jnp.zeros(code.shape, jnp.int32)
        for k in range(1, GROUP):
            ahead = pltpu.roll(code, LANES - k, 1)
            clash = jnp.where((ahead == code) & (within + k < GROUP) & (code < spare), 1, clash)
        k = 1
        while k < GROUP:
            ahead = pltpu.roll(clash, LANES - k, 1)
            clash = jnp.where(within + k < GROUP, jnp.maximum(clash, ahead), clash)
            k *= 2
        code_ref[i * blocks : (i + 1) * blocks, :] = jnp.where((within == 0) & (clash > 0), code + CLASH, code)
    rest_ref[...] = code_ref[first_rows // LANES * blocks :, :]
    count_ref[...] = jnp.broadcast_to(count, (blocks, LANES)).astype(jnp.int32)
    code_copy = pltpu.make_async_copy(code_ref, code_s, sems.at[0])
    count_copy = pltpu.make_async_copy(count_ref, count_s, sems.at[1])
    code_copy.start()
    count_copy.start()

    for b in range(blocks):
        column = column_ref[:first_rows, b : b + 1]
        pixf[b * first_rows : (b + 1) * first_rows, :] = moved_ref[b, :first_rows, :].astype(jnp.float32) * column

    def clear(i, _):
        total_ref[pl.ds(pl.multiple_of(i * DAYS, DAYS), DAYS), :] = jnp.zeros((DAYS, LANES), jnp.float32)
        return 0

    lax.fori_loop(0, rows_tm, clear, 0)
    total_ref[spare:, :] = jnp.zeros((8, LANES), jnp.float32)
    code_copy.wait()
    count_copy.wait()

    def add(b, _):
        add_rows(total_ref, pixf, code_s, lambda i: i * blocks + b, 0, first_rows, b * first_rows, count_s[b, 0])
        return 0

    lax.fori_loop(0, blocks, add, 0)


def grid_last_kernel(
    dims, code_s, count_s, column_ref, moved_ref, first_ref, field_ref, keep_ref, give_ref,
    total, first_v, moved_v, pixf, field_v, gram_v, first_sems, block_sems, out_sem
):
    time_count, space_count, rows_tm, slot_rows, first_rows, width = dims
    blocks = time_count * space_count
    last_rows = slot_rows - first_rows
    group = rows_tm // STEPS
    skipped = first_rows // LANES

    def load(i):
        at = pl.ds(pl.multiple_of(i * group * DAYS, DAYS), group * DAYS)
        return pltpu.make_async_copy(first_ref.at[at], first_v.at[at], first_sems.at[i])

    def fetch(b):
        return pltpu.make_async_copy(moved_ref.at[b], moved_v.at[b], block_sems.at[b])

    for b in range(blocks):
        pl.when(count_s[b, 0] > first_rows)(fetch(b).start)
    for i in range(STEPS):
        load(i).start()

    def clear(i, _):
        total[pl.ds(pl.multiple_of(i * DAYS, DAYS), DAYS), :] = jnp.zeros((DAYS, LANES), jnp.float32)
        return 0

    lax.fori_loop(0, rows_tm, clear, 0)
    total[rows_tm * DAYS :, :] = jnp.zeros((8, LANES), jnp.float32)
    for b in range(blocks):

        @pl.when(count_s[b, 0] > first_rows)
        def _():
            fetch(b).wait()
            column = column_ref[first_rows:slot_rows, b : b + 1]
            pixf[b * last_rows : (b + 1) * last_rows, :] = moved_v[b].astype(jnp.float32) * column

    def add(b, _):
        rest = count_s[b, 0] - first_rows

        @pl.when(rest > 0)
        def _():
            add_rows(
                total, pixf, code_s, lambda i: (i - skipped) * blocks + b, first_rows, last_rows, b * last_rows, rest
            )

        return 0

    lax.fori_loop(0, blocks, add, 0)

    def send(i):
        at = pl.ds(i * group, group)
        return pltpu.make_async_copy(field_v.at[at], field_ref.at[at], out_sem)

    def settle(i):
        for q in range(i * group, (i + 1) * group):
            at = pl.ds(q * DAYS, DAYS)
            field_v[q] = (first_v[at, :] + total[at, :]).astype(jnp.bfloat16)

    def multiply(i):
        both = jnp.concatenate([field_v[q] for q in range(i * group, (i + 1) * group)], axis=1)
        part = lax.dot_general(both[:RANK], both, LAST_LAST, preferred_element_type=jnp.float32)
        for c in range(DAYS // LANES):
            here = part[:, c * LANES : (c + 1) * LANES]
            gram_v[c] = here if i == 0 else gram_v[c] + here

    for i in range(STEPS):
        load(i).wait()
        settle(i)
        if i > 0:
            send(i - 1).start()
            multiply(i - 1)
    send(STEPS - 1).start()
    multiply(STEPS - 1)
    odd = lax.axis_index("tm") % 2
    half = DAYS // LANES // 2
    for c in range(half):
        keep_ref[c] = gram_v[odd * half + c]
        give_ref[c] = gram_v[(1 - odd) * half + c]
    pltpu.make_async_copy(field_v, field_ref, out_sem).wait()


def grid_rows(moved_first, moved_last, time_count, space_count, rows_tm, slots):
    slot_rows, first_rows = split_rows(slots)
    last_rows = slot_rows - first_rows
    width = round_up(slots, LANES)
    blocks = time_count * space_count
    dims = (time_count, space_count, rows_tm, slot_rows, first_rows, width)
    codes = (blocks * width // LANES, LANES)
    rest = (codes[0] - first_rows // LANES * blocks, LANES)
    counts = (blocks, LANES)
    columns = (width, blocks)
    sums = (rows_tm * DAYS + 8, LANES)
    half = (DAYS // LANES // 2, RANK, LANES)
    params = pltpu.CompilerParams(vmem_limit_bytes=VMEM)
    total, _, code, count, column = pl.pallas_call(
        functools.partial(grid_first_kernel, dims),
        out_shape=[
            jax.ShapeDtypeStruct(sums, jnp.float32),
            jax.ShapeDtypeStruct(codes, jnp.int32),
            jax.ShapeDtypeStruct(rest, jnp.int32),
            jax.ShapeDtypeStruct(counts, jnp.int32),
            jax.ShapeDtypeStruct(columns, jnp.float32),
        ],
        scratch_shapes=[
            pltpu.VMEM((blocks * META_ROWS, LANES), jnp.float32),
            pltpu.VMEM((blocks * first_rows, LANES), jnp.float32),
            pltpu.SMEM(codes, jnp.int32),
            pltpu.SMEM(counts, jnp.int32),
            pltpu.SemaphoreType.DMA((2,)),
        ],
        compiler_params=params,
        cost_estimate=pl.CostEstimate(flops=0, bytes_accessed=60_000_000, transcendentals=0),
        name="grid_first",
    )(moved_first)
    whole = pl.BlockSpec(memory_space=pltpu.VMEM)
    return pl.pallas_call(
        functools.partial(grid_last_kernel, dims),
        in_specs=[
            pl.BlockSpec(memory_space=pltpu.SMEM),
            pl.BlockSpec(memory_space=pltpu.SMEM),
            whole,
            pl.BlockSpec(memory_space=pl.ANY),
            pl.BlockSpec(memory_space=pl.ANY),
        ],
        out_specs=[pl.BlockSpec(memory_space=pl.ANY), whole, whole],
        out_shape=[
            jax.ShapeDtypeStruct((rows_tm, DAYS, LANES), jnp.bfloat16),
            jax.ShapeDtypeStruct(half, jnp.float32),
            jax.ShapeDtypeStruct(half, jnp.float32),
        ],
        scratch_shapes=[
            pltpu.VMEM(sums, jnp.float32),
            pltpu.VMEM((rows_tm * DAYS, LANES), jnp.float32),
            pltpu.VMEM((blocks, last_rows, LANES), jnp.bfloat16),
            pltpu.VMEM((blocks * last_rows, LANES), jnp.float32),
            pltpu.VMEM((rows_tm, DAYS, LANES), jnp.bfloat16),
            pltpu.VMEM((DAYS // LANES, RANK, LANES), jnp.float32),
            pltpu.SemaphoreType.DMA((STEPS,)),
            pltpu.SemaphoreType.DMA((blocks,)),
            pltpu.SemaphoreType.DMA,
        ],
        compiler_params=params,
        name="grid_last_and_gram",
    )(code, count, column, moved_last, total)


def dot_f32(a, b, dims=(((1,), (0,)), ((), ()))):
    return lax.dot_general(a, b, dims, precision=lax.Precision.HIGHEST, preferred_element_type=jnp.float32)


def dot_three(a, b, dims=(((1,), (0,)), ((), ()))):
    a_high, b_high = a.astype(jnp.bfloat16), b.astype(jnp.bfloat16)
    a_low = (a - a_high.astype(jnp.float32)).astype(jnp.bfloat16)
    b_low = (b - b_high.astype(jnp.float32)).astype(jnp.bfloat16)
    left, right = dims[0][0][0], dims[0][1][0]
    a_all = jnp.concatenate([a_high, a_high, a_low], axis=left)
    b_all = jnp.concatenate([b_high, b_low, b_high], axis=right)
    return lax.dot_general(a_all, b_all, dims, preferred_element_type=jnp.float32)


def invert(x):
    guess = pl.reciprocal(x, approx=True)
    guess = guess * (2.0 - x * guess)
    return guess * (2.0 - x * guess)


def lower_inverse(a):
    n = a.shape[0]
    full = (8, n)
    tiles = [a[8 * i : 8 * i + 8, :] for i in range(n // 8)]
    lane = lax.broadcasted_iota(jnp.int32, full, 1)
    down = lax.broadcasted_iota(jnp.int32, full, 0)
    out = []
    for t in range(n // 8):
        k = 8 * t
        block = (lane >= k) & (lane < k + 8)
        panel = tiles[t]
        cols = [jnp.broadcast_to(panel[:, k + c : k + c + 1], full) for c in range(8)]
        e = {(i, c): jnp.broadcast_to(cols[c][i : i + 1, :], full) for c in range(8) for i in range(c, 8)}
        start = jnp.where(block, jnp.where(lane == k + down, 1.0, 0.0), panel)
        rows = [jnp.broadcast_to(start[i : i + 1, :], full) for i in range(8)]
        held = []
        for s in range(0, 8, 2):
            p, q, r = e[s, s], e[s + 1, s], e[s + 1, s + 1]
            det = p * r - q * q
            inv = invert(det)
            factors = {}
            for i in range(s + 2, 8):
                x, y = e[i, s], e[i, s + 1]
                factors[i] = (r * x - q * y, p * y - q * x)
            for i in range(s + 2, 8):
                u, v = factors[i]
                for c in range(s + 2, i + 1):
                    e[i, c] = e[i, c] - (u * e[c, s] + v * e[c, s + 1]) * inv
                rows[i] = rows[i] - (u * rows[s] + v * rows[s + 1]) * inv
            held.append((p, q, r, det, inv, factors))
        done = jnp.zeros(full, jnp.float32)
        solved = [None] * 8
        for s in (6, 4, 2, 0):
            p, q, r, det, inv, factors = held[s // 2]
            root = lax.rsqrt(p)
            done = jnp.where(down == s, rows[s] * root, done)
            done = jnp.where(down == s + 1, (rows[s + 1] * p - q * rows[s]) * (root * lax.rsqrt(det)), done)
            first, second = r * rows[s] - q * rows[s + 1], p * rows[s + 1] - q * rows[s]
            for i in range(7, s + 1, -1):
                u, v = factors[i]
                first, second = first - u * solved[i], second - v * solved[i]
            solved[s], solved[s + 1] = first * inv, second * inv
        out.append(jnp.where(lane < k + 8, done, 0.0))
        for i in range(t + 1, n // 8):
            terms = [jnp.broadcast_to(tiles[i][:, k + c : k + c + 1], full) * solved[c] for c in range(8)]
            while len(terms) > 1:
                terms = [terms[j] + terms[j + 1] for j in range(0, len(terms), 2)]
            tiles[i] = jnp.where(block, 0.0, tiles[i]) - terms[0]
    return jnp.concatenate(out, axis=0)


def solve_kernel(scale, own_ref, other_ref, field_ref, basis_ref, prop_ref, gram_v, field_v, basis_v, sems):
    h = LANES
    pieces = DAYS // h
    rows_here = field_v.shape[0]
    load = pltpu.make_async_copy(field_ref.at[:, pl.ds(0, RANK), :], field_v, sems.at[0])
    load.start()
    odd = lax.axis_index("tm") % 2
    for c in range(pieces // 2):
        gram_v[odd * (pieces // 2) + c] = own_ref[c]
        gram_v[(1 - odd) * (pieces // 2) + c] = other_ref[c]

    gram = jnp.concatenate([gram_v[i] for i in range(pieces)], axis=1)
    eye = lax.broadcasted_iota(jnp.int32, (h, h), 0) == lax.broadcasted_iota(jnp.int32, (h, h), 1)
    a11, a12, a22 = gram_v[0, :h, :], gram_v[1, :h, :], gram_v[1, h:, :]
    size_col, size_row = [], []
    for part in (a11, a22):
        diag = jnp.where(eye, part, 0.0)
        size_col.append(lax.rsqrt(jnp.sum(diag, axis=1, keepdims=True)))
        size_row.append(lax.rsqrt(jnp.sum(diag, axis=0, keepdims=True)))
    top, low = gram[:h], gram[h:]
    x1 = lower_inverse(a11 * size_col[0] * size_row[0])
    r12 = dot_f32(x1, a12 * size_col[0] * size_row[1])
    x2 = lower_inverse(a22 * size_col[1] * size_row[1] - dot_f32(r12, r12, FIRST_FIRST))
    factor_top = dot_f32(x1, top * size_col[0])
    schur = low[:, h:] * size_col[1] - dot_f32(r12, factor_top[:, h:], FIRST_FIRST)
    mixed = -dot_f32(x2, dot_f32(r12, x1, FIRST_FIRST))
    factor_low = dot_f32(x2, schur)
    lower = jnp.concatenate(
        [
            jnp.concatenate([x1 * size_row[0], jnp.zeros((h, h), jnp.float32)], axis=1),
            jnp.concatenate([mixed * size_row[0], x2 * size_row[1]], axis=1),
        ],
        axis=0,
    )
    inverse = (scale * lower).astype(jnp.bfloat16)
    load.wait()

    def project(i):
        both = jnp.concatenate([field_v[2 * i], field_v[2 * i + 1]], axis=1)
        made = jnp.dot(inverse, both, preferred_element_type=jnp.float32).astype(jnp.bfloat16)
        basis_v[2 * i] = made[:, :h]
        basis_v[2 * i + 1] = made[:, h:]

    down = lax.broadcasted_iota(jnp.int32, (RANK, DAYS), 0)
    across = lax.broadcasted_iota(jnp.int32, (RANK, DAYS), 1)
    factor = jnp.concatenate(
        [factor_top, jnp.concatenate([jnp.zeros((h, h), jnp.float32), factor_low], axis=1)], axis=0
    )
    factor = jnp.where(across >= down, factor, 0.0)
    ahead = jnp.where(across < DAYS - 1, pltpu.roll(factor, DAYS - 1, 1), 0.0)
    cross = dot_three(ahead, factor, LAST_LAST)
    polar = cross / jnp.sqrt(jnp.sum(cross * cross) + 1e-06)
    todo = list(range(rows_here // 2))
    share = -(-len(todo) // (ITERS - 1))
    store = pltpu.make_async_copy(basis_v, basis_ref, sems.at[1])
    for n in range(ITERS):
        square = dot_three(polar, polar, LAST_LAST)
        for i in todo[n * share : (n + 1) * share]:
            project(i)
        if n == ITERS - 2:
            store.start()
        polar = 1.5 * polar - 0.5 * dot_three(square, polar)
    prop_ref[...] = math.sqrt(RANK) * polar
    store.wait()


def solve(own, other, field, cell_total):
    rows_tm = field.shape[0]
    part = (rows_tm, RANK, LANES)
    whole = pl.BlockSpec(memory_space=pltpu.VMEM)
    return pl.pallas_call(
        functools.partial(solve_kernel, math.sqrt(cell_total)),
        in_specs=[whole, whole, pl.BlockSpec(memory_space=pl.ANY)],
        out_specs=[pl.BlockSpec(memory_space=pl.ANY), whole],
        out_shape=[
            jax.ShapeDtypeStruct(part, jnp.bfloat16),
            jax.ShapeDtypeStruct((RANK, RANK), jnp.float32),
        ],
        scratch_shapes=[
            pltpu.VMEM((DAYS // LANES, RANK, LANES), jnp.float32),
            pltpu.VMEM(part, jnp.bfloat16),
            pltpu.VMEM(part, jnp.bfloat16),
            pltpu.SemaphoreType.DMA((2,)),
        ],
        compiler_params=pltpu.CompilerParams(vmem_limit_bytes=VMEM),
        name="factor_basis_and_polar",
    )(own, other, field)


def body(pixels, weights, tile_index, tile_row, granule_day):
    swath_rows = pixels.shape[0]
    width = pixels.shape[1]
    space_count = lax.axis_size("space")
    time_count = lax.axis_size("tm")
    dest_count = time_count * space_count
    rows_tm = GR_DEV // time_count
    slots = 2 * swath_rows // space_count // time_count
    axes = ("tm", "space")
    first, last = pack(pixels, weights, tile_index, tile_row, granule_day, time_count, space_count, rows_tm, slots)
    first = lax.all_to_all(first, axes, split_axis=0, concat_axis=0, tiled=True)
    last = lax.all_to_all(last, axes, split_axis=0, concat_axis=0, tiled=True)
    field, keep, give = grid_rows(first, last, time_count, space_count, rows_tm, slots)

    swap = [(t, t ^ 1) for t in range(time_count)]
    peers = [[t * space_count + s for t in range(core, time_count, 2) for s in range(space_count)] for core in (0, 1)]
    among = functools.partial(
        lax.all_to_all, axis_name=axes, split_axis=0, concat_axis=0, axis_index_groups=peers, tiled=True
    )
    pieces = (keep + lax.ppermute(give, "tm", swap)).reshape(dest_count // 2, -1, LANES)
    mine = jnp.sum(among(pieces), axis=0, keepdims=True)
    own = among(jnp.broadcast_to(mine, pieces.shape)).reshape(keep.shape)
    other = lax.ppermute(own, "tm", swap)
    cell_total = space_count * GR_DEV * width
    basis, propagator = solve(own, other, field, cell_total)
    return (field[None], basis[None], propagator)


def solution(mesh):
    placed = (
        P(("tm", "space"), None),
        P(("tm", "space")),
        P(("tm", "space")),
        P(("tm", "space")),
        P(("tm", "space")),
    )
    return jax.shard_map(
        body,
        mesh=mesh,
        in_specs=placed,
        out_specs=(P("space", "tm", None, None), P("space", "tm", None, None), P()),
        check_vma=False,
    )
```

```python
import functools
import math

import jax
import jax.numpy as jnp
from jax import lax
from jax.experimental import pallas as pl
from jax.experimental.pallas import tpu as pltpu
from jax.sharding import PartitionSpec as P

GR_DEV = 160
DAYS = 512
RANK = 256
ITERS = 8
LANES = 128
META_ROWS = 16
GROUP = 16
CLASH = 1 << 20
STEPS = 5
VMEM = 56 * 1024 * 1024

LAST_LAST = (((1,), (1,)), ((), ()))
FIRST_FIRST = (((0,), (0,)), ((), ()))


def round_up(value, unit):
    return -(-value // unit) * unit


def split_rows(slots):
    rows = round_up(slots, 16)
    return rows, rows * 7 // 10 // 16 * 16


def pack_kernel(
    dims, tile_ref, row_ref, day_ref, weight_ref, pix_ref, first_ref, last_ref, pos_v, pos_s, rows_v, meta_v, pixf, outf, mrow,
    first_v, last_v, pix_v, hot_v, prefix_v, sems
):
    time_count, space_count, rows_tm, slot_rows, first_rows, width = dims
    dest_count = time_count * space_count
    chunks = tile_ref.shape[0]
    pieces = width // LANES

    fetch = pltpu.make_async_copy(pix_ref, pix_v, sems.at[3])
    fetch.start()
    tile = tile_ref[...]
    row = row_ref[...]
    group = jnp.zeros_like(row)
    for k in range(1, time_count):
        group = group + jnp.where(row >= k * rows_tm, 1, 0)
    dest_all = group * space_count + tile
    rows_v[0] = dest_all.astype(jnp.float32)
    rows_v[2] = weight_ref[...].astype(jnp.float32)
    rows_v[3] = (row - group * rows_tm).astype(jnp.float32)
    rows_v[4] = day_ref[...].astype(jnp.float32)

    dest_iota = lax.broadcasted_iota(jnp.int32, (dest_count, LANES), 0)
    upper = jnp.where(
        lax.broadcasted_iota(jnp.int32, (LANES, LANES), 0) <= lax.broadcasted_iota(jnp.int32, (LANES, LANES), 1), 1.0, 0.0
    ).astype(jnp.bfloat16)
    for c in range(chunks):
        hot = dest_iota == dest_all[c : c + 1, :]
        hot_v[c * dest_count : (c + 1) * dest_count, :] = jnp.where(hot, 1.0, 0.0).astype(jnp.bfloat16)
    prefix_v[...] = jnp.dot(hot_v[...], upper, preferred_element_type=jnp.float32)
    carry = jnp.zeros((dest_count, 1), jnp.float32)
    for c in range(chunks):
        prefix = prefix_v[c * dest_count : (c + 1) * dest_count, :]
        hot = dest_iota == dest_all[c : c + 1, :]
        rows_v[1, c : c + 1, :] = jnp.sum(jnp.where(hot, prefix + carry, 0.0), axis=0, keepdims=True) - 1.0
        carry = carry + prefix[:, LANES - 1 : LANES]
    pos_v[...] = dest_all * slot_rows + rows_v[1].astype(jnp.int32)
    copy = pltpu.make_async_copy(pos_v, pos_s, sems.at[0])
    copy.start()
    meta_v[...] = jnp.zeros_like(meta_v)
    mrow[...] = jnp.zeros_like(mrow)

    def clear(b, _):
        outf[pl.ds(pl.multiple_of(b * slot_rows, 16), slot_rows), :] = jnp.zeros((slot_rows, LANES), jnp.float32)
        return 0

    lax.fori_loop(0, dest_count, clear, 0)
    fetch.wait()
    copy.wait()
    dest_number = dest_iota.astype(jnp.float32)
    slot_number = lax.broadcasted_iota(jnp.int32, (width, LANES), 0).astype(jnp.float32)

    def move(c, _):
        base = pl.multiple_of(c * LANES, LANES)
        pixf[pl.ds(base, LANES), :] = pix_v[pl.ds(base, LANES), :].astype(jnp.float32)
        dest, rank, weight, local_row, day = (rows_v[v, pl.ds(c, 1), :] for v in range(5))
        hot = dest_number == dest
        place = jnp.where(slot_number == rank, 1.0, 0.0).astype(jnp.bfloat16)
        values = jnp.concatenate([jnp.where(hot, v, 0.0) for v in (weight, local_row, day)], axis=0).astype(jnp.bfloat16)
        meta_v[...] += lax.dot_general(values, place, LAST_LAST, preferred_element_type=jnp.float32)
        for lane in range(LANES):
            outf[pl.ds(pos_s[c, lane], 1), :] = pixf[pl.ds(base + lane, 1), :]
        return 0

    lax.fori_loop(0, chunks, move, 0)
    for v in range(3):
        for i in range(pieces):
            mrow[pl.ds(v * pieces + i, dest_count, stride=META_ROWS), :] = meta_v[
                v * dest_count : (v + 1) * dest_count, i * LANES : (i + 1) * LANES
            ]

    together = 8

    def narrow(i, _):
        for q in range(together):
            b = i * together + q
            at = pl.multiple_of(b * slot_rows, 16)
            first_v[b, :first_rows, :] = outf[pl.ds(at, first_rows), :].astype(jnp.bfloat16)
            first_v[b, first_rows:, :] = mrow[pl.ds(pl.multiple_of(b * META_ROWS, 16), META_ROWS), :].astype(jnp.bfloat16)
            last_v[b] = outf[pl.ds(at + first_rows, slot_rows - first_rows), :].astype(jnp.bfloat16)
        some = pl.ds(i * together, together)
        pltpu.make_async_copy(first_v.at[some], first_ref.at[some], sems.at[1]).start()
        pltpu.make_async_copy(last_v.at[some], last_ref.at[some], sems.at[2]).start()
        return 0

    lax.fori_loop(0, dest_count // together, narrow, 0)
    pltpu.make_async_copy(first_v, first_ref, sems.at[1]).wait()
    pltpu.make_async_copy(last_v, last_ref, sems.at[2]).wait()


def pack(pixels, weights, tile_index, tile_row, granule_day, time_count, space_count, rows_tm, slots):
    swath_rows = pixels.shape[0]
    chunks = swath_rows // LANES
    dest_count = time_count * space_count
    slot_rows, first_rows = split_rows(slots)
    width = round_up(slots, LANES)
    shape = (chunks, LANES)
    first_shape = (dest_count, first_rows + META_ROWS, LANES)
    last_shape = (dest_count, slot_rows - first_rows, LANES)
    return pl.pallas_call(
        functools.partial(pack_kernel, (time_count, space_count, rows_tm, slot_rows, first_rows, width)),
        in_specs=[pl.BlockSpec(memory_space=pltpu.VMEM)] * 4 + [pl.BlockSpec(memory_space=pl.ANY)],
        out_specs=[pl.BlockSpec(memory_space=pl.ANY)] * 2,
        out_shape=[jax.ShapeDtypeStruct(first_shape, jnp.bfloat16), jax.ShapeDtypeStruct(last_shape, jnp.bfloat16)],
        scratch_shapes=[
            pltpu.VMEM(shape, jnp.int32),
            pltpu.SMEM(shape, jnp.int32),
            pltpu.VMEM((5,) + shape, jnp.float32),
            pltpu.VMEM((3 * dest_count, width), jnp.float32),
            pltpu.VMEM((swath_rows, LANES), jnp.float32),
            pltpu.VMEM((dest_count * slot_rows, LANES), jnp.float32),
            pltpu.VMEM((dest_count * META_ROWS, LANES), jnp.float32),
            pltpu.VMEM(first_shape, jnp.bfloat16),
            pltpu.VMEM(last_shape, jnp.bfloat16),
            pltpu.VMEM((swath_rows, LANES), jnp.bfloat16),
            pltpu.VMEM((chunks * dest_count, LANES), jnp.bfloat16),
            pltpu.VMEM((chunks * dest_count, LANES), jnp.float32),
            pltpu.SemaphoreType.DMA((4,)),
        ],
        compiler_params=pltpu.CompilerParams(vmem_limit_bytes=VMEM),
        name="pack",
    )(
        tile_index.reshape(shape),
        tile_row.reshape(shape),
        granule_day.reshape(shape),
        weights.reshape(shape),
        pixels,
    )


def chunk_of(rows):
    return max(c for c in (32, 16) if rows % c == 0)


def add_rows(total, pixf, code_s, code_row, first_slot, rows, pix_at, count):
    chunk = chunk_of(rows)

    def add_group(row, lane, at):
        places = [code_s[row, lane + u] for u in range(GROUP)]
        made = [total[pl.ds(p, 1), :] + pixf[pl.ds(at + u, 1), :] for u, p in enumerate(places)]
        for p, value in zip(places, made):
            total[pl.ds(p, 1), :] = value

    def add_singly(row, lane, at):
        def one(u, _):
            p = code_s[row, lane + u]
            p = jnp.where(p >= CLASH, p - CLASH, p)
            total[pl.ds(p, 1), :] = total[pl.ds(p, 1), :] + pixf[pl.ds(at + u, 1), :]
            return 0

        lax.fori_loop(0, GROUP, one, 0)

    for start in range(0, rows, chunk):
        slot = first_slot + start
        row, lane = code_row(slot // LANES), slot % LANES
        at = pix_at + start
        heads = [code_s[row, lane + g] for g in range(0, chunk, GROUP)]
        clash = functools.reduce(jnp.maximum, heads) >= CLASH

        @pl.when((count > start) & jnp.logical_not(clash))
        def _():
            for g in range(0, chunk, GROUP):
                add_group(row, lane + g, at + g)

        @pl.when((count > start) & clash)
        def _():
            for g, head in zip(range(0, chunk, GROUP), heads):
                pl.when(head < CLASH)(functools.partial(add_group, row, lane + g, at + g))
                pl.when(head >= CLASH)(functools.partial(add_singly, row, lane + g, at + g))


def grid_first_kernel(
    dims, moved_ref, total_ref, code_ref, rest_ref, count_ref, column_ref, meta_v, pixf, code_s, count_s, sems
):
    time_count, space_count, rows_tm, slot_rows, first_rows, width = dims
    day_dev = DAYS // time_count
    blocks = time_count * space_count
    pieces = width // LANES
    spare = rows_tm * DAYS

    meta_v[...] = moved_ref[:, first_rows:, :].astype(jnp.float32).reshape(blocks * META_ROWS, LANES)
    block = lax.broadcasted_iota(jnp.int32, (blocks, LANES), 0)
    offset = jnp.zeros((blocks, LANES), jnp.float32)
    for m in range(1, time_count):
        offset = offset + jnp.where(block >= m * space_count, float(day_dev), 0.0)
    within = lax.broadcasted_iota(jnp.int32, (blocks, LANES), 1) % GROUP
    count = jnp.zeros((blocks, 1), jnp.float32)
    for i in range(pieces):
        weight, local_row, day = (meta_v[pl.ds(v * pieces + i, blocks, stride=META_ROWS), :] for v in range(3))
        used = weight > 0.0
        count = count + jnp.sum(jnp.where(used, 1.0, 0.0), axis=1, keepdims=True)
        column_ref[i * LANES : (i + 1) * LANES, :] = jnp.transpose(weight)
        code = jnp.where(used, local_row * DAYS + (day + offset), float(spare)).astype(jnp.int32)
        clash = jnp.zeros(code.shape, jnp.int32)
        for k in range(1, GROUP):
            ahead = pltpu.roll(code, LANES - k, 1)
            clash = jnp.where((ahead == code) & (within + k < GROUP) & (code < spare), 1, clash)
        k = 1
        while k < GROUP:
            ahead = pltpu.roll(clash, LANES - k, 1)
            clash = jnp.where(within + k < GROUP, jnp.maximum(clash, ahead), clash)
            k *= 2
        code_ref[i * blocks : (i + 1) * blocks, :] = jnp.where((within == 0) & (clash > 0), code + CLASH, code)
    rest_ref[...] = code_ref[first_rows // LANES * blocks :, :]
    count_ref[...] = jnp.broadcast_to(count, (blocks, LANES)).astype(jnp.int32)
    code_copy = pltpu.make_async_copy(code_ref, code_s, sems.at[0])
    count_copy = pltpu.make_async_copy(count_ref, count_s, sems.at[1])
    code_copy.start()
    count_copy.start()

    for b in range(blocks):
        column = column_ref[:first_rows, b : b + 1]
        pixf[b * first_rows : (b + 1) * first_rows, :] = moved_ref[b, :first_rows, :].astype(jnp.float32) * column

    def clear(i, _):
        total_ref[pl.ds(pl.multiple_of(i * DAYS, DAYS), DAYS), :] = jnp.zeros((DAYS, LANES), jnp.float32)
        return 0

    lax.fori_loop(0, rows_tm, clear, 0)
    total_ref[spare:, :] = jnp.zeros((8, LANES), jnp.float32)
    code_copy.wait()
    count_copy.wait()

    def add(b, _):
        add_rows(total_ref, pixf, code_s, lambda i: i * blocks + b, 0, first_rows, b * first_rows, count_s[b, 0])
        return 0

    lax.fori_loop(0, blocks, add, 0)


def grid_last_kernel(
    dims, code_s, count_s, column_ref, moved_ref, first_ref, field_ref, keep_ref, give_ref,
    total, first_v, moved_v, pixf, field_v, gram_v, first_sems, block_sems, out_sem
):
    time_count, space_count, rows_tm, slot_rows, first_rows, width = dims
    blocks = time_count * space_count
    last_rows = slot_rows - first_rows
    group = rows_tm // STEPS
    skipped = first_rows // LANES

    def load(i):
        at = pl.ds(pl.multiple_of(i * group * DAYS, DAYS), group * DAYS)
        return pltpu.make_async_copy(first_ref.at[at], first_v.at[at], first_sems.at[i])

    def fetch(b):
        return pltpu.make_async_copy(moved_ref.at[b], moved_v.at[b], block_sems.at[b])

    for b in range(blocks):
        pl.when(count_s[b, 0] > first_rows)(fetch(b).start)
    for i in range(STEPS):
        load(i).start()

    def clear(i, _):
        total[pl.ds(pl.multiple_of(i * DAYS, DAYS), DAYS), :] = jnp.zeros((DAYS, LANES), jnp.float32)
        return 0

    lax.fori_loop(0, rows_tm, clear, 0)
    total[rows_tm * DAYS :, :] = jnp.zeros((8, LANES), jnp.float32)
    for b in range(blocks):

        @pl.when(count_s[b, 0] > first_rows)
        def _():
            fetch(b).wait()
            column = column_ref[first_rows:slot_rows, b : b + 1]
            pixf[b * last_rows : (b + 1) * last_rows, :] = moved_v[b].astype(jnp.float32) * column

    def add(b, _):
        rest = count_s[b, 0] - first_rows

        @pl.when(rest > 0)
        def _():
            add_rows(
                total, pixf, code_s, lambda i: (i - skipped) * blocks + b, first_rows, last_rows, b * last_rows, rest
            )

        return 0

    lax.fori_loop(0, blocks, add, 0)

    def send(i):
        at = pl.ds(i * group, group)
        return pltpu.make_async_copy(field_v.at[at], field_ref.at[at], out_sem)

    def settle(i):
        for q in range(i * group, (i + 1) * group):
            at = pl.ds(q * DAYS, DAYS)
            field_v[q] = (first_v[at, :] + total[at, :]).astype(jnp.bfloat16)

    def multiply(i):
        both = jnp.concatenate([field_v[q] for q in range(i * group, (i + 1) * group)], axis=1)
        part = lax.dot_general(both[:RANK], both, LAST_LAST, preferred_element_type=jnp.float32)
        for c in range(DAYS // LANES):
            here = part[:, c * LANES : (c + 1) * LANES]
            at = slice(c * RANK, (c + 1) * RANK)
            gram_v[at, :] = here if i == 0 else gram_v[at, :] + here

    for i in range(STEPS):
        load(i).wait()
        settle(i)
        if i > 0:
            send(i - 1).start()
            multiply(i - 1)
    send(STEPS - 1).start()
    multiply(STEPS - 1)
    me = lax.axis_index("tm")
    rows = gram_v.shape[0] // time_count
    for i in range(time_count // 2):
        keep_ref[i] = gram_v[pl.ds(pl.multiple_of((me ^ (2 * i)) * rows, rows), rows), :]
        give_ref[i] = gram_v[pl.ds(pl.multiple_of((me ^ (2 * i + 1)) * rows, rows), rows), :]
    pltpu.make_async_copy(field_v, field_ref, out_sem).wait()


def grid_rows(moved_first, moved_last, time_count, space_count, rows_tm, slots):
    slot_rows, first_rows = split_rows(slots)
    last_rows = slot_rows - first_rows
    width = round_up(slots, LANES)
    blocks = time_count * space_count
    dims = (time_count, space_count, rows_tm, slot_rows, first_rows, width)
    codes = (blocks * width // LANES, LANES)
    rest = (codes[0] - first_rows // LANES * blocks, LANES)
    counts = (blocks, LANES)
    columns = (width, blocks)
    sums = (rows_tm * DAYS + 8, LANES)
    half = (time_count // 2, DAYS // LANES * RANK // time_count, LANES)
    params = pltpu.CompilerParams(vmem_limit_bytes=VMEM)
    total, _, code, count, column = pl.pallas_call(
        functools.partial(grid_first_kernel, dims),
        out_shape=[
            jax.ShapeDtypeStruct(sums, jnp.float32),
            jax.ShapeDtypeStruct(codes, jnp.int32),
            jax.ShapeDtypeStruct(rest, jnp.int32),
            jax.ShapeDtypeStruct(counts, jnp.int32),
            jax.ShapeDtypeStruct(columns, jnp.float32),
        ],
        scratch_shapes=[
            pltpu.VMEM((blocks * META_ROWS, LANES), jnp.float32),
            pltpu.VMEM((blocks * first_rows, LANES), jnp.float32),
            pltpu.SMEM(codes, jnp.int32),
            pltpu.SMEM(counts, jnp.int32),
            pltpu.SemaphoreType.DMA((2,)),
        ],
        compiler_params=params,
        cost_estimate=pl.CostEstimate(flops=0, bytes_accessed=60_000_000, transcendentals=0),
        name="grid_first",
    )(moved_first)
    whole = pl.BlockSpec(memory_space=pltpu.VMEM)
    return pl.pallas_call(
        functools.partial(grid_last_kernel, dims),
        in_specs=[
            pl.BlockSpec(memory_space=pltpu.SMEM),
            pl.BlockSpec(memory_space=pltpu.SMEM),
            whole,
            pl.BlockSpec(memory_space=pl.ANY),
            pl.BlockSpec(memory_space=pl.ANY),
        ],
        out_specs=[pl.BlockSpec(memory_space=pl.ANY), whole, whole],
        out_shape=[
            jax.ShapeDtypeStruct((rows_tm, DAYS, LANES), jnp.bfloat16),
            jax.ShapeDtypeStruct(half, jnp.float32),
            jax.ShapeDtypeStruct(half, jnp.float32),
        ],
        scratch_shapes=[
            pltpu.VMEM(sums, jnp.float32),
            pltpu.VMEM((rows_tm * DAYS, LANES), jnp.float32),
            pltpu.VMEM((blocks, last_rows, LANES), jnp.bfloat16),
            pltpu.VMEM((blocks * last_rows, LANES), jnp.float32),
            pltpu.VMEM((rows_tm, DAYS, LANES), jnp.bfloat16),
            pltpu.VMEM((DAYS // LANES * RANK, LANES), jnp.float32),
            pltpu.SemaphoreType.DMA((STEPS,)),
            pltpu.SemaphoreType.DMA((blocks,)),
            pltpu.SemaphoreType.DMA,
        ],
        compiler_params=params,
        name="grid_last_and_gram",
    )(code, count, column, moved_last, total)


def dot_f32(a, b, dims=(((1,), (0,)), ((), ()))):
    return lax.dot_general(a, b, dims, precision=lax.Precision.HIGHEST, preferred_element_type=jnp.float32)


def dot_three(a, b, dims=(((1,), (0,)), ((), ()))):
    a_high, b_high = a.astype(jnp.bfloat16), b.astype(jnp.bfloat16)
    a_low = (a - a_high.astype(jnp.float32)).astype(jnp.bfloat16)
    b_low = (b - b_high.astype(jnp.float32)).astype(jnp.bfloat16)
    left, right = dims[0][0][0], dims[0][1][0]
    a_all = jnp.concatenate([a_high, a_high, a_low], axis=left)
    b_all = jnp.concatenate([b_high, b_low, b_high], axis=right)
    return lax.dot_general(a_all, b_all, dims, preferred_element_type=jnp.float32)


def invert(x):
    guess = pl.reciprocal(x, approx=True)
    guess = guess * (2.0 - x * guess)
    return guess * (2.0 - x * guess)


def lower_inverse(a):
    n = a.shape[0]
    full = (8, n)
    tiles = [a[8 * i : 8 * i + 8, :] for i in range(n // 8)]
    lane = lax.broadcasted_iota(jnp.int32, full, 1)
    down = lax.broadcasted_iota(jnp.int32, full, 0)
    out = []
    for t in range(n // 8):
        k = 8 * t
        block = (lane >= k) & (lane < k + 8)
        panel = tiles[t]
        cols = [jnp.broadcast_to(panel[:, k + c : k + c + 1], full) for c in range(8)]
        e = {(i, c): jnp.broadcast_to(cols[c][i : i + 1, :], full) for c in range(8) for i in range(c, 8)}
        start = jnp.where(block, jnp.where(lane == k + down, 1.0, 0.0), panel)
        rows = [jnp.broadcast_to(start[i : i + 1, :], full) for i in range(8)]
        held = []
        for s in range(0, 8, 2):
            p, q, r = e[s, s], e[s + 1, s], e[s + 1, s + 1]
            det = p * r - q * q
            inv = invert(det)
            factors = {}
            for i in range(s + 2, 8):
                x, y = e[i, s], e[i, s + 1]
                factors[i] = (r * x - q * y, p * y - q * x)
            for i in range(s + 2, 8):
                u, v = factors[i]
                for c in range(s + 2, i + 1):
                    e[i, c] = e[i, c] - (u * e[c, s] + v * e[c, s + 1]) * inv
                rows[i] = rows[i] - (u * rows[s] + v * rows[s + 1]) * inv
            held.append((p, q, r, det, inv, factors))
        done = jnp.zeros(full, jnp.float32)
        solved = [None] * 8
        for s in (6, 4, 2, 0):
            p, q, r, det, inv, factors = held[s // 2]
            root = lax.rsqrt(p)
            done = jnp.where(down == s, rows[s] * root, done)
            done = jnp.where(down == s + 1, (rows[s + 1] * p - q * rows[s]) * (root * lax.rsqrt(det)), done)
            first, second = r * rows[s] - q * rows[s + 1], p * rows[s + 1] - q * rows[s]
            for i in range(7, s + 1, -1):
                u, v = factors[i]
                first, second = first - u * solved[i], second - v * solved[i]
            solved[s], solved[s + 1] = first * inv, second * inv
        out.append(jnp.where(lane < k + 8, done, 0.0))
        for i in range(t + 1, n // 8):
            terms = [jnp.broadcast_to(tiles[i][:, k + c : k + c + 1], full) * solved[c] for c in range(8)]
            while len(terms) > 1:
                terms = [terms[j] + terms[j + 1] for j in range(0, len(terms), 2)]
            tiles[i] = jnp.where(block, 0.0, tiles[i]) - terms[0]
    return jnp.concatenate(out, axis=0)


def solve_kernel(scale, *refs):
    *part_refs, field_ref, basis_ref, prop_ref, gram_v, field_v, basis_v, sems = refs
    h = LANES
    pieces = DAYS // h
    rows_here = field_v.shape[0]
    load = pltpu.make_async_copy(field_ref.at[:, pl.ds(0, RANK), :], field_v, sems.at[0])
    load.start()
    me = lax.axis_index("tm")
    rows = gram_v.shape[0] // len(part_refs)
    for j, part_ref in enumerate(part_refs):
        gram_v[pl.ds(pl.multiple_of((me ^ j) * rows, rows), rows), :] = part_ref[...]

    gram = jnp.concatenate([gram_v[i * RANK : (i + 1) * RANK, :] for i in range(pieces)], axis=1)
    eye = lax.broadcasted_iota(jnp.int32, (h, h), 0) == lax.broadcasted_iota(jnp.int32, (h, h), 1)
    a11, a12, a22 = gram[:h, :h], gram[:h, h : 2 * h], gram[h:, h : 2 * h]
    size_col, size_row = [], []
    for part in (a11, a22):
        diag = jnp.where(eye, part, 0.0)
        size_col.append(lax.rsqrt(jnp.sum(diag, axis=1, keepdims=True)))
        size_row.append(lax.rsqrt(jnp.sum(diag, axis=0, keepdims=True)))
    top, low = gram[:h], gram[h:]
    x1 = lower_inverse(a11 * size_col[0] * size_row[0])
    r12 = dot_f32(x1, a12 * size_col[0] * size_row[1])
    x2 = lower_inverse(a22 * size_col[1] * size_row[1] - dot_f32(r12, r12, FIRST_FIRST))
    factor_top = dot_f32(x1, top * size_col[0])
    schur = low[:, h:] * size_col[1] - dot_f32(r12, factor_top[:, h:], FIRST_FIRST)
    mixed = -dot_f32(x2, dot_f32(r12, x1, FIRST_FIRST))
    factor_low = dot_f32(x2, schur)
    lower = jnp.concatenate(
        [
            jnp.concatenate([x1 * size_row[0], jnp.zeros((h, h), jnp.float32)], axis=1),
            jnp.concatenate([mixed * size_row[0], x2 * size_row[1]], axis=1),
        ],
        axis=0,
    )
    inverse = (scale * lower).astype(jnp.bfloat16)
    load.wait()

    def project(i):
        both = jnp.concatenate([field_v[2 * i], field_v[2 * i + 1]], axis=1)
        made = jnp.dot(inverse, both, preferred_element_type=jnp.float32).astype(jnp.bfloat16)
        basis_v[2 * i] = made[:, :h]
        basis_v[2 * i + 1] = made[:, h:]

    down = lax.broadcasted_iota(jnp.int32, (RANK, DAYS), 0)
    across = lax.broadcasted_iota(jnp.int32, (RANK, DAYS), 1)
    factor = jnp.concatenate(
        [factor_top, jnp.concatenate([jnp.zeros((h, h), jnp.float32), factor_low], axis=1)], axis=0
    )
    factor = jnp.where(across >= down, factor, 0.0)
    ahead = jnp.where(across < DAYS - 1, pltpu.roll(factor, DAYS - 1, 1), 0.0)
    cross = dot_three(ahead, factor, LAST_LAST)
    polar = cross / jnp.sqrt(jnp.sum(cross * cross) + 1e-06)
    todo = list(range(rows_here // 2))
    share = -(-len(todo) // (ITERS - 1))
    store = pltpu.make_async_copy(basis_v, basis_ref, sems.at[1])
    for n in range(ITERS):
        square = dot_three(polar, polar, LAST_LAST)
        for i in todo[n * share : (n + 1) * share]:
            project(i)
        if n == ITERS - 2:
            store.start()
        polar = 1.5 * polar - 0.5 * dot_three(square, polar)
    prop_ref[...] = math.sqrt(RANK) * polar
    store.wait()


def solve(parts, field, cell_total):
    rows_tm = field.shape[0]
    part = (rows_tm, RANK, LANES)
    whole = pl.BlockSpec(memory_space=pltpu.VMEM)
    return pl.pallas_call(
        functools.partial(solve_kernel, math.sqrt(cell_total)),
        in_specs=[whole] * len(parts) + [pl.BlockSpec(memory_space=pl.ANY)],
        out_specs=[pl.BlockSpec(memory_space=pl.ANY), whole],
        out_shape=[
            jax.ShapeDtypeStruct(part, jnp.bfloat16),
            jax.ShapeDtypeStruct((RANK, RANK), jnp.float32),
        ],
        scratch_shapes=[
            pltpu.VMEM((DAYS // LANES * RANK, LANES), jnp.float32),
            pltpu.VMEM(part, jnp.bfloat16),
            pltpu.VMEM(part, jnp.bfloat16),
            pltpu.SemaphoreType.DMA((2,)),
        ],
        compiler_params=pltpu.CompilerParams(vmem_limit_bytes=VMEM),
        name="factor_basis_and_polar",
    )(*parts, field)


def body(pixels, weights, tile_index, tile_row, granule_day):
    swath_rows = pixels.shape[0]
    width = pixels.shape[1]
    space_count = lax.axis_size("space")
    time_count = lax.axis_size("tm")
    dest_count = time_count * space_count
    rows_tm = GR_DEV // time_count
    slots = 2 * swath_rows // space_count // time_count
    axes = ("tm", "space")
    first, last = pack(pixels, weights, tile_index, tile_row, granule_day, time_count, space_count, rows_tm, slots)
    first = lax.all_to_all(first, axes, split_axis=0, concat_axis=0, tiled=True)
    last = lax.all_to_all(last, axes, split_axis=0, concat_axis=0, tiled=True)
    field, keep, give = grid_rows(first, last, time_count, space_count, rows_tm, slots)

    def swap(value, distance):
        return lax.ppermute(value, "tm", [(t, t ^ distance) for t in range(time_count)])

    def among(value):
        return lax.all_to_all(value, "space", split_axis=0, concat_axis=0, tiled=True)

    held = keep + swap(give, 1)
    distances = []
    while held.shape[0] > 1:
        half = held.shape[0] // 2
        distances.append(2 * half)
        held = held[:half] + swap(held[half:], 2 * half)
    pieces = held.reshape(space_count, -1, LANES)
    mine = jnp.sum(among(pieces), axis=0, keepdims=True)
    parts = {0: among(jnp.broadcast_to(mine, pieces.shape)).reshape(-1, LANES)}
    for distance in reversed([1] + distances):
        parts.update({j ^ distance: swap(value, distance) for j, value in parts.items()})
    parts = [parts[j] for j in range(time_count)]
    cell_total = space_count * GR_DEV * width
    basis, propagator = solve(parts, field, cell_total)
    return (field[None], basis[None], propagator)


def solution(mesh):
    placed = (
        P(("tm", "space"), None),
        P(("tm", "space")),
        P(("tm", "space")),
        P(("tm", "space")),
        P(("tm", "space")),
    )
    return jax.shard_map(
        body,
        mesh=mesh,
        in_specs=placed,
        out_specs=(P("space", "tm", None, None), P("space", "tm", None, None), P()),
        check_vma=False,
    )
```

```python
import functools
import math

import jax
import jax.numpy as jnp
from jax import lax
from jax.experimental import pallas as pl
from jax.experimental.pallas import tpu as pltpu
from jax.sharding import PartitionSpec as P

GR_DEV = 160
DAYS = 512
RANK = 256
ITERS = 8
LANES = 128
META_ROWS = 16
GROUP = 16
CLASH = 1 << 20
STEPS = 5
VMEM = 46 * 1024 * 1024

LAST_LAST = (((1,), (1,)), ((), ()))
FIRST_FIRST = (((0,), (0,)), ((), ()))


def round_up(value, unit):
    return -(-value // unit) * unit


def split_rows(slots):
    rows = round_up(slots, 16)
    return rows, rows * 7 // 10 // 16 * 16


def pack_kernel(
    dims, tile_ref, row_ref, day_ref, weight_ref, pix_ref, first_ref, last_ref, pos_v, pos_s, rows_v, meta_v, pixf, outf, mrow,
    first_v, last_v, pix_v, hot_v, prefix_v, sems
):
    time_count, space_count, rows_tm, slot_rows, first_rows, width = dims
    dest_count = time_count * space_count
    chunks = tile_ref.shape[0]
    pieces = width // LANES

    fetch = pltpu.make_async_copy(pix_ref, pix_v, sems.at[3])
    fetch.start()
    tile = tile_ref[...]
    row = row_ref[...]
    group = jnp.zeros_like(row)
    for k in range(1, time_count):
        group = group + jnp.where(row >= k * rows_tm, 1, 0)
    dest_all = group * space_count + tile
    rows_v[0] = dest_all.astype(jnp.float32)
    rows_v[2] = weight_ref[...].astype(jnp.float32)
    rows_v[3] = (row - group * rows_tm).astype(jnp.float32)
    rows_v[4] = day_ref[...].astype(jnp.float32)

    dest_iota = lax.broadcasted_iota(jnp.int32, (dest_count, LANES), 0)
    upper = jnp.where(
        lax.broadcasted_iota(jnp.int32, (LANES, LANES), 0) <= lax.broadcasted_iota(jnp.int32, (LANES, LANES), 1), 1.0, 0.0
    ).astype(jnp.bfloat16)
    for c in range(chunks):
        hot = dest_iota == dest_all[c : c + 1, :]
        hot_v[c * dest_count : (c + 1) * dest_count, :] = jnp.where(hot, 1.0, 0.0).astype(jnp.bfloat16)
    prefix_v[...] = jnp.dot(hot_v[...], upper, preferred_element_type=jnp.float32)
    carry = jnp.zeros((dest_count, 1), jnp.float32)
    for c in range(chunks):
        prefix = prefix_v[c * dest_count : (c + 1) * dest_count, :]
        hot = dest_iota == dest_all[c : c + 1, :]
        rows_v[1, c : c + 1, :] = jnp.sum(jnp.where(hot, prefix + carry, 0.0), axis=0, keepdims=True) - 1.0
        carry = carry + prefix[:, LANES - 1 : LANES]
    pos_v[...] = dest_all * slot_rows + rows_v[1].astype(jnp.int32)
    copy = pltpu.make_async_copy(pos_v, pos_s, sems.at[0])
    copy.start()
    meta_v[...] = jnp.zeros_like(meta_v)
    mrow[...] = jnp.zeros_like(mrow)

    def clear(b, _):
        outf[pl.ds(pl.multiple_of(b * slot_rows, 16), slot_rows), :] = jnp.zeros((slot_rows, LANES), jnp.float32)
        return 0

    lax.fori_loop(0, dest_count, clear, 0)
    fetch.wait()
    copy.wait()
    dest_number = dest_iota.astype(jnp.float32)
    slot_number = lax.broadcasted_iota(jnp.int32, (width, LANES), 0).astype(jnp.float32)

    def move(c, _):
        base = pl.multiple_of(c * LANES, LANES)
        pixf[pl.ds(base, LANES), :] = pix_v[pl.ds(base, LANES), :].astype(jnp.float32)
        dest, rank, weight, local_row, day = (rows_v[v, pl.ds(c, 1), :] for v in range(5))
        hot = dest_number == dest
        place = jnp.where(slot_number == rank, 1.0, 0.0).astype(jnp.bfloat16)
        values = jnp.concatenate([jnp.where(hot, v, 0.0) for v in (weight, local_row, day)], axis=0).astype(jnp.bfloat16)
        meta_v[...] += lax.dot_general(values, place, LAST_LAST, preferred_element_type=jnp.float32)
        for lane in range(LANES):
            outf[pl.ds(pos_s[c, lane], 1), :] = pixf[pl.ds(base + lane, 1), :]
        return 0

    lax.fori_loop(0, chunks, move, 0)
    for v in range(3):
        for i in range(pieces):
            mrow[pl.ds(v * pieces + i, dest_count, stride=META_ROWS), :] = meta_v[
                v * dest_count : (v + 1) * dest_count, i * LANES : (i + 1) * LANES
            ]

    together = 8

    def narrow(i, _):
        for q in range(together):
            b = i * together + q
            at = pl.multiple_of(b * slot_rows, 16)
            first_v[b, :first_rows, :] = outf[pl.ds(at, first_rows), :].astype(jnp.bfloat16)
            first_v[b, first_rows:, :] = mrow[pl.ds(pl.multiple_of(b * META_ROWS, 16), META_ROWS), :].astype(jnp.bfloat16)
            last_v[b] = outf[pl.ds(at + first_rows, slot_rows - first_rows), :].astype(jnp.bfloat16)
        some = pl.ds(i * together, together)
        pltpu.make_async_copy(first_v.at[some], first_ref.at[some], sems.at[1]).start()
        pltpu.make_async_copy(last_v.at[some], last_ref.at[some], sems.at[2]).start()
        return 0

    lax.fori_loop(0, dest_count // together, narrow, 0)
    pltpu.make_async_copy(first_v, first_ref, sems.at[1]).wait()
    pltpu.make_async_copy(last_v, last_ref, sems.at[2]).wait()


def pack(pixels, weights, tile_index, tile_row, granule_day, time_count, space_count, rows_tm, slots):
    swath_rows = pixels.shape[0]
    chunks = swath_rows // LANES
    dest_count = time_count * space_count
    slot_rows, first_rows = split_rows(slots)
    width = round_up(slots, LANES)
    shape = (chunks, LANES)
    first_shape = (dest_count, first_rows + META_ROWS, LANES)
    last_shape = (dest_count, slot_rows - first_rows, LANES)
    return pl.pallas_call(
        functools.partial(pack_kernel, (time_count, space_count, rows_tm, slot_rows, first_rows, width)),
        in_specs=[pl.BlockSpec(memory_space=pltpu.VMEM)] * 4 + [pl.BlockSpec(memory_space=pl.ANY)],
        out_specs=[pl.BlockSpec(memory_space=pl.ANY)] * 2,
        out_shape=[jax.ShapeDtypeStruct(first_shape, jnp.bfloat16), jax.ShapeDtypeStruct(last_shape, jnp.bfloat16)],
        scratch_shapes=[
            pltpu.VMEM(shape, jnp.int32),
            pltpu.SMEM(shape, jnp.int32),
            pltpu.VMEM((5,) + shape, jnp.float32),
            pltpu.VMEM((3 * dest_count, width), jnp.float32),
            pltpu.VMEM((swath_rows, LANES), jnp.float32),
            pltpu.VMEM((dest_count * slot_rows, LANES), jnp.float32),
            pltpu.VMEM((dest_count * META_ROWS, LANES), jnp.float32),
            pltpu.VMEM(first_shape, jnp.bfloat16),
            pltpu.VMEM(last_shape, jnp.bfloat16),
            pltpu.VMEM((swath_rows, LANES), jnp.bfloat16),
            pltpu.VMEM((chunks * dest_count, LANES), jnp.bfloat16),
            pltpu.VMEM((chunks * dest_count, LANES), jnp.float32),
            pltpu.SemaphoreType.DMA((4,)),
        ],
        compiler_params=pltpu.CompilerParams(vmem_limit_bytes=VMEM),
        name="pack",
    )(
        tile_index.reshape(shape),
        tile_row.reshape(shape),
        granule_day.reshape(shape),
        weights.reshape(shape),
        pixels,
    )


def chunk_of(rows):
    return max(c for c in (32, 16) if rows % c == 0)


def add_rows(total, pixf, code_s, code_row, first_slot, rows, pix_at, count):
    chunk = chunk_of(rows)

    def add_group(row, lane, at):
        places = [code_s[row, lane + u] for u in range(GROUP)]
        made = [total[pl.ds(p, 1), :] + pixf[pl.ds(at + u, 1), :] for u, p in enumerate(places)]
        for p, value in zip(places, made):
            total[pl.ds(p, 1), :] = value

    def add_singly(row, lane, at):
        def one(u, _):
            p = code_s[row, lane + u]
            p = jnp.where(p >= CLASH, p - CLASH, p)
            total[pl.ds(p, 1), :] = total[pl.ds(p, 1), :] + pixf[pl.ds(at + u, 1), :]
            return 0

        lax.fori_loop(0, GROUP, one, 0)

    for start in range(0, rows, chunk):
        slot = first_slot + start
        row, lane = code_row(slot // LANES), slot % LANES
        at = pix_at + start
        heads = [code_s[row, lane + g] for g in range(0, chunk, GROUP)]
        clash = functools.reduce(jnp.maximum, heads) >= CLASH

        @pl.when((count > start) & jnp.logical_not(clash))
        def _():
            for g in range(0, chunk, GROUP):
                add_group(row, lane + g, at + g)

        @pl.when((count > start) & clash)
        def _():
            for g, head in zip(range(0, chunk, GROUP), heads):
                pl.when(head < CLASH)(functools.partial(add_group, row, lane + g, at + g))
                pl.when(head >= CLASH)(functools.partial(add_singly, row, lane + g, at + g))


def grid_first_kernel(
    dims, moved_ref, total_ref, code_ref, rest_ref, count_ref, column_ref, meta_v, pixf, code_s, count_s, sems
):
    time_count, space_count, rows_tm, slot_rows, first_rows, width = dims
    day_dev = DAYS // time_count
    blocks = time_count * space_count
    pieces = width // LANES
    spare = rows_tm * DAYS

    meta_v[...] = moved_ref[:, first_rows:, :].astype(jnp.float32).reshape(blocks * META_ROWS, LANES)
    block = lax.broadcasted_iota(jnp.int32, (blocks, LANES), 0)
    offset = jnp.zeros((blocks, LANES), jnp.float32)
    for m in range(1, time_count):
        offset = offset + jnp.where(block >= m * space_count, float(day_dev), 0.0)
    within = lax.broadcasted_iota(jnp.int32, (blocks, LANES), 1) % GROUP
    count = jnp.zeros((blocks, 1), jnp.float32)
    for i in range(pieces):
        weight, local_row, day = (meta_v[pl.ds(v * pieces + i, blocks, stride=META_ROWS), :] for v in range(3))
        used = weight > 0.0
        count = count + jnp.sum(jnp.where(used, 1.0, 0.0), axis=1, keepdims=True)
        column_ref[i * LANES : (i + 1) * LANES, :] = jnp.transpose(weight)
        code = jnp.where(used, local_row * DAYS + (day + offset), float(spare)).astype(jnp.int32)
        clash = jnp.zeros(code.shape, jnp.int32)
        for k in range(1, GROUP):
            ahead = pltpu.roll(code, LANES - k, 1)
            clash = jnp.where((ahead == code) & (within + k < GROUP) & (code < spare), 1, clash)
        k = 1
        while k < GROUP:
            ahead = pltpu.roll(clash, LANES - k, 1)
            clash = jnp.where(within + k < GROUP, jnp.maximum(clash, ahead), clash)
            k *= 2
        code_ref[i * blocks : (i + 1) * blocks, :] = jnp.where((within == 0) & (clash > 0), code + CLASH, code)
    rest_ref[...] = code_ref[first_rows // LANES * blocks :, :]
    count_ref[...] = jnp.broadcast_to(count, (blocks, LANES)).astype(jnp.int32)
    code_copy = pltpu.make_async_copy(code_ref, code_s, sems.at[0])
    count_copy = pltpu.make_async_copy(count_ref, count_s, sems.at[1])
    code_copy.start()
    count_copy.start()

    for b in range(blocks):
        column = column_ref[:first_rows, b : b + 1]
        pixf[b * first_rows : (b + 1) * first_rows, :] = moved_ref[b, :first_rows, :].astype(jnp.float32) * column

    def clear(i, _):
        total_ref[pl.ds(pl.multiple_of(i * DAYS, DAYS), DAYS), :] = jnp.zeros((DAYS, LANES), jnp.float32)
        return 0

    lax.fori_loop(0, rows_tm, clear, 0)
    total_ref[spare:, :] = jnp.zeros((8, LANES), jnp.float32)
    code_copy.wait()
    count_copy.wait()

    def add(b, _):
        add_rows(total_ref, pixf, code_s, lambda i: i * blocks + b, 0, first_rows, b * first_rows, count_s[b, 0])
        return 0

    lax.fori_loop(0, blocks, add, 0)


def grid_last_kernel(
    dims, code_s, count_s, column_ref, moved_ref, first_ref, field_ref, keep_ref, give_ref,
    total, first_v, moved_v, pixf, field_v, gram_v, first_sems, block_sems, out_sem
):
    time_count, space_count, rows_tm, slot_rows, first_rows, width = dims
    blocks = time_count * space_count
    last_rows = slot_rows - first_rows
    group = rows_tm // STEPS
    skipped = first_rows // LANES

    def load(i):
        at = pl.ds(pl.multiple_of(i * group * DAYS, DAYS), group * DAYS)
        return pltpu.make_async_copy(first_ref.at[at], first_v.at[at], first_sems.at[i])

    def fetch(b):
        return pltpu.make_async_copy(moved_ref.at[b], moved_v.at[b], block_sems.at[b])

    for b in range(blocks):
        pl.when(count_s[b, 0] > first_rows)(fetch(b).start)
    for i in range(STEPS):
        load(i).start()

    def clear(i, _):
        total[pl.ds(pl.multiple_of(i * DAYS, DAYS), DAYS), :] = jnp.zeros((DAYS, LANES), jnp.float32)
        return 0

    lax.fori_loop(0, rows_tm, clear, 0)
    total[rows_tm * DAYS :, :] = jnp.zeros((8, LANES), jnp.float32)
    for b in range(blocks):

        @pl.when(count_s[b, 0] > first_rows)
        def _():
            fetch(b).wait()
            column = column_ref[first_rows:slot_rows, b : b + 1]
            pixf[b * last_rows : (b + 1) * last_rows, :] = moved_v[b].astype(jnp.float32) * column

    def add(b, _):
        rest = count_s[b, 0] - first_rows

        @pl.when(rest > 0)
        def _():
            add_rows(
                total, pixf, code_s, lambda i: (i - skipped) * blocks + b, first_rows, last_rows, b * last_rows, rest
            )

        return 0

    lax.fori_loop(0, blocks, add, 0)

    def send(i):
        at = pl.ds(i * group, group)
        return pltpu.make_async_copy(field_v.at[at], field_ref.at[at], out_sem)

    def settle(i):
        for q in range(i * group, (i + 1) * group):
            at = pl.ds(q * DAYS, DAYS)
            field_v[q] = (first_v[at, :] + total[at, :]).astype(jnp.bfloat16)

    def multiply(i):
        both = jnp.concatenate([field_v[q] for q in range(i * group, (i + 1) * group)], axis=1)
        part = lax.dot_general(both[:RANK], both, LAST_LAST, preferred_element_type=jnp.float32)
        for c in range(DAYS // LANES):
            here = part[:, c * LANES : (c + 1) * LANES]
            gram_v[c] = here if i == 0 else gram_v[c] + here

    for i in range(STEPS):
        load(i).wait()
        settle(i)
        if i > 0:
            send(i - 1).start()
            multiply(i - 1)
    send(STEPS - 1).start()
    multiply(STEPS - 1)
    odd = lax.axis_index("tm") % 2
    half = DAYS // LANES // 2
    for c in range(half):
        keep_ref[c] = gram_v[odd * half + c]
        give_ref[c] = gram_v[(1 - odd) * half + c]
    pltpu.make_async_copy(field_v, field_ref, out_sem).wait()


def grid_rows(moved_first, moved_last, time_count, space_count, rows_tm, slots):
    slot_rows, first_rows = split_rows(slots)
    last_rows = slot_rows - first_rows
    width = round_up(slots, LANES)
    blocks = time_count * space_count
    dims = (time_count, space_count, rows_tm, slot_rows, first_rows, width)
    codes = (blocks * width // LANES, LANES)
    rest = (codes[0] - first_rows // LANES * blocks, LANES)
    counts = (blocks, LANES)
    columns = (width, blocks)
    sums = (rows_tm * DAYS + 8, LANES)
    half = (DAYS // LANES // 2, RANK, LANES)
    params = pltpu.CompilerParams(vmem_limit_bytes=VMEM)
    total, _, code, count, column = pl.pallas_call(
        functools.partial(grid_first_kernel, dims),
        out_shape=[
            pltpu.VMEM(sums, jnp.float32),
            jax.ShapeDtypeStruct(codes, jnp.int32),
            jax.ShapeDtypeStruct(rest, jnp.int32),
            jax.ShapeDtypeStruct(counts, jnp.int32),
            jax.ShapeDtypeStruct(columns, jnp.float32),
        ],
        scratch_shapes=[
            pltpu.VMEM((blocks * META_ROWS, LANES), jnp.float32),
            pltpu.VMEM((blocks * first_rows, LANES), jnp.float32),
            pltpu.SMEM(codes, jnp.int32),
            pltpu.SMEM(counts, jnp.int32),
            pltpu.SemaphoreType.DMA((2,)),
        ],
        compiler_params=params,
        cost_estimate=pl.CostEstimate(flops=0, bytes_accessed=60_000_000, transcendentals=0),
        name="grid_first",
    )(moved_first)
    total = pltpu.with_memory_space_constraint(total, pltpu.VMEM)
    moved_last = pltpu.with_memory_space_constraint(moved_last, pltpu.VMEM)
    whole = pl.BlockSpec(memory_space=pltpu.VMEM)
    return pl.pallas_call(
        functools.partial(grid_last_kernel, dims),
        in_specs=[
            pl.BlockSpec(memory_space=pltpu.SMEM),
            pl.BlockSpec(memory_space=pltpu.SMEM),
            whole,
            pl.BlockSpec(memory_space=pl.ANY),
            pl.BlockSpec(memory_space=pl.ANY),
        ],
        out_specs=[pl.BlockSpec(memory_space=pl.ANY), whole, whole],
        out_shape=[
            jax.ShapeDtypeStruct((rows_tm, DAYS, LANES), jnp.bfloat16),
            jax.ShapeDtypeStruct(half, jnp.float32),
            jax.ShapeDtypeStruct(half, jnp.float32),
        ],
        scratch_shapes=[
            pltpu.VMEM(sums, jnp.float32),
            pltpu.VMEM((rows_tm * DAYS, LANES), jnp.float32),
            pltpu.VMEM((blocks, last_rows, LANES), jnp.bfloat16),
            pltpu.VMEM((blocks * last_rows, LANES), jnp.float32),
            pltpu.VMEM((rows_tm, DAYS, LANES), jnp.bfloat16),
            pltpu.VMEM((DAYS // LANES, RANK, LANES), jnp.float32),
            pltpu.SemaphoreType.DMA((STEPS,)),
            pltpu.SemaphoreType.DMA((blocks,)),
            pltpu.SemaphoreType.DMA,
        ],
        compiler_params=params,
        name="grid_last_and_gram",
    )(code, count, column, moved_last, total)


def dot_f32(a, b, dims=(((1,), (0,)), ((), ()))):
    return lax.dot_general(a, b, dims, precision=lax.Precision.HIGHEST, preferred_element_type=jnp.float32)


def dot_three(a, b, dims=(((1,), (0,)), ((), ()))):
    a_high, b_high = a.astype(jnp.bfloat16), b.astype(jnp.bfloat16)
    a_low = (a - a_high.astype(jnp.float32)).astype(jnp.bfloat16)
    b_low = (b - b_high.astype(jnp.float32)).astype(jnp.bfloat16)
    left, right = dims[0][0][0], dims[0][1][0]
    a_all = jnp.concatenate([a_high, a_high, a_low], axis=left)
    b_all = jnp.concatenate([b_high, b_low, b_high], axis=right)
    return lax.dot_general(a_all, b_all, dims, preferred_element_type=jnp.float32)


def invert(x):
    guess = pl.reciprocal(x, approx=True)
    guess = guess * (2.0 - x * guess)
    return guess * (2.0 - x * guess)


def lower_inverse(a):
    n = a.shape[0]
    full = (8, n)
    tiles = [a[8 * i : 8 * i + 8, :] for i in range(n // 8)]
    lane = lax.broadcasted_iota(jnp.int32, full, 1)
    down = lax.broadcasted_iota(jnp.int32, full, 0)
    out = []
    for t in range(n // 8):
        k = 8 * t
        block = (lane >= k) & (lane < k + 8)
        panel = tiles[t]
        cols = [jnp.broadcast_to(panel[:, k + c : k + c + 1], full) for c in range(8)]
        e = {(i, c): jnp.broadcast_to(cols[c][i : i + 1, :], full) for c in range(8) for i in range(c, 8)}
        start = jnp.where(block, jnp.where(lane == k + down, 1.0, 0.0), panel)
        rows = [jnp.broadcast_to(start[i : i + 1, :], full) for i in range(8)]
        held = []
        for s in range(0, 8, 2):
            p, q, r = e[s, s], e[s + 1, s], e[s + 1, s + 1]
            det = p * r - q * q
            inv = invert(det)
            factors = {}
            for i in range(s + 2, 8):
                x, y = e[i, s], e[i, s + 1]
                factors[i] = (r * x - q * y, p * y - q * x)
            for i in range(s + 2, 8):
                u, v = factors[i]
                for c in range(s + 2, i + 1):
                    e[i, c] = e[i, c] - (u * e[c, s] + v * e[c, s + 1]) * inv
                rows[i] = rows[i] - (u * rows[s] + v * rows[s + 1]) * inv
            held.append((p, q, r, det, inv, factors))
        done = jnp.zeros(full, jnp.float32)
        solved = [None] * 8
        for s in (6, 4, 2, 0):
            p, q, r, det, inv, factors = held[s // 2]
            root = lax.rsqrt(p)
            done = jnp.where(down == s, rows[s] * root, done)
            done = jnp.where(down == s + 1, (rows[s + 1] * p - q * rows[s]) * (root * lax.rsqrt(det)), done)
            first, second = r * rows[s] - q * rows[s + 1], p * rows[s + 1] - q * rows[s]
            for i in range(7, s + 1, -1):
                u, v = factors[i]
                first, second = first - u * solved[i], second - v * solved[i]
            solved[s], solved[s + 1] = first * inv, second * inv
        out.append(jnp.where(lane < k + 8, done, 0.0))
        for i in range(t + 1, n // 8):
            terms = [jnp.broadcast_to(tiles[i][:, k + c : k + c + 1], full) * solved[c] for c in range(8)]
            while len(terms) > 1:
                terms = [terms[j] + terms[j + 1] for j in range(0, len(terms), 2)]
            tiles[i] = jnp.where(block, 0.0, tiles[i]) - terms[0]
    return jnp.concatenate(out, axis=0)


def solve_kernel(scale, own_ref, other_ref, field_ref, basis_ref, prop_ref, gram_v, field_v, basis_v, sems):
    h = LANES
    pieces = DAYS // h
    rows_here = field_v.shape[0]
    load = pltpu.make_async_copy(field_ref.at[:, pl.ds(0, RANK), :], field_v, sems.at[0])
    load.start()
    odd = lax.axis_index("tm") % 2
    for c in range(pieces // 2):
        gram_v[odd * (pieces // 2) + c] = own_ref[c]
        gram_v[(1 - odd) * (pieces // 2) + c] = other_ref[c]

    gram = jnp.concatenate([gram_v[i] for i in range(pieces)], axis=1)
    eye = lax.broadcasted_iota(jnp.int32, (h, h), 0) == lax.broadcasted_iota(jnp.int32, (h, h), 1)
    a11, a12, a22 = gram_v[0, :h, :], gram_v[1, :h, :], gram_v[1, h:, :]
    size_col, size_row = [], []
    for part in (a11, a22):
        diag = jnp.where(eye, part, 0.0)
        size_col.append(lax.rsqrt(jnp.sum(diag, axis=1, keepdims=True)))
        size_row.append(lax.rsqrt(jnp.sum(diag, axis=0, keepdims=True)))
    top, low = gram[:h], gram[h:]
    x1 = lower_inverse(a11 * size_col[0] * size_row[0])
    r12 = dot_f32(x1, a12 * size_col[0] * size_row[1])
    x2 = lower_inverse(a22 * size_col[1] * size_row[1] - dot_f32(r12, r12, FIRST_FIRST))
    factor_top = dot_f32(x1, top * size_col[0])
    schur = low[:, h:] * size_col[1] - dot_f32(r12, factor_top[:, h:], FIRST_FIRST)
    mixed = -dot_f32(x2, dot_f32(r12, x1, FIRST_FIRST))
    factor_low = dot_f32(x2, schur)
    lower = jnp.concatenate(
        [
            jnp.concatenate([x1 * size_row[0], jnp.zeros((h, h), jnp.float32)], axis=1),
            jnp.concatenate([mixed * size_row[0], x2 * size_row[1]], axis=1),
        ],
        axis=0,
    )
    inverse = (scale * lower).astype(jnp.bfloat16)
    load.wait()

    def project(i):
        both = jnp.concatenate([field_v[2 * i], field_v[2 * i + 1]], axis=1)
        made = jnp.dot(inverse, both, preferred_element_type=jnp.float32).astype(jnp.bfloat16)
        basis_v[2 * i] = made[:, :h]
        basis_v[2 * i + 1] = made[:, h:]

    down = lax.broadcasted_iota(jnp.int32, (RANK, DAYS), 0)
    across = lax.broadcasted_iota(jnp.int32, (RANK, DAYS), 1)
    factor = jnp.concatenate(
        [factor_top, jnp.concatenate([jnp.zeros((h, h), jnp.float32), factor_low], axis=1)], axis=0
    )
    factor = jnp.where(across >= down, factor, 0.0)
    ahead = jnp.where(across < DAYS - 1, pltpu.roll(factor, DAYS - 1, 1), 0.0)
    cross = dot_three(ahead, factor, LAST_LAST)
    polar = cross / jnp.sqrt(jnp.sum(cross * cross) + 1e-06)
    todo = list(range(rows_here // 2))
    share = -(-len(todo) // (ITERS - 1))
    store = pltpu.make_async_copy(basis_v, basis_ref, sems.at[1])
    for n in range(ITERS):
        square = dot_three(polar, polar, LAST_LAST)
        for i in todo[n * share : (n + 1) * share]:
            project(i)
        if n == ITERS - 2:
            store.start()
        polar = 1.5 * polar - 0.5 * dot_three(square, polar)
    prop_ref[...] = math.sqrt(RANK) * polar
    store.wait()


def solve(own, other, field, cell_total):
    rows_tm = field.shape[0]
    part = (rows_tm, RANK, LANES)
    whole = pl.BlockSpec(memory_space=pltpu.VMEM)
    own, other = (pltpu.with_memory_space_constraint(v, pltpu.VMEM) for v in (own, other))
    return pl.pallas_call(
        functools.partial(solve_kernel, math.sqrt(cell_total)),
        in_specs=[whole, whole, pl.BlockSpec(memory_space=pl.ANY)],
        out_specs=[pl.BlockSpec(memory_space=pl.ANY), whole],
        out_shape=[
            jax.ShapeDtypeStruct(part, jnp.bfloat16),
            jax.ShapeDtypeStruct((RANK, RANK), jnp.float32),
        ],
        scratch_shapes=[
            pltpu.VMEM((DAYS // LANES, RANK, LANES), jnp.float32),
            pltpu.VMEM(part, jnp.bfloat16),
            pltpu.VMEM(part, jnp.bfloat16),
            pltpu.SemaphoreType.DMA((2,)),
        ],
        compiler_params=pltpu.CompilerParams(vmem_limit_bytes=VMEM),
        name="factor_basis_and_polar",
    )(own, other, field)


def body(pixels, weights, tile_index, tile_row, granule_day):
    swath_rows = pixels.shape[0]
    width = pixels.shape[1]
    space_count = lax.axis_size("space")
    time_count = lax.axis_size("tm")
    dest_count = time_count * space_count
    rows_tm = GR_DEV // time_count
    slots = 2 * swath_rows // space_count // time_count
    axes = ("tm", "space")
    first, last = pack(pixels, weights, tile_index, tile_row, granule_day, time_count, space_count, rows_tm, slots)
    first = lax.all_to_all(first, axes, split_axis=0, concat_axis=0, tiled=True)
    last = lax.all_to_all(last, axes, split_axis=0, concat_axis=0, tiled=True)
    field, keep, give = grid_rows(first, last, time_count, space_count, rows_tm, slots)

    swap = [(t, t ^ 1) for t in range(time_count)]
    peers = [[t * space_count + s for t in range(core, time_count, 2) for s in range(space_count)] for core in (0, 1)]
    among = functools.partial(
        lax.all_to_all, axis_name=axes, split_axis=0, concat_axis=0, axis_index_groups=peers, tiled=True
    )
    pieces = (keep + lax.ppermute(give, "tm", swap)).reshape(dest_count // 2, -1, LANES)
    mine = jnp.sum(among(pieces), axis=0, keepdims=True)
    own = among(jnp.broadcast_to(mine, pieces.shape)).reshape(keep.shape)
    other = lax.ppermute(own, "tm", swap)
    cell_total = space_count * GR_DEV * width
    basis, propagator = solve(own, other, field, cell_total)
    return (field[None], basis[None], propagator)


def solution(mesh):
    placed = (
        P(("tm", "space"), None),
        P(("tm", "space")),
        P(("tm", "space")),
        P(("tm", "space")),
        P(("tm", "space")),
    )
    return jax.shard_map(
        body,
        mesh=mesh,
        in_specs=placed,
        out_specs=(P("space", "tm", None, None), P("space", "tm", None, None), P()),
        check_vma=False,
    )
```

```python
import functools
import math

import jax
import jax.numpy as jnp
from jax import lax
from jax.experimental import pallas as pl
from jax.experimental.pallas import tpu as pltpu
from jax.sharding import PartitionSpec as P

GR_DEV = 160
DAYS = 512
RANK = 256
ITERS = 8
LANES = 128
META_ROWS = 16
GROUP = 16
CLASH = 1 << 20
STEPS = 5
VMEM = 56 * 1024 * 1024

LAST_LAST = (((1,), (1,)), ((), ()))
FIRST_FIRST = (((0,), (0,)), ((), ()))


def round_up(value, unit):
    return -(-value // unit) * unit


def split_rows(slots):
    rows = round_up(slots, 16)
    return rows, rows * 13 // 20 // 16 * 16


def pack_kernel(
    dims, tile_ref, row_ref, day_ref, weight_ref, pix_ref, first_ref, last_ref, pos_v, pos_s, rows_v, meta_v, pixf, outf, mrow,
    first_v, last_v, pix_v, hot_v, prefix_v, sems
):
    time_count, space_count, rows_tm, slot_rows, first_rows, width = dims
    dest_count = time_count * space_count
    chunks = tile_ref.shape[0]
    pieces = width // LANES

    fetch = pltpu.make_async_copy(pix_ref, pix_v, sems.at[3])
    fetch.start()
    tile = tile_ref[...]
    row = row_ref[...]
    group = jnp.zeros_like(row)
    for k in range(1, time_count):
        group = group + jnp.where(row >= k * rows_tm, 1, 0)
    dest_all = group * space_count + tile
    rows_v[0] = dest_all.astype(jnp.float32)
    rows_v[2] = weight_ref[...].astype(jnp.float32)
    rows_v[3] = (row - group * rows_tm).astype(jnp.float32)
    rows_v[4] = day_ref[...].astype(jnp.float32)

    dest_iota = lax.broadcasted_iota(jnp.int32, (dest_count, LANES), 0)
    upper = jnp.where(
        lax.broadcasted_iota(jnp.int32, (LANES, LANES), 0) <= lax.broadcasted_iota(jnp.int32, (LANES, LANES), 1), 1.0, 0.0
    ).astype(jnp.bfloat16)
    for c in range(chunks):
        hot = dest_iota == dest_all[c : c + 1, :]
        hot_v[c * dest_count : (c + 1) * dest_count, :] = jnp.where(hot, 1.0, 0.0).astype(jnp.bfloat16)
    prefix_v[...] = jnp.dot(hot_v[...], upper, preferred_element_type=jnp.float32)
    carry = jnp.zeros((dest_count, 1), jnp.float32)
    for c in range(chunks):
        prefix = prefix_v[c * dest_count : (c + 1) * dest_count, :]
        hot = dest_iota == dest_all[c : c + 1, :]
        rows_v[1, c : c + 1, :] = jnp.sum(jnp.where(hot, prefix + carry, 0.0), axis=0, keepdims=True) - 1.0
        carry = carry + prefix[:, LANES - 1 : LANES]
    pos_v[...] = dest_all * slot_rows + rows_v[1].astype(jnp.int32)
    copy = pltpu.make_async_copy(pos_v, pos_s, sems.at[0])
    copy.start()
    meta_v[...] = jnp.zeros_like(meta_v)
    mrow[...] = jnp.zeros_like(mrow)

    def clear(b, _):
        outf[pl.ds(pl.multiple_of(b * slot_rows, 16), slot_rows), :] = jnp.zeros((slot_rows, LANES), jnp.float32)
        return 0

    lax.fori_loop(0, dest_count, clear, 0)
    fetch.wait()
    copy.wait()
    dest_number = dest_iota.astype(jnp.float32)
    slot_number = lax.broadcasted_iota(jnp.int32, (width, LANES), 0).astype(jnp.float32)

    def move(c, _):
        base = pl.multiple_of(c * LANES, LANES)
        pixf[pl.ds(base, LANES), :] = pix_v[pl.ds(base, LANES), :].astype(jnp.float32)
        dest, rank, weight, local_row, day = (rows_v[v, pl.ds(c, 1), :] for v in range(5))
        hot = dest_number == dest
        place = jnp.where(slot_number == rank, 1.0, 0.0).astype(jnp.bfloat16)
        values = jnp.concatenate([jnp.where(hot, v, 0.0) for v in (weight, local_row, day)], axis=0).astype(jnp.bfloat16)
        meta_v[...] += lax.dot_general(values, place, LAST_LAST, preferred_element_type=jnp.float32)
        for lane in range(LANES):
            outf[pl.ds(pos_s[c, lane], 1), :] = pixf[pl.ds(base + lane, 1), :]
        return 0

    lax.fori_loop(0, chunks, move, 0)
    for v in range(3):
        for i in range(pieces):
            mrow[pl.ds(v * pieces + i, dest_count, stride=META_ROWS), :] = meta_v[
                v * dest_count : (v + 1) * dest_count, i * LANES : (i + 1) * LANES
            ]

    together = 8

    def narrow(i, _):
        for q in range(together):
            b = i * together + q
            at = pl.multiple_of(b * slot_rows, 16)
            first_v[b, :first_rows, :] = outf[pl.ds(at, first_rows), :].astype(jnp.bfloat16)
            first_v[b, first_rows:, :] = mrow[pl.ds(pl.multiple_of(b * META_ROWS, 16), META_ROWS), :].astype(jnp.bfloat16)
            last_v[b] = outf[pl.ds(at + first_rows, slot_rows - first_rows), :].astype(jnp.bfloat16)
        some = pl.ds(i * together, together)
        pltpu.make_async_copy(first_v.at[some], first_ref.at[some], sems.at[1]).start()
        pltpu.make_async_copy(last_v.at[some], last_ref.at[some], sems.at[2]).start()
        return 0

    lax.fori_loop(0, dest_count // together, narrow, 0)
    pltpu.make_async_copy(first_v, first_ref, sems.at[1]).wait()
    pltpu.make_async_copy(last_v, last_ref, sems.at[2]).wait()


def pack(pixels, weights, tile_index, tile_row, granule_day, time_count, space_count, rows_tm, slots):
    swath_rows = pixels.shape[0]
    chunks = swath_rows // LANES
    dest_count = time_count * space_count
    slot_rows, first_rows = split_rows(slots)
    width = round_up(slots, LANES)
    shape = (chunks, LANES)
    first_shape = (dest_count, first_rows + META_ROWS, LANES)
    last_shape = (dest_count, slot_rows - first_rows, LANES)
    return pl.pallas_call(
        functools.partial(pack_kernel, (time_count, space_count, rows_tm, slot_rows, first_rows, width)),
        in_specs=[pl.BlockSpec(memory_space=pltpu.VMEM)] * 4 + [pl.BlockSpec(memory_space=pl.ANY)],
        out_specs=[pl.BlockSpec(memory_space=pl.ANY)] * 2,
        out_shape=[jax.ShapeDtypeStruct(first_shape, jnp.bfloat16), jax.ShapeDtypeStruct(last_shape, jnp.bfloat16)],
        scratch_shapes=[
            pltpu.VMEM(shape, jnp.int32),
            pltpu.SMEM(shape, jnp.int32),
            pltpu.VMEM((5,) + shape, jnp.float32),
            pltpu.VMEM((3 * dest_count, width), jnp.float32),
            pltpu.VMEM((swath_rows, LANES), jnp.float32),
            pltpu.VMEM((dest_count * slot_rows, LANES), jnp.float32),
            pltpu.VMEM((dest_count * META_ROWS, LANES), jnp.float32),
            pltpu.VMEM(first_shape, jnp.bfloat16),
            pltpu.VMEM(last_shape, jnp.bfloat16),
            pltpu.VMEM((swath_rows, LANES), jnp.bfloat16),
            pltpu.VMEM((chunks * dest_count, LANES), jnp.bfloat16),
            pltpu.VMEM((chunks * dest_count, LANES), jnp.float32),
            pltpu.SemaphoreType.DMA((4,)),
        ],
        compiler_params=pltpu.CompilerParams(vmem_limit_bytes=VMEM),
        name="pack",
    )(
        tile_index.reshape(shape),
        tile_row.reshape(shape),
        granule_day.reshape(shape),
        weights.reshape(shape),
        pixels,
    )


def chunks_of(first_slot, rows):
    slot, found = first_slot, []
    while slot < first_slot + rows:
        size = min(32 - slot % 32, first_slot + rows - slot)
        found.append((slot, size))
        slot += size
    return found


def add_rows(total, pixf, code_s, code_row, first_slot, rows, pix_at, count):
    def add_group(row, lane, at):
        places = [code_s[row, lane + u] for u in range(GROUP)]
        made = [total[pl.ds(p, 1), :] + pixf[pl.ds(at + u, 1), :] for u, p in enumerate(places)]
        for p, value in zip(places, made):
            total[pl.ds(p, 1), :] = value

    def add_singly(row, lane, at):
        def one(u, _):
            p = code_s[row, lane + u]
            p = jnp.where(p >= CLASH, p - CLASH, p)
            total[pl.ds(p, 1), :] = total[pl.ds(p, 1), :] + pixf[pl.ds(at + u, 1), :]
            return 0

        lax.fori_loop(0, GROUP, one, 0)

    for slot, chunk in chunks_of(first_slot, rows):
        start = slot - first_slot
        row, lane = code_row(slot // LANES), slot % LANES
        at = pix_at + start
        heads = [code_s[row, lane + g] for g in range(0, chunk, GROUP)]
        clash = functools.reduce(jnp.maximum, heads) >= CLASH

        @pl.when((count > start) & jnp.logical_not(clash))
        def _():
            for g in range(0, chunk, GROUP):
                add_group(row, lane + g, at + g)

        @pl.when((count > start) & clash)
        def _():
            for g, head in zip(range(0, chunk, GROUP), heads):
                pl.when(head < CLASH)(functools.partial(add_group, row, lane + g, at + g))
                pl.when(head >= CLASH)(functools.partial(add_singly, row, lane + g, at + g))


def grid_first_kernel(
    dims, moved_ref, total_ref, code_ref, rest_ref, count_ref, column_ref, meta_v, pixf, code_s, count_s, sems
):
    time_count, space_count, rows_tm, slot_rows, first_rows, width = dims
    day_dev = DAYS // time_count
    blocks = time_count * space_count
    pieces = width // LANES
    spare = rows_tm * DAYS

    meta_v[...] = moved_ref[:, first_rows:, :].astype(jnp.float32).reshape(blocks * META_ROWS, LANES)
    block = lax.broadcasted_iota(jnp.int32, (blocks, LANES), 0)
    offset = jnp.zeros((blocks, LANES), jnp.float32)
    for m in range(1, time_count):
        offset = offset + jnp.where(block >= m * space_count, float(day_dev), 0.0)
    within = lax.broadcasted_iota(jnp.int32, (blocks, LANES), 1) % GROUP
    count = jnp.zeros((blocks, 1), jnp.float32)
    for i in range(pieces):
        weight, local_row, day = (meta_v[pl.ds(v * pieces + i, blocks, stride=META_ROWS), :] for v in range(3))
        used = weight > 0.0
        count = count + jnp.sum(jnp.where(used, 1.0, 0.0), axis=1, keepdims=True)
        column_ref[i * LANES : (i + 1) * LANES, :] = jnp.transpose(weight)
        code = jnp.where(used, local_row * DAYS + (day + offset), float(spare)).astype(jnp.int32)
        clash = jnp.zeros(code.shape, jnp.int32)
        for k in range(1, GROUP):
            ahead = pltpu.roll(code, LANES - k, 1)
            clash = jnp.where((ahead == code) & (within + k < GROUP) & (code < spare), 1, clash)
        k = 1
        while k < GROUP:
            ahead = pltpu.roll(clash, LANES - k, 1)
            clash = jnp.where(within + k < GROUP, jnp.maximum(clash, ahead), clash)
            k *= 2
        code_ref[i * blocks : (i + 1) * blocks, :] = jnp.where((within == 0) & (clash > 0), code + CLASH, code)
    rest_ref[...] = code_ref[first_rows // LANES * blocks :, :]
    count_ref[...] = jnp.broadcast_to(count, (blocks, LANES)).astype(jnp.int32)
    code_copy = pltpu.make_async_copy(code_ref, code_s, sems.at[0])
    count_copy = pltpu.make_async_copy(count_ref, count_s, sems.at[1])
    code_copy.start()
    count_copy.start()

    for b in range(blocks):
        column = column_ref[:first_rows, b : b + 1]
        pixf[b * first_rows : (b + 1) * first_rows, :] = moved_ref[b, :first_rows, :].astype(jnp.float32) * column

    def clear(i, _):
        total_ref[pl.ds(pl.multiple_of(i * DAYS, DAYS), DAYS), :] = jnp.zeros((DAYS, LANES), jnp.float32)
        return 0

    lax.fori_loop(0, rows_tm, clear, 0)
    total_ref[spare:, :] = jnp.zeros((8, LANES), jnp.float32)
    code_copy.wait()
    count_copy.wait()

    def add(b, _):
        add_rows(total_ref, pixf, code_s, lambda i: i * blocks + b, 0, first_rows, b * first_rows, count_s[b, 0])
        return 0

    lax.fori_loop(0, blocks, add, 0)


def grid_last_kernel(
    dims, code_s, count_s, column_ref, moved_ref, first_ref, field_ref, keep_ref, give_ref,
    total, first_v, moved_v, pixf, field_v, gram_v, first_sems, block_sems, out_sem
):
    time_count, space_count, rows_tm, slot_rows, first_rows, width = dims
    blocks = time_count * space_count
    last_rows = slot_rows - first_rows
    group = rows_tm // STEPS
    skipped = first_rows // LANES

    def load(i):
        at = pl.ds(pl.multiple_of(i * group * DAYS, DAYS), group * DAYS)
        return pltpu.make_async_copy(first_ref.at[at], first_v.at[at], first_sems.at[i])

    def fetch(b):
        return pltpu.make_async_copy(moved_ref.at[b], moved_v.at[b], block_sems.at[b])

    for b in range(blocks):
        pl.when(count_s[b, 0] > first_rows)(fetch(b).start)
    for i in range(STEPS):
        load(i).start()

    def clear(i, _):
        total[pl.ds(pl.multiple_of(i * DAYS, DAYS), DAYS), :] = jnp.zeros((DAYS, LANES), jnp.float32)
        return 0

    lax.fori_loop(0, rows_tm, clear, 0)
    total[rows_tm * DAYS :, :] = jnp.zeros((8, LANES), jnp.float32)
    for b in range(blocks):

        @pl.when(count_s[b, 0] > first_rows)
        def _():
            fetch(b).wait()
            column = column_ref[first_rows:slot_rows, b : b + 1]
            pixf[b * last_rows : (b + 1) * last_rows, :] = moved_v[b].astype(jnp.float32) * column

    def add(b, _):
        rest = count_s[b, 0] - first_rows

        @pl.when(rest > 0)
        def _():
            add_rows(
                total, pixf, code_s, lambda i: (i - skipped) * blocks + b, first_rows, last_rows, b * last_rows, rest
            )

        return 0

    lax.fori_loop(0, blocks, add, 0)

    def send(i):
        at = pl.ds(i * group, group)
        return pltpu.make_async_copy(field_v.at[at], field_ref.at[at], out_sem)

    def settle(i):
        for q in range(i * group, (i + 1) * group):
            at = pl.ds(q * DAYS, DAYS)
            field_v[q] = (first_v[at, :] + total[at, :]).astype(jnp.bfloat16)

    def multiply(i):
        both = jnp.concatenate([field_v[q] for q in range(i * group, (i + 1) * group)], axis=1)
        part = lax.dot_general(both[:RANK], both, LAST_LAST, preferred_element_type=jnp.float32)
        for c in range(DAYS // LANES):
            here = part[:, c * LANES : (c + 1) * LANES]
            gram_v[c] = here if i == 0 else gram_v[c] + here

    for i in range(STEPS):
        load(i).wait()
        settle(i)
        if i > 0:
            send(i - 1).start()
            multiply(i - 1)
    send(STEPS - 1).start()
    multiply(STEPS - 1)
    odd = lax.axis_index("tm") % 2
    half = DAYS // LANES // 2
    for c in range(half):
        keep_ref[c] = gram_v[odd * half + c]
        give_ref[c] = gram_v[(1 - odd) * half + c]
    pltpu.make_async_copy(field_v, field_ref, out_sem).wait()


def grid_rows(moved_first, moved_last, time_count, space_count, rows_tm, slots):
    slot_rows, first_rows = split_rows(slots)
    last_rows = slot_rows - first_rows
    width = round_up(slots, LANES)
    blocks = time_count * space_count
    dims = (time_count, space_count, rows_tm, slot_rows, first_rows, width)
    codes = (blocks * width // LANES, LANES)
    rest = (codes[0] - first_rows // LANES * blocks, LANES)
    counts = (blocks, LANES)
    columns = (width, blocks)
    sums = (rows_tm * DAYS + 8, LANES)
    half = (DAYS // LANES // 2, RANK, LANES)
    params = pltpu.CompilerParams(vmem_limit_bytes=VMEM)
    moved_first, moved_last = (pltpu.with_memory_space_constraint(v, pltpu.VMEM) for v in (moved_first, moved_last))
    total, _, code, count, column = pl.pallas_call(
        functools.partial(grid_first_kernel, dims),
        out_shape=[
            jax.ShapeDtypeStruct(sums, jnp.float32),
            jax.ShapeDtypeStruct(codes, jnp.int32),
            jax.ShapeDtypeStruct(rest, jnp.int32),
            jax.ShapeDtypeStruct(counts, jnp.int32),
            jax.ShapeDtypeStruct(columns, jnp.float32),
        ],
        scratch_shapes=[
            pltpu.VMEM((blocks * META_ROWS, LANES), jnp.float32),
            pltpu.VMEM((blocks * first_rows, LANES), jnp.float32),
            pltpu.SMEM(codes, jnp.int32),
            pltpu.SMEM(counts, jnp.int32),
            pltpu.SemaphoreType.DMA((2,)),
        ],
        compiler_params=params,
        cost_estimate=pl.CostEstimate(flops=0, bytes_accessed=60_000_000, transcendentals=0),
        name="grid_first",
    )(moved_first)
    whole = pl.BlockSpec(memory_space=pltpu.VMEM)
    return pl.pallas_call(
        functools.partial(grid_last_kernel, dims),
        in_specs=[
            pl.BlockSpec(memory_space=pltpu.SMEM),
            pl.BlockSpec(memory_space=pltpu.SMEM),
            whole,
            pl.BlockSpec(memory_space=pl.ANY),
            pl.BlockSpec(memory_space=pl.ANY),
        ],
        out_specs=[pl.BlockSpec(memory_space=pl.ANY), whole, whole],
        out_shape=[
            jax.ShapeDtypeStruct((rows_tm, DAYS, LANES), jnp.bfloat16),
            pltpu.VMEM(half, jnp.float32),
            pltpu.VMEM(half, jnp.float32),
        ],
        scratch_shapes=[
            pltpu.VMEM(sums, jnp.float32),
            pltpu.VMEM((rows_tm * DAYS, LANES), jnp.float32),
            pltpu.VMEM((blocks, last_rows, LANES), jnp.bfloat16),
            pltpu.VMEM((blocks * last_rows, LANES), jnp.float32),
            pltpu.VMEM((rows_tm, DAYS, LANES), jnp.bfloat16),
            pltpu.VMEM((DAYS // LANES, RANK, LANES), jnp.float32),
            pltpu.SemaphoreType.DMA((STEPS,)),
            pltpu.SemaphoreType.DMA((blocks,)),
            pltpu.SemaphoreType.DMA,
        ],
        compiler_params=params,
        name="grid_last_and_gram",
    )(code, count, column, moved_last, total)


def dot_f32(a, b, dims=(((1,), (0,)), ((), ()))):
    return lax.dot_general(a, b, dims, precision=lax.Precision.HIGHEST, preferred_element_type=jnp.float32)


def dot_three(a, b, dims=(((1,), (0,)), ((), ()))):
    a_high, b_high = a.astype(jnp.bfloat16), b.astype(jnp.bfloat16)
    a_low = (a - a_high.astype(jnp.float32)).astype(jnp.bfloat16)
    b_low = (b - b_high.astype(jnp.float32)).astype(jnp.bfloat16)
    left, right = dims[0][0][0], dims[0][1][0]
    a_all = jnp.concatenate([a_high, a_high, a_low], axis=left)
    b_all = jnp.concatenate([b_high, b_low, b_high], axis=right)
    return lax.dot_general(a_all, b_all, dims, preferred_element_type=jnp.float32)


def invert(x):
    guess = pl.reciprocal(x, approx=True)
    guess = guess * (2.0 - x * guess)
    return guess * (2.0 - x * guess)


def lower_inverse(a):
    n = a.shape[0]
    full = (8, n)
    tiles = [a[8 * i : 8 * i + 8, :] for i in range(n // 8)]
    lane = lax.broadcasted_iota(jnp.int32, full, 1)
    down = lax.broadcasted_iota(jnp.int32, full, 0)
    out = []
    for t in range(n // 8):
        k = 8 * t
        block = (lane >= k) & (lane < k + 8)
        panel = tiles[t]
        cols = [jnp.broadcast_to(panel[:, k + c : k + c + 1], full) for c in range(8)]
        e = {(i, c): jnp.broadcast_to(cols[c][i : i + 1, :], full) for c in range(8) for i in range(c, 8)}
        start = jnp.where(block, jnp.where(lane == k + down, 1.0, 0.0), panel)
        rows = [jnp.broadcast_to(start[i : i + 1, :], full) for i in range(8)]
        held = []
        for s in range(0, 8, 2):
            p, q, r = e[s, s], e[s + 1, s], e[s + 1, s + 1]
            det = p * r - q * q
            inv = invert(det)
            factors = {}
            for i in range(s + 2, 8):
                x, y = e[i, s], e[i, s + 1]
                factors[i] = (r * x - q * y, p * y - q * x)
            for i in range(s + 2, 8):
                u, v = factors[i]
                for c in range(s + 2, i + 1):
                    e[i, c] = e[i, c] - (u * e[c, s] + v * e[c, s + 1]) * inv
                rows[i] = rows[i] - (u * rows[s] + v * rows[s + 1]) * inv
            held.append((p, q, r, det, inv, factors))
        done = jnp.zeros(full, jnp.float32)
        solved = [None] * 8
        for s in (6, 4, 2, 0):
            p, q, r, det, inv, factors = held[s // 2]
            root = lax.rsqrt(p)
            done = jnp.where(down == s, rows[s] * root, done)
            done = jnp.where(down == s + 1, (rows[s + 1] * p - q * rows[s]) * (root * lax.rsqrt(det)), done)
            first, second = r * rows[s] - q * rows[s + 1], p * rows[s + 1] - q * rows[s]
            for i in range(7, s + 1, -1):
                u, v = factors[i]
                first, second = first - u * solved[i], second - v * solved[i]
            solved[s], solved[s + 1] = first * inv, second * inv
        out.append(jnp.where(lane < k + 8, done, 0.0))
        for i in range(t + 1, n // 8):
            terms = [jnp.broadcast_to(tiles[i][:, k + c : k + c + 1], full) * solved[c] for c in range(8)]
            while len(terms) > 1:
                terms = [terms[j] + terms[j + 1] for j in range(0, len(terms), 2)]
            tiles[i] = jnp.where(block, 0.0, tiles[i]) - terms[0]
    return jnp.concatenate(out, axis=0)


def solve_kernel(scale, own_ref, other_ref, field_ref, basis_ref, prop_ref, gram_v, field_v, basis_v, sems):
    h = LANES
    pieces = DAYS // h
    rows_here = field_v.shape[0]
    load = pltpu.make_async_copy(field_ref.at[:, pl.ds(0, RANK), :], field_v, sems.at[0])
    load.start()
    odd = lax.axis_index("tm") % 2
    for c in range(pieces // 2):
        gram_v[odd * (pieces // 2) + c] = own_ref[c]
        gram_v[(1 - odd) * (pieces // 2) + c] = other_ref[c]

    gram = jnp.concatenate([gram_v[i] for i in range(pieces)], axis=1)
    eye = lax.broadcasted_iota(jnp.int32, (h, h), 0) == lax.broadcasted_iota(jnp.int32, (h, h), 1)
    a11, a12, a22 = gram_v[0, :h, :], gram_v[1, :h, :], gram_v[1, h:, :]
    size_col, size_row = [], []
    for part in (a11, a22):
        diag = jnp.where(eye, part, 0.0)
        size_col.append(lax.rsqrt(jnp.sum(diag, axis=1, keepdims=True)))
        size_row.append(lax.rsqrt(jnp.sum(diag, axis=0, keepdims=True)))
    top, low = gram[:h], gram[h:]
    x1 = lower_inverse(a11 * size_col[0] * size_row[0])
    r12 = dot_f32(x1, a12 * size_col[0] * size_row[1])
    x2 = lower_inverse(a22 * size_col[1] * size_row[1] - dot_f32(r12, r12, FIRST_FIRST))
    factor_top = dot_f32(x1, top * size_col[0])
    schur = low[:, h:] * size_col[1] - dot_f32(r12, factor_top[:, h:], FIRST_FIRST)
    mixed = -dot_f32(x2, dot_f32(r12, x1, FIRST_FIRST))
    factor_low = dot_f32(x2, schur)
    lower = jnp.concatenate(
        [
            jnp.concatenate([x1 * size_row[0], jnp.zeros((h, h), jnp.float32)], axis=1),
            jnp.concatenate([mixed * size_row[0], x2 * size_row[1]], axis=1),
        ],
        axis=0,
    )
    inverse = (scale * lower).astype(jnp.bfloat16)
    load.wait()

    def project(i):
        both = jnp.concatenate([field_v[2 * i], field_v[2 * i + 1]], axis=1)
        made = jnp.dot(inverse, both, preferred_element_type=jnp.float32).astype(jnp.bfloat16)
        basis_v[2 * i] = made[:, :h]
        basis_v[2 * i + 1] = made[:, h:]

    down = lax.broadcasted_iota(jnp.int32, (RANK, DAYS), 0)
    across = lax.broadcasted_iota(jnp.int32, (RANK, DAYS), 1)
    factor = jnp.concatenate(
        [factor_top, jnp.concatenate([jnp.zeros((h, h), jnp.float32), factor_low], axis=1)], axis=0
    )
    factor = jnp.where(across >= down, factor, 0.0)
    ahead = jnp.where(across < DAYS - 1, pltpu.roll(factor, DAYS - 1, 1), 0.0)
    cross = dot_three(ahead, factor, LAST_LAST)
    polar = cross / jnp.sqrt(jnp.sum(cross * cross) + 1e-06)
    todo = list(range(rows_here // 2))
    share = -(-len(todo) // (ITERS - 1))
    store = pltpu.make_async_copy(basis_v, basis_ref, sems.at[1])
    for n in range(ITERS):
        square = dot_three(polar, polar, LAST_LAST)
        for i in todo[n * share : (n + 1) * share]:
            project(i)
        if n == ITERS - 2:
            store.start()
        polar = 1.5 * polar - 0.5 * dot_three(square, polar)
    prop_ref[...] = math.sqrt(RANK) * polar
    store.wait()


def solve(own, other, field, cell_total):
    rows_tm = field.shape[0]
    part = (rows_tm, RANK, LANES)
    whole = pl.BlockSpec(memory_space=pltpu.VMEM)
    own, other = (pltpu.with_memory_space_constraint(v, pltpu.VMEM) for v in (own, other))
    return pl.pallas_call(
        functools.partial(solve_kernel, math.sqrt(cell_total)),
        in_specs=[whole, whole, pl.BlockSpec(memory_space=pl.ANY)],
        out_specs=[pl.BlockSpec(memory_space=pl.ANY), whole],
        out_shape=[
            jax.ShapeDtypeStruct(part, jnp.bfloat16),
            jax.ShapeDtypeStruct((RANK, RANK), jnp.float32),
        ],
        scratch_shapes=[
            pltpu.VMEM((DAYS // LANES, RANK, LANES), jnp.float32),
            pltpu.VMEM(part, jnp.bfloat16),
            pltpu.VMEM(part, jnp.bfloat16),
            pltpu.SemaphoreType.DMA((2,)),
        ],
        compiler_params=pltpu.CompilerParams(vmem_limit_bytes=VMEM),
        name="factor_basis_and_polar",
    )(own, other, field)


def body(pixels, weights, tile_index, tile_row, granule_day):
    swath_rows = pixels.shape[0]
    width = pixels.shape[1]
    space_count = lax.axis_size("space")
    time_count = lax.axis_size("tm")
    dest_count = time_count * space_count
    rows_tm = GR_DEV // time_count
    slots = 2 * swath_rows // space_count // time_count
    axes = ("tm", "space")
    first, last = pack(pixels, weights, tile_index, tile_row, granule_day, time_count, space_count, rows_tm, slots)
    first = lax.all_to_all(first, axes, split_axis=0, concat_axis=0, tiled=True)
    last = lax.all_to_all(last, axes, split_axis=0, concat_axis=0, tiled=True)
    field, keep, give = grid_rows(first, last, time_count, space_count, rows_tm, slots)

    swap = [(t, t ^ 1) for t in range(time_count)]
    peers = [[t * space_count + s for t in range(core, time_count, 2) for s in range(space_count)] for core in (0, 1)]
    among = functools.partial(
        lax.all_to_all, axis_name=axes, split_axis=0, concat_axis=0, axis_index_groups=peers, tiled=True
    )
    pieces = (keep + lax.ppermute(give, "tm", swap)).reshape(dest_count // 2, -1, LANES)
    mine = jnp.sum(among(pieces), axis=0, keepdims=True)
    own = among(jnp.broadcast_to(mine, pieces.shape)).reshape(keep.shape)
    other = lax.ppermute(own, "tm", swap)
    cell_total = space_count * GR_DEV * width
    basis, propagator = solve(own, other, field, cell_total)
    return (field[None], basis[None], propagator)


def solution(mesh):
    placed = (
        P(("tm", "space"), None),
        P(("tm", "space")),
        P(("tm", "space")),
        P(("tm", "space")),
        P(("tm", "space")),
    )
    return jax.shard_map(
        body,
        mesh=mesh,
        in_specs=placed,
        out_specs=(P("space", "tm", None, None), P("space", "tm", None, None), P()),
        check_vma=False,
    )
```

```python
import functools
import math

import jax
import jax.numpy as jnp
from jax import lax
from jax.experimental import pallas as pl
from jax.experimental.pallas import tpu as pltpu
from jax.sharding import PartitionSpec as P

GR_DEV = 160
DAYS = 512
RANK = 256
ITERS = 8
LANES = 128
GROUP = 16
CLASH = 1 << 20
STEPS = 5
VMEM = 56 * 1024 * 1024

LAST_LAST = (((1,), (1,)), ((), ()))
FIRST_FIRST = (((0,), (0,)), ((), ()))


def round_up(value, unit):
    return -(-value // unit) * unit


def split_rows(slots):
    rows = round_up(slots, 16)
    return rows, rows * 13 // 20 // 16 * 16


def meta_layout(slots):
    pieces = round_up(slots, LANES) // LANES
    folded = 3 * pieces > 8 and 3 * pieces - 1 <= 8 and slots % LANES <= LANES // 2
    return (8 if folded else round_up(3 * pieces, 8)), folded


def pack_kernel(
    dims, tile_ref, row_ref, day_ref, weight_ref, pix_ref, first_ref, last_ref, pos_v, pos_s, rows_v, meta_v, pixf, outf, mrow,
    first_v, last_v, pix_v, hot_v, prefix_v, sems
):
    time_count, space_count, rows_tm, slot_rows, first_rows, width, (meta_rows, folded) = dims
    dest_count = time_count * space_count
    chunks = tile_ref.shape[0]
    pieces = width // LANES

    fetch = pltpu.make_async_copy(pix_ref, pix_v, sems.at[3])
    fetch.start()
    tile = tile_ref[...]
    row = row_ref[...]
    group = jnp.zeros_like(row)
    for k in range(1, time_count):
        group = group + jnp.where(row >= k * rows_tm, 1, 0)
    dest_all = group * space_count + tile
    rows_v[0] = dest_all.astype(jnp.float32)
    rows_v[2] = weight_ref[...].astype(jnp.float32)
    rows_v[3] = (row - group * rows_tm).astype(jnp.float32)
    rows_v[4] = day_ref[...].astype(jnp.float32)

    dest_iota = lax.broadcasted_iota(jnp.int32, (dest_count, LANES), 0)
    upper = jnp.where(
        lax.broadcasted_iota(jnp.int32, (LANES, LANES), 0) <= lax.broadcasted_iota(jnp.int32, (LANES, LANES), 1), 1.0, 0.0
    ).astype(jnp.bfloat16)
    for c in range(chunks):
        hot = dest_iota == dest_all[c : c + 1, :]
        hot_v[c * dest_count : (c + 1) * dest_count, :] = jnp.where(hot, 1.0, 0.0).astype(jnp.bfloat16)
    prefix_v[...] = jnp.dot(hot_v[...], upper, preferred_element_type=jnp.float32)
    carry = jnp.zeros((dest_count, 1), jnp.float32)
    for c in range(chunks):
        prefix = prefix_v[c * dest_count : (c + 1) * dest_count, :]
        hot = dest_iota == dest_all[c : c + 1, :]
        rows_v[1, c : c + 1, :] = jnp.sum(jnp.where(hot, prefix + carry, 0.0), axis=0, keepdims=True) - 1.0
        carry = carry + prefix[:, LANES - 1 : LANES]
    pos_v[...] = dest_all * slot_rows + rows_v[1].astype(jnp.int32)
    copy = pltpu.make_async_copy(pos_v, pos_s, sems.at[0])
    copy.start()
    meta_v[...] = jnp.zeros_like(meta_v)
    mrow[...] = jnp.zeros_like(mrow)

    def clear(b, _):
        outf[pl.ds(pl.multiple_of(b * slot_rows, 16), slot_rows), :] = jnp.zeros((slot_rows, LANES), jnp.float32)
        return 0

    lax.fori_loop(0, dest_count, clear, 0)
    fetch.wait()
    copy.wait()
    both = 2 * LANES
    dest_number = lax.broadcasted_iota(jnp.int32, (dest_count, both), 0).astype(jnp.float32)
    slot_number = lax.broadcasted_iota(jnp.int32, (width, both), 0).astype(jnp.float32)

    def move(c, _):
        base = pl.multiple_of(c * both, both)
        pixf[pl.ds(base, both), :] = pix_v[pl.ds(base, both), :].astype(jnp.float32)
        dest, rank, weight, local_row, day = (
            jnp.concatenate([rows_v[v, pl.ds(2 * c, 1), :], rows_v[v, pl.ds(2 * c + 1, 1), :]], axis=1) for v in range(5)
        )
        hot = dest_number == dest
        place = jnp.where(slot_number == rank, 1.0, 0.0).astype(jnp.bfloat16)
        values = jnp.concatenate([jnp.where(hot, v, 0.0) for v in (weight, local_row, day)], axis=0).astype(jnp.bfloat16)
        meta_v[...] += lax.dot_general(values, place, LAST_LAST, preferred_element_type=jnp.float32)
        for half in range(2):
            for lane in range(LANES):
                outf[pl.ds(pos_s[2 * c + half, lane], 1), :] = pixf[pl.ds(base + half * LANES + lane, 1), :]
        return 0

    lax.fori_loop(0, chunks // 2, move, 0)
    whole = pieces - 1 if folded else pieces

    def lanes(v, i):
        return meta_v[v * dest_count : (v + 1) * dest_count, i * LANES : (i + 1) * LANES]

    def put(at, value):
        mrow[pl.ds(at, dest_count, stride=meta_rows), :] = value

    for v in range(3):
        for i in range(whole):
            put(v * whole + i, lanes(v, i))
    if folded:
        put(3 * whole, lanes(0, whole) + pltpu.roll(lanes(1, whole), LANES // 2, 1))
        put(3 * whole + 1, lanes(2, whole))

    together = 8

    def narrow(i, _):
        for q in range(together):
            b = i * together + q
            at = pl.multiple_of(b * slot_rows, 16)
            first_v[b, :first_rows, :] = outf[pl.ds(at, first_rows), :].astype(jnp.bfloat16)
            first_v[b, first_rows:, :] = mrow[pl.ds(pl.multiple_of(b * meta_rows, 8), meta_rows), :].astype(jnp.bfloat16)
            last_v[b] = outf[pl.ds(at + first_rows, slot_rows - first_rows), :].astype(jnp.bfloat16)
        some = pl.ds(i * together, together)
        pltpu.make_async_copy(first_v.at[some], first_ref.at[some], sems.at[1]).start()
        pltpu.make_async_copy(last_v.at[some], last_ref.at[some], sems.at[2]).start()
        return 0

    lax.fori_loop(0, dest_count // together, narrow, 0)
    pltpu.make_async_copy(first_v, first_ref, sems.at[1]).wait()
    pltpu.make_async_copy(last_v, last_ref, sems.at[2]).wait()


def pack(pixels, weights, tile_index, tile_row, granule_day, time_count, space_count, rows_tm, slots):
    swath_rows = pixels.shape[0]
    chunks = swath_rows // LANES
    dest_count = time_count * space_count
    slot_rows, first_rows = split_rows(slots)
    width = round_up(slots, LANES)
    shape = (chunks, LANES)
    layout = meta_layout(slots)
    first_shape = (dest_count, first_rows + layout[0], LANES)
    last_shape = (dest_count, slot_rows - first_rows, LANES)
    return pl.pallas_call(
        functools.partial(pack_kernel, (time_count, space_count, rows_tm, slot_rows, first_rows, width, layout)),
        in_specs=[pl.BlockSpec(memory_space=pltpu.VMEM)] * 4 + [pl.BlockSpec(memory_space=pl.ANY)],
        out_specs=[pl.BlockSpec(memory_space=pl.ANY)] * 2,
        out_shape=[jax.ShapeDtypeStruct(first_shape, jnp.bfloat16), jax.ShapeDtypeStruct(last_shape, jnp.bfloat16)],
        scratch_shapes=[
            pltpu.VMEM(shape, jnp.int32),
            pltpu.SMEM(shape, jnp.int32),
            pltpu.VMEM((5,) + shape, jnp.float32),
            pltpu.VMEM((3 * dest_count, width), jnp.float32),
            pltpu.VMEM((swath_rows, LANES), jnp.float32),
            pltpu.VMEM((dest_count * slot_rows, LANES), jnp.float32),
            pltpu.VMEM((dest_count * layout[0], LANES), jnp.float32),
            pltpu.VMEM(first_shape, jnp.bfloat16),
            pltpu.VMEM(last_shape, jnp.bfloat16),
            pltpu.VMEM((swath_rows, LANES), jnp.bfloat16),
            pltpu.VMEM((chunks * dest_count, LANES), jnp.bfloat16),
            pltpu.VMEM((chunks * dest_count, LANES), jnp.float32),
            pltpu.SemaphoreType.DMA((4,)),
        ],
        compiler_params=pltpu.CompilerParams(vmem_limit_bytes=VMEM),
        name="pack",
    )(
        tile_index.reshape(shape),
        tile_row.reshape(shape),
        granule_day.reshape(shape),
        weights.reshape(shape),
        pixels,
    )


def chunks_of(first_slot, rows):
    slot, found = first_slot, []
    while slot < first_slot + rows:
        size = min(32 - slot % 32, first_slot + rows - slot)
        found.append((slot, size))
        slot += size
    return found


def add_rows(total, pixf, code_s, code_row, first_slot, rows, pix_at, count):
    def add_group(row, lane, at):
        places = [code_s[row, lane + u] for u in range(GROUP)]
        made = [total[pl.ds(p, 1), :] + pixf[pl.ds(at + u, 1), :] for u, p in enumerate(places)]
        for p, value in zip(places, made):
            total[pl.ds(p, 1), :] = value

    def add_singly(row, lane, at):
        def one(u, _):
            p = code_s[row, lane + u]
            p = jnp.where(p >= CLASH, p - CLASH, p)
            total[pl.ds(p, 1), :] = total[pl.ds(p, 1), :] + pixf[pl.ds(at + u, 1), :]
            return 0

        lax.fori_loop(0, GROUP, one, 0)

    for slot, chunk in chunks_of(first_slot, rows):
        start = slot - first_slot
        row, lane = code_row(slot // LANES), slot % LANES
        at = pix_at + start
        heads = [code_s[row, lane + g] for g in range(0, chunk, GROUP)]
        clash = functools.reduce(jnp.maximum, heads) >= CLASH

        @pl.when((count > start) & jnp.logical_not(clash))
        def _():
            for g in range(0, chunk, GROUP):
                add_group(row, lane + g, at + g)

        @pl.when((count > start) & clash)
        def _():
            for g, head in zip(range(0, chunk, GROUP), heads):
                pl.when(head < CLASH)(functools.partial(add_group, row, lane + g, at + g))
                pl.when(head >= CLASH)(functools.partial(add_singly, row, lane + g, at + g))


def grid_first_kernel(
    dims, moved_ref, total_ref, code_ref, rest_ref, count_ref, column_ref, meta_v, pixf, code_s, count_s, sems
):
    time_count, space_count, rows_tm, slot_rows, first_rows, width, (meta_rows, folded) = dims
    day_dev = DAYS // time_count
    blocks = time_count * space_count
    pieces = width // LANES
    spare = rows_tm * DAYS

    meta_v[...] = moved_ref[:, first_rows:, :].astype(jnp.float32).reshape(blocks * meta_rows, LANES)
    whole = pieces - 1 if folded else pieces
    early = lax.broadcasted_iota(jnp.int32, (blocks, LANES), 1) < LANES // 2

    def lanes(v, i):
        if i < whole:
            return meta_v[pl.ds(v * whole + i, blocks, stride=meta_rows), :]
        tail = meta_v[pl.ds(3 * whole + v // 2, blocks, stride=meta_rows), :]
        return jnp.where(early, pltpu.roll(tail, LANES // 2, 1) if v == 1 else tail, 0.0)

    block = lax.broadcasted_iota(jnp.int32, (blocks, LANES), 0)
    offset = jnp.zeros((blocks, LANES), jnp.float32)
    for m in range(1, time_count):
        offset = offset + jnp.where(block >= m * space_count, float(day_dev), 0.0)
    within = lax.broadcasted_iota(jnp.int32, (blocks, LANES), 1) % GROUP
    count = jnp.zeros((blocks, 1), jnp.float32)
    for i in range(pieces):
        weight, local_row, day = (lanes(v, i) for v in range(3))
        used = weight > 0.0
        count = count + jnp.sum(jnp.where(used, 1.0, 0.0), axis=1, keepdims=True)
        column_ref[i * LANES : (i + 1) * LANES, :] = jnp.transpose(weight)
        code = jnp.where(used, local_row * DAYS + (day + offset), float(spare)).astype(jnp.int32)
        clash = jnp.zeros(code.shape, jnp.int32)
        for k in range(1, GROUP):
            ahead = pltpu.roll(code, LANES - k, 1)
            clash = jnp.where((ahead == code) & (within + k < GROUP) & (code < spare), 1, clash)
        k = 1
        while k < GROUP:
            ahead = pltpu.roll(clash, LANES - k, 1)
            clash = jnp.where(within + k < GROUP, jnp.maximum(clash, ahead), clash)
            k *= 2
        code_ref[i * blocks : (i + 1) * blocks, :] = jnp.where((within == 0) & (clash > 0), code + CLASH, code)
    rest_ref[...] = code_ref[first_rows // LANES * blocks :, :]
    count_ref[...] = jnp.broadcast_to(count, (blocks, LANES)).astype(jnp.int32)
    code_copy = pltpu.make_async_copy(code_ref, code_s, sems.at[0])
    count_copy = pltpu.make_async_copy(count_ref, count_s, sems.at[1])
    code_copy.start()
    count_copy.start()

    for b in range(blocks):
        column = column_ref[:first_rows, b : b + 1]
        pixf[b * first_rows : (b + 1) * first_rows, :] = moved_ref[b, :first_rows, :].astype(jnp.float32) * column

    def clear(i, _):
        total_ref[pl.ds(pl.multiple_of(i * DAYS, DAYS), DAYS), :] = jnp.zeros((DAYS, LANES), jnp.float32)
        return 0

    lax.fori_loop(0, rows_tm, clear, 0)
    total_ref[spare:, :] = jnp.zeros((8, LANES), jnp.float32)
    code_copy.wait()
    count_copy.wait()

    def add(b, _):
        add_rows(total_ref, pixf, code_s, lambda i: i * blocks + b, 0, first_rows, b * first_rows, count_s[b, 0])
        return 0

    lax.fori_loop(0, blocks, add, 0)


def grid_last_kernel(
    dims, code_ref, count_ref, column_any, moved_ref, first_ref, field_ref, keep_ref, give_ref,
    code_s, count_s, column_ref, total, first_v, moved_v, pixf, field_v, gram_v, small_sems, first_sems, block_sems, out_sem
):
    time_count, space_count, rows_tm, slot_rows, first_rows, width, (meta_rows, folded) = dims
    blocks = time_count * space_count
    last_rows = slot_rows - first_rows
    group = rows_tm // STEPS
    skipped = first_rows // LANES

    def load(i):
        at = pl.ds(pl.multiple_of(i * group * DAYS, DAYS), group * DAYS)
        return pltpu.make_async_copy(first_ref.at[at], first_v.at[at], first_sems.at[i])

    def fetch(b):
        return pltpu.make_async_copy(moved_ref.at[b], moved_v.at[b], block_sems.at[b])

    small = [
        pltpu.make_async_copy(source, target, small_sems.at[i])
        for i, (source, target) in enumerate(((count_ref, count_s), (code_ref, code_s), (column_any, column_ref)))
    ]
    for copy in small:
        copy.start()
    for i in range(STEPS):
        load(i).start()

    def clear(i, _):
        total[pl.ds(pl.multiple_of(i * DAYS, DAYS), DAYS), :] = jnp.zeros((DAYS, LANES), jnp.float32)
        return 0

    lax.fori_loop(0, rows_tm // 2, clear, 0)
    small[0].wait()
    for b in range(blocks):
        pl.when(count_s[b, 0] > first_rows)(fetch(b).start)
    lax.fori_loop(rows_tm // 2, rows_tm, clear, 0)
    total[rows_tm * DAYS :, :] = jnp.zeros((8, LANES), jnp.float32)
    small[1].wait()
    small[2].wait()
    for b in range(blocks):

        @pl.when(count_s[b, 0] > first_rows)
        def _():
            fetch(b).wait()
            column = column_ref[first_rows:slot_rows, b : b + 1]
            pixf[b * last_rows : (b + 1) * last_rows, :] = moved_v[b].astype(jnp.float32) * column

    def add(b, _):
        rest = count_s[b, 0] - first_rows

        @pl.when(rest > 0)
        def _():
            add_rows(
                total, pixf, code_s, lambda i: (i - skipped) * blocks + b, first_rows, last_rows, b * last_rows, rest
            )

        return 0

    lax.fori_loop(0, blocks, add, 0)

    def send(i):
        at = pl.ds(i * group, group)
        return pltpu.make_async_copy(field_v.at[at], field_ref.at[at], out_sem)

    def settle(i):
        for q in range(i * group, (i + 1) * group):
            at = pl.ds(q * DAYS, DAYS)
            field_v[q] = (first_v[at, :] + total[at, :]).astype(jnp.bfloat16)

    def multiply(i):
        both = jnp.concatenate([field_v[q] for q in range(i * group, (i + 1) * group)], axis=1)
        part = lax.dot_general(both[:RANK], both, LAST_LAST, preferred_element_type=jnp.float32)
        for c in range(DAYS // LANES):
            here = part[:, c * LANES : (c + 1) * LANES]
            gram_v[c] = here if i == 0 else gram_v[c] + here

    for i in range(STEPS):
        load(i).wait()
        settle(i)
        if i > 0:
            send(i - 1).start()
            multiply(i - 1)
    send(STEPS - 1).start()
    multiply(STEPS - 1)
    odd = lax.axis_index("tm") % 2
    half = DAYS // LANES // 2
    for c in range(half):
        keep_ref[c] = gram_v[odd * half + c]
        give_ref[c] = gram_v[(1 - odd) * half + c]
    pltpu.make_async_copy(field_v, field_ref, out_sem).wait()


def grid_rows(moved_first, moved_last, time_count, space_count, rows_tm, slots):
    slot_rows, first_rows = split_rows(slots)
    last_rows = slot_rows - first_rows
    width = round_up(slots, LANES)
    blocks = time_count * space_count
    dims = (time_count, space_count, rows_tm, slot_rows, first_rows, width, meta_layout(slots))
    codes = (blocks * width // LANES, LANES)
    rest = (codes[0] - first_rows // LANES * blocks, LANES)
    counts = (blocks, LANES)
    columns = (width, blocks)
    sums = (rows_tm * DAYS + 8, LANES)
    half = (DAYS // LANES // 2, RANK, LANES)
    params = pltpu.CompilerParams(vmem_limit_bytes=VMEM)
    moved_first, moved_last = (pltpu.with_memory_space_constraint(v, pltpu.VMEM) for v in (moved_first, moved_last))
    total, _, rest_code, count, column = pl.pallas_call(
        functools.partial(grid_first_kernel, dims),
        out_shape=[
            jax.ShapeDtypeStruct(sums, jnp.float32),
            jax.ShapeDtypeStruct(codes, jnp.int32),
            jax.ShapeDtypeStruct(rest, jnp.int32),
            jax.ShapeDtypeStruct(counts, jnp.int32),
            jax.ShapeDtypeStruct(columns, jnp.float32),
        ],
        scratch_shapes=[
            pltpu.VMEM((blocks * meta_layout(slots)[0], LANES), jnp.float32),
            pltpu.VMEM((blocks * first_rows, LANES), jnp.float32),
            pltpu.SMEM(codes, jnp.int32),
            pltpu.SMEM(counts, jnp.int32),
            pltpu.SemaphoreType.DMA((2,)),
        ],
        compiler_params=params,
        cost_estimate=pl.CostEstimate(flops=0, bytes_accessed=60_000_000, transcendentals=0),
        name="grid_first",
    )(moved_first)
    whole = pl.BlockSpec(memory_space=pltpu.VMEM)
    return pl.pallas_call(
        functools.partial(grid_last_kernel, dims),
        in_specs=[
            pl.BlockSpec(memory_space=pl.ANY),
        ]
        * 5,
        out_specs=[pl.BlockSpec(memory_space=pl.ANY), whole, whole],
        out_shape=[
            jax.ShapeDtypeStruct((rows_tm, DAYS, LANES), jnp.bfloat16),
            pltpu.VMEM(half, jnp.float32),
            pltpu.VMEM(half, jnp.float32),
        ],
        scratch_shapes=[
            pltpu.SMEM(rest, jnp.int32),
            pltpu.SMEM(counts, jnp.int32),
            pltpu.VMEM(columns, jnp.float32),
            pltpu.VMEM(sums, jnp.float32),
            pltpu.VMEM((rows_tm * DAYS, LANES), jnp.float32),
            pltpu.VMEM((blocks, last_rows, LANES), jnp.bfloat16),
            pltpu.VMEM((blocks * last_rows, LANES), jnp.float32),
            pltpu.VMEM((rows_tm, DAYS, LANES), jnp.bfloat16),
            pltpu.VMEM((DAYS // LANES, RANK, LANES), jnp.float32),
            pltpu.SemaphoreType.DMA((3,)),
            pltpu.SemaphoreType.DMA((STEPS,)),
            pltpu.SemaphoreType.DMA((blocks,)),
            pltpu.SemaphoreType.DMA,
        ],
        compiler_params=params,
        name="grid_last_and_gram",
    )(rest_code, count, column, moved_last, total)


def dot_f32(a, b, dims=(((1,), (0,)), ((), ()))):
    return lax.dot_general(a, b, dims, precision=lax.Precision.HIGHEST, preferred_element_type=jnp.float32)


def dot_three(a, b, dims=(((1,), (0,)), ((), ()))):
    a_high, b_high = a.astype(jnp.bfloat16), b.astype(jnp.bfloat16)
    a_low = (a - a_high.astype(jnp.float32)).astype(jnp.bfloat16)
    b_low = (b - b_high.astype(jnp.float32)).astype(jnp.bfloat16)
    left, right = dims[0][0][0], dims[0][1][0]
    a_all = jnp.concatenate([a_high, a_high, a_low], axis=left)
    b_all = jnp.concatenate([b_high, b_low, b_high], axis=right)
    half = a.shape[0] // 2
    parts = [lax.dot_general(p, b_all, dims, preferred_element_type=jnp.float32) for p in (a_all[:half], a_all[half:])]
    return jnp.concatenate(parts, axis=0)


def lower_inverse(a):
    n = a.shape[0]
    full = (8, n)
    tiles = [a[8 * i : 8 * i + 8, :] for i in range(n // 8)]
    lane = lax.broadcasted_iota(jnp.int32, full, 1)
    down = lax.broadcasted_iota(jnp.int32, full, 0)
    out = []
    for t in range(n // 8):
        k = 8 * t
        block = (lane >= k) & (lane < k + 8)
        panel = tiles[t]
        cols = [jnp.broadcast_to(panel[:, k + c : k + c + 1], full) for c in range(8)]
        e = {(i, c): jnp.broadcast_to(cols[c][i : i + 1, :], full) for c in range(8) for i in range(c, 8)}
        start = jnp.where(block, jnp.where(lane == k + down, 1.0, 0.0), panel)
        rows = [jnp.broadcast_to(start[i : i + 1, :], full) for i in range(8)]
        held = []
        for s in range(0, 8, 2):
            p, q, r = e[s, s], e[s + 1, s], e[s + 1, s + 1]
            det = p * r - q * q
            inv = pl.reciprocal(det, approx=True)
            factors = {}
            for i in range(s + 2, 8):
                x, y = e[i, s], e[i, s + 1]
                factors[i] = (r * x - q * y, p * y - q * x)
            for i in range(s + 2, 8):
                u, v = factors[i]
                for c in range(s + 2, i + 1):
                    e[i, c] = e[i, c] - (u * e[c, s] + v * e[c, s + 1]) * inv
                rows[i] = rows[i] - (u * rows[s] + v * rows[s + 1]) * inv
            held.append((p, q, r, det, inv, factors))
        done = jnp.zeros(full, jnp.float32)
        solved = [None] * 8
        for s in (6, 4, 2, 0):
            p, q, r, det, inv, factors = held[s // 2]
            root = lax.rsqrt(p)
            done = jnp.where(down == s, rows[s] * root, done)
            done = jnp.where(down == s + 1, (rows[s + 1] * p - q * rows[s]) * (root * lax.rsqrt(det)), done)
            first, second = r * rows[s] - q * rows[s + 1], p * rows[s + 1] - q * rows[s]
            for i in range(7, s + 1, -1):
                u, v = factors[i]
                first, second = first - u * solved[i], second - v * solved[i]
            solved[s], solved[s + 1] = first * inv, second * inv
        out.append(jnp.where(lane < k + 8, done, 0.0))
        for i in range(t + 1, n // 8):
            terms = [jnp.broadcast_to(tiles[i][:, k + c : k + c + 1], full) * solved[c] for c in range(8)]
            while len(terms) > 1:
                terms = [terms[j] + terms[j + 1] for j in range(0, len(terms), 2)]
            tiles[i] = jnp.where(block, 0.0, tiles[i]) - terms[0]
    return jnp.concatenate(out, axis=0)


def solve_kernel(scale, own_ref, other_ref, field_ref, basis_ref, prop_ref, gram_v, field_v, basis_v, sems):
    h = LANES
    pieces = DAYS // h
    rows_here = field_v.shape[0]
    load = pltpu.make_async_copy(field_ref.at[:, pl.ds(0, RANK), :], field_v, sems.at[0])
    load.start()
    odd = lax.axis_index("tm") % 2
    for c in range(pieces // 2):
        gram_v[odd * (pieces // 2) + c] = own_ref[c]
        gram_v[(1 - odd) * (pieces // 2) + c] = other_ref[c]

    gram = jnp.concatenate([gram_v[i] for i in range(pieces)], axis=1)
    eye = lax.broadcasted_iota(jnp.int32, (h, h), 0) == lax.broadcasted_iota(jnp.int32, (h, h), 1)
    a11, a12, a22 = gram_v[0, :h, :], gram_v[1, :h, :], gram_v[1, h:, :]
    size_col, size_row = [], []
    for part in (a11, a22):
        diag = jnp.where(eye, part, 0.0)
        size_col.append(lax.rsqrt(jnp.sum(diag, axis=1, keepdims=True)))
        size_row.append(lax.rsqrt(jnp.sum(diag, axis=0, keepdims=True)))
    top, low = gram[:h], gram[h:]
    x1 = lower_inverse(a11 * size_col[0] * size_row[0])
    r12 = dot_f32(x1, a12 * size_col[0] * size_row[1])
    x2 = lower_inverse(a22 * size_col[1] * size_row[1] - dot_f32(r12, r12, FIRST_FIRST))
    factor_top = dot_f32(x1, top * size_col[0])
    schur = low[:, h:] * size_col[1] - dot_f32(r12, factor_top[:, h:], FIRST_FIRST)
    mixed = -dot_f32(x2, dot_f32(r12, x1, FIRST_FIRST))
    factor_low = dot_f32(x2, schur)
    lower = jnp.concatenate(
        [
            jnp.concatenate([x1 * size_row[0], jnp.zeros((h, h), jnp.float32)], axis=1),
            jnp.concatenate([mixed * size_row[0], x2 * size_row[1]], axis=1),
        ],
        axis=0,
    )
    inverse = (scale * lower).astype(jnp.bfloat16)
    load.wait()

    def project(i):
        both = jnp.concatenate([field_v[2 * i], field_v[2 * i + 1]], axis=1)
        made = jnp.dot(inverse, both, preferred_element_type=jnp.float32).astype(jnp.bfloat16)
        basis_v[2 * i] = made[:, :h]
        basis_v[2 * i + 1] = made[:, h:]

    down = lax.broadcasted_iota(jnp.int32, (RANK, DAYS), 0)
    across = lax.broadcasted_iota(jnp.int32, (RANK, DAYS), 1)
    factor = jnp.concatenate(
        [factor_top, jnp.concatenate([jnp.zeros((h, h), jnp.float32), factor_low], axis=1)], axis=0
    )
    factor = jnp.where(across >= down, factor, 0.0)
    ahead = jnp.where(across < DAYS - 1, pltpu.roll(factor, DAYS - 1, 1), 0.0)
    cross = dot_three(ahead, factor, LAST_LAST)
    polar = cross / jnp.sqrt(jnp.sum(cross * cross) + 1e-06)
    todo = list(range(rows_here // 2))
    share = -(-len(todo) // (ITERS - 1))
    store = pltpu.make_async_copy(basis_v, basis_ref, sems.at[1])
    for n in range(ITERS):
        square = dot_three(polar, polar, LAST_LAST)
        for i in todo[n * share : (n + 1) * share]:
            project(i)
        if n == ITERS - 2:
            store.start()
        polar = 1.5 * polar - 0.5 * dot_three(square, polar)
    prop_ref[...] = math.sqrt(RANK) * polar
    store.wait()


def solve(own, other, field, cell_total):
    rows_tm = field.shape[0]
    part = (rows_tm, RANK, LANES)
    whole = pl.BlockSpec(memory_space=pltpu.VMEM)
    own, other = (pltpu.with_memory_space_constraint(v, pltpu.VMEM) for v in (own, other))
    return pl.pallas_call(
        functools.partial(solve_kernel, math.sqrt(cell_total)),
        in_specs=[whole, whole, pl.BlockSpec(memory_space=pl.ANY)],
        out_specs=[pl.BlockSpec(memory_space=pl.ANY), whole],
        out_shape=[
            jax.ShapeDtypeStruct(part, jnp.bfloat16),
            jax.ShapeDtypeStruct((RANK, RANK), jnp.float32),
        ],
        scratch_shapes=[
            pltpu.VMEM((DAYS // LANES, RANK, LANES), jnp.float32),
            pltpu.VMEM(part, jnp.bfloat16),
            pltpu.VMEM(part, jnp.bfloat16),
            pltpu.SemaphoreType.DMA((2,)),
        ],
        compiler_params=pltpu.CompilerParams(vmem_limit_bytes=VMEM),
        name="factor_basis_and_polar",
    )(own, other, field)


def body(pixels, weights, tile_index, tile_row, granule_day):
    swath_rows = pixels.shape[0]
    width = pixels.shape[1]
    space_count = lax.axis_size("space")
    time_count = lax.axis_size("tm")
    dest_count = time_count * space_count
    rows_tm = GR_DEV // time_count
    slots = 2 * swath_rows // space_count // time_count
    axes = ("tm", "space")
    first, last = pack(pixels, weights, tile_index, tile_row, granule_day, time_count, space_count, rows_tm, slots)
    first = lax.all_to_all(first, axes, split_axis=0, concat_axis=0, tiled=True)
    last = lax.all_to_all(last, axes, split_axis=0, concat_axis=0, tiled=True)
    field, keep, give = grid_rows(first, last, time_count, space_count, rows_tm, slots)

    swap = [(t, t ^ 1) for t in range(time_count)]
    peers = [[t * space_count + s for t in range(core, time_count, 2) for s in range(space_count)] for core in (0, 1)]
    among = functools.partial(
        lax.all_to_all, axis_name=axes, split_axis=0, concat_axis=0, axis_index_groups=peers, tiled=True
    )
    pieces = (keep + lax.ppermute(give, "tm", swap)).reshape(dest_count // 2, -1, LANES)
    mine = jnp.sum(among(pieces), axis=0, keepdims=True)
    own = among(jnp.broadcast_to(mine, pieces.shape)).reshape(keep.shape)
    other = lax.ppermute(own, "tm", swap)
    cell_total = space_count * GR_DEV * width
    basis, propagator = solve(own, other, field, cell_total)
    return (field[None], basis[None], propagator)


def solution(mesh):
    placed = (
        P(("tm", "space"), None),
        P(("tm", "space")),
        P(("tm", "space")),
        P(("tm", "space")),
        P(("tm", "space")),
    )
    return jax.shard_map(
        body,
        mesh=mesh,
        in_specs=placed,
        out_specs=(P("space", "tm", None, None), P("space", "tm", None, None), P()),
        check_vma=False,
    )
```

```python
import functools
import math

import jax
import jax.numpy as jnp
from jax import lax
from jax.experimental import pallas as pl
from jax.experimental.pallas import tpu as pltpu
from jax.sharding import PartitionSpec as P

GR_DEV = 160
DAYS = 512
RANK = 256
ITERS = 8
LANES = 128
GROUP = 16
CLASH = 1 << 20
STEPS = 5
VMEM = 56 * 1024 * 1024

LAST_LAST = (((1,), (1,)), ((), ()))
FIRST_FIRST = (((0,), (0,)), ((), ()))


def round_up(value, unit):
    return -(-value // unit) * unit


def split_rows(slots):
    rows = round_up(slots, 16)
    return rows, rows * 13 // 20 // 16 * 16


def meta_layout(slots):
    pieces = round_up(slots, LANES) // LANES
    folded = 3 * pieces > 8 and 3 * pieces - 1 <= 8 and slots % LANES <= LANES // 2
    return (8 if folded else round_up(3 * pieces, 8)), folded


def pack_kernel(
    dims, tile_ref, row_ref, day_ref, weight_ref, pix_ref, first_ref, last_ref, pos_v, pos_s, rows_v, meta_v, pixf, outf, mrow,
    first_v, last_v, pix_v, hot_v, prefix_v, sems
):
    time_count, space_count, rows_tm, slot_rows, first_rows, width, (meta_rows, folded) = dims
    dest_count = time_count * space_count
    chunks = tile_ref.shape[0]
    pieces = width // LANES

    fetch = pltpu.make_async_copy(pix_ref, pix_v, sems.at[3])
    fetch.start()
    tile = tile_ref[...]
    row = row_ref[...]
    group = jnp.zeros_like(row)
    for k in range(1, time_count):
        group = group + jnp.where(row >= k * rows_tm, 1, 0)
    dest_all = group * space_count + tile
    rows_v[0] = dest_all.astype(jnp.float32)
    rows_v[2] = weight_ref[...].astype(jnp.float32)
    rows_v[3] = (row - group * rows_tm).astype(jnp.float32)
    rows_v[4] = day_ref[...].astype(jnp.float32)

    dest_iota = lax.broadcasted_iota(jnp.int32, (dest_count, LANES), 0)
    upper = jnp.where(
        lax.broadcasted_iota(jnp.int32, (LANES, LANES), 0) <= lax.broadcasted_iota(jnp.int32, (LANES, LANES), 1), 1.0, 0.0
    ).astype(jnp.bfloat16)
    for c in range(chunks):
        hot = dest_iota == dest_all[c : c + 1, :]
        hot_v[c * dest_count : (c + 1) * dest_count, :] = jnp.where(hot, 1.0, 0.0).astype(jnp.bfloat16)
    prefix_v[...] = jnp.dot(hot_v[...], upper, preferred_element_type=jnp.float32)
    carry = jnp.zeros((dest_count, 1), jnp.float32)
    for c in range(chunks):
        prefix = prefix_v[c * dest_count : (c + 1) * dest_count, :]
        hot = dest_iota == dest_all[c : c + 1, :]
        rows_v[1, c : c + 1, :] = jnp.sum(jnp.where(hot, prefix + carry, 0.0), axis=0, keepdims=True) - 1.0
        carry = carry + prefix[:, LANES - 1 : LANES]
    pos_v[...] = dest_all * slot_rows + rows_v[1].astype(jnp.int32)
    copy = pltpu.make_async_copy(pos_v, pos_s, sems.at[0])
    copy.start()
    meta_v[...] = jnp.zeros_like(meta_v)
    mrow[...] = jnp.zeros_like(mrow)

    def clear(b, _):
        outf[pl.ds(pl.multiple_of(b * slot_rows, 16), slot_rows), :] = jnp.zeros((slot_rows, LANES), jnp.float32)
        return 0

    lax.fori_loop(0, dest_count, clear, 0)
    fetch.wait()
    copy.wait()
    both = 2 * LANES
    dest_number = lax.broadcasted_iota(jnp.int32, (dest_count, both), 0).astype(jnp.float32)
    slot_number = lax.broadcasted_iota(jnp.int32, (width, both), 0).astype(jnp.float32)

    def move(c, _):
        base = pl.multiple_of(c * both, both)
        pixf[pl.ds(base, both), :] = pix_v[pl.ds(base, both), :].astype(jnp.float32)
        dest, rank, weight, local_row, day = (
            jnp.concatenate([rows_v[v, pl.ds(2 * c, 1), :], rows_v[v, pl.ds(2 * c + 1, 1), :]], axis=1) for v in range(5)
        )
        hot = dest_number == dest
        place = jnp.where(slot_number == rank, 1.0, 0.0).astype(jnp.bfloat16)
        values = jnp.concatenate([jnp.where(hot, v, 0.0) for v in (weight, local_row, day)], axis=0).astype(jnp.bfloat16)
        meta_v[...] += lax.dot_general(place, values, LAST_LAST, preferred_element_type=jnp.float32)
        for half in range(2):
            for lane in range(LANES):
                outf[pl.ds(pos_s[2 * c + half, lane], 1), :] = pixf[pl.ds(base + half * LANES + lane, 1), :]
        return 0

    lax.fori_loop(0, chunks // 2, move, 0)
    whole = pieces - 1 if folded else pieces

    turned = [jnp.transpose(meta_v[i * LANES : (i + 1) * LANES, :]) for i in range(pieces)]

    def lanes(v, i):
        return turned[i][v * dest_count : (v + 1) * dest_count, :]

    def put(at, value):
        mrow[pl.ds(at, dest_count, stride=meta_rows), :] = value

    for v in range(3):
        for i in range(whole):
            put(v * whole + i, lanes(v, i))
    if folded:
        put(3 * whole, lanes(0, whole) + pltpu.roll(lanes(1, whole), LANES // 2, 1))
        put(3 * whole + 1, lanes(2, whole))

    together = 8

    def narrow(i, _):
        for q in range(together):
            b = i * together + q
            at = pl.multiple_of(b * slot_rows, 16)
            first_v[b, :first_rows, :] = outf[pl.ds(at, first_rows), :].astype(jnp.bfloat16)
            first_v[b, first_rows:, :] = mrow[pl.ds(pl.multiple_of(b * meta_rows, 8), meta_rows), :].astype(jnp.bfloat16)
            last_v[b] = outf[pl.ds(at + first_rows, slot_rows - first_rows), :].astype(jnp.bfloat16)
        some = pl.ds(i * together, together)
        pltpu.make_async_copy(first_v.at[some], first_ref.at[some], sems.at[1]).start()
        pltpu.make_async_copy(last_v.at[some], last_ref.at[some], sems.at[2]).start()
        return 0

    lax.fori_loop(0, dest_count // together, narrow, 0)
    pltpu.make_async_copy(first_v, first_ref, sems.at[1]).wait()
    pltpu.make_async_copy(last_v, last_ref, sems.at[2]).wait()


def pack(pixels, weights, tile_index, tile_row, granule_day, time_count, space_count, rows_tm, slots):
    swath_rows = pixels.shape[0]
    chunks = swath_rows // LANES
    dest_count = time_count * space_count
    slot_rows, first_rows = split_rows(slots)
    width = round_up(slots, LANES)
    shape = (chunks, LANES)
    layout = meta_layout(slots)
    first_shape = (dest_count, first_rows + layout[0], LANES)
    last_shape = (dest_count, slot_rows - first_rows, LANES)
    return pl.pallas_call(
        functools.partial(pack_kernel, (time_count, space_count, rows_tm, slot_rows, first_rows, width, layout)),
        in_specs=[pl.BlockSpec(memory_space=pltpu.VMEM)] * 4 + [pl.BlockSpec(memory_space=pl.ANY)],
        out_specs=[pl.BlockSpec(memory_space=pl.ANY)] * 2,
        out_shape=[jax.ShapeDtypeStruct(first_shape, jnp.bfloat16), jax.ShapeDtypeStruct(last_shape, jnp.bfloat16)],
        scratch_shapes=[
            pltpu.VMEM(shape, jnp.int32),
            pltpu.SMEM(shape, jnp.int32),
            pltpu.VMEM((5,) + shape, jnp.float32),
            pltpu.VMEM((width, 3 * dest_count), jnp.float32),
            pltpu.VMEM((swath_rows, LANES), jnp.float32),
            pltpu.VMEM((dest_count * slot_rows, LANES), jnp.float32),
            pltpu.VMEM((dest_count * layout[0], LANES), jnp.float32),
            pltpu.VMEM(first_shape, jnp.bfloat16),
            pltpu.VMEM(last_shape, jnp.bfloat16),
            pltpu.VMEM((swath_rows, LANES), jnp.bfloat16),
            pltpu.VMEM((chunks * dest_count, LANES), jnp.bfloat16),
            pltpu.VMEM((chunks * dest_count, LANES), jnp.float32),
            pltpu.SemaphoreType.DMA((4,)),
        ],
        compiler_params=pltpu.CompilerParams(vmem_limit_bytes=VMEM),
        name="pack",
    )(
        tile_index.reshape(shape),
        tile_row.reshape(shape),
        granule_day.reshape(shape),
        weights.reshape(shape),
        pixels,
    )


def chunks_of(first_slot, rows):
    slot, found = first_slot, []
    while slot < first_slot + rows:
        size = min(32 - slot % 32, first_slot + rows - slot)
        found.append((slot, size))
        slot += size
    return found


def add_rows(total, pixf, code_s, code_row, first_slot, rows, pix_at, count):
    def add_group(row, lane, at):
        places = [code_s[row, lane + u] for u in range(GROUP)]
        made = [total[pl.ds(p, 1), :] + pixf[pl.ds(at + u, 1), :] for u, p in enumerate(places)]
        for p, value in zip(places, made):
            total[pl.ds(p, 1), :] = value

    def add_singly(row, lane, at):
        def one(u, _):
            p = code_s[row, lane + u]
            p = jnp.where(p >= CLASH, p - CLASH, p)
            total[pl.ds(p, 1), :] = total[pl.ds(p, 1), :] + pixf[pl.ds(at + u, 1), :]
            return 0

        lax.fori_loop(0, GROUP, one, 0)

    for slot, chunk in chunks_of(first_slot, rows):
        start = slot - first_slot
        row, lane = code_row(slot // LANES), slot % LANES
        at = pix_at + start
        heads = [code_s[row, lane + g] for g in range(0, chunk, GROUP)]
        clash = functools.reduce(jnp.maximum, heads) >= CLASH

        @pl.when((count > start) & jnp.logical_not(clash))
        def _():
            for g in range(0, chunk, GROUP):
                add_group(row, lane + g, at + g)

        @pl.when((count > start) & clash)
        def _():
            for g, head in zip(range(0, chunk, GROUP), heads):
                pl.when(head < CLASH)(functools.partial(add_group, row, lane + g, at + g))
                pl.when(head >= CLASH)(functools.partial(add_singly, row, lane + g, at + g))


def grid_first_kernel(
    dims, moved_ref, total_ref, code_ref, rest_ref, count_ref, column_ref, meta_v, pixf, code_s, count_s, sems
):
    time_count, space_count, rows_tm, slot_rows, first_rows, width, (meta_rows, folded) = dims
    day_dev = DAYS // time_count
    blocks = time_count * space_count
    pieces = width // LANES
    spare = rows_tm * DAYS

    meta_v[...] = moved_ref[:, first_rows:, :].astype(jnp.float32).reshape(blocks * meta_rows, LANES)
    whole = pieces - 1 if folded else pieces
    early = lax.broadcasted_iota(jnp.int32, (blocks, LANES), 1) < LANES // 2

    def lanes(v, i):
        if i < whole:
            return meta_v[pl.ds(v * whole + i, blocks, stride=meta_rows), :]
        tail = meta_v[pl.ds(3 * whole + v // 2, blocks, stride=meta_rows), :]
        return jnp.where(early, pltpu.roll(tail, LANES // 2, 1) if v == 1 else tail, 0.0)

    block = lax.broadcasted_iota(jnp.int32, (blocks, LANES), 0)
    offset = jnp.zeros((blocks, LANES), jnp.float32)
    for m in range(1, time_count):
        offset = offset + jnp.where(block >= m * space_count, float(day_dev), 0.0)
    within = lax.broadcasted_iota(jnp.int32, (blocks, LANES), 1) % GROUP
    count = jnp.zeros((blocks, 1), jnp.float32)
    for i in range(pieces):
        weight, local_row, day = (lanes(v, i) for v in range(3))
        used = weight > 0.0
        count = count + jnp.sum(jnp.where(used, 1.0, 0.0), axis=1, keepdims=True)
        column_ref[i * LANES : (i + 1) * LANES, :] = jnp.transpose(weight)
        code = jnp.where(used, local_row * DAYS + (day + offset), float(spare)).astype(jnp.int32)
        clash = jnp.zeros(code.shape, jnp.int32)
        for k in range(1, GROUP):
            ahead = pltpu.roll(code, LANES - k, 1)
            clash = jnp.where((ahead == code) & (within + k < GROUP) & (code < spare), 1, clash)
        k = 1
        while k < GROUP:
            ahead = pltpu.roll(clash, LANES - k, 1)
            clash = jnp.where(within + k < GROUP, jnp.maximum(clash, ahead), clash)
            k *= 2
        code_ref[i * blocks : (i + 1) * blocks, :] = jnp.where((within == 0) & (clash > 0), code + CLASH, code)
    rest_ref[...] = code_ref[first_rows // LANES * blocks :, :]
    count_ref[...] = jnp.broadcast_to(count, (blocks, LANES)).astype(jnp.int32)
    code_copy = pltpu.make_async_copy(code_ref, code_s, sems.at[0])
    count_copy = pltpu.make_async_copy(count_ref, count_s, sems.at[1])
    code_copy.start()
    count_copy.start()

    for b in range(blocks):
        column = column_ref[:first_rows, b : b + 1]
        pixf[b * first_rows : (b + 1) * first_rows, :] = moved_ref[b, :first_rows, :].astype(jnp.float32) * column

    def clear(i, _):
        total_ref[pl.ds(pl.multiple_of(i * DAYS, DAYS), DAYS), :] = jnp.zeros((DAYS, LANES), jnp.float32)
        return 0

    lax.fori_loop(0, rows_tm, clear, 0)
    total_ref[spare:, :] = jnp.zeros((8, LANES), jnp.float32)
    code_copy.wait()
    count_copy.wait()

    def add(b, _):
        add_rows(total_ref, pixf, code_s, lambda i: i * blocks + b, 0, first_rows, b * first_rows, count_s[b, 0])
        return 0

    lax.fori_loop(0, blocks, add, 0)


def grid_last_kernel(
    dims, code_s, count_s, column_ref, moved_ref, first_ref, field_ref, keep_ref, give_ref,
    total, first_v, moved_v, pixf, field_v, gram_v, first_sems, block_sems, out_sem
):
    time_count, space_count, rows_tm, slot_rows, first_rows, width, (meta_rows, folded) = dims
    blocks = time_count * space_count
    last_rows = slot_rows - first_rows
    group = rows_tm // STEPS
    skipped = first_rows // LANES

    def load(i):
        at = pl.ds(pl.multiple_of(i * group * DAYS, DAYS), group * DAYS)
        return pltpu.make_async_copy(first_ref.at[at], first_v.at[at], first_sems.at[i])

    def fetch(b):
        return pltpu.make_async_copy(moved_ref.at[b], moved_v.at[b], block_sems.at[b])

    for b in range(blocks):
        pl.when(count_s[b, 0] > first_rows)(fetch(b).start)
    for i in range(STEPS):
        load(i).start()

    def clear(i, _):
        total[pl.ds(pl.multiple_of(i * DAYS, DAYS), DAYS), :] = jnp.zeros((DAYS, LANES), jnp.float32)
        return 0

    lax.fori_loop(0, rows_tm, clear, 0)
    total[rows_tm * DAYS :, :] = jnp.zeros((8, LANES), jnp.float32)
    for b in range(blocks):

        @pl.when(count_s[b, 0] > first_rows)
        def _():
            fetch(b).wait()
            column = column_ref[first_rows:slot_rows, b : b + 1]
            pixf[b * last_rows : (b + 1) * last_rows, :] = moved_v[b].astype(jnp.float32) * column

    def add(b, _):
        rest = count_s[b, 0] - first_rows

        @pl.when(rest > 0)
        def _():
            add_rows(
                total, pixf, code_s, lambda i: (i - skipped) * blocks + b, first_rows, last_rows, b * last_rows, rest
            )

        return 0

    lax.fori_loop(0, blocks, add, 0)

    def send(i):
        at = pl.ds(i * group, group)
        return pltpu.make_async_copy(field_v.at[at], field_ref.at[at], out_sem)

    def settle(i):
        for q in range(i * group, (i + 1) * group):
            at = pl.ds(q * DAYS, DAYS)
            field_v[q] = (first_v[at, :] + total[at, :]).astype(jnp.bfloat16)

    def multiply(i):
        both = jnp.concatenate([field_v[q] for q in range(i * group, (i + 1) * group)], axis=1)
        part = lax.dot_general(both[:RANK], both, LAST_LAST, preferred_element_type=jnp.float32)
        for c in range(DAYS // LANES):
            here = part[:, c * LANES : (c + 1) * LANES]
            gram_v[c] = here if i == 0 else gram_v[c] + here

    for i in range(STEPS):
        load(i).wait()
        settle(i)
        if i > 0:
            send(i - 1).start()
            multiply(i - 1)
    send(STEPS - 1).start()
    multiply(STEPS - 1)
    odd = lax.axis_index("tm") % 2
    half = DAYS // LANES // 2
    for c in range(half):
        keep_ref[c] = gram_v[odd * half + c]
        give_ref[c] = gram_v[(1 - odd) * half + c]
    pltpu.make_async_copy(field_v, field_ref, out_sem).wait()


def grid_rows(moved_first, moved_last, time_count, space_count, rows_tm, slots):
    slot_rows, first_rows = split_rows(slots)
    last_rows = slot_rows - first_rows
    width = round_up(slots, LANES)
    blocks = time_count * space_count
    dims = (time_count, space_count, rows_tm, slot_rows, first_rows, width, meta_layout(slots))
    codes = (blocks * width // LANES, LANES)
    rest = (codes[0] - first_rows // LANES * blocks, LANES)
    counts = (blocks, LANES)
    columns = (width, blocks)
    sums = (rows_tm * DAYS + 8, LANES)
    half = (DAYS // LANES // 2, RANK, LANES)
    params = pltpu.CompilerParams(vmem_limit_bytes=VMEM)
    moved_first, moved_last = (pltpu.with_memory_space_constraint(v, pltpu.VMEM) for v in (moved_first, moved_last))
    total, _, rest_code, count, column = pl.pallas_call(
        functools.partial(grid_first_kernel, dims),
        out_shape=[
            jax.ShapeDtypeStruct(sums, jnp.float32),
            jax.ShapeDtypeStruct(codes, jnp.int32),
            jax.ShapeDtypeStruct(rest, jnp.int32),
            jax.ShapeDtypeStruct(counts, jnp.int32),
            jax.ShapeDtypeStruct(columns, jnp.float32),
        ],
        scratch_shapes=[
            pltpu.VMEM((blocks * meta_layout(slots)[0], LANES), jnp.float32),
            pltpu.VMEM((blocks * first_rows, LANES), jnp.float32),
            pltpu.SMEM(codes, jnp.int32),
            pltpu.SMEM(counts, jnp.int32),
            pltpu.SemaphoreType.DMA((2,)),
        ],
        compiler_params=params,
        cost_estimate=pl.CostEstimate(flops=0, bytes_accessed=60_000_000, transcendentals=0),
        name="grid_first",
    )(moved_first)
    whole = pl.BlockSpec(memory_space=pltpu.VMEM)
    return pl.pallas_call(
        functools.partial(grid_last_kernel, dims),
        in_specs=[
            pl.BlockSpec(memory_space=pltpu.SMEM),
            pl.BlockSpec(memory_space=pltpu.SMEM),
            whole,
            pl.BlockSpec(memory_space=pl.ANY),
            pl.BlockSpec(memory_space=pl.ANY),
        ],
        out_specs=[pl.BlockSpec(memory_space=pl.ANY), whole, whole],
        out_shape=[
            jax.ShapeDtypeStruct((rows_tm, DAYS, LANES), jnp.bfloat16),
            pltpu.VMEM(half, jnp.float32),
            pltpu.VMEM(half, jnp.float32),
        ],
        scratch_shapes=[
            pltpu.VMEM(sums, jnp.float32),
            pltpu.VMEM((rows_tm * DAYS, LANES), jnp.float32),
            pltpu.VMEM((blocks, last_rows, LANES), jnp.bfloat16),
            pltpu.VMEM((blocks * last_rows, LANES), jnp.float32),
            pltpu.VMEM((rows_tm, DAYS, LANES), jnp.bfloat16),
            pltpu.VMEM((DAYS // LANES, RANK, LANES), jnp.float32),
            pltpu.SemaphoreType.DMA((STEPS,)),
            pltpu.SemaphoreType.DMA((blocks,)),
            pltpu.SemaphoreType.DMA,
        ],
        compiler_params=params,
        name="grid_last_and_gram",
    )(rest_code, count, column, moved_last, total)


def bf16_parts(x, count):
    found = []
    for _ in range(count):
        found.append(x.astype(jnp.bfloat16))
        x = x - found[-1].astype(jnp.float32)
    return found


def dot_parts(a, b, dims, count, splits):
    (left,), (right,) = dims[0]
    a_parts, b_parts = bf16_parts(a, count), bf16_parts(b, count)
    pairs = [(i, j) for i in range(count) for j in range(count - i)]
    a_all = jnp.concatenate([a_parts[i] for i, _ in pairs], axis=left)
    b_all = jnp.concatenate([b_parts[j] for _, j in pairs], axis=right)
    dot = functools.partial(lax.dot_general, dimension_numbers=dims, preferred_element_type=jnp.float32)
    if splits == 1:
        return dot(a_all, b_all)
    size = a.shape[0] // splits
    return jnp.concatenate([dot(a_all[i * size : (i + 1) * size], b_all) for i in range(splits)], axis=0)


def dot_f32(a, b, dims=(((1,), (0,)), ((), ()))):
    return dot_parts(a, b, dims, 3, 1)


def dot_three(a, b, dims=(((1,), (0,)), ((), ()))):
    return dot_parts(a, b, dims, 2, 4)


def lower_inverse(a):
    n = a.shape[0]
    full = (8, n)
    tiles = [a[8 * i : 8 * i + 8, :] for i in range(n // 8)]
    lane = lax.broadcasted_iota(jnp.int32, full, 1)
    down = lax.broadcasted_iota(jnp.int32, full, 0)
    out = []
    for t in range(n // 8):
        k = 8 * t
        block = (lane >= k) & (lane < k + 8)
        panel = tiles[t]
        cols = [jnp.broadcast_to(panel[:, k + c : k + c + 1], full) for c in range(8)]
        e = {(i, c): jnp.broadcast_to(cols[c][i : i + 1, :], full) for c in range(8) for i in range(c, 8)}
        start = jnp.where(block, jnp.where(lane == k + down, 1.0, 0.0), panel)
        rows = [jnp.broadcast_to(start[i : i + 1, :], full) for i in range(8)]
        held = []
        for s in range(0, 8, 2):
            p, q, r = e[s, s], e[s + 1, s], e[s + 1, s + 1]
            det = p * r - q * q
            inv = pl.reciprocal(det, approx=True)
            factors = {}
            for i in range(s + 2, 8):
                x, y = e[i, s], e[i, s + 1]
                factors[i] = (r * x - q * y, p * y - q * x)
            for i in range(s + 2, 8):
                u, v = factors[i]
                for c in range(s + 2, i + 1):
                    e[i, c] = e[i, c] - (u * e[c, s] + v * e[c, s + 1]) * inv
                rows[i] = rows[i] - (u * rows[s] + v * rows[s + 1]) * inv
            held.append((p, q, r, det, inv, factors))
        done = jnp.zeros(full, jnp.float32)
        solved = [None] * 8
        for s in (6, 4, 2, 0):
            p, q, r, det, inv, factors = held[s // 2]
            root = lax.rsqrt(p)
            done = jnp.where(down == s, rows[s] * root, done)
            done = jnp.where(down == s + 1, (rows[s + 1] * p - q * rows[s]) * (root * lax.rsqrt(det)), done)
            first, second = r * rows[s] - q * rows[s + 1], p * rows[s + 1] - q * rows[s]
            for i in range(7, s + 1, -1):
                u, v = factors[i]
                first, second = first - u * solved[i], second - v * solved[i]
            solved[s], solved[s + 1] = first * inv, second * inv
        out.append(jnp.where(lane < k + 8, done, 0.0))
        for i in range(t + 1, n // 8):
            terms = [jnp.broadcast_to(tiles[i][:, k + c : k + c + 1], full) * solved[c] for c in range(8)]
            while len(terms) > 1:
                terms = [terms[j] + terms[j + 1] for j in range(0, len(terms), 2)]
            tiles[i] = jnp.where(block, 0.0, tiles[i]) - terms[0]
    return jnp.concatenate(out, axis=0)


def solve_kernel(scale, own_ref, other_ref, field_ref, basis_ref, prop_ref, gram_v, field_v, basis_v, sems):
    h = LANES
    pieces = DAYS // h
    rows_here = field_v.shape[0]
    load = pltpu.make_async_copy(field_ref.at[:, pl.ds(0, RANK), :], field_v, sems.at[0])
    load.start()
    odd = lax.axis_index("tm") % 2
    for c in range(pieces // 2):
        gram_v[odd * (pieces // 2) + c] = own_ref[c]
        gram_v[(1 - odd) * (pieces // 2) + c] = other_ref[c]

    gram = jnp.concatenate([gram_v[i] for i in range(pieces)], axis=1)
    eye = lax.broadcasted_iota(jnp.int32, (h, h), 0) == lax.broadcasted_iota(jnp.int32, (h, h), 1)
    a11, a12, a22 = gram_v[0, :h, :], gram_v[1, :h, :], gram_v[1, h:, :]
    size_col, size_row = [], []
    for part in (a11, a22):
        diag = jnp.where(eye, part, 0.0)
        size_col.append(lax.rsqrt(jnp.sum(diag, axis=1, keepdims=True)))
        size_row.append(lax.rsqrt(jnp.sum(diag, axis=0, keepdims=True)))
    top, low = gram[:h], gram[h:]
    x1 = lower_inverse(a11 * size_col[0] * size_row[0])
    r12 = dot_f32(x1, a12 * size_col[0] * size_row[1])
    x2 = lower_inverse(a22 * size_col[1] * size_row[1] - dot_f32(r12, r12, FIRST_FIRST))
    factor_top = dot_f32(x1, top * size_col[0])
    schur = low[:, h:] * size_col[1] - dot_f32(r12, factor_top[:, h:], FIRST_FIRST)
    mixed = -dot_f32(x2, dot_f32(r12, x1, FIRST_FIRST))
    factor_low = dot_f32(x2, schur)
    lower = jnp.concatenate(
        [
            jnp.concatenate([x1 * size_row[0], jnp.zeros((h, h), jnp.float32)], axis=1),
            jnp.concatenate([mixed * size_row[0], x2 * size_row[1]], axis=1),
        ],
        axis=0,
    )
    inverse = (scale * lower).astype(jnp.bfloat16)
    load.wait()

    def project(i):
        both = jnp.concatenate([field_v[2 * i], field_v[2 * i + 1]], axis=1)
        made = jnp.dot(inverse, both, preferred_element_type=jnp.float32).astype(jnp.bfloat16)
        basis_v[2 * i] = made[:, :h]
        basis_v[2 * i + 1] = made[:, h:]

    down = lax.broadcasted_iota(jnp.int32, (RANK, DAYS), 0)
    across = lax.broadcasted_iota(jnp.int32, (RANK, DAYS), 1)
    factor = jnp.concatenate(
        [factor_top, jnp.concatenate([jnp.zeros((h, h), jnp.float32), factor_low], axis=1)], axis=0
    )
    factor = jnp.where(across >= down, factor, 0.0)
    ahead = jnp.where(across < DAYS - 1, pltpu.roll(factor, DAYS - 1, 1), 0.0)
    cross = dot_three(ahead, factor, LAST_LAST)
    polar = cross / jnp.sqrt(jnp.sum(cross * cross) + 1e-06)
    todo = list(range(rows_here // 2))
    share = -(-len(todo) // (ITERS - 1))
    store = pltpu.make_async_copy(basis_v, basis_ref, sems.at[1])
    for n in range(ITERS):
        square = dot_three(polar, polar, LAST_LAST)
        for i in todo[n * share : (n + 1) * share]:
            project(i)
        if n == ITERS - 2:
            store.start()
        polar = 1.5 * polar - 0.5 * dot_three(square, polar)
    prop_ref[...] = math.sqrt(RANK) * polar
    store.wait()


def solve(own, other, field, cell_total):
    rows_tm = field.shape[0]
    part = (rows_tm, RANK, LANES)
    whole = pl.BlockSpec(memory_space=pltpu.VMEM)
    own, other = (pltpu.with_memory_space_constraint(v, pltpu.VMEM) for v in (own, other))
    return pl.pallas_call(
        functools.partial(solve_kernel, math.sqrt(cell_total)),
        in_specs=[whole, whole, pl.BlockSpec(memory_space=pl.ANY)],
        out_specs=[pl.BlockSpec(memory_space=pl.ANY), whole],
        out_shape=[
            jax.ShapeDtypeStruct(part, jnp.bfloat16),
            jax.ShapeDtypeStruct((RANK, RANK), jnp.float32),
        ],
        scratch_shapes=[
            pltpu.VMEM((DAYS // LANES, RANK, LANES), jnp.float32),
            pltpu.VMEM(part, jnp.bfloat16),
            pltpu.VMEM(part, jnp.bfloat16),
            pltpu.SemaphoreType.DMA((2,)),
        ],
        compiler_params=pltpu.CompilerParams(vmem_limit_bytes=VMEM),
        name="factor_basis_and_polar",
    )(own, other, field)


def body(pixels, weights, tile_index, tile_row, granule_day):
    swath_rows = pixels.shape[0]
    width = pixels.shape[1]
    space_count = lax.axis_size("space")
    time_count = lax.axis_size("tm")
    dest_count = time_count * space_count
    rows_tm = GR_DEV // time_count
    slots = 2 * swath_rows // space_count // time_count
    axes = ("tm", "space")
    first, last = pack(pixels, weights, tile_index, tile_row, granule_day, time_count, space_count, rows_tm, slots)
    first = lax.all_to_all(first, axes, split_axis=0, concat_axis=0, tiled=True)
    last = lax.all_to_all(last, axes, split_axis=0, concat_axis=0, tiled=True)
    field, keep, give = grid_rows(first, last, time_count, space_count, rows_tm, slots)

    swap = [(t, t ^ 1) for t in range(time_count)]
    peers = [[t * space_count + s for t in range(core, time_count, 2) for s in range(space_count)] for core in (0, 1)]
    among = functools.partial(
        lax.all_to_all, axis_name=axes, split_axis=0, concat_axis=0, axis_index_groups=peers, tiled=True
    )
    pieces = (keep + lax.ppermute(give, "tm", swap)).reshape(dest_count // 2, -1, LANES)
    mine = jnp.sum(among(pieces), axis=0, keepdims=True)
    own = among(jnp.broadcast_to(mine, pieces.shape)).reshape(keep.shape)
    other = lax.ppermute(own, "tm", swap)
    cell_total = space_count * GR_DEV * width
    basis, propagator = solve(own, other, field, cell_total)
    return (field[None], basis[None], propagator)


def solution(mesh):
    placed = (
        P(("tm", "space"), None),
        P(("tm", "space")),
        P(("tm", "space")),
        P(("tm", "space")),
        P(("tm", "space")),
    )
    return jax.shard_map(
        body,
        mesh=mesh,
        in_specs=placed,
        out_specs=(P("space", "tm", None, None), P("space", "tm", None, None), P()),
        check_vma=False,
    )
```

```python
import functools
import math

import jax
import jax.numpy as jnp
from jax import lax
from jax.experimental import pallas as pl
from jax.experimental.pallas import tpu as pltpu
from jax.sharding import PartitionSpec as P

GR_DEV = 160
DAYS = 512
RANK = 256
ITERS = 8
LANES = 128
GROUP = 16
CLASH = 1 << 20
STEPS = 5
VMEM = 56 * 1024 * 1024

LAST_LAST = (((1,), (1,)), ((), ()))
FIRST_FIRST = (((0,), (0,)), ((), ()))


def round_up(value, unit):
    return -(-value // unit) * unit


def split_rows(slots):
    rows = round_up(slots, 16)
    return rows, rows * 13 // 20 // 16 * 16


def meta_layout(slots):
    pieces = round_up(slots, LANES) // LANES
    folded = 3 * pieces > 8 and 3 * pieces - 1 <= 8 and slots % LANES <= LANES // 2
    return (8 if folded else round_up(3 * pieces, 8)), folded


def pack_kernel(
    dims, tile_ref, row_ref, day_ref, weight_ref, pix_ref, first_ref, last_ref, pos_v, pos_s, rows_v, meta_v, pixf, outf, mrow,
    first_v, last_v, pix_v, hot_v, prefix_v, sems
):
    time_count, space_count, rows_tm, slot_rows, first_rows, width, (meta_rows, folded) = dims
    dest_count = time_count * space_count
    chunks = tile_ref.shape[0]
    pieces = width // LANES

    fetch = pltpu.make_async_copy(pix_ref, pix_v, sems.at[3])
    fetch.start()
    tile = tile_ref[...]
    row = row_ref[...]
    group = jnp.zeros_like(row)
    for k in range(1, time_count):
        group = group + jnp.where(row >= k * rows_tm, 1, 0)
    dest_all = group * space_count + tile
    rows_v[0] = dest_all.astype(jnp.float32)
    rows_v[2] = weight_ref[...].astype(jnp.float32)
    rows_v[3] = (row - group * rows_tm).astype(jnp.float32)
    rows_v[4] = day_ref[...].astype(jnp.float32)

    dest_iota = lax.broadcasted_iota(jnp.int32, (dest_count, LANES), 0)
    upper = jnp.where(
        lax.broadcasted_iota(jnp.int32, (LANES, LANES), 0) <= lax.broadcasted_iota(jnp.int32, (LANES, LANES), 1), 1.0, 0.0
    ).astype(jnp.bfloat16)
    for c in range(chunks):
        hot = dest_iota == dest_all[c : c + 1, :]
        hot_v[c * dest_count : (c + 1) * dest_count, :] = jnp.where(hot, 1.0, 0.0).astype(jnp.bfloat16)
    prefix_v[...] = jnp.dot(hot_v[...], upper, preferred_element_type=jnp.float32)
    carry = jnp.zeros((dest_count, 1), jnp.float32)
    for c in range(chunks):
        prefix = prefix_v[c * dest_count : (c + 1) * dest_count, :]
        hot = dest_iota == dest_all[c : c + 1, :]
        rows_v[1, c : c + 1, :] = jnp.sum(jnp.where(hot, prefix + carry, 0.0), axis=0, keepdims=True) - 1.0
        carry = carry + prefix[:, LANES - 1 : LANES]
    pos_v[...] = dest_all * slot_rows + rows_v[1].astype(jnp.int32)
    copy = pltpu.make_async_copy(pos_v, pos_s, sems.at[0])
    copy.start()
    meta_v[...] = jnp.zeros_like(meta_v)
    mrow[...] = jnp.zeros_like(mrow)

    def clear(b, _):
        outf[pl.ds(pl.multiple_of(b * slot_rows, 16), slot_rows), :] = jnp.zeros((slot_rows, LANES), jnp.float32)
        return 0

    lax.fori_loop(0, dest_count, clear, 0)
    fetch.wait()
    copy.wait()
    deep = 4
    both = deep * LANES
    dest_number = lax.broadcasted_iota(jnp.int32, (dest_count, both), 0).astype(jnp.float32)
    slot_number = lax.broadcasted_iota(jnp.int32, (width, both), 0).astype(jnp.float32)

    def move(c, _):
        base = pl.multiple_of(c * both, both)
        pixf[pl.ds(base, both), :] = pix_v[pl.ds(base, both), :].astype(jnp.float32)
        dest, rank, weight, local_row, day = (
            jnp.concatenate([rows_v[v, pl.ds(deep * c + i, 1), :] for i in range(deep)], axis=1) for v in range(5)
        )
        hot = dest_number == dest
        place = jnp.where(slot_number == rank, 1.0, 0.0).astype(jnp.bfloat16)
        values = jnp.concatenate([jnp.where(hot, v, 0.0) for v in (weight, local_row, day)], axis=0).astype(jnp.bfloat16)
        meta_v[...] += lax.dot_general(values, place, LAST_LAST, preferred_element_type=jnp.float32)
        for i in range(deep):
            for lane in range(LANES):
                outf[pl.ds(pos_s[deep * c + i, lane], 1), :] = pixf[pl.ds(base + i * LANES + lane, 1), :]
        return 0

    lax.fori_loop(0, chunks // deep, move, 0)
    whole = pieces - 1 if folded else pieces

    def lanes(v, i):
        return meta_v[v * dest_count : (v + 1) * dest_count, i * LANES : (i + 1) * LANES]

    def put(at, value):
        mrow[pl.ds(at, dest_count, stride=meta_rows), :] = value

    for v in range(3):
        for i in range(whole):
            put(v * whole + i, lanes(v, i))
    if folded:
        put(3 * whole, lanes(0, whole) + pltpu.roll(lanes(1, whole), LANES // 2, 1))
        put(3 * whole + 1, lanes(2, whole))

    together = 8

    def narrow(i, _):
        for q in range(together):
            b = i * together + q
            at = pl.multiple_of(b * slot_rows, 16)
            first_v[b, :first_rows, :] = outf[pl.ds(at, first_rows), :].astype(jnp.bfloat16)
            first_v[b, first_rows:, :] = mrow[pl.ds(pl.multiple_of(b * meta_rows, 8), meta_rows), :].astype(jnp.bfloat16)
            last_v[b] = outf[pl.ds(at + first_rows, slot_rows - first_rows), :].astype(jnp.bfloat16)
        some = pl.ds(i * together, together)
        pltpu.make_async_copy(first_v.at[some], first_ref.at[some], sems.at[1]).start()
        pltpu.make_async_copy(last_v.at[some], last_ref.at[some], sems.at[2]).start()
        return 0

    lax.fori_loop(0, dest_count // together, narrow, 0)
    pltpu.make_async_copy(first_v, first_ref, sems.at[1]).wait()
    pltpu.make_async_copy(last_v, last_ref, sems.at[2]).wait()


def pack(pixels, weights, tile_index, tile_row, granule_day, time_count, space_count, rows_tm, slots):
    swath_rows = pixels.shape[0]
    chunks = swath_rows // LANES
    dest_count = time_count * space_count
    slot_rows, first_rows = split_rows(slots)
    width = round_up(slots, LANES)
    shape = (chunks, LANES)
    layout = meta_layout(slots)
    first_shape = (dest_count, first_rows + layout[0], LANES)
    last_shape = (dest_count, slot_rows - first_rows, LANES)
    return pl.pallas_call(
        functools.partial(pack_kernel, (time_count, space_count, rows_tm, slot_rows, first_rows, width, layout)),
        in_specs=[pl.BlockSpec(memory_space=pltpu.VMEM)] * 4 + [pl.BlockSpec(memory_space=pl.ANY)],
        out_specs=[pl.BlockSpec(memory_space=pl.ANY)] * 2,
        out_shape=[jax.ShapeDtypeStruct(first_shape, jnp.bfloat16), jax.ShapeDtypeStruct(last_shape, jnp.bfloat16)],
        scratch_shapes=[
            pltpu.VMEM(shape, jnp.int32),
            pltpu.SMEM(shape, jnp.int32),
            pltpu.VMEM((5,) + shape, jnp.float32),
            pltpu.VMEM((3 * dest_count, width), jnp.float32),
            pltpu.VMEM((swath_rows, LANES), jnp.float32),
            pltpu.VMEM((dest_count * slot_rows, LANES), jnp.float32),
            pltpu.VMEM((dest_count * layout[0], LANES), jnp.float32),
            pltpu.VMEM(first_shape, jnp.bfloat16),
            pltpu.VMEM(last_shape, jnp.bfloat16),
            pltpu.VMEM((swath_rows, LANES), jnp.bfloat16),
            pltpu.VMEM((chunks * dest_count, LANES), jnp.bfloat16),
            pltpu.VMEM((chunks * dest_count, LANES), jnp.float32),
            pltpu.SemaphoreType.DMA((4,)),
        ],
        compiler_params=pltpu.CompilerParams(vmem_limit_bytes=VMEM),
        name="pack",
    )(
        tile_index.reshape(shape),
        tile_row.reshape(shape),
        granule_day.reshape(shape),
        weights.reshape(shape),
        pixels,
    )


def chunks_of(first_slot, rows):
    slot, found = first_slot, []
    while slot < first_slot + rows:
        size = min(32 - slot % 32, first_slot + rows - slot)
        found.append((slot, size))
        slot += size
    return found


def add_rows(total, pixf, code_s, code_row, first_slot, rows, pix_at, count):
    def add_group(row, lane, at):
        places = [code_s[row, lane + u] for u in range(GROUP)]
        made = [total[pl.ds(p, 1), :] + pixf[pl.ds(at + u, 1), :] for u, p in enumerate(places)]
        for p, value in zip(places, made):
            total[pl.ds(p, 1), :] = value

    def add_singly(row, lane, at):
        def one(u, _):
            p = code_s[row, lane + u]
            p = jnp.where(p >= CLASH, p - CLASH, p)
            total[pl.ds(p, 1), :] = total[pl.ds(p, 1), :] + pixf[pl.ds(at + u, 1), :]
            return 0

        lax.fori_loop(0, GROUP, one, 0)

    for slot, chunk in chunks_of(first_slot, rows):
        start = slot - first_slot
        row, lane = code_row(slot // LANES), slot % LANES
        at = pix_at + start
        heads = [code_s[row, lane + g] for g in range(0, chunk, GROUP)]
        clash = functools.reduce(jnp.maximum, heads) >= CLASH

        @pl.when((count > start) & jnp.logical_not(clash))
        def _():
            for g in range(0, chunk, GROUP):
                add_group(row, lane + g, at + g)

        @pl.when((count > start) & clash)
        def _():
            for g, head in zip(range(0, chunk, GROUP), heads):
                pl.when(head < CLASH)(functools.partial(add_group, row, lane + g, at + g))
                pl.when(head >= CLASH)(functools.partial(add_singly, row, lane + g, at + g))


def grid_first_kernel(
    dims, moved_ref, total_ref, code_ref, rest_ref, count_ref, column_ref, meta_v, pixf, code_s, count_s, sems
):
    time_count, space_count, rows_tm, slot_rows, first_rows, width, (meta_rows, folded) = dims
    day_dev = DAYS // time_count
    blocks = time_count * space_count
    pieces = width // LANES
    spare = rows_tm * DAYS

    meta_v[...] = moved_ref[:, first_rows:, :].astype(jnp.float32).reshape(blocks * meta_rows, LANES)
    whole = pieces - 1 if folded else pieces
    early = lax.broadcasted_iota(jnp.int32, (blocks, LANES), 1) < LANES // 2

    def lanes(v, i):
        if i < whole:
            return meta_v[pl.ds(v * whole + i, blocks, stride=meta_rows), :]
        tail = meta_v[pl.ds(3 * whole + v // 2, blocks, stride=meta_rows), :]
        return jnp.where(early, pltpu.roll(tail, LANES // 2, 1) if v == 1 else tail, 0.0)

    block = lax.broadcasted_iota(jnp.int32, (blocks, LANES), 0)
    offset = jnp.zeros((blocks, LANES), jnp.float32)
    for m in range(1, time_count):
        offset = offset + jnp.where(block >= m * space_count, float(day_dev), 0.0)
    within = lax.broadcasted_iota(jnp.int32, (blocks, LANES), 1) % GROUP
    count = jnp.zeros((blocks, 1), jnp.float32)
    for i in range(pieces):
        weight, local_row, day = (lanes(v, i) for v in range(3))
        used = weight > 0.0
        count = count + jnp.sum(jnp.where(used, 1.0, 0.0), axis=1, keepdims=True)
        column_ref[i * LANES : (i + 1) * LANES, :] = jnp.transpose(weight)
        code = jnp.where(used, local_row * DAYS + (day + offset), float(spare)).astype(jnp.int32)
        clash = jnp.zeros(code.shape, jnp.int32)
        for k in range(1, GROUP):
            ahead = pltpu.roll(code, LANES - k, 1)
            clash = jnp.where((ahead == code) & (within + k < GROUP) & (code < spare), 1, clash)
        k = 1
        while k < GROUP:
            ahead = pltpu.roll(clash, LANES - k, 1)
            clash = jnp.where(within + k < GROUP, jnp.maximum(clash, ahead), clash)
            k *= 2
        code_ref[i * blocks : (i + 1) * blocks, :] = jnp.where((within == 0) & (clash > 0), code + CLASH, code)
    rest_ref[...] = code_ref[first_rows // LANES * blocks :, :]
    count_ref[...] = jnp.broadcast_to(count, (blocks, LANES)).astype(jnp.int32)
    code_copy = pltpu.make_async_copy(code_ref, code_s, sems.at[0])
    count_copy = pltpu.make_async_copy(count_ref, count_s, sems.at[1])
    code_copy.start()
    count_copy.start()

    for b in range(blocks):
        column = column_ref[:first_rows, b : b + 1]
        pixf[b * first_rows : (b + 1) * first_rows, :] = moved_ref[b, :first_rows, :].astype(jnp.float32) * column

    def clear(i, _):
        total_ref[pl.ds(pl.multiple_of(i * DAYS, DAYS), DAYS), :] = jnp.zeros((DAYS, LANES), jnp.float32)
        return 0

    lax.fori_loop(0, rows_tm, clear, 0)
    total_ref[spare:, :] = jnp.zeros((8, LANES), jnp.float32)
    code_copy.wait()
    count_copy.wait()

    def add(b, _):
        add_rows(total_ref, pixf, code_s, lambda i: i * blocks + b, 0, first_rows, b * first_rows, count_s[b, 0])
        return 0

    lax.fori_loop(0, blocks, add, 0)


def grid_last_kernel(
    dims, code_s, count_s, column_ref, moved_ref, first_ref, field_ref, keep_ref, give_ref,
    total, first_v, moved_v, pixf, field_v, gram_v, first_sems, block_sems, out_sem
):
    time_count, space_count, rows_tm, slot_rows, first_rows, width, (meta_rows, folded) = dims
    blocks = time_count * space_count
    last_rows = slot_rows - first_rows
    group = rows_tm // STEPS
    skipped = first_rows // LANES

    def load(i):
        at = pl.ds(pl.multiple_of(i * group * DAYS, DAYS), group * DAYS)
        return pltpu.make_async_copy(first_ref.at[at], first_v.at[at], first_sems.at[i])

    def fetch(b):
        return pltpu.make_async_copy(moved_ref.at[b], moved_v.at[b], block_sems.at[b])

    for b in range(blocks):
        pl.when(count_s[b, 0] > first_rows)(fetch(b).start)
    for i in range(STEPS):
        load(i).start()

    def clear(i, _):
        total[pl.ds(pl.multiple_of(i * DAYS, DAYS), DAYS), :] = jnp.zeros((DAYS, LANES), jnp.float32)
        return 0

    lax.fori_loop(0, rows_tm, clear, 0)
    total[rows_tm * DAYS :, :] = jnp.zeros((8, LANES), jnp.float32)
    for b in range(blocks):

        @pl.when(count_s[b, 0] > first_rows)
        def _():
            fetch(b).wait()
            column = column_ref[first_rows:slot_rows, b : b + 1]
            pixf[b * last_rows : (b + 1) * last_rows, :] = moved_v[b].astype(jnp.float32) * column

    def add(b, _):
        rest = count_s[b, 0] - first_rows

        @pl.when(rest > 0)
        def _():
            add_rows(
                total, pixf, code_s, lambda i: (i - skipped) * blocks + b, first_rows, last_rows, b * last_rows, rest
            )

        return 0

    lax.fori_loop(0, blocks, add, 0)

    def send(i):
        at = pl.ds(i * group, group)
        return pltpu.make_async_copy(field_v.at[at], field_ref.at[at], out_sem)

    def settle(i):
        for q in range(i * group, (i + 1) * group):
            at = pl.ds(q * DAYS, DAYS)
            field_v[q] = (first_v[at, :] + total[at, :]).astype(jnp.bfloat16)

    def multiply(i):
        both = jnp.concatenate([field_v[q] for q in range(i * group, (i + 1) * group)], axis=1)
        part = lax.dot_general(both[:RANK], both, LAST_LAST, preferred_element_type=jnp.float32)
        for c in range(DAYS // LANES):
            here = part[:, c * LANES : (c + 1) * LANES]
            gram_v[c] = here if i == 0 else gram_v[c] + here

    for i in range(STEPS):
        load(i).wait()
        settle(i)
        if i > 0:
            send(i - 1).start()
            multiply(i - 1)
    send(STEPS - 1).start()
    multiply(STEPS - 1)
    odd = lax.axis_index("tm") % 2
    half = DAYS // LANES // 2
    for c in range(half):
        keep_ref[c] = gram_v[odd * half + c]
        give_ref[c] = gram_v[(1 - odd) * half + c]
    pltpu.make_async_copy(field_v, field_ref, out_sem).wait()


def grid_rows(moved_first, moved_last, time_count, space_count, rows_tm, slots):
    slot_rows, first_rows = split_rows(slots)
    last_rows = slot_rows - first_rows
    width = round_up(slots, LANES)
    blocks = time_count * space_count
    dims = (time_count, space_count, rows_tm, slot_rows, first_rows, width, meta_layout(slots))
    codes = (blocks * width // LANES, LANES)
    rest = (codes[0] - first_rows // LANES * blocks, LANES)
    counts = (blocks, LANES)
    columns = (width, blocks)
    sums = (rows_tm * DAYS + 8, LANES)
    half = (DAYS // LANES // 2, RANK, LANES)
    params = pltpu.CompilerParams(vmem_limit_bytes=VMEM)
    moved_first, moved_last = (pltpu.with_memory_space_constraint(v, pltpu.VMEM) for v in (moved_first, moved_last))
    total, _, rest_code, count, column = pl.pallas_call(
        functools.partial(grid_first_kernel, dims),
        out_shape=[
            jax.ShapeDtypeStruct(sums, jnp.float32),
            jax.ShapeDtypeStruct(codes, jnp.int32),
            jax.ShapeDtypeStruct(rest, jnp.int32),
            jax.ShapeDtypeStruct(counts, jnp.int32),
            jax.ShapeDtypeStruct(columns, jnp.float32),
        ],
        scratch_shapes=[
            pltpu.VMEM((blocks * meta_layout(slots)[0], LANES), jnp.float32),
            pltpu.VMEM((blocks * first_rows, LANES), jnp.float32),
            pltpu.SMEM(codes, jnp.int32),
            pltpu.SMEM(counts, jnp.int32),
            pltpu.SemaphoreType.DMA((2,)),
        ],
        compiler_params=params,
        cost_estimate=pl.CostEstimate(flops=0, bytes_accessed=60_000_000, transcendentals=0),
        name="grid_first",
    )(moved_first)
    whole = pl.BlockSpec(memory_space=pltpu.VMEM)
    return pl.pallas_call(
        functools.partial(grid_last_kernel, dims),
        in_specs=[
            pl.BlockSpec(memory_space=pltpu.SMEM),
            pl.BlockSpec(memory_space=pltpu.SMEM),
            whole,
            pl.BlockSpec(memory_space=pl.ANY),
            pl.BlockSpec(memory_space=pl.ANY),
        ],
        out_specs=[pl.BlockSpec(memory_space=pl.ANY), whole, whole],
        out_shape=[
            jax.ShapeDtypeStruct((rows_tm, DAYS, LANES), jnp.bfloat16),
            pltpu.VMEM(half, jnp.float32),
            pltpu.VMEM(half, jnp.float32),
        ],
        scratch_shapes=[
            pltpu.VMEM(sums, jnp.float32),
            pltpu.VMEM((rows_tm * DAYS, LANES), jnp.float32),
            pltpu.VMEM((blocks, last_rows, LANES), jnp.bfloat16),
            pltpu.VMEM((blocks * last_rows, LANES), jnp.float32),
            pltpu.VMEM((rows_tm, DAYS, LANES), jnp.bfloat16),
            pltpu.VMEM((DAYS // LANES, RANK, LANES), jnp.float32),
            pltpu.SemaphoreType.DMA((STEPS,)),
            pltpu.SemaphoreType.DMA((blocks,)),
            pltpu.SemaphoreType.DMA,
        ],
        compiler_params=params,
        name="grid_last_and_gram",
    )(rest_code, count, column, moved_last, total)


def bf16_parts(x, count):
    found = []
    for _ in range(count):
        found.append(x.astype(jnp.bfloat16))
        x = x - found[-1].astype(jnp.float32)
    return found


def dot_f32(a, b, dims=(((1,), (0,)), ((), ()))):
    return lax.dot_general(a, b, dims, precision=lax.Precision.HIGHEST, preferred_element_type=jnp.float32)


def dot_three(a, b, dims=(((1,), (0,)), ((), ()))):
    (left,), (right,) = dims[0]
    a_high, a_low = bf16_parts(a, 2)
    b_high, b_low = bf16_parts(b, 2)
    a_all = jnp.concatenate([a_high, a_high, a_low], axis=left)
    b_all = jnp.concatenate([b_high, b_low, b_high], axis=right)
    return lax.dot_general(a_all, b_all, dims, preferred_element_type=jnp.float32)


def lower_inverse(a):
    n = a.shape[0]
    full = (8, n)
    tiles = [a[8 * i : 8 * i + 8, :] for i in range(n // 8)]
    lane = lax.broadcasted_iota(jnp.int32, full, 1)
    down = lax.broadcasted_iota(jnp.int32, full, 0)
    out = []
    for t in range(n // 8):
        k = 8 * t
        block = (lane >= k) & (lane < k + 8)
        panel = tiles[t]
        cols = [jnp.broadcast_to(panel[:, k + c : k + c + 1], full) for c in range(8)]
        e = {(i, c): jnp.broadcast_to(cols[c][i : i + 1, :], full) for c in range(8) for i in range(c, 8)}
        start = jnp.where(block, jnp.where(lane == k + down, 1.0, 0.0), panel)
        rows = [jnp.broadcast_to(start[i : i + 1, :], full) for i in range(8)]
        held = []
        for s in range(0, 8, 2):
            p, q, r = e[s, s], e[s + 1, s], e[s + 1, s + 1]
            det = p * r - q * q
            inv = pl.reciprocal(det, approx=True)
            factors = {}
            for i in range(s + 2, 8):
                x, y = e[i, s], e[i, s + 1]
                factors[i] = (r * x - q * y, p * y - q * x)
            for i in range(s + 2, 8):
                u, v = factors[i]
                for c in range(s + 2, i + 1):
                    e[i, c] = e[i, c] - (u * e[c, s] + v * e[c, s + 1]) * inv
                rows[i] = rows[i] - (u * rows[s] + v * rows[s + 1]) * inv
            held.append((p, q, r, det, inv, factors))
        done = jnp.zeros(full, jnp.float32)
        solved = [None] * 8
        for s in (6, 4, 2, 0):
            p, q, r, det, inv, factors = held[s // 2]
            root = lax.rsqrt(p)
            done = jnp.where(down == s, rows[s] * root, done)
            done = jnp.where(down == s + 1, (rows[s + 1] * p - q * rows[s]) * (root * lax.rsqrt(det)), done)
            first, second = r * rows[s] - q * rows[s + 1], p * rows[s + 1] - q * rows[s]
            for i in range(7, s + 1, -1):
                u, v = factors[i]
                first, second = first - u * solved[i], second - v * solved[i]
            solved[s], solved[s + 1] = first * inv, second * inv
        out.append(jnp.where(lane < k + 8, done, 0.0))
        for i in range(t + 1, n // 8):
            terms = [jnp.broadcast_to(tiles[i][:, k + c : k + c + 1], full) * solved[c] for c in range(8)]
            while len(terms) > 1:
                terms = [terms[j] + terms[j + 1] for j in range(0, len(terms), 2)]
            tiles[i] = jnp.where(block, 0.0, tiles[i]) - terms[0]
    return jnp.concatenate(out, axis=0)


def solve_kernel(scale, own_ref, other_ref, field_ref, basis_ref, prop_ref, gram_v, field_v, basis_v, sems):
    h = LANES
    pieces = DAYS // h
    rows_here = field_v.shape[0]
    load = pltpu.make_async_copy(field_ref.at[:, pl.ds(0, RANK), :], field_v, sems.at[0])
    load.start()
    odd = lax.axis_index("tm") % 2
    for c in range(pieces // 2):
        gram_v[odd * (pieces // 2) + c] = own_ref[c]
        gram_v[(1 - odd) * (pieces // 2) + c] = other_ref[c]

    gram = jnp.concatenate([gram_v[i] for i in range(pieces)], axis=1)
    eye = lax.broadcasted_iota(jnp.int32, (h, h), 0) == lax.broadcasted_iota(jnp.int32, (h, h), 1)
    a11, a12, a22 = gram_v[0, :h, :], gram_v[1, :h, :], gram_v[1, h:, :]
    size_col, size_row = [], []
    for part in (a11, a22):
        diag = jnp.where(eye, part, 0.0)
        size_col.append(lax.rsqrt(jnp.sum(diag, axis=1, keepdims=True)))
        size_row.append(lax.rsqrt(jnp.sum(diag, axis=0, keepdims=True)))
    top, low = gram[:h], gram[h:]
    x1 = lower_inverse(a11 * size_col[0] * size_row[0])
    r12 = dot_f32(x1, a12 * size_col[0] * size_row[1])
    x2 = lower_inverse(a22 * size_col[1] * size_row[1] - dot_f32(r12, r12, FIRST_FIRST))
    factor_top = dot_f32(x1, top * size_col[0])
    schur = low[:, h:] * size_col[1] - dot_f32(r12, factor_top[:, h:], FIRST_FIRST)
    mixed = -dot_f32(x2, dot_f32(r12, x1, FIRST_FIRST))
    factor_low = dot_f32(x2, schur)
    lower = jnp.concatenate(
        [
            jnp.concatenate([x1 * size_row[0], jnp.zeros((h, h), jnp.float32)], axis=1),
            jnp.concatenate([mixed * size_row[0], x2 * size_row[1]], axis=1),
        ],
        axis=0,
    )
    inverse = (scale * lower).astype(jnp.bfloat16)
    load.wait()

    def project(i):
        both = jnp.concatenate([field_v[2 * i], field_v[2 * i + 1]], axis=1)
        made = jnp.dot(inverse, both, preferred_element_type=jnp.float32).astype(jnp.bfloat16)
        basis_v[2 * i] = made[:, :h]
        basis_v[2 * i + 1] = made[:, h:]

    down = lax.broadcasted_iota(jnp.int32, (RANK, DAYS), 0)
    across = lax.broadcasted_iota(jnp.int32, (RANK, DAYS), 1)
    factor = jnp.concatenate(
        [factor_top, jnp.concatenate([jnp.zeros((h, h), jnp.float32), factor_low], axis=1)], axis=0
    )
    factor = jnp.where(across >= down, factor, 0.0)
    ahead = jnp.where(across < DAYS - 1, pltpu.roll(factor, DAYS - 1, 1), 0.0)
    cross = dot_three(ahead, factor, LAST_LAST)
    polar = cross / jnp.sqrt(jnp.sum(cross * cross) + 1e-06)
    todo = list(range(rows_here // 2))
    share = -(-len(todo) // (ITERS - 1))
    store = pltpu.make_async_copy(basis_v, basis_ref, sems.at[1])
    for n in range(ITERS):
        square = dot_three(polar, polar, LAST_LAST)
        for i in todo[n * share : (n + 1) * share]:
            project(i)
        if n == ITERS - 2:
            store.start()
        polar = 1.5 * polar - 0.5 * dot_three(square, polar)
    prop_ref[...] = math.sqrt(RANK) * polar
    store.wait()


def solve(own, other, field, cell_total):
    rows_tm = field.shape[0]
    part = (rows_tm, RANK, LANES)
    whole = pl.BlockSpec(memory_space=pltpu.VMEM)
    own, other = (pltpu.with_memory_space_constraint(v, pltpu.VMEM) for v in (own, other))
    return pl.pallas_call(
        functools.partial(solve_kernel, math.sqrt(cell_total)),
        in_specs=[whole, whole, pl.BlockSpec(memory_space=pl.ANY)],
        out_specs=[pl.BlockSpec(memory_space=pl.ANY), whole],
        out_shape=[
            jax.ShapeDtypeStruct(part, jnp.bfloat16),
            jax.ShapeDtypeStruct((RANK, RANK), jnp.float32),
        ],
        scratch_shapes=[
            pltpu.VMEM((DAYS // LANES, RANK, LANES), jnp.float32),
            pltpu.VMEM(part, jnp.bfloat16),
            pltpu.VMEM(part, jnp.bfloat16),
            pltpu.SemaphoreType.DMA((2,)),
        ],
        compiler_params=pltpu.CompilerParams(vmem_limit_bytes=VMEM),
        name="factor_basis_and_polar",
    )(own, other, field)


def body(pixels, weights, tile_index, tile_row, granule_day):
    swath_rows = pixels.shape[0]
    width = pixels.shape[1]
    space_count = lax.axis_size("space")
    time_count = lax.axis_size("tm")
    dest_count = time_count * space_count
    rows_tm = GR_DEV // time_count
    slots = 2 * swath_rows // space_count // time_count
    axes = ("tm", "space")
    first, last = pack(pixels, weights, tile_index, tile_row, granule_day, time_count, space_count, rows_tm, slots)
    first = lax.all_to_all(first, axes, split_axis=0, concat_axis=0, tiled=True)
    last = lax.all_to_all(last, axes, split_axis=0, concat_axis=0, tiled=True)
    field, keep, give = grid_rows(first, last, time_count, space_count, rows_tm, slots)

    swap = [(t, t ^ 1) for t in range(time_count)]
    peers = [[t * space_count + s for t in range(core, time_count, 2) for s in range(space_count)] for core in (0, 1)]
    among = functools.partial(
        lax.all_to_all, axis_name=axes, split_axis=0, concat_axis=0, axis_index_groups=peers, tiled=True
    )
    pieces = (keep + lax.ppermute(give, "tm", swap)).reshape(dest_count // 2, -1, LANES)
    mine = jnp.sum(among(pieces), axis=0, keepdims=True)
    own = among(jnp.broadcast_to(mine, pieces.shape)).reshape(keep.shape)
    other = lax.ppermute(own, "tm", swap)
    cell_total = space_count * GR_DEV * width
    basis, propagator = solve(own, other, field, cell_total)
    return (field[None], basis[None], propagator)


def solution(mesh):
    placed = (
        P(("tm", "space"), None),
        P(("tm", "space")),
        P(("tm", "space")),
        P(("tm", "space")),
        P(("tm", "space")),
    )
    return jax.shard_map(
        body,
        mesh=mesh,
        in_specs=placed,
        out_specs=(P("space", "tm", None, None), P("space", "tm", None, None), P()),
        check_vma=False,
    )
```

```python
import functools
import math

import jax
import jax.numpy as jnp
from jax import lax
from jax.experimental import pallas as pl
from jax.experimental.pallas import tpu as pltpu
from jax.sharding import PartitionSpec as P

GR_DEV = 160
DAYS = 512
RANK = 256
ITERS = 8
LANES = 128
GROUP = 16
CLASH = 1 << 20
STEPS = 5
VMEM = 56 * 1024 * 1024

LAST_LAST = (((1,), (1,)), ((), ()))
FIRST_FIRST = (((0,), (0,)), ((), ()))


def round_up(value, unit):
    return -(-value // unit) * unit


def split_rows(slots):
    rows = round_up(slots, 16)
    return rows, rows * 13 // 20 // 16 * 16


def meta_layout(slots):
    pieces = round_up(slots, LANES) // LANES
    folded = 3 * pieces > 8 and 3 * pieces - 1 <= 8 and slots % LANES <= LANES // 2
    return (8 if folded else round_up(3 * pieces, 8)), folded


def pack_kernel(
    dims, tile_ref, row_ref, day_ref, weight_ref, pix_ref, first_ref, last_ref, pos_v, pos_s, rows_v, meta_v, pixf, outf, mrow,
    last_v, pix_v, hot_v, prefix_v, sems
):
    time_count, space_count, rows_tm, slot_rows, first_rows, width, (meta_rows, folded) = dims
    dest_count = time_count * space_count
    chunks = tile_ref.shape[0]
    pieces = width // LANES

    fetch = pltpu.make_async_copy(pix_ref, pix_v, sems.at[2])
    fetch.start()
    tile = tile_ref[...]
    row = row_ref[...]
    group = jnp.zeros_like(row)
    for k in range(1, time_count):
        group = group + jnp.where(row >= k * rows_tm, 1, 0)
    dest_all = group * space_count + tile
    rows_v[0] = dest_all.astype(jnp.float32)
    rows_v[2] = weight_ref[...].astype(jnp.float32)
    rows_v[3] = (row - group * rows_tm).astype(jnp.float32)
    rows_v[4] = day_ref[...].astype(jnp.float32)

    dest_iota = lax.broadcasted_iota(jnp.int32, (dest_count, LANES), 0)
    upper = jnp.where(
        lax.broadcasted_iota(jnp.int32, (LANES, LANES), 0) <= lax.broadcasted_iota(jnp.int32, (LANES, LANES), 1), 1.0, 0.0
    ).astype(jnp.bfloat16)
    for c in range(chunks):
        hot = dest_iota == dest_all[c : c + 1, :]
        hot_v[c * dest_count : (c + 1) * dest_count, :] = jnp.where(hot, 1.0, 0.0).astype(jnp.bfloat16)
    prefix_v[...] = jnp.dot(hot_v[...], upper, preferred_element_type=jnp.float32)
    carry = jnp.zeros((dest_count, 1), jnp.float32)
    for c in range(chunks):
        prefix = prefix_v[c * dest_count : (c + 1) * dest_count, :]
        hot = dest_iota == dest_all[c : c + 1, :]
        rows_v[1, c : c + 1, :] = jnp.sum(jnp.where(hot, prefix + carry, 0.0), axis=0, keepdims=True) - 1.0
        carry = carry + prefix[:, LANES - 1 : LANES]
    pos_v[...] = dest_all * slot_rows + rows_v[1].astype(jnp.int32)
    copy = pltpu.make_async_copy(pos_v, pos_s, sems.at[0])
    copy.start()
    meta_v[...] = jnp.zeros_like(meta_v)
    mrow[...] = jnp.zeros_like(mrow)

    def clear(b, _):
        outf[pl.ds(pl.multiple_of(b * slot_rows, 16), slot_rows), :] = jnp.zeros((slot_rows, LANES), jnp.float32)
        return 0

    lax.fori_loop(0, dest_count, clear, 0)
    fetch.wait()
    copy.wait()
    deep = 4
    both = deep * LANES
    dest_number = lax.broadcasted_iota(jnp.int32, (dest_count, both), 0).astype(jnp.float32)
    slot_number = lax.broadcasted_iota(jnp.int32, (width, both), 0).astype(jnp.float32)

    def move(c, _):
        base = pl.multiple_of(c * both, both)
        pixf[pl.ds(base, both), :] = pix_v[pl.ds(base, both), :].astype(jnp.float32)
        dest, rank, weight, local_row, day = (
            jnp.concatenate([rows_v[v, pl.ds(deep * c + i, 1), :] for i in range(deep)], axis=1) for v in range(5)
        )
        hot = dest_number == dest
        place = jnp.where(slot_number == rank, 1.0, 0.0).astype(jnp.bfloat16)
        values = jnp.concatenate([jnp.where(hot, v, 0.0) for v in (weight, local_row, day)], axis=0).astype(jnp.bfloat16)
        meta_v[...] += lax.dot_general(values, place, LAST_LAST, preferred_element_type=jnp.float32)
        for i in range(deep):
            for lane in range(LANES):
                outf[pl.ds(pos_s[deep * c + i, lane], 1), :] = pixf[pl.ds(base + i * LANES + lane, 1), :]
        return 0

    lax.fori_loop(0, chunks // deep, move, 0)
    whole = pieces - 1 if folded else pieces

    def lanes(v, i):
        return meta_v[v * dest_count : (v + 1) * dest_count, i * LANES : (i + 1) * LANES]

    def put(at, value):
        mrow[pl.ds(at, dest_count, stride=meta_rows), :] = value

    for v in range(3):
        for i in range(whole):
            put(v * whole + i, lanes(v, i))
    if folded:
        put(3 * whole, lanes(0, whole) + pltpu.roll(lanes(1, whole), LANES // 2, 1))
        put(3 * whole + 1, lanes(2, whole))

    together = 8

    def narrow(i, _):
        for q in range(together):
            b = i * together + q
            at = pl.multiple_of(b * slot_rows, 16)
            first_ref[b, :first_rows, :] = outf[pl.ds(at, first_rows), :].astype(jnp.bfloat16)
            first_ref[b, first_rows:, :] = mrow[pl.ds(pl.multiple_of(b * meta_rows, 8), meta_rows), :].astype(jnp.bfloat16)
            last_v[b] = outf[pl.ds(at + first_rows, slot_rows - first_rows), :].astype(jnp.bfloat16)
        some = pl.ds(i * together, together)
        pltpu.make_async_copy(last_v.at[some], last_ref.at[some], sems.at[1]).start()
        return 0

    lax.fori_loop(0, dest_count // together, narrow, 0)
    pltpu.make_async_copy(last_v, last_ref, sems.at[1]).wait()


def pack(pixels, weights, tile_index, tile_row, granule_day, time_count, space_count, rows_tm, slots):
    swath_rows = pixels.shape[0]
    chunks = swath_rows // LANES
    dest_count = time_count * space_count
    slot_rows, first_rows = split_rows(slots)
    width = round_up(slots, LANES)
    shape = (chunks, LANES)
    layout = meta_layout(slots)
    first_shape = (dest_count, first_rows + layout[0], LANES)
    last_shape = (dest_count, slot_rows - first_rows, LANES)
    return pl.pallas_call(
        functools.partial(pack_kernel, (time_count, space_count, rows_tm, slot_rows, first_rows, width, layout)),
        in_specs=[pl.BlockSpec(memory_space=pltpu.VMEM)] * 4 + [pl.BlockSpec(memory_space=pl.ANY)],
        out_specs=[pl.BlockSpec(memory_space=pltpu.VMEM), pl.BlockSpec(memory_space=pl.ANY)],
        out_shape=[pltpu.VMEM(first_shape, jnp.bfloat16), jax.ShapeDtypeStruct(last_shape, jnp.bfloat16)],
        scratch_shapes=[
            pltpu.VMEM(shape, jnp.int32),
            pltpu.SMEM(shape, jnp.int32),
            pltpu.VMEM((5,) + shape, jnp.float32),
            pltpu.VMEM((3 * dest_count, width), jnp.float32),
            pltpu.VMEM((swath_rows, LANES), jnp.float32),
            pltpu.VMEM((dest_count * slot_rows, LANES), jnp.float32),
            pltpu.VMEM((dest_count * layout[0], LANES), jnp.float32),
            pltpu.VMEM(last_shape, jnp.bfloat16),
            pltpu.VMEM((swath_rows, LANES), jnp.bfloat16),
            pltpu.VMEM((chunks * dest_count, LANES), jnp.bfloat16),
            pltpu.VMEM((chunks * dest_count, LANES), jnp.float32),
            pltpu.SemaphoreType.DMA((3,)),
        ],
        compiler_params=pltpu.CompilerParams(vmem_limit_bytes=VMEM),
        name="pack",
    )(
        tile_index.reshape(shape),
        tile_row.reshape(shape),
        granule_day.reshape(shape),
        weights.reshape(shape),
        pixels,
    )


def chunks_of(first_slot, rows):
    slot, found = first_slot, []
    while slot < first_slot + rows:
        size = min(32 - slot % 32, first_slot + rows - slot)
        found.append((slot, size))
        slot += size
    return found


def add_rows(total, pixf, code_s, code_row, first_slot, rows, pix_at, count):
    def add_group(row, lane, at):
        places = [code_s[row, lane + u] for u in range(GROUP)]
        made = [total[pl.ds(p, 1), :] + pixf[pl.ds(at + u, 1), :] for u, p in enumerate(places)]
        for p, value in zip(places, made):
            total[pl.ds(p, 1), :] = value

    def add_singly(row, lane, at):
        def one(u, _):
            p = code_s[row, lane + u]
            p = jnp.where(p >= CLASH, p - CLASH, p)
            total[pl.ds(p, 1), :] = total[pl.ds(p, 1), :] + pixf[pl.ds(at + u, 1), :]
            return 0

        lax.fori_loop(0, GROUP, one, 0)

    for slot, chunk in chunks_of(first_slot, rows):
        start = slot - first_slot
        row, lane = code_row(slot // LANES), slot % LANES
        at = pix_at + start
        heads = [code_s[row, lane + g] for g in range(0, chunk, GROUP)]
        clash = functools.reduce(jnp.maximum, heads) >= CLASH

        @pl.when((count > start) & jnp.logical_not(clash))
        def _():
            for g in range(0, chunk, GROUP):
                add_group(row, lane + g, at + g)

        @pl.when((count > start) & clash)
        def _():
            for g, head in zip(range(0, chunk, GROUP), heads):
                pl.when(head < CLASH)(functools.partial(add_group, row, lane + g, at + g))
                pl.when(head >= CLASH)(functools.partial(add_singly, row, lane + g, at + g))


def grid_first_kernel(
    dims, moved_ref, total_ref, code_ref, rest_ref, count_ref, column_ref, meta_v, pixf, code_s, count_s, sems
):
    time_count, space_count, rows_tm, slot_rows, first_rows, width, (meta_rows, folded) = dims
    day_dev = DAYS // time_count
    blocks = time_count * space_count
    pieces = width // LANES
    spare = rows_tm * DAYS

    meta_v[...] = moved_ref[:, first_rows:, :].astype(jnp.float32).reshape(blocks * meta_rows, LANES)
    whole = pieces - 1 if folded else pieces
    early = lax.broadcasted_iota(jnp.int32, (blocks, LANES), 1) < LANES // 2

    def lanes(v, i):
        if i < whole:
            return meta_v[pl.ds(v * whole + i, blocks, stride=meta_rows), :]
        tail = meta_v[pl.ds(3 * whole + v // 2, blocks, stride=meta_rows), :]
        return jnp.where(early, pltpu.roll(tail, LANES // 2, 1) if v == 1 else tail, 0.0)

    block = lax.broadcasted_iota(jnp.int32, (blocks, LANES), 0)
    offset = jnp.zeros((blocks, LANES), jnp.float32)
    for m in range(1, time_count):
        offset = offset + jnp.where(block >= m * space_count, float(day_dev), 0.0)
    within = lax.broadcasted_iota(jnp.int32, (blocks, LANES), 1) % GROUP
    count = jnp.zeros((blocks, 1), jnp.float32)
    for i in range(pieces):
        weight, local_row, day = (lanes(v, i) for v in range(3))
        used = weight > 0.0
        count = count + jnp.sum(jnp.where(used, 1.0, 0.0), axis=1, keepdims=True)
        column_ref[i * LANES : (i + 1) * LANES, :] = jnp.transpose(weight)
        code = jnp.where(used, local_row * DAYS + (day + offset), float(spare)).astype(jnp.int32)
        clash = jnp.zeros(code.shape, jnp.int32)
        for k in range(1, GROUP):
            ahead = pltpu.roll(code, LANES - k, 1)
            clash = jnp.where((ahead == code) & (within + k < GROUP) & (code < spare), 1, clash)
        k = 1
        while k < GROUP:
            ahead = pltpu.roll(clash, LANES - k, 1)
            clash = jnp.where(within + k < GROUP, jnp.maximum(clash, ahead), clash)
            k *= 2
        code_ref[i * blocks : (i + 1) * blocks, :] = jnp.where((within == 0) & (clash > 0), code + CLASH, code)
    rest_ref[...] = code_ref[first_rows // LANES * blocks :, :]
    count_ref[...] = jnp.broadcast_to(count, (blocks, LANES)).astype(jnp.int32)
    code_copy = pltpu.make_async_copy(code_ref, code_s, sems.at[0])
    count_copy = pltpu.make_async_copy(count_ref, count_s, sems.at[1])
    code_copy.start()
    count_copy.start()

    for b in range(blocks):
        column = column_ref[:first_rows, b : b + 1]
        pixf[b * first_rows : (b + 1) * first_rows, :] = moved_ref[b, :first_rows, :].astype(jnp.float32) * column

    def clear(i, _):
        total_ref[pl.ds(pl.multiple_of(i * DAYS, DAYS), DAYS), :] = jnp.zeros((DAYS, LANES), jnp.float32)
        return 0

    lax.fori_loop(0, rows_tm, clear, 0)
    total_ref[spare:, :] = jnp.zeros((8, LANES), jnp.float32)
    code_copy.wait()
    count_copy.wait()

    def add(b, _):
        add_rows(total_ref, pixf, code_s, lambda i: i * blocks + b, 0, first_rows, b * first_rows, count_s[b, 0])
        return 0

    lax.fori_loop(0, blocks, add, 0)


def grid_last_kernel(
    dims, code_s, count_s, column_ref, moved_ref, first_ref, field_ref, keep_ref, give_ref,
    total, first_v, moved_v, pixf, field_v, gram_v, first_sems, block_sems, out_sem
):
    time_count, space_count, rows_tm, slot_rows, first_rows, width, (meta_rows, folded) = dims
    blocks = time_count * space_count
    last_rows = slot_rows - first_rows
    group = rows_tm // STEPS
    skipped = first_rows // LANES

    def load(i):
        at = pl.ds(pl.multiple_of(i * group * DAYS, DAYS), group * DAYS)
        return pltpu.make_async_copy(first_ref.at[at], first_v.at[at], first_sems.at[i])

    def fetch(b):
        return pltpu.make_async_copy(moved_ref.at[b], moved_v.at[b], block_sems.at[b])

    for b in range(blocks):
        pl.when(count_s[b, 0] > first_rows)(fetch(b).start)
    for i in range(STEPS):
        load(i).start()

    def clear(i, _):
        total[pl.ds(pl.multiple_of(i * DAYS, DAYS), DAYS), :] = jnp.zeros((DAYS, LANES), jnp.float32)
        return 0

    lax.fori_loop(0, rows_tm, clear, 0)
    total[rows_tm * DAYS :, :] = jnp.zeros((8, LANES), jnp.float32)
    for b in range(blocks):

        @pl.when(count_s[b, 0] > first_rows)
        def _():
            fetch(b).wait()
            column = column_ref[first_rows:slot_rows, b : b + 1]
            pixf[b * last_rows : (b + 1) * last_rows, :] = moved_v[b].astype(jnp.float32) * column

    def add(b, _):
        rest = count_s[b, 0] - first_rows

        @pl.when(rest > 0)
        def _():
            add_rows(
                total, pixf, code_s, lambda i: (i - skipped) * blocks + b, first_rows, last_rows, b * last_rows, rest
            )

        return 0

    lax.fori_loop(0, blocks, add, 0)

    def send(i):
        at = pl.ds(i * group, group)
        return pltpu.make_async_copy(field_v.at[at], field_ref.at[at], out_sem)

    def settle(i):
        for q in range(i * group, (i + 1) * group):
            at = pl.ds(q * DAYS, DAYS)
            field_v[q] = (first_v[at, :] + total[at, :]).astype(jnp.bfloat16)

    def multiply(i):
        both = jnp.concatenate([field_v[q] for q in range(i * group, (i + 1) * group)], axis=1)
        part = lax.dot_general(both[:RANK], both, LAST_LAST, preferred_element_type=jnp.float32)
        for c in range(DAYS // LANES):
            here = part[:, c * LANES : (c + 1) * LANES]
            gram_v[c] = here if i == 0 else gram_v[c] + here

    for i in range(STEPS):
        load(i).wait()
        settle(i)
        if i > 0:
            send(i - 1).start()
            multiply(i - 1)
    send(STEPS - 1).start()
    multiply(STEPS - 1)
    odd = lax.axis_index("tm") % 2
    half = DAYS // LANES // 2
    for c in range(half):
        keep_ref[c] = gram_v[odd * half + c]
        give_ref[c] = gram_v[(1 - odd) * half + c]
    pltpu.make_async_copy(field_v, field_ref, out_sem).wait()


def grid_rows(moved_first, moved_last, time_count, space_count, rows_tm, slots):
    slot_rows, first_rows = split_rows(slots)
    last_rows = slot_rows - first_rows
    width = round_up(slots, LANES)
    blocks = time_count * space_count
    dims = (time_count, space_count, rows_tm, slot_rows, first_rows, width, meta_layout(slots))
    codes = (blocks * width // LANES, LANES)
    rest = (codes[0] - first_rows // LANES * blocks, LANES)
    counts = (blocks, LANES)
    columns = (width, blocks)
    sums = (rows_tm * DAYS + 8, LANES)
    half = (DAYS // LANES // 2, RANK, LANES)
    params = pltpu.CompilerParams(vmem_limit_bytes=VMEM)
    moved_first, moved_last = (pltpu.with_memory_space_constraint(v, pltpu.VMEM) for v in (moved_first, moved_last))
    total, _, rest_code, count, column = pl.pallas_call(
        functools.partial(grid_first_kernel, dims),
        out_shape=[
            jax.ShapeDtypeStruct(sums, jnp.float32),
            jax.ShapeDtypeStruct(codes, jnp.int32),
            jax.ShapeDtypeStruct(rest, jnp.int32),
            jax.ShapeDtypeStruct(counts, jnp.int32),
            jax.ShapeDtypeStruct(columns, jnp.float32),
        ],
        scratch_shapes=[
            pltpu.VMEM((blocks * meta_layout(slots)[0], LANES), jnp.float32),
            pltpu.VMEM((blocks * first_rows, LANES), jnp.float32),
            pltpu.SMEM(codes, jnp.int32),
            pltpu.SMEM(counts, jnp.int32),
            pltpu.SemaphoreType.DMA((2,)),
        ],
        compiler_params=params,
        cost_estimate=pl.CostEstimate(flops=0, bytes_accessed=60_000_000, transcendentals=0),
        name="grid_first",
    )(moved_first)
    whole = pl.BlockSpec(memory_space=pltpu.VMEM)
    return pl.pallas_call(
        functools.partial(grid_last_kernel, dims),
        in_specs=[
            pl.BlockSpec(memory_space=pltpu.SMEM),
            pl.BlockSpec(memory_space=pltpu.SMEM),
            whole,
            pl.BlockSpec(memory_space=pl.ANY),
            pl.BlockSpec(memory_space=pl.ANY),
        ],
        out_specs=[pl.BlockSpec(memory_space=pl.ANY), whole, whole],
        out_shape=[
            jax.ShapeDtypeStruct((rows_tm, DAYS, LANES), jnp.bfloat16),
            pltpu.VMEM(half, jnp.float32),
            pltpu.VMEM(half, jnp.float32),
        ],
        scratch_shapes=[
            pltpu.VMEM(sums, jnp.float32),
            pltpu.VMEM((rows_tm * DAYS, LANES), jnp.float32),
            pltpu.VMEM((blocks, last_rows, LANES), jnp.bfloat16),
            pltpu.VMEM((blocks * last_rows, LANES), jnp.float32),
            pltpu.VMEM((rows_tm, DAYS, LANES), jnp.bfloat16),
            pltpu.VMEM((DAYS // LANES, RANK, LANES), jnp.float32),
            pltpu.SemaphoreType.DMA((STEPS,)),
            pltpu.SemaphoreType.DMA((blocks,)),
            pltpu.SemaphoreType.DMA,
        ],
        compiler_params=params,
        name="grid_last_and_gram",
    )(rest_code, count, column, moved_last, total)


def bf16_parts(x, count):
    found = []
    for _ in range(count):
        found.append(x.astype(jnp.bfloat16))
        x = x - found[-1].astype(jnp.float32)
    return found


def dot_f32(a, b, dims=(((1,), (0,)), ((), ()))):
    return lax.dot_general(a, b, dims, precision=lax.Precision.HIGHEST, preferred_element_type=jnp.float32)


def dot_three(a_parts, b_parts):
    a_high, a_low = a_parts
    b_high, b_low = b_parts
    a_all = jnp.concatenate([a_high, a_high, a_low], axis=1)
    b_all = jnp.concatenate([b_high, b_low, b_high], axis=0)
    half = a_all.shape[0] // 2
    rows = [jnp.dot(part, b_all, preferred_element_type=jnp.float32) for part in (a_all[:half], a_all[half:])]
    return jnp.concatenate(rows, axis=0)


def lower_inverse(a):
    n = a.shape[0]
    full = (8, n)
    tiles = [a[8 * i : 8 * i + 8, :] for i in range(n // 8)]
    lane = lax.broadcasted_iota(jnp.int32, full, 1)
    down = lax.broadcasted_iota(jnp.int32, full, 0)
    out = []
    for t in range(n // 8):
        k = 8 * t
        block = (lane >= k) & (lane < k + 8)
        panel = tiles[t]
        cols = [jnp.broadcast_to(panel[:, k + c : k + c + 1], full) for c in range(8)]
        e = {(i, c): jnp.broadcast_to(cols[c][i : i + 1, :], full) for c in range(8) for i in range(c, 8)}
        start = jnp.where(block, jnp.where(lane == k + down, 1.0, 0.0), panel)
        rows = [jnp.broadcast_to(start[i : i + 1, :], full) for i in range(8)]
        held = []
        for s in range(0, 8, 2):
            p, q, r = e[s, s], e[s + 1, s], e[s + 1, s + 1]
            det = p * r - q * q
            inv = pl.reciprocal(det, approx=True)
            factors = {}
            for i in range(s + 2, 8):
                x, y = e[i, s], e[i, s + 1]
                factors[i] = (r * x - q * y, p * y - q * x)
            for i in range(s + 2, 8):
                u, v = factors[i]
                for c in range(s + 2, i + 1):
                    e[i, c] = e[i, c] - (u * e[c, s] + v * e[c, s + 1]) * inv
                rows[i] = rows[i] - (u * rows[s] + v * rows[s + 1]) * inv
            held.append((p, q, r, det, inv, factors))
        done = jnp.zeros(full, jnp.float32)
        solved = [None] * 8
        for s in (6, 4, 2, 0):
            p, q, r, det, inv, factors = held[s // 2]
            root = lax.rsqrt(p)
            done = jnp.where(down == s, rows[s] * root, done)
            done = jnp.where(down == s + 1, (rows[s + 1] * p - q * rows[s]) * (root * lax.rsqrt(det)), done)
            first, second = r * rows[s] - q * rows[s + 1], p * rows[s + 1] - q * rows[s]
            for i in range(7, s + 1, -1):
                u, v = factors[i]
                first, second = first - u * solved[i], second - v * solved[i]
            solved[s], solved[s + 1] = first * inv, second * inv
        out.append(jnp.where(lane < k + 8, done, 0.0))
        for i in range(t + 1, n // 8):
            terms = [jnp.broadcast_to(tiles[i][:, k + c : k + c + 1], full) * solved[c] for c in range(8)]
            while len(terms) > 1:
                terms = [terms[j] + terms[j + 1] for j in range(0, len(terms), 2)]
            tiles[i] = jnp.where(block, 0.0, tiles[i]) - terms[0]
    return jnp.concatenate(out, axis=0)


def solve_kernel(scale, own_ref, other_ref, field_ref, basis_ref, prop_ref, gram_v, field_v, basis_v, sems):
    h = LANES
    pieces = DAYS // h
    rows_here = field_v.shape[0]
    load = pltpu.make_async_copy(field_ref.at[:, pl.ds(0, RANK), :], field_v, sems.at[0])
    load.start()
    odd = lax.axis_index("tm") % 2
    for c in range(pieces // 2):
        gram_v[odd * (pieces // 2) + c] = own_ref[c]
        gram_v[(1 - odd) * (pieces // 2) + c] = other_ref[c]

    gram = jnp.concatenate([gram_v[i] for i in range(pieces)], axis=1)
    eye = lax.broadcasted_iota(jnp.int32, (h, h), 0) == lax.broadcasted_iota(jnp.int32, (h, h), 1)
    a11, a12, a22 = gram_v[0, :h, :], gram_v[1, :h, :], gram_v[1, h:, :]
    size_col, size_row = [], []
    for part in (a11, a22):
        diag = jnp.where(eye, part, 0.0)
        size_col.append(lax.rsqrt(jnp.sum(diag, axis=1, keepdims=True)))
        size_row.append(lax.rsqrt(jnp.sum(diag, axis=0, keepdims=True)))
    top, low = gram[:h], gram[h:]
    x1 = lower_inverse(a11 * size_col[0] * size_row[0])
    r12 = dot_f32(x1, a12 * size_col[0] * size_row[1])
    x2 = lower_inverse(a22 * size_col[1] * size_row[1] - dot_f32(r12, r12, FIRST_FIRST))
    factor_top = dot_f32(x1, top * size_col[0])
    schur = low[:, h:] * size_col[1] - dot_f32(r12, factor_top[:, h:], FIRST_FIRST)
    mixed = -dot_f32(x2, dot_f32(r12, x1, FIRST_FIRST))
    factor_low = dot_f32(x2, schur)
    lower = jnp.concatenate(
        [
            jnp.concatenate([x1 * size_row[0], jnp.zeros((h, h), jnp.float32)], axis=1),
            jnp.concatenate([mixed * size_row[0], x2 * size_row[1]], axis=1),
        ],
        axis=0,
    )
    inverse = (scale * lower).astype(jnp.bfloat16)
    load.wait()

    def project(i):
        both = jnp.concatenate([field_v[2 * i], field_v[2 * i + 1]], axis=1)
        made = jnp.dot(inverse, both, preferred_element_type=jnp.float32).astype(jnp.bfloat16)
        basis_v[2 * i] = made[:, :h]
        basis_v[2 * i + 1] = made[:, h:]

    down = lax.broadcasted_iota(jnp.int32, (RANK, DAYS), 0)
    across = lax.broadcasted_iota(jnp.int32, (RANK, DAYS), 1)
    factor = jnp.concatenate(
        [factor_top, jnp.concatenate([jnp.zeros((h, h), jnp.float32), factor_low], axis=1)], axis=0
    )
    factor = jnp.where(across >= down, factor, 0.0)
    ahead = jnp.where(across < DAYS - 1, pltpu.roll(factor, DAYS - 1, 1), 0.0)
    cross = dot_three(bf16_parts(ahead, 2), [part.T for part in bf16_parts(factor, 2)])
    polar = cross * lax.rsqrt(jnp.sum(cross * cross) + 1e-06)
    todo = list(range(rows_here // 2))
    share = -(-len(todo) // (ITERS - 1))
    store = pltpu.make_async_copy(basis_v, basis_ref, sems.at[1])
    for n in range(ITERS):
        parts = bf16_parts(polar, 2)
        square = dot_three(parts, [part.T for part in parts])
        for i in todo[n * share : (n + 1) * share]:
            project(i)
        if n == ITERS - 2:
            store.start()
        polar = 1.5 * polar - 0.5 * dot_three(bf16_parts(square, 2), parts)
    prop_ref[...] = math.sqrt(RANK) * polar
    store.wait()


def solve(own, other, field, cell_total):
    rows_tm = field.shape[0]
    part = (rows_tm, RANK, LANES)
    whole = pl.BlockSpec(memory_space=pltpu.VMEM)
    own, other = (pltpu.with_memory_space_constraint(v, pltpu.VMEM) for v in (own, other))
    return pl.pallas_call(
        functools.partial(solve_kernel, math.sqrt(cell_total)),
        in_specs=[whole, whole, pl.BlockSpec(memory_space=pl.ANY)],
        out_specs=[pl.BlockSpec(memory_space=pl.ANY), whole],
        out_shape=[
            jax.ShapeDtypeStruct(part, jnp.bfloat16),
            jax.ShapeDtypeStruct((RANK, RANK), jnp.float32),
        ],
        scratch_shapes=[
            pltpu.VMEM((DAYS // LANES, RANK, LANES), jnp.float32),
            pltpu.VMEM(part, jnp.bfloat16),
            pltpu.VMEM(part, jnp.bfloat16),
            pltpu.SemaphoreType.DMA((2,)),
        ],
        compiler_params=pltpu.CompilerParams(vmem_limit_bytes=VMEM),
        name="factor_basis_and_polar",
    )(own, other, field)


def body(pixels, weights, tile_index, tile_row, granule_day):
    swath_rows = pixels.shape[0]
    width = pixels.shape[1]
    space_count = lax.axis_size("space")
    time_count = lax.axis_size("tm")
    dest_count = time_count * space_count
    rows_tm = GR_DEV // time_count
    slots = 2 * swath_rows // space_count // time_count
    axes = ("tm", "space")
    first, last = pack(pixels, weights, tile_index, tile_row, granule_day, time_count, space_count, rows_tm, slots)
    first = lax.all_to_all(first, axes, split_axis=0, concat_axis=0, tiled=True)
    last = lax.all_to_all(last, axes, split_axis=0, concat_axis=0, tiled=True)
    field, keep, give = grid_rows(first, last, time_count, space_count, rows_tm, slots)

    swap = [(t, t ^ 1) for t in range(time_count)]
    peers = [[t * space_count + s for t in range(core, time_count, 2) for s in range(space_count)] for core in (0, 1)]
    among = functools.partial(
        lax.all_to_all, axis_name=axes, split_axis=0, concat_axis=0, axis_index_groups=peers, tiled=True
    )
    pieces = (keep + lax.ppermute(give, "tm", swap)).reshape(dest_count // 2, -1, LANES)
    mine = jnp.sum(among(pieces), axis=0, keepdims=True)
    own = among(jnp.broadcast_to(mine, pieces.shape)).reshape(keep.shape)
    other = lax.ppermute(own, "tm", swap)
    cell_total = space_count * GR_DEV * width
    basis, propagator = solve(own, other, field, cell_total)
    return (field[None], basis[None], propagator)


def solution(mesh):
    placed = (
        P(("tm", "space"), None),
        P(("tm", "space")),
        P(("tm", "space")),
        P(("tm", "space")),
        P(("tm", "space")),
    )
    return jax.shard_map(
        body,
        mesh=mesh,
        in_specs=placed,
        out_specs=(P("space", "tm", None, None), P("space", "tm", None, None), P()),
        check_vma=False,
    )
```

```python
import functools
import math

import jax
import jax.numpy as jnp
from jax import lax
from jax.experimental import pallas as pl
from jax.experimental.pallas import tpu as pltpu
from jax.sharding import PartitionSpec as P

GR_DEV = 160
DAYS = 512
RANK = 256
ITERS = 8
LANES = 128
GROUP = 16
CLASH = 1 << 20
STEPS = 5
VMEM = 56 * 1024 * 1024

LAST_LAST = (((1,), (1,)), ((), ()))
FIRST_FIRST = (((0,), (0,)), ((), ()))


def round_up(value, unit):
    return -(-value // unit) * unit


def split_rows(slots):
    rows = round_up(slots, 16)
    return rows, rows * 13 // 20 // 16 * 16


def meta_layout(slots):
    pieces = round_up(slots, LANES) // LANES
    folded = 3 * pieces > 8 and 3 * pieces - 1 <= 8 and slots % LANES <= LANES // 2
    return (8 if folded else round_up(3 * pieces, 8)), folded


def pack_kernel(
    dims, tile_ref, row_ref, day_ref, weight_ref, pix_ref, first_ref, last_ref, pos_v, pos_s, rows_v, meta_v, pixf, outf, mrow,
    pix_v, hot_v, prefix_v, sems
):
    time_count, space_count, rows_tm, slot_rows, first_rows, width, (meta_rows, folded) = dims
    dest_count = time_count * space_count
    chunks = tile_ref.shape[0]
    pieces = width // LANES

    fetch = pltpu.make_async_copy(pix_ref, pix_v, sems.at[1])
    fetch.start()
    tile = tile_ref[...]
    row = row_ref[...]
    group = jnp.zeros_like(row)
    for k in range(1, time_count):
        group = group + jnp.where(row >= k * rows_tm, 1, 0)
    dest_all = group * space_count + tile
    rows_v[0] = dest_all.astype(jnp.float32)
    rows_v[2] = weight_ref[...].astype(jnp.float32)
    rows_v[3] = (row - group * rows_tm).astype(jnp.float32)
    rows_v[4] = day_ref[...].astype(jnp.float32)

    dest_iota = lax.broadcasted_iota(jnp.int32, (dest_count, LANES), 0)
    upper = jnp.where(
        lax.broadcasted_iota(jnp.int32, (LANES, LANES), 0) <= lax.broadcasted_iota(jnp.int32, (LANES, LANES), 1), 1.0, 0.0
    ).astype(jnp.bfloat16)
    for c in range(chunks):
        hot = dest_iota == dest_all[c : c + 1, :]
        hot_v[c * dest_count : (c + 1) * dest_count, :] = jnp.where(hot, 1.0, 0.0).astype(jnp.bfloat16)
    prefix_v[...] = jnp.dot(hot_v[...], upper, preferred_element_type=jnp.float32)
    carry = jnp.zeros((dest_count, 1), jnp.float32)
    for c in range(chunks):
        prefix = prefix_v[c * dest_count : (c + 1) * dest_count, :]
        hot = dest_iota == dest_all[c : c + 1, :]
        rows_v[1, c : c + 1, :] = jnp.sum(jnp.where(hot, prefix + carry, 0.0), axis=0, keepdims=True) - 1.0
        carry = carry + prefix[:, LANES - 1 : LANES]
    pos_v[...] = dest_all * slot_rows + rows_v[1].astype(jnp.int32)
    copy = pltpu.make_async_copy(pos_v, pos_s, sems.at[0])
    copy.start()
    meta_v[...] = jnp.zeros_like(meta_v)
    mrow[...] = jnp.zeros_like(mrow)

    def clear(b, _):
        outf[pl.ds(pl.multiple_of(b * slot_rows, 16), slot_rows), :] = jnp.zeros((slot_rows, LANES), jnp.float32)
        return 0

    lax.fori_loop(0, dest_count, clear, 0)
    fetch.wait()
    copy.wait()
    deep = 4
    both = deep * LANES
    dest_number = lax.broadcasted_iota(jnp.int32, (dest_count, both), 0).astype(jnp.float32)
    slot_number = lax.broadcasted_iota(jnp.int32, (width, both), 0).astype(jnp.float32)

    def move(c, _):
        base = pl.multiple_of(c * both, both)
        pixf[pl.ds(base, both), :] = pix_v[pl.ds(base, both), :].astype(jnp.float32)
        dest, rank, weight, local_row, day = (
            jnp.concatenate([rows_v[v, pl.ds(deep * c + i, 1), :] for i in range(deep)], axis=1) for v in range(5)
        )
        hot = dest_number == dest
        place = jnp.where(slot_number == rank, 1.0, 0.0).astype(jnp.bfloat16)
        values = jnp.concatenate([jnp.where(hot, v, 0.0) for v in (weight, local_row, day)], axis=0).astype(jnp.bfloat16)
        meta_v[...] += lax.dot_general(values, place, LAST_LAST, preferred_element_type=jnp.float32)
        for i in range(deep):
            for lane in range(LANES):
                outf[pl.ds(pos_s[deep * c + i, lane], 1), :] = pixf[pl.ds(base + i * LANES + lane, 1), :]
        return 0

    lax.fori_loop(0, chunks // deep, move, 0)
    whole = pieces - 1 if folded else pieces

    def lanes(v, i):
        return meta_v[v * dest_count : (v + 1) * dest_count, i * LANES : (i + 1) * LANES]

    def put(at, value):
        mrow[pl.ds(at, dest_count, stride=meta_rows), :] = value

    for v in range(3):
        for i in range(whole):
            put(v * whole + i, lanes(v, i))
    if folded:
        put(3 * whole, lanes(0, whole) + pltpu.roll(lanes(1, whole), LANES // 2, 1))
        put(3 * whole + 1, lanes(2, whole))

    together = 8

    def narrow(i, _):
        for q in range(together):
            b = i * together + q
            at = pl.multiple_of(b * slot_rows, 16)
            first_ref[b, :first_rows, :] = outf[pl.ds(at, first_rows), :].astype(jnp.bfloat16)
            first_ref[b, first_rows:, :] = mrow[pl.ds(pl.multiple_of(b * meta_rows, 8), meta_rows), :].astype(jnp.bfloat16)
            last_ref[b] = outf[pl.ds(at + first_rows, slot_rows - first_rows), :].astype(jnp.bfloat16)
        return 0

    lax.fori_loop(0, dest_count // together, narrow, 0)


def pack(pixels, weights, tile_index, tile_row, granule_day, time_count, space_count, rows_tm, slots):
    swath_rows = pixels.shape[0]
    chunks = swath_rows // LANES
    dest_count = time_count * space_count
    slot_rows, first_rows = split_rows(slots)
    width = round_up(slots, LANES)
    shape = (chunks, LANES)
    layout = meta_layout(slots)
    first_shape = (dest_count, first_rows + layout[0], LANES)
    last_shape = (dest_count, slot_rows - first_rows, LANES)
    return pl.pallas_call(
        functools.partial(pack_kernel, (time_count, space_count, rows_tm, slot_rows, first_rows, width, layout)),
        in_specs=[pl.BlockSpec(memory_space=pltpu.VMEM)] * 4 + [pl.BlockSpec(memory_space=pl.ANY)],
        out_specs=[pl.BlockSpec(memory_space=pltpu.VMEM)] * 2,
        out_shape=[pltpu.VMEM(first_shape, jnp.bfloat16), pltpu.VMEM(last_shape, jnp.bfloat16)],
        scratch_shapes=[
            pltpu.VMEM(shape, jnp.int32),
            pltpu.SMEM(shape, jnp.int32),
            pltpu.VMEM((5,) + shape, jnp.float32),
            pltpu.VMEM((3 * dest_count, width), jnp.float32),
            pltpu.VMEM((swath_rows, LANES), jnp.float32),
            pltpu.VMEM((dest_count * slot_rows, LANES), jnp.float32),
            pltpu.VMEM((dest_count * layout[0], LANES), jnp.float32),
            pltpu.VMEM((swath_rows, LANES), jnp.bfloat16),
            pltpu.VMEM((chunks * dest_count, LANES), jnp.bfloat16),
            pltpu.VMEM((chunks * dest_count, LANES), jnp.float32),
            pltpu.SemaphoreType.DMA((2,)),
        ],
        compiler_params=pltpu.CompilerParams(vmem_limit_bytes=VMEM),
        name="pack",
    )(
        tile_index.reshape(shape),
        tile_row.reshape(shape),
        granule_day.reshape(shape),
        weights.reshape(shape),
        pixels,
    )


def chunks_of(first_slot, rows):
    slot, found = first_slot, []
    while slot < first_slot + rows:
        size = min(32 - slot % 32, first_slot + rows - slot)
        found.append((slot, size))
        slot += size
    return found


def add_rows(total, pixf, code_s, code_row, first_slot, rows, pix_at, count):
    def add_group(row, lane, at):
        places = [code_s[row, lane + u] for u in range(GROUP)]
        made = [total[pl.ds(p, 1), :] + pixf[pl.ds(at + u, 1), :] for u, p in enumerate(places)]
        for p, value in zip(places, made):
            total[pl.ds(p, 1), :] = value

    def add_singly(row, lane, at):
        def one(u, _):
            p = code_s[row, lane + u]
            p = jnp.where(p >= CLASH, p - CLASH, p)
            total[pl.ds(p, 1), :] = total[pl.ds(p, 1), :] + pixf[pl.ds(at + u, 1), :]
            return 0

        lax.fori_loop(0, GROUP, one, 0)

    for slot, chunk in chunks_of(first_slot, rows):
        start = slot - first_slot
        row, lane = code_row(slot // LANES), slot % LANES
        at = pix_at + start
        heads = [code_s[row, lane + g] for g in range(0, chunk, GROUP)]
        clash = functools.reduce(jnp.maximum, heads) >= CLASH

        @pl.when((count > start) & jnp.logical_not(clash))
        def _():
            for g in range(0, chunk, GROUP):
                add_group(row, lane + g, at + g)

        @pl.when((count > start) & clash)
        def _():
            for g, head in zip(range(0, chunk, GROUP), heads):
                pl.when(head < CLASH)(functools.partial(add_group, row, lane + g, at + g))
                pl.when(head >= CLASH)(functools.partial(add_singly, row, lane + g, at + g))


def grid_first_kernel(
    dims, moved_ref, total_ref, code_ref, rest_ref, count_ref, column_ref, meta_v, pixf, code_s, count_s, sems
):
    time_count, space_count, rows_tm, slot_rows, first_rows, width, (meta_rows, folded) = dims
    day_dev = DAYS // time_count
    blocks = time_count * space_count
    pieces = width // LANES
    spare = rows_tm * DAYS

    meta_v[...] = moved_ref[:, first_rows:, :].astype(jnp.float32).reshape(blocks * meta_rows, LANES)
    whole = pieces - 1 if folded else pieces
    early = lax.broadcasted_iota(jnp.int32, (blocks, LANES), 1) < LANES // 2

    def lanes(v, i):
        if i < whole:
            return meta_v[pl.ds(v * whole + i, blocks, stride=meta_rows), :]
        tail = meta_v[pl.ds(3 * whole + v // 2, blocks, stride=meta_rows), :]
        return jnp.where(early, pltpu.roll(tail, LANES // 2, 1) if v == 1 else tail, 0.0)

    block = lax.broadcasted_iota(jnp.int32, (blocks, LANES), 0)
    offset = jnp.zeros((blocks, LANES), jnp.float32)
    for m in range(1, time_count):
        offset = offset + jnp.where(block >= m * space_count, float(day_dev), 0.0)
    within = lax.broadcasted_iota(jnp.int32, (blocks, LANES), 1) % GROUP
    count = jnp.zeros((blocks, 1), jnp.float32)
    for i in range(pieces):
        weight, local_row, day = (lanes(v, i) for v in range(3))
        used = weight > 0.0
        count = count + jnp.sum(jnp.where(used, 1.0, 0.0), axis=1, keepdims=True)
        column_ref[i * LANES : (i + 1) * LANES, :] = jnp.transpose(weight)
        code = jnp.where(used, local_row * DAYS + (day + offset), float(spare)).astype(jnp.int32)
        clash = jnp.zeros(code.shape, jnp.int32)
        for k in range(1, GROUP):
            ahead = pltpu.roll(code, LANES - k, 1)
            clash = jnp.where((ahead == code) & (within + k < GROUP) & (code < spare), 1, clash)
        k = 1
        while k < GROUP:
            ahead = pltpu.roll(clash, LANES - k, 1)
            clash = jnp.where(within + k < GROUP, jnp.maximum(clash, ahead), clash)
            k *= 2
        code_ref[i * blocks : (i + 1) * blocks, :] = jnp.where((within == 0) & (clash > 0), code + CLASH, code)
    rest_ref[...] = code_ref[first_rows // LANES * blocks :, :]
    count_ref[...] = jnp.broadcast_to(count, (blocks, LANES)).astype(jnp.int32)
    code_copy = pltpu.make_async_copy(code_ref, code_s, sems.at[0])
    count_copy = pltpu.make_async_copy(count_ref, count_s, sems.at[1])
    code_copy.start()
    count_copy.start()

    for b in range(blocks):
        column = column_ref[:first_rows, b : b + 1]
        pixf[b * first_rows : (b + 1) * first_rows, :] = moved_ref[b, :first_rows, :].astype(jnp.float32) * column

    def clear(i, _):
        total_ref[pl.ds(pl.multiple_of(i * DAYS, DAYS), DAYS), :] = jnp.zeros((DAYS, LANES), jnp.float32)
        return 0

    lax.fori_loop(0, rows_tm, clear, 0)
    total_ref[spare:, :] = jnp.zeros((8, LANES), jnp.float32)
    code_copy.wait()
    count_copy.wait()

    def add(b, _):
        add_rows(total_ref, pixf, code_s, lambda i: i * blocks + b, 0, first_rows, b * first_rows, count_s[b, 0])
        return 0

    lax.fori_loop(0, blocks, add, 0)


def grid_last_kernel(
    dims, code_s, count_s, column_ref, moved_ref, first_ref, field_ref, keep_ref, give_ref,
    total, first_v, moved_v, pixf, field_v, gram_v, first_sems, block_sems, out_sem
):
    time_count, space_count, rows_tm, slot_rows, first_rows, width, (meta_rows, folded) = dims
    blocks = time_count * space_count
    last_rows = slot_rows - first_rows
    group = rows_tm // STEPS
    skipped = first_rows // LANES

    def load(i):
        at = pl.ds(pl.multiple_of(i * group * DAYS, DAYS), group * DAYS)
        return pltpu.make_async_copy(first_ref.at[at], first_v.at[at], first_sems.at[i])

    def fetch(b):
        return pltpu.make_async_copy(moved_ref.at[b], moved_v.at[b], block_sems.at[b])

    for b in range(blocks):
        pl.when(count_s[b, 0] > first_rows)(fetch(b).start)
    for i in range(STEPS):
        load(i).start()

    def clear(i, _):
        total[pl.ds(pl.multiple_of(i * DAYS, DAYS), DAYS), :] = jnp.zeros((DAYS, LANES), jnp.float32)
        return 0

    lax.fori_loop(0, rows_tm, clear, 0)
    total[rows_tm * DAYS :, :] = jnp.zeros((8, LANES), jnp.float32)
    for b in range(blocks):
        pl.when(count_s[b, 0] > first_rows)(fetch(b).wait)
    for b in range(blocks):
        column = column_ref[first_rows:slot_rows, b : b + 1]
        pixf[b * last_rows : (b + 1) * last_rows, :] = moved_v[b].astype(jnp.float32) * column

    def add(b, _):
        rest = count_s[b, 0] - first_rows

        @pl.when(rest > 0)
        def _():
            add_rows(
                total, pixf, code_s, lambda i: (i - skipped) * blocks + b, first_rows, last_rows, b * last_rows, rest
            )

        return 0

    lax.fori_loop(0, blocks, add, 0)

    def send(i):
        at = pl.ds(i * group, group)
        return pltpu.make_async_copy(field_v.at[at], field_ref.at[at], out_sem)

    def settle(i):
        for q in range(i * group, (i + 1) * group):
            at = pl.ds(q * DAYS, DAYS)
            field_v[q] = (first_v[at, :] + total[at, :]).astype(jnp.bfloat16)

    def multiply(i):
        both = jnp.concatenate([field_v[q] for q in range(i * group, (i + 1) * group)], axis=1)
        part = lax.dot_general(both[:RANK], both, LAST_LAST, preferred_element_type=jnp.float32)
        for c in range(DAYS // LANES):
            here = part[:, c * LANES : (c + 1) * LANES]
            gram_v[c] = here if i == 0 else gram_v[c] + here

    for i in range(STEPS):
        load(i).wait()
        settle(i)
        if i > 0:
            send(i - 1).start()
            multiply(i - 1)
    send(STEPS - 1).start()
    multiply(STEPS - 1)
    odd = lax.axis_index("tm") % 2
    half = DAYS // LANES // 2
    for c in range(half):
        keep_ref[c] = gram_v[odd * half + c]
        give_ref[c] = gram_v[(1 - odd) * half + c]
    pltpu.make_async_copy(field_v, field_ref, out_sem).wait()


def grid_rows(moved_first, moved_last, time_count, space_count, rows_tm, slots):
    slot_rows, first_rows = split_rows(slots)
    last_rows = slot_rows - first_rows
    width = round_up(slots, LANES)
    blocks = time_count * space_count
    dims = (time_count, space_count, rows_tm, slot_rows, first_rows, width, meta_layout(slots))
    codes = (blocks * width // LANES, LANES)
    rest = (codes[0] - first_rows // LANES * blocks, LANES)
    counts = (blocks, LANES)
    columns = (width, blocks)
    sums = (rows_tm * DAYS + 8, LANES)
    half = (DAYS // LANES // 2, RANK, LANES)
    params = pltpu.CompilerParams(vmem_limit_bytes=VMEM)
    moved_first, moved_last = (pltpu.with_memory_space_constraint(v, pltpu.VMEM) for v in (moved_first, moved_last))
    total, _, rest_code, count, column = pl.pallas_call(
        functools.partial(grid_first_kernel, dims),
        out_shape=[
            jax.ShapeDtypeStruct(sums, jnp.float32),
            jax.ShapeDtypeStruct(codes, jnp.int32),
            jax.ShapeDtypeStruct(rest, jnp.int32),
            jax.ShapeDtypeStruct(counts, jnp.int32),
            jax.ShapeDtypeStruct(columns, jnp.float32),
        ],
        scratch_shapes=[
            pltpu.VMEM((blocks * meta_layout(slots)[0], LANES), jnp.float32),
            pltpu.VMEM((blocks * first_rows, LANES), jnp.float32),
            pltpu.SMEM(codes, jnp.int32),
            pltpu.SMEM(counts, jnp.int32),
            pltpu.SemaphoreType.DMA((2,)),
        ],
        compiler_params=params,
        cost_estimate=pl.CostEstimate(flops=0, bytes_accessed=60_000_000, transcendentals=0),
        name="grid_first",
    )(moved_first)
    whole = pl.BlockSpec(memory_space=pltpu.VMEM)
    return pl.pallas_call(
        functools.partial(grid_last_kernel, dims),
        in_specs=[
            pl.BlockSpec(memory_space=pltpu.SMEM),
            pl.BlockSpec(memory_space=pltpu.SMEM),
            whole,
            pl.BlockSpec(memory_space=pl.ANY),
            pl.BlockSpec(memory_space=pl.ANY),
        ],
        out_specs=[pl.BlockSpec(memory_space=pl.ANY), whole, whole],
        out_shape=[
            jax.ShapeDtypeStruct((rows_tm, DAYS, LANES), jnp.bfloat16),
            pltpu.VMEM(half, jnp.float32),
            pltpu.VMEM(half, jnp.float32),
        ],
        scratch_shapes=[
            pltpu.VMEM(sums, jnp.float32),
            pltpu.VMEM((rows_tm * DAYS, LANES), jnp.float32),
            pltpu.VMEM((blocks, last_rows, LANES), jnp.bfloat16),
            pltpu.VMEM((blocks * last_rows, LANES), jnp.float32),
            pltpu.VMEM((rows_tm, DAYS, LANES), jnp.bfloat16),
            pltpu.VMEM((DAYS // LANES, RANK, LANES), jnp.float32),
            pltpu.SemaphoreType.DMA((STEPS,)),
            pltpu.SemaphoreType.DMA((blocks,)),
            pltpu.SemaphoreType.DMA,
        ],
        compiler_params=params,
        name="grid_last_and_gram",
    )(rest_code, count, column, moved_last, total)


def bf16_parts(x, count):
    found = []
    for _ in range(count):
        found.append(x.astype(jnp.bfloat16))
        x = x - found[-1].astype(jnp.float32)
    return found


def dot_f32(a, b, dims=(((1,), (0,)), ((), ()))):
    return lax.dot_general(a, b, dims, precision=lax.Precision.HIGHEST, preferred_element_type=jnp.float32)


def dot_three(a_parts, b_parts):
    a_high, a_low = a_parts
    b_high, b_low = b_parts
    a_all = jnp.concatenate([a_high, a_high, a_low], axis=1)
    b_all = jnp.concatenate([b_high, b_low, b_high], axis=0)
    half = a_all.shape[0] // 2
    rows = [jnp.dot(part, b_all, preferred_element_type=jnp.float32) for part in (a_all[:half], a_all[half:])]
    return jnp.concatenate(rows, axis=0)


def lower_inverse(a):
    n = a.shape[0]
    full = (8, n)
    tiles = [a[8 * i : 8 * i + 8, :] for i in range(n // 8)]
    lane = lax.broadcasted_iota(jnp.int32, full, 1)
    down = lax.broadcasted_iota(jnp.int32, full, 0)
    out = []
    for t in range(n // 8):
        k = 8 * t
        block = (lane >= k) & (lane < k + 8)
        panel = tiles[t]
        cols = [jnp.broadcast_to(panel[:, k + c : k + c + 1], full) for c in range(8)]
        e = {(i, c): jnp.broadcast_to(cols[c][i : i + 1, :], full) for c in range(8) for i in range(c, 8)}
        start = jnp.where(block, jnp.where(lane == k + down, 1.0, 0.0), panel)
        rows = [jnp.broadcast_to(start[i : i + 1, :], full) for i in range(8)]
        held = []
        for s in range(0, 8, 2):
            p, q, r = e[s, s], e[s + 1, s], e[s + 1, s + 1]
            det = p * r - q * q
            inv = pl.reciprocal(det, approx=True)
            factors = {}
            for i in range(s + 2, 8):
                x, y = e[i, s], e[i, s + 1]
                factors[i] = (r * x - q * y, p * y - q * x)
            for i in range(s + 2, 8):
                u, v = factors[i]
                for c in range(s + 2, i + 1):
                    e[i, c] = e[i, c] - (u * e[c, s] + v * e[c, s + 1]) * inv
                rows[i] = rows[i] - (u * rows[s] + v * rows[s + 1]) * inv
            held.append((p, q, r, det, inv, factors))
        done = jnp.zeros(full, jnp.float32)
        solved = [None] * 8
        for s in (6, 4, 2, 0):
            p, q, r, det, inv, factors = held[s // 2]
            root = lax.rsqrt(p)
            done = jnp.where(down == s, rows[s] * root, done)
            done = jnp.where(down == s + 1, (rows[s + 1] * p - q * rows[s]) * (root * lax.rsqrt(det)), done)
            first, second = r * rows[s] - q * rows[s + 1], p * rows[s + 1] - q * rows[s]
            for i in range(7, s + 1, -1):
                u, v = factors[i]
                first, second = first - u * solved[i], second - v * solved[i]
            solved[s], solved[s + 1] = first * inv, second * inv
        out.append(jnp.where(lane < k + 8, done, 0.0))
        for i in range(t + 1, n // 8):
            terms = [jnp.broadcast_to(tiles[i][:, k + c : k + c + 1], full) * solved[c] for c in range(8)]
            while len(terms) > 1:
                terms = [terms[j] + terms[j + 1] for j in range(0, len(terms), 2)]
            tiles[i] = jnp.where(block, 0.0, tiles[i]) - terms[0]
    return jnp.concatenate(out, axis=0)


def solve_kernel(scale, own_ref, other_ref, field_ref, basis_ref, prop_ref, gram_v, field_v, basis_v, sems):
    h = LANES
    pieces = DAYS // h
    rows_here = field_v.shape[0]
    load = pltpu.make_async_copy(field_ref.at[:, pl.ds(0, RANK), :], field_v, sems.at[0])
    load.start()
    odd = lax.axis_index("tm") % 2
    for c in range(pieces // 2):
        gram_v[odd * (pieces // 2) + c] = own_ref[c]
        gram_v[(1 - odd) * (pieces // 2) + c] = other_ref[c]

    gram = jnp.concatenate([gram_v[i] for i in range(pieces)], axis=1)
    eye = lax.broadcasted_iota(jnp.int32, (h, h), 0) == lax.broadcasted_iota(jnp.int32, (h, h), 1)
    a11, a12, a22 = gram_v[0, :h, :], gram_v[1, :h, :], gram_v[1, h:, :]
    size_col, size_row = [], []
    for part in (a11, a22):
        diag = jnp.where(eye, part, 0.0)
        size_col.append(lax.rsqrt(jnp.sum(diag, axis=1, keepdims=True)))
        size_row.append(lax.rsqrt(jnp.sum(diag, axis=0, keepdims=True)))
    top, low = gram[:h], gram[h:]
    x1 = lower_inverse(a11 * size_col[0] * size_row[0])
    r12 = dot_f32(x1, a12 * size_col[0] * size_row[1])
    x2 = lower_inverse(a22 * size_col[1] * size_row[1] - dot_f32(r12, r12, FIRST_FIRST))
    factor_top = dot_f32(x1, top * size_col[0])
    schur = low[:, h:] * size_col[1] - dot_f32(r12, factor_top[:, h:], FIRST_FIRST)
    mixed = -dot_f32(x2, dot_f32(r12, x1, FIRST_FIRST))
    factor_low = dot_f32(x2, schur)
    lower = jnp.concatenate(
        [
            jnp.concatenate([x1 * size_row[0], jnp.zeros((h, h), jnp.float32)], axis=1),
            jnp.concatenate([mixed * size_row[0], x2 * size_row[1]], axis=1),
        ],
        axis=0,
    )
    inverse = (scale * lower).astype(jnp.bfloat16)
    load.wait()

    def project(i):
        both = jnp.concatenate([field_v[2 * i], field_v[2 * i + 1]], axis=1)
        made = jnp.dot(inverse, both, preferred_element_type=jnp.float32).astype(jnp.bfloat16)
        basis_v[2 * i] = made[:, :h]
        basis_v[2 * i + 1] = made[:, h:]

    down = lax.broadcasted_iota(jnp.int32, (RANK, DAYS), 0)
    across = lax.broadcasted_iota(jnp.int32, (RANK, DAYS), 1)
    factor = jnp.concatenate(
        [factor_top, jnp.concatenate([jnp.zeros((h, h), jnp.float32), factor_low], axis=1)], axis=0
    )
    factor = jnp.where(across >= down, factor, 0.0)
    ahead = jnp.where(across < DAYS - 1, pltpu.roll(factor, DAYS - 1, 1), 0.0)
    cross = dot_three(bf16_parts(ahead, 2), [part.T for part in bf16_parts(factor, 2)])
    polar = cross * lax.rsqrt(jnp.sum(cross * cross) + 1e-06)
    todo = list(range(rows_here // 2))
    share = -(-len(todo) // (ITERS - 1))
    store = pltpu.make_async_copy(basis_v, basis_ref, sems.at[1])
    for n in range(ITERS):
        parts = bf16_parts(polar, 2)
        square = dot_three(parts, [part.T for part in parts])
        for i in todo[n * share : (n + 1) * share]:
            project(i)
        if n == ITERS - 2:
            store.start()
        polar = 1.5 * polar - 0.5 * dot_three(bf16_parts(square, 2), parts)
    prop_ref[...] = math.sqrt(RANK) * polar
    store.wait()


def solve(own, other, field, cell_total):
    rows_tm = field.shape[0]
    part = (rows_tm, RANK, LANES)
    whole = pl.BlockSpec(memory_space=pltpu.VMEM)
    own, other = (pltpu.with_memory_space_constraint(v, pltpu.VMEM) for v in (own, other))
    return pl.pallas_call(
        functools.partial(solve_kernel, math.sqrt(cell_total)),
        in_specs=[whole, whole, pl.BlockSpec(memory_space=pl.ANY)],
        out_specs=[pl.BlockSpec(memory_space=pl.ANY), whole],
        out_shape=[
            jax.ShapeDtypeStruct(part, jnp.bfloat16),
            jax.ShapeDtypeStruct((RANK, RANK), jnp.float32),
        ],
        scratch_shapes=[
            pltpu.VMEM((DAYS // LANES, RANK, LANES), jnp.float32),
            pltpu.VMEM(part, jnp.bfloat16),
            pltpu.VMEM(part, jnp.bfloat16),
            pltpu.SemaphoreType.DMA((2,)),
        ],
        compiler_params=pltpu.CompilerParams(vmem_limit_bytes=VMEM),
        name="factor_basis_and_polar",
    )(own, other, field)


def body(pixels, weights, tile_index, tile_row, granule_day):
    swath_rows = pixels.shape[0]
    width = pixels.shape[1]
    space_count = lax.axis_size("space")
    time_count = lax.axis_size("tm")
    dest_count = time_count * space_count
    rows_tm = GR_DEV // time_count
    slots = 2 * swath_rows // space_count // time_count
    axes = ("tm", "space")
    first, last = pack(pixels, weights, tile_index, tile_row, granule_day, time_count, space_count, rows_tm, slots)
    first = lax.all_to_all(first, axes, split_axis=0, concat_axis=0, tiled=True)
    last = lax.all_to_all(last, axes, split_axis=0, concat_axis=0, tiled=True)
    field, keep, give = grid_rows(first, last, time_count, space_count, rows_tm, slots)

    swap = [(t, t ^ 1) for t in range(time_count)]
    peers = [[t * space_count + s for t in range(core, time_count, 2) for s in range(space_count)] for core in (0, 1)]
    among = functools.partial(
        lax.all_to_all, axis_name=axes, split_axis=0, concat_axis=0, axis_index_groups=peers, tiled=True
    )
    pieces = (keep + lax.ppermute(give, "tm", swap)).reshape(dest_count // 2, -1, LANES)
    mine = jnp.sum(among(pieces), axis=0, keepdims=True)
    own = among(jnp.broadcast_to(mine, pieces.shape)).reshape(keep.shape)
    other = lax.ppermute(own, "tm", swap)
    cell_total = space_count * GR_DEV * width
    basis, propagator = solve(own, other, field, cell_total)
    return (field[None], basis[None], propagator)


def solution(mesh):
    placed = (
        P(("tm", "space"), None),
        P(("tm", "space")),
        P(("tm", "space")),
        P(("tm", "space")),
        P(("tm", "space")),
    )
    return jax.shard_map(
        body,
        mesh=mesh,
        in_specs=placed,
        out_specs=(P("space", "tm", None, None), P("space", "tm", None, None), P()),
        check_vma=False,
    )
```

```python
import functools
import math

import jax
import jax.numpy as jnp
from jax import lax
from jax.experimental import pallas as pl
from jax.experimental.pallas import tpu as pltpu
from jax.sharding import PartitionSpec as P

GR_DEV = 160
DAYS = 512
RANK = 256
ITERS = 8
LANES = 128
GROUP = 16
CLASH = 1 << 20
STEPS = 5
VMEM = 56 * 1024 * 1024

LAST_LAST = (((1,), (1,)), ((), ()))
FIRST_FIRST = (((0,), (0,)), ((), ()))


def round_up(value, unit):
    return -(-value // unit) * unit


def split_rows(slots):
    rows = round_up(slots, 16)
    return rows, rows * 13 // 20 // 16 * 16


def meta_layout(slots):
    pieces = round_up(slots, LANES) // LANES
    folded = 3 * pieces > 8 and 3 * pieces - 1 <= 8 and slots % LANES <= LANES // 2
    return (8 if folded else round_up(3 * pieces, 8)), folded


def pack_kernel(
    dims, tile_ref, row_ref, day_ref, weight_ref, pix_ref, first_ref, last_ref, pos_v, pos_s, rows_v, meta_v, pixf, outf, mrow,
    pix_v, hot_v, prefix_v, sems
):
    time_count, space_count, rows_tm, slot_rows, first_rows, width, (meta_rows, folded) = dims
    dest_count = time_count * space_count
    chunks = tile_ref.shape[0]
    pieces = width // LANES

    fetch = pltpu.make_async_copy(pix_ref, pix_v, sems.at[1])
    fetch.start()
    tile = tile_ref[...]
    row = row_ref[...]
    group = jnp.zeros_like(row)
    for k in range(1, time_count):
        group = group + jnp.where(row >= k * rows_tm, 1, 0)
    dest_all = group * space_count + tile
    rows_v[0] = dest_all.astype(jnp.float32)
    rows_v[2] = weight_ref[...].astype(jnp.float32)
    rows_v[3] = (row - group * rows_tm).astype(jnp.float32)
    rows_v[4] = day_ref[...].astype(jnp.float32)

    dest_iota = lax.broadcasted_iota(jnp.int32, (dest_count, LANES), 0)
    upper = jnp.where(
        lax.broadcasted_iota(jnp.int32, (LANES, LANES), 0) <= lax.broadcasted_iota(jnp.int32, (LANES, LANES), 1), 1.0, 0.0
    ).astype(jnp.bfloat16)
    for c in range(chunks):
        hot = dest_iota == dest_all[c : c + 1, :]
        hot_v[c * dest_count : (c + 1) * dest_count, :] = jnp.where(hot, 1.0, 0.0).astype(jnp.bfloat16)
    prefix_v[...] = jnp.dot(hot_v[...], upper, preferred_element_type=jnp.float32)
    carry = jnp.zeros((dest_count, 1), jnp.float32)
    for c in range(chunks):
        prefix = prefix_v[c * dest_count : (c + 1) * dest_count, :]
        hot = dest_iota == dest_all[c : c + 1, :]
        rows_v[1, c : c + 1, :] = jnp.sum(jnp.where(hot, prefix + carry, 0.0), axis=0, keepdims=True) - 1.0
        carry = carry + prefix[:, LANES - 1 : LANES]
    pos_v[...] = dest_all * slot_rows + rows_v[1].astype(jnp.int32)
    copy = pltpu.make_async_copy(pos_v, pos_s, sems.at[0])
    copy.start()
    meta_v[...] = jnp.zeros_like(meta_v)
    mrow[...] = jnp.zeros_like(mrow)

    def clear(b, _):
        outf[pl.ds(pl.multiple_of(b * slot_rows, 16), slot_rows), :] = jnp.zeros((slot_rows, LANES), jnp.float32)
        return 0

    lax.fori_loop(0, dest_count, clear, 0)
    fetch.wait()
    copy.wait()
    deep = 4
    both = deep * LANES
    dest_number = lax.broadcasted_iota(jnp.int32, (dest_count, both), 0).astype(jnp.float32)
    slot_number = lax.broadcasted_iota(jnp.int32, (width, both), 0).astype(jnp.float32)

    def move(c, _):
        base = pl.multiple_of(c * both, both)
        pixf[pl.ds(base, both), :] = pix_v[pl.ds(base, both), :].astype(jnp.float32)
        dest, rank, weight, local_row, day = (
            jnp.concatenate([rows_v[v, pl.ds(deep * c + i, 1), :] for i in range(deep)], axis=1) for v in range(5)
        )
        hot = dest_number == dest
        place = jnp.where(slot_number == rank, 1.0, 0.0).astype(jnp.bfloat16)
        values = jnp.concatenate([jnp.where(hot, v, 0.0) for v in (weight, local_row, day)], axis=0).astype(jnp.bfloat16)
        meta_v[...] += lax.dot_general(values, place, LAST_LAST, preferred_element_type=jnp.float32)
        for i in range(deep):
            for lane in range(LANES):
                outf[pl.ds(pos_s[deep * c + i, lane], 1), :] = pixf[pl.ds(base + i * LANES + lane, 1), :]
        return 0

    lax.fori_loop(0, chunks // deep, move, 0)
    whole = pieces - 1 if folded else pieces

    def lanes(v, i):
        return meta_v[v * dest_count : (v + 1) * dest_count, i * LANES : (i + 1) * LANES]

    def put(at, value):
        mrow[pl.ds(at, dest_count, stride=meta_rows), :] = value

    for v in range(3):
        for i in range(whole):
            put(v * whole + i, lanes(v, i))
    if folded:
        put(3 * whole, lanes(0, whole) + pltpu.roll(lanes(1, whole), LANES // 2, 1))
        put(3 * whole + 1, lanes(2, whole))

    together = 8

    def narrow(i, _):
        for q in range(together):
            b = i * together + q
            at = pl.multiple_of(b * slot_rows, 16)
            first_ref[b, :first_rows, :] = outf[pl.ds(at, first_rows), :].astype(jnp.bfloat16)
            first_ref[b, first_rows:, :] = mrow[pl.ds(pl.multiple_of(b * meta_rows, 8), meta_rows), :].astype(jnp.bfloat16)
            last_ref[b] = outf[pl.ds(at + first_rows, slot_rows - first_rows), :].astype(jnp.bfloat16)
        return 0

    lax.fori_loop(0, dest_count // together, narrow, 0)


def pack(pixels, weights, tile_index, tile_row, granule_day, time_count, space_count, rows_tm, slots):
    swath_rows = pixels.shape[0]
    chunks = swath_rows // LANES
    dest_count = time_count * space_count
    slot_rows, first_rows = split_rows(slots)
    width = round_up(slots, LANES)
    shape = (chunks, LANES)
    layout = meta_layout(slots)
    first_shape = (dest_count, first_rows + layout[0], LANES)
    last_shape = (dest_count, slot_rows - first_rows, LANES)
    return pl.pallas_call(
        functools.partial(pack_kernel, (time_count, space_count, rows_tm, slot_rows, first_rows, width, layout)),
        in_specs=[pl.BlockSpec(memory_space=pltpu.VMEM)] * 4 + [pl.BlockSpec(memory_space=pl.ANY)],
        out_specs=[pl.BlockSpec(memory_space=pltpu.VMEM)] * 2,
        out_shape=[pltpu.VMEM(first_shape, jnp.bfloat16), pltpu.VMEM(last_shape, jnp.bfloat16)],
        scratch_shapes=[
            pltpu.VMEM(shape, jnp.int32),
            pltpu.SMEM(shape, jnp.int32),
            pltpu.VMEM((5,) + shape, jnp.float32),
            pltpu.VMEM((3 * dest_count, width), jnp.float32),
            pltpu.VMEM((swath_rows, LANES), jnp.float32),
            pltpu.VMEM((dest_count * slot_rows, LANES), jnp.float32),
            pltpu.VMEM((dest_count * layout[0], LANES), jnp.float32),
            pltpu.VMEM((swath_rows, LANES), jnp.bfloat16),
            pltpu.VMEM((chunks * dest_count, LANES), jnp.bfloat16),
            pltpu.VMEM((chunks * dest_count, LANES), jnp.float32),
            pltpu.SemaphoreType.DMA((2,)),
        ],
        compiler_params=pltpu.CompilerParams(vmem_limit_bytes=VMEM),
        name="pack",
    )(
        tile_index.reshape(shape),
        tile_row.reshape(shape),
        granule_day.reshape(shape),
        weights.reshape(shape),
        pixels,
    )


def chunks_of(first_slot, rows):
    slot, found = first_slot, []
    while slot < first_slot + rows:
        size = min(32 - slot % 32, first_slot + rows - slot)
        found.append((slot, size))
        slot += size
    return found


def add_rows(total, pixf, code_s, code_row, first_slot, rows, pix_at, count):
    def add_group(row, lane, at):
        places = [code_s[row, lane + u] for u in range(GROUP)]
        made = [total[pl.ds(p, 1), :] + pixf[pl.ds(at + u, 1), :] for u, p in enumerate(places)]
        for p, value in zip(places, made):
            total[pl.ds(p, 1), :] = value

    def add_singly(row, lane, at):
        def one(u, _):
            p = code_s[row, lane + u]
            p = jnp.where(p >= CLASH, p - CLASH, p)
            total[pl.ds(p, 1), :] = total[pl.ds(p, 1), :] + pixf[pl.ds(at + u, 1), :]
            return 0

        lax.fori_loop(0, GROUP, one, 0)

    for slot, chunk in chunks_of(first_slot, rows):
        start = slot - first_slot
        row, lane = code_row(slot // LANES), slot % LANES
        at = pix_at + start
        heads = [code_s[row, lane + g] for g in range(0, chunk, GROUP)]
        clash = functools.reduce(jnp.maximum, heads) >= CLASH

        @pl.when((count > start) & jnp.logical_not(clash))
        def _():
            for g in range(0, chunk, GROUP):
                add_group(row, lane + g, at + g)

        @pl.when((count > start) & clash)
        def _():
            for g, head in zip(range(0, chunk, GROUP), heads):
                pl.when(head < CLASH)(functools.partial(add_group, row, lane + g, at + g))
                pl.when(head >= CLASH)(functools.partial(add_singly, row, lane + g, at + g))


def grid_first_kernel(
    dims, moved_ref, total_ref, code_ref, rest_ref, count_ref, column_ref, meta_v, pixf, code_s, count_s, sems
):
    time_count, space_count, rows_tm, slot_rows, first_rows, width, (meta_rows, folded) = dims
    day_dev = DAYS // time_count
    blocks = time_count * space_count
    pieces = width // LANES
    spare = rows_tm * DAYS

    meta_v[...] = moved_ref[:, first_rows:, :].astype(jnp.float32).reshape(blocks * meta_rows, LANES)
    whole = pieces - 1 if folded else pieces
    early = lax.broadcasted_iota(jnp.int32, (blocks, LANES), 1) < LANES // 2

    def lanes(v, i):
        if i < whole:
            return meta_v[pl.ds(v * whole + i, blocks, stride=meta_rows), :]
        tail = meta_v[pl.ds(3 * whole + v // 2, blocks, stride=meta_rows), :]
        return jnp.where(early, pltpu.roll(tail, LANES // 2, 1) if v == 1 else tail, 0.0)

    block = lax.broadcasted_iota(jnp.int32, (blocks, LANES), 0)
    offset = jnp.zeros((blocks, LANES), jnp.float32)
    for m in range(1, time_count):
        offset = offset + jnp.where(block >= m * space_count, float(day_dev), 0.0)
    within = lax.broadcasted_iota(jnp.int32, (blocks, LANES), 1) % GROUP
    count = jnp.zeros((blocks, 1), jnp.float32)
    for i in range(pieces):
        weight, local_row, day = (lanes(v, i) for v in range(3))
        used = weight > 0.0
        count = count + jnp.sum(jnp.where(used, 1.0, 0.0), axis=1, keepdims=True)
        column_ref[i * LANES : (i + 1) * LANES, :] = jnp.transpose(weight)
        code = jnp.where(used, local_row * DAYS + (day + offset), float(spare)).astype(jnp.int32)
        clash = jnp.zeros(code.shape, jnp.int32)
        for k in range(1, GROUP):
            ahead = pltpu.roll(code, LANES - k, 1)
            clash = jnp.where((ahead == code) & (within + k < GROUP) & (code < spare), 1, clash)
        k = 1
        while k < GROUP:
            ahead = pltpu.roll(clash, LANES - k, 1)
            clash = jnp.where(within + k < GROUP, jnp.maximum(clash, ahead), clash)
            k *= 2
        code_ref[i * blocks : (i + 1) * blocks, :] = jnp.where((within == 0) & (clash > 0), code + CLASH, code)
    rest_ref[...] = code_ref[first_rows // LANES * blocks :, :]
    count_ref[...] = jnp.broadcast_to(count, (blocks, LANES)).astype(jnp.int32)
    code_copy = pltpu.make_async_copy(code_ref, code_s, sems.at[0])
    count_copy = pltpu.make_async_copy(count_ref, count_s, sems.at[1])
    code_copy.start()
    count_copy.start()

    for b in range(blocks):
        column = column_ref[:first_rows, b : b + 1]
        pixf[b * first_rows : (b + 1) * first_rows, :] = moved_ref[b, :first_rows, :].astype(jnp.float32) * column

    def clear(i, _):
        total_ref[pl.ds(pl.multiple_of(i * DAYS, DAYS), DAYS), :] = jnp.zeros((DAYS, LANES), jnp.float32)
        return 0

    lax.fori_loop(0, rows_tm, clear, 0)
    total_ref[spare:, :] = jnp.zeros((8, LANES), jnp.float32)
    code_copy.wait()
    count_copy.wait()

    def add(b, _):
        add_rows(total_ref, pixf, code_s, lambda i: i * blocks + b, 0, first_rows, b * first_rows, count_s[b, 0])
        return 0

    lax.fori_loop(0, blocks, add, 0)


def grid_last_kernel(
    dims, code_s, count_s, column_ref, moved_ref, first_ref, field_ref, keep_ref, give_ref,
    total, first_v, moved_v, pixf, field_v, gram_v, first_sems, block_sems, out_sem
):
    time_count, space_count, rows_tm, slot_rows, first_rows, width, (meta_rows, folded) = dims
    blocks = time_count * space_count
    last_rows = slot_rows - first_rows
    group = rows_tm // STEPS
    skipped = first_rows // LANES

    def load(i):
        at = pl.ds(pl.multiple_of(i * group * DAYS, DAYS), group * DAYS)
        return pltpu.make_async_copy(first_ref.at[at], first_v.at[at], first_sems.at[i])

    def fetch(b):
        return pltpu.make_async_copy(moved_ref.at[b], moved_v.at[b], block_sems.at[b])

    for b in range(blocks):
        pl.when(count_s[b, 0] > first_rows)(fetch(b).start)
    for i in range(STEPS):
        load(i).start()

    def clear(i, _):
        total[pl.ds(pl.multiple_of(i * DAYS, DAYS), DAYS), :] = jnp.zeros((DAYS, LANES), jnp.float32)
        return 0

    lax.fori_loop(0, rows_tm, clear, 0)
    total[rows_tm * DAYS :, :] = jnp.zeros((8, LANES), jnp.float32)
    for b in range(blocks):
        pl.when(count_s[b, 0] > first_rows)(fetch(b).wait)
    for b in range(blocks):
        column = column_ref[first_rows:slot_rows, b : b + 1]
        pixf[b * last_rows : (b + 1) * last_rows, :] = moved_v[b].astype(jnp.float32) * column

    def add(b, _):
        rest = count_s[b, 0] - first_rows

        @pl.when(rest > 0)
        def _():
            add_rows(
                total, pixf, code_s, lambda i: (i - skipped) * blocks + b, first_rows, last_rows, b * last_rows, rest
            )

        return 0

    lax.fori_loop(0, blocks, add, 0)

    def send(i):
        at = pl.ds(i * group, group)
        return pltpu.make_async_copy(field_v.at[at], field_ref.at[at], out_sem)

    def settle(i):
        for q in range(i * group, (i + 1) * group):
            at = pl.ds(q * DAYS, DAYS)
            field_v[q] = (first_v[at, :] + total[at, :]).astype(jnp.bfloat16)

    def multiply(i):
        both = jnp.concatenate([field_v[q] for q in range(i * group, (i + 1) * group)], axis=1)
        part = lax.dot_general(both[:RANK], both, LAST_LAST, preferred_element_type=jnp.float32)
        for c in range(DAYS // LANES):
            here = part[:, c * LANES : (c + 1) * LANES]
            gram_v[c] = here if i == 0 else gram_v[c] + here

    for i in range(STEPS):
        load(i).wait()
        settle(i)
        if i > 0:
            send(i - 1).start()
            multiply(i - 1)
    send(STEPS - 1).start()
    multiply(STEPS - 1)
    odd = lax.axis_index("tm") % 2
    half = DAYS // LANES // 2
    for c in range(half):
        keep_ref[c] = gram_v[odd * half + c]
        give_ref[c] = gram_v[(1 - odd) * half + c]
    pltpu.make_async_copy(field_v, field_ref, out_sem).wait()


def grid_rows(moved_first, moved_last, time_count, space_count, rows_tm, slots):
    slot_rows, first_rows = split_rows(slots)
    last_rows = slot_rows - first_rows
    width = round_up(slots, LANES)
    blocks = time_count * space_count
    dims = (time_count, space_count, rows_tm, slot_rows, first_rows, width, meta_layout(slots))
    codes = (blocks * width // LANES, LANES)
    rest = (codes[0] - first_rows // LANES * blocks, LANES)
    counts = (blocks, LANES)
    columns = (width, blocks)
    sums = (rows_tm * DAYS + 8, LANES)
    half = (DAYS // LANES // 2, RANK, LANES)
    params = pltpu.CompilerParams(vmem_limit_bytes=VMEM)
    moved_first, moved_last = (pltpu.with_memory_space_constraint(v, pltpu.VMEM) for v in (moved_first, moved_last))
    total, _, rest_code, count, column = pl.pallas_call(
        functools.partial(grid_first_kernel, dims),
        out_shape=[
            jax.ShapeDtypeStruct(sums, jnp.float32),
            jax.ShapeDtypeStruct(codes, jnp.int32),
            jax.ShapeDtypeStruct(rest, jnp.int32),
            jax.ShapeDtypeStruct(counts, jnp.int32),
            jax.ShapeDtypeStruct(columns, jnp.float32),
        ],
        scratch_shapes=[
            pltpu.VMEM((blocks * meta_layout(slots)[0], LANES), jnp.float32),
            pltpu.VMEM((blocks * first_rows, LANES), jnp.float32),
            pltpu.SMEM(codes, jnp.int32),
            pltpu.SMEM(counts, jnp.int32),
            pltpu.SemaphoreType.DMA((2,)),
        ],
        compiler_params=params,
        cost_estimate=pl.CostEstimate(flops=0, bytes_accessed=60_000_000, transcendentals=0),
        name="grid_first",
    )(moved_first)
    whole = pl.BlockSpec(memory_space=pltpu.VMEM)
    return pl.pallas_call(
        functools.partial(grid_last_kernel, dims),
        in_specs=[
            pl.BlockSpec(memory_space=pltpu.SMEM),
            pl.BlockSpec(memory_space=pltpu.SMEM),
            whole,
            pl.BlockSpec(memory_space=pl.ANY),
            pl.BlockSpec(memory_space=pl.ANY),
        ],
        out_specs=[pl.BlockSpec(memory_space=pl.ANY), whole, whole],
        out_shape=[
            jax.ShapeDtypeStruct((rows_tm, DAYS, LANES), jnp.bfloat16),
            pltpu.VMEM(half, jnp.float32),
            pltpu.VMEM(half, jnp.float32),
        ],
        scratch_shapes=[
            pltpu.VMEM(sums, jnp.float32),
            pltpu.VMEM((rows_tm * DAYS, LANES), jnp.float32),
            pltpu.VMEM((blocks, last_rows, LANES), jnp.bfloat16),
            pltpu.VMEM((blocks * last_rows, LANES), jnp.float32),
            pltpu.VMEM((rows_tm, DAYS, LANES), jnp.bfloat16),
            pltpu.VMEM((DAYS // LANES, RANK, LANES), jnp.float32),
            pltpu.SemaphoreType.DMA((STEPS,)),
            pltpu.SemaphoreType.DMA((blocks,)),
            pltpu.SemaphoreType.DMA,
        ],
        compiler_params=params,
        name="grid_last_and_gram",
    )(rest_code, count, column, moved_last, total)


def bf16_parts(x, count):
    found = []
    for _ in range(count):
        found.append(x.astype(jnp.bfloat16))
        x = x - found[-1].astype(jnp.float32)
    return found


def dot_f32(a, b, dims=(((1,), (0,)), ((), ()))):
    return lax.dot_general(a, b, dims, precision=lax.Precision.HIGHEST, preferred_element_type=jnp.float32)


def dot_three(a_parts, b_parts):
    a_high, a_low = a_parts
    b_high, b_low = b_parts
    a_all = jnp.concatenate([a_high, a_high, a_low], axis=1)
    b_all = jnp.concatenate([b_high, b_low, b_high], axis=0)
    half = a_all.shape[0] // 2
    rows = [jnp.dot(part, b_all, preferred_element_type=jnp.float32) for part in (a_all[:half], a_all[half:])]
    return jnp.concatenate(rows, axis=0)


def lower_inverse(a, beside=()):
    n = a.shape[0]
    full = (8, n)
    tiles = [a[8 * i : 8 * i + 8, :] for i in range(n // 8)]
    lane = lax.broadcasted_iota(jnp.int32, full, 1)
    down = lax.broadcasted_iota(jnp.int32, full, 0)
    out = []
    share = -(-len(beside) // (n // 8))
    for t in range(n // 8):
        for task in beside[t * share : (t + 1) * share]:
            task()
        k = 8 * t
        block = (lane >= k) & (lane < k + 8)
        panel = tiles[t]
        cols = [jnp.broadcast_to(panel[:, k + c : k + c + 1], full) for c in range(8)]
        e = {(i, c): jnp.broadcast_to(cols[c][i : i + 1, :], full) for c in range(8) for i in range(c, 8)}
        start = jnp.where(block, jnp.where(lane == k + down, 1.0, 0.0), panel)
        rows = [jnp.broadcast_to(start[i : i + 1, :], full) for i in range(8)]
        held = []
        for s in range(0, 8, 2):
            p, q, r = e[s, s], e[s + 1, s], e[s + 1, s + 1]
            det = p * r - q * q
            inv = pl.reciprocal(det, approx=True)
            factors = {}
            for i in range(s + 2, 8):
                x, y = e[i, s], e[i, s + 1]
                factors[i] = (r * x - q * y, p * y - q * x)
            for i in range(s + 2, 8):
                u, v = factors[i]
                for c in range(s + 2, i + 1):
                    e[i, c] = e[i, c] - (u * e[c, s] + v * e[c, s + 1]) * inv
                rows[i] = rows[i] - (u * rows[s] + v * rows[s + 1]) * inv
            held.append((p, q, r, det, inv, factors))
        done = jnp.zeros(full, jnp.float32)
        solved = [None] * 8
        for s in (6, 4, 2, 0):
            p, q, r, det, inv, factors = held[s // 2]
            root = lax.rsqrt(p)
            done = jnp.where(down == s, rows[s] * root, done)
            done = jnp.where(down == s + 1, (rows[s + 1] * p - q * rows[s]) * (root * lax.rsqrt(det)), done)
            first, second = r * rows[s] - q * rows[s + 1], p * rows[s + 1] - q * rows[s]
            for i in range(7, s + 1, -1):
                u, v = factors[i]
                first, second = first - u * solved[i], second - v * solved[i]
            solved[s], solved[s + 1] = first * inv, second * inv
        out.append(jnp.where(lane < k + 8, done, 0.0))
        for i in range(t + 1, n // 8):
            terms = [jnp.broadcast_to(tiles[i][:, k + c : k + c + 1], full) * solved[c] for c in range(8)]
            while len(terms) > 1:
                terms = [terms[j] + terms[j + 1] for j in range(0, len(terms), 2)]
            tiles[i] = jnp.where(block, 0.0, tiles[i]) - terms[0]
    return jnp.concatenate(out, axis=0)


def solve_kernel(scale, own_ref, other_ref, field_ref, basis_ref, prop_ref, gram_v, field_v, basis_v, sems):
    h = LANES
    pieces = DAYS // h
    rows_here = field_v.shape[0]
    load = pltpu.make_async_copy(field_ref.at[:, pl.ds(0, RANK), :], field_v, sems.at[0])
    load.start()
    odd = lax.axis_index("tm") % 2
    for c in range(pieces // 2):
        gram_v[odd * (pieces // 2) + c] = own_ref[c]
        gram_v[(1 - odd) * (pieces // 2) + c] = other_ref[c]

    gram = jnp.concatenate([gram_v[i] for i in range(pieces)], axis=1)
    eye = lax.broadcasted_iota(jnp.int32, (h, h), 0) == lax.broadcasted_iota(jnp.int32, (h, h), 1)
    a11, a12, a22 = gram_v[0, :h, :], gram_v[1, :h, :], gram_v[1, h:, :]
    size_col, size_row = [], []
    for part in (a11, a22):
        diag = jnp.where(eye, part, 0.0)
        size_col.append(lax.rsqrt(jnp.sum(diag, axis=1, keepdims=True)))
        size_row.append(lax.rsqrt(jnp.sum(diag, axis=0, keepdims=True)))
    top, low = gram[:h], gram[h:]
    x1 = lower_inverse(a11 * size_col[0] * size_row[0])
    r12 = dot_f32(x1, a12 * size_col[0] * size_row[1])
    inverse_top = (scale * (x1 * size_row[0])).astype(jnp.bfloat16)
    load.wait()

    def project_top(i):
        both = jnp.concatenate([field_v[2 * i, :h], field_v[2 * i + 1, :h]], axis=1)
        made = jnp.dot(inverse_top, both, preferred_element_type=jnp.float32).astype(jnp.bfloat16)
        basis_v[2 * i, :h] = made[:, :h]
        basis_v[2 * i + 1, :h] = made[:, h:]

    tasks = [functools.partial(project_top, i) for i in range(rows_here // 2)]
    x2 = lower_inverse(a22 * size_col[1] * size_row[1] - dot_f32(r12, r12, FIRST_FIRST), tasks)
    factor_top = dot_f32(x1, top * size_col[0])
    schur = low[:, h:] * size_col[1] - dot_f32(r12, factor_top[:, h:], FIRST_FIRST)
    mixed = -dot_f32(x2, dot_f32(r12, x1, FIRST_FIRST))
    factor_low = dot_f32(x2, schur)
    lower = jnp.concatenate([mixed * size_row[0], x2 * size_row[1]], axis=1)
    inverse_low = (scale * lower).astype(jnp.bfloat16)

    def project_low(i):
        both = jnp.concatenate([field_v[2 * i], field_v[2 * i + 1]], axis=1)
        made = jnp.dot(inverse_low, both, preferred_element_type=jnp.float32).astype(jnp.bfloat16)
        basis_v[2 * i, h:] = made[:, :h]
        basis_v[2 * i + 1, h:] = made[:, h:]

    down = lax.broadcasted_iota(jnp.int32, (RANK, DAYS), 0)
    across = lax.broadcasted_iota(jnp.int32, (RANK, DAYS), 1)
    factor = jnp.concatenate(
        [factor_top, jnp.concatenate([jnp.zeros((h, h), jnp.float32), factor_low], axis=1)], axis=0
    )
    factor = jnp.where(across >= down, factor, 0.0)
    ahead = jnp.where(across < DAYS - 1, pltpu.roll(factor, DAYS - 1, 1), 0.0)
    cross = dot_three(bf16_parts(ahead, 2), [part.T for part in bf16_parts(factor, 2)])
    polar = cross * lax.rsqrt(jnp.sum(cross * cross) + 1e-06)
    todo = list(range(rows_here // 2))
    share = -(-len(todo) // (ITERS - 1))
    store = pltpu.make_async_copy(basis_v, basis_ref, sems.at[1])
    for n in range(ITERS):
        parts = bf16_parts(polar, 2)
        square = dot_three(parts, [part.T for part in parts])
        for i in todo[n * share : (n + 1) * share]:
            project_low(i)
        if n == ITERS - 2:
            store.start()
        polar = 1.5 * polar - 0.5 * dot_three(bf16_parts(square, 2), parts)
    prop_ref[...] = math.sqrt(RANK) * polar
    store.wait()


def solve(own, other, field, cell_total):
    rows_tm = field.shape[0]
    part = (rows_tm, RANK, LANES)
    whole = pl.BlockSpec(memory_space=pltpu.VMEM)
    own, other = (pltpu.with_memory_space_constraint(v, pltpu.VMEM) for v in (own, other))
    return pl.pallas_call(
        functools.partial(solve_kernel, math.sqrt(cell_total)),
        in_specs=[whole, whole, pl.BlockSpec(memory_space=pl.ANY)],
        out_specs=[pl.BlockSpec(memory_space=pl.ANY), whole],
        out_shape=[
            jax.ShapeDtypeStruct(part, jnp.bfloat16),
            jax.ShapeDtypeStruct((RANK, RANK), jnp.float32),
        ],
        scratch_shapes=[
            pltpu.VMEM((DAYS // LANES, RANK, LANES), jnp.float32),
            pltpu.VMEM(part, jnp.bfloat16),
            pltpu.VMEM(part, jnp.bfloat16),
            pltpu.SemaphoreType.DMA((2,)),
        ],
        compiler_params=pltpu.CompilerParams(vmem_limit_bytes=VMEM),
        name="factor_basis_and_polar",
    )(own, other, field)


def body(pixels, weights, tile_index, tile_row, granule_day):
    swath_rows = pixels.shape[0]
    width = pixels.shape[1]
    space_count = lax.axis_size("space")
    time_count = lax.axis_size("tm")
    dest_count = time_count * space_count
    rows_tm = GR_DEV // time_count
    slots = 2 * swath_rows // space_count // time_count
    axes = ("tm", "space")
    first, last = pack(pixels, weights, tile_index, tile_row, granule_day, time_count, space_count, rows_tm, slots)
    first = lax.all_to_all(first, axes, split_axis=0, concat_axis=0, tiled=True)
    last = lax.all_to_all(last, axes, split_axis=0, concat_axis=0, tiled=True)
    field, keep, give = grid_rows(first, last, time_count, space_count, rows_tm, slots)

    swap = [(t, t ^ 1) for t in range(time_count)]
    peers = [[t * space_count + s for t in range(core, time_count, 2) for s in range(space_count)] for core in (0, 1)]
    among = functools.partial(
        lax.all_to_all, axis_name=axes, split_axis=0, concat_axis=0, axis_index_groups=peers, tiled=True
    )
    pieces = (keep + lax.ppermute(give, "tm", swap)).reshape(dest_count // 2, -1, LANES)
    mine = jnp.sum(among(pieces), axis=0, keepdims=True)
    own = among(jnp.broadcast_to(mine, pieces.shape)).reshape(keep.shape)
    other = lax.ppermute(own, "tm", swap)
    cell_total = space_count * GR_DEV * width
    basis, propagator = solve(own, other, field, cell_total)
    return (field[None], basis[None], propagator)


def solution(mesh):
    placed = (
        P(("tm", "space"), None),
        P(("tm", "space")),
        P(("tm", "space")),
        P(("tm", "space")),
        P(("tm", "space")),
    )
    return jax.shard_map(
        body,
        mesh=mesh,
        in_specs=placed,
        out_specs=(P("space", "tm", None, None), P("space", "tm", None, None), P()),
        check_vma=False,
    )
```

```python
import functools
import math

import jax
import jax.numpy as jnp
from jax import lax
from jax.experimental import pallas as pl
from jax.experimental.pallas import tpu as pltpu
from jax.sharding import PartitionSpec as P

GR_DEV = 160
DAYS = 512
RANK = 256
ITERS = 8
LANES = 128
GROUP = 16
CLASH = 1 << 20
STEPS = 5
VMEM = 56 * 1024 * 1024

LAST_LAST = (((1,), (1,)), ((), ()))
FIRST_FIRST = (((0,), (0,)), ((), ()))


def round_up(value, unit):
    return -(-value // unit) * unit


def split_rows(slots):
    rows = round_up(slots, 16)
    return rows, rows * 13 // 20 // 16 * 16


def meta_layout(slots):
    pieces = round_up(slots, LANES) // LANES
    folded = 3 * pieces > 8 and 3 * pieces - 1 <= 8 and slots % LANES <= LANES // 2
    return (8 if folded else round_up(3 * pieces, 8)), folded


def pack_kernel(
    dims, tile_ref, row_ref, day_ref, weight_ref, pix_ref, first_ref, last_ref, pos_v, pos_s, rows_v, meta_v, pixf, outf, mrow,
    pix_v, hot_v, prefix_v, sems
):
    time_count, space_count, rows_tm, slot_rows, first_rows, width, (meta_rows, folded) = dims
    dest_count = time_count * space_count
    chunks = tile_ref.shape[0]
    pieces = width // LANES

    fetch = pltpu.make_async_copy(pix_ref, pix_v, sems.at[1])
    fetch.start()
    tile = tile_ref[...]
    row = row_ref[...]
    group = jnp.zeros_like(row)
    for k in range(1, time_count):
        group = group + jnp.where(row >= k * rows_tm, 1, 0)
    dest_all = group * space_count + tile
    rows_v[0] = dest_all.astype(jnp.float32)
    rows_v[2] = weight_ref[...].astype(jnp.float32)
    rows_v[3] = (row - group * rows_tm).astype(jnp.float32)
    rows_v[4] = day_ref[...].astype(jnp.float32)

    dest_iota = lax.broadcasted_iota(jnp.int32, (dest_count, LANES), 0)
    upper = jnp.where(
        lax.broadcasted_iota(jnp.int32, (LANES, LANES), 0) <= lax.broadcasted_iota(jnp.int32, (LANES, LANES), 1), 1.0, 0.0
    ).astype(jnp.bfloat16)
    for c in range(chunks):
        hot = dest_iota == dest_all[c : c + 1, :]
        hot_v[c * dest_count : (c + 1) * dest_count, :] = jnp.where(hot, 1.0, 0.0).astype(jnp.bfloat16)
    prefix_v[...] = jnp.dot(hot_v[...], upper, preferred_element_type=jnp.float32)
    carry = jnp.zeros((dest_count, 1), jnp.float32)
    for c in range(chunks):
        prefix = prefix_v[c * dest_count : (c + 1) * dest_count, :]
        hot = dest_iota == dest_all[c : c + 1, :]
        rows_v[1, c : c + 1, :] = jnp.sum(jnp.where(hot, prefix + carry, 0.0), axis=0, keepdims=True) - 1.0
        carry = carry + prefix[:, LANES - 1 : LANES]
    pos_v[...] = dest_all * slot_rows + rows_v[1].astype(jnp.int32)
    copy = pltpu.make_async_copy(pos_v, pos_s, sems.at[0])
    copy.start()
    meta_v[...] = jnp.zeros_like(meta_v)
    mrow[...] = jnp.zeros_like(mrow)

    def clear(b, _):
        outf[pl.ds(pl.multiple_of(b * slot_rows, 16), slot_rows), :] = jnp.zeros((slot_rows, LANES), jnp.float32)
        return 0

    lax.fori_loop(0, dest_count, clear, 0)
    fetch.wait()
    copy.wait()
    deep = 8 if chunks % 8 == 0 else 4
    both = deep * LANES
    dest_number = lax.broadcasted_iota(jnp.int32, (dest_count, both), 0).astype(jnp.float32)
    slot_number = lax.broadcasted_iota(jnp.int32, (width, both), 0).astype(jnp.float32)

    def move(c, _):
        base = pl.multiple_of(c * both, both)
        pixf[pl.ds(base, both), :] = pix_v[pl.ds(base, both), :].astype(jnp.float32)
        dest, rank, weight, local_row, day = (
            jnp.concatenate([rows_v[v, pl.ds(deep * c + i, 1), :] for i in range(deep)], axis=1) for v in range(5)
        )
        hot = dest_number == dest
        place = jnp.where(slot_number == rank, 1.0, 0.0).astype(jnp.bfloat16)
        values = jnp.concatenate([jnp.where(hot, v, 0.0) for v in (weight, local_row, day)], axis=0).astype(jnp.bfloat16)
        meta_v[...] += lax.dot_general(values, place, LAST_LAST, preferred_element_type=jnp.float32)
        for i in range(deep):
            for lane in range(LANES):
                outf[pl.ds(pos_s[deep * c + i, lane], 1), :] = pixf[pl.ds(base + i * LANES + lane, 1), :]
        return 0

    lax.fori_loop(0, chunks // deep, move, 0)
    whole = pieces - 1 if folded else pieces

    def lanes(v, i):
        return meta_v[v * dest_count : (v + 1) * dest_count, i * LANES : (i + 1) * LANES]

    def put(at, value):
        mrow[pl.ds(at, dest_count, stride=meta_rows), :] = value

    for v in range(3):
        for i in range(whole):
            put(v * whole + i, lanes(v, i))
    if folded:
        put(3 * whole, lanes(0, whole) + pltpu.roll(lanes(1, whole), LANES // 2, 1))
        put(3 * whole + 1, lanes(2, whole))

    together = 8

    def narrow(i, _):
        for q in range(together):
            b = i * together + q
            at = pl.multiple_of(b * slot_rows, 16)
            first_ref[b, :first_rows, :] = outf[pl.ds(at, first_rows), :].astype(jnp.bfloat16)
            first_ref[b, first_rows:, :] = mrow[pl.ds(pl.multiple_of(b * meta_rows, 8), meta_rows), :].astype(jnp.bfloat16)
            last_ref[b] = outf[pl.ds(at + first_rows, slot_rows - first_rows), :].astype(jnp.bfloat16)
        return 0

    lax.fori_loop(0, dest_count // together, narrow, 0)


def pack(pixels, weights, tile_index, tile_row, granule_day, time_count, space_count, rows_tm, slots):
    swath_rows = pixels.shape[0]
    chunks = swath_rows // LANES
    dest_count = time_count * space_count
    slot_rows, first_rows = split_rows(slots)
    width = round_up(slots, LANES)
    shape = (chunks, LANES)
    layout = meta_layout(slots)
    first_shape = (dest_count, first_rows + layout[0], LANES)
    last_shape = (dest_count, slot_rows - first_rows, LANES)
    return pl.pallas_call(
        functools.partial(pack_kernel, (time_count, space_count, rows_tm, slot_rows, first_rows, width, layout)),
        in_specs=[pl.BlockSpec(memory_space=pltpu.VMEM)] * 4 + [pl.BlockSpec(memory_space=pl.ANY)],
        out_specs=[pl.BlockSpec(memory_space=pltpu.VMEM)] * 2,
        out_shape=[pltpu.VMEM(first_shape, jnp.bfloat16), pltpu.VMEM(last_shape, jnp.bfloat16)],
        scratch_shapes=[
            pltpu.VMEM(shape, jnp.int32),
            pltpu.SMEM(shape, jnp.int32),
            pltpu.VMEM((5,) + shape, jnp.float32),
            pltpu.VMEM((3 * dest_count, width), jnp.float32),
            pltpu.VMEM((swath_rows, LANES), jnp.float32),
            pltpu.VMEM((dest_count * slot_rows, LANES), jnp.float32),
            pltpu.VMEM((dest_count * layout[0], LANES), jnp.float32),
            pltpu.VMEM((swath_rows, LANES), jnp.bfloat16),
            pltpu.VMEM((chunks * dest_count, LANES), jnp.bfloat16),
            pltpu.VMEM((chunks * dest_count, LANES), jnp.float32),
            pltpu.SemaphoreType.DMA((2,)),
        ],
        compiler_params=pltpu.CompilerParams(vmem_limit_bytes=VMEM),
        name="pack",
    )(
        tile_index.reshape(shape),
        tile_row.reshape(shape),
        granule_day.reshape(shape),
        weights.reshape(shape),
        pixels,
    )


def chunks_of(first_slot, rows):
    slot, found = first_slot, []
    while slot < first_slot + rows:
        size = min(32 - slot % 32, first_slot + rows - slot)
        found.append((slot, size))
        slot += size
    return found


def add_rows(total, pixf, code_s, code_row, first_slot, rows, pix_at, count):
    def add_group(row, lane, at):
        places = [code_s[row, lane + u] for u in range(GROUP)]
        made = [total[pl.ds(p, 1), :] + pixf[pl.ds(at + u, 1), :] for u, p in enumerate(places)]
        for p, value in zip(places, made):
            total[pl.ds(p, 1), :] = value

    def add_singly(row, lane, at):
        def one(u, _):
            p = code_s[row, lane + u]
            p = jnp.where(p >= CLASH, p - CLASH, p)
            total[pl.ds(p, 1), :] = total[pl.ds(p, 1), :] + pixf[pl.ds(at + u, 1), :]
            return 0

        lax.fori_loop(0, GROUP, one, 0)

    for slot, chunk in chunks_of(first_slot, rows):
        start = slot - first_slot
        row, lane = code_row(slot // LANES), slot % LANES
        at = pix_at + start
        heads = [code_s[row, lane + g] for g in range(0, chunk, GROUP)]
        clash = functools.reduce(jnp.maximum, heads) >= CLASH

        @pl.when((count > start) & jnp.logical_not(clash))
        def _():
            for g in range(0, chunk, GROUP):
                add_group(row, lane + g, at + g)

        @pl.when((count > start) & clash)
        def _():
            for g, head in zip(range(0, chunk, GROUP), heads):
                pl.when(head < CLASH)(functools.partial(add_group, row, lane + g, at + g))
                pl.when(head >= CLASH)(functools.partial(add_singly, row, lane + g, at + g))


def grid_first_kernel(
    dims, moved_ref, total_ref, code_ref, rest_ref, count_ref, column_ref, meta_v, pixf, code_s, count_s, sems
):
    time_count, space_count, rows_tm, slot_rows, first_rows, width, (meta_rows, folded) = dims
    day_dev = DAYS // time_count
    blocks = time_count * space_count
    pieces = width // LANES
    spare = rows_tm * DAYS

    meta_v[...] = moved_ref[:, first_rows:, :].astype(jnp.float32).reshape(blocks * meta_rows, LANES)
    whole = pieces - 1 if folded else pieces
    early = lax.broadcasted_iota(jnp.int32, (blocks, LANES), 1) < LANES // 2

    def lanes(v, i):
        if i < whole:
            return meta_v[pl.ds(v * whole + i, blocks, stride=meta_rows), :]
        tail = meta_v[pl.ds(3 * whole + v // 2, blocks, stride=meta_rows), :]
        return jnp.where(early, pltpu.roll(tail, LANES // 2, 1) if v == 1 else tail, 0.0)

    block = lax.broadcasted_iota(jnp.int32, (blocks, LANES), 0)
    offset = jnp.zeros((blocks, LANES), jnp.float32)
    for m in range(1, time_count):
        offset = offset + jnp.where(block >= m * space_count, float(day_dev), 0.0)
    within = lax.broadcasted_iota(jnp.int32, (blocks, LANES), 1) % GROUP
    count = jnp.zeros((blocks, 1), jnp.float32)
    for i in range(pieces):
        weight, local_row, day = (lanes(v, i) for v in range(3))
        used = weight > 0.0
        count = count + jnp.sum(jnp.where(used, 1.0, 0.0), axis=1, keepdims=True)
        column_ref[i * LANES : (i + 1) * LANES, :] = jnp.transpose(weight)
        code = jnp.where(used, local_row * DAYS + (day + offset), float(spare)).astype(jnp.int32)
        clash = jnp.zeros(code.shape, jnp.int32)
        for k in range(1, GROUP):
            ahead = pltpu.roll(code, LANES - k, 1)
            clash = jnp.where((ahead == code) & (within + k < GROUP) & (code < spare), 1, clash)
        k = 1
        while k < GROUP:
            ahead = pltpu.roll(clash, LANES - k, 1)
            clash = jnp.where(within + k < GROUP, jnp.maximum(clash, ahead), clash)
            k *= 2
        code_ref[i * blocks : (i + 1) * blocks, :] = jnp.where((within == 0) & (clash > 0), code + CLASH, code)
    rest_ref[...] = code_ref[first_rows // LANES * blocks :, :]
    count_ref[...] = jnp.broadcast_to(count, (blocks, LANES)).astype(jnp.int32)
    code_copy = pltpu.make_async_copy(code_ref, code_s, sems.at[0])
    count_copy = pltpu.make_async_copy(count_ref, count_s, sems.at[1])
    code_copy.start()
    count_copy.start()

    for b in range(blocks):
        column = column_ref[:first_rows, b : b + 1]
        pixf[b * first_rows : (b + 1) * first_rows, :] = moved_ref[b, :first_rows, :].astype(jnp.float32) * column

    def clear(i, _):
        total_ref[pl.ds(pl.multiple_of(i * DAYS, DAYS), DAYS), :] = jnp.zeros((DAYS, LANES), jnp.float32)
        return 0

    lax.fori_loop(0, rows_tm, clear, 0)
    total_ref[spare:, :] = jnp.zeros((8, LANES), jnp.float32)
    code_copy.wait()
    count_copy.wait()

    def add(b, _):
        add_rows(total_ref, pixf, code_s, lambda i: i * blocks + b, 0, first_rows, b * first_rows, count_s[b, 0])
        return 0

    lax.fori_loop(0, blocks, add, 0)


def grid_last_kernel(
    dims, code_s, count_s, column_ref, moved_ref, first_ref, field_ref, keep_ref, give_ref,
    total, first_v, moved_v, pixf, field_v, gram_v, first_sems, block_sems, out_sem
):
    time_count, space_count, rows_tm, slot_rows, first_rows, width, (meta_rows, folded) = dims
    blocks = time_count * space_count
    last_rows = slot_rows - first_rows
    group = rows_tm // STEPS
    skipped = first_rows // LANES

    def load(i):
        at = pl.ds(pl.multiple_of(i * group * DAYS, DAYS), group * DAYS)
        return pltpu.make_async_copy(first_ref.at[at], first_v.at[at], first_sems.at[i])

    def fetch(b):
        return pltpu.make_async_copy(moved_ref.at[b], moved_v.at[b], block_sems.at[b])

    for b in range(blocks):
        pl.when(count_s[b, 0] > first_rows)(fetch(b).start)
    for i in range(STEPS):
        load(i).start()

    def clear(i, _):
        total[pl.ds(pl.multiple_of(i * DAYS, DAYS), DAYS), :] = jnp.zeros((DAYS, LANES), jnp.float32)
        return 0

    lax.fori_loop(0, rows_tm, clear, 0)
    total[rows_tm * DAYS :, :] = jnp.zeros((8, LANES), jnp.float32)
    for b in range(blocks):
        pl.when(count_s[b, 0] > first_rows)(fetch(b).wait)
    for b in range(blocks):
        column = column_ref[first_rows:slot_rows, b : b + 1]
        pixf[b * last_rows : (b + 1) * last_rows, :] = moved_v[b].astype(jnp.float32) * column

    def add(b, _):
        rest = count_s[b, 0] - first_rows

        @pl.when(rest > 0)
        def _():
            add_rows(
                total, pixf, code_s, lambda i: (i - skipped) * blocks + b, first_rows, last_rows, b * last_rows, rest
            )

        return 0

    lax.fori_loop(0, blocks, add, 0)

    def send(i):
        at = pl.ds(i * group, group)
        return pltpu.make_async_copy(field_v.at[at], field_ref.at[at], out_sem)

    def settle(i):
        for q in range(i * group, (i + 1) * group):
            at = pl.ds(q * DAYS, DAYS)
            field_v[q] = (first_v[at, :] + total[at, :]).astype(jnp.bfloat16)

    def multiply(i):
        both = jnp.concatenate([field_v[q] for q in range(i * group, (i + 1) * group)], axis=1)
        part = lax.dot_general(both[:RANK], both, LAST_LAST, preferred_element_type=jnp.float32)
        for c in range(DAYS // LANES):
            here = part[:, c * LANES : (c + 1) * LANES]
            gram_v[c] = here if i == 0 else gram_v[c] + here

    for i in range(STEPS):
        load(i).wait()
        settle(i)
        if i > 0:
            send(i - 1).start()
            multiply(i - 1)
    send(STEPS - 1).start()
    multiply(STEPS - 1)
    odd = lax.axis_index("tm") % 2
    half = DAYS // LANES // 2
    for c in range(half):
        keep_ref[c] = gram_v[odd * half + c]
        give_ref[c] = gram_v[(1 - odd) * half + c]
    pltpu.make_async_copy(field_v, field_ref, out_sem).wait()


def grid_rows(moved_first, moved_last, time_count, space_count, rows_tm, slots):
    slot_rows, first_rows = split_rows(slots)
    last_rows = slot_rows - first_rows
    width = round_up(slots, LANES)
    blocks = time_count * space_count
    dims = (time_count, space_count, rows_tm, slot_rows, first_rows, width, meta_layout(slots))
    codes = (blocks * width // LANES, LANES)
    rest = (codes[0] - first_rows // LANES * blocks, LANES)
    counts = (blocks, LANES)
    columns = (width, blocks)
    sums = (rows_tm * DAYS + 8, LANES)
    half = (DAYS // LANES // 2, RANK, LANES)
    params = pltpu.CompilerParams(vmem_limit_bytes=VMEM)
    moved_first, moved_last = (pltpu.with_memory_space_constraint(v, pltpu.VMEM) for v in (moved_first, moved_last))
    total, _, rest_code, count, column = pl.pallas_call(
        functools.partial(grid_first_kernel, dims),
        out_shape=[
            jax.ShapeDtypeStruct(sums, jnp.float32),
            jax.ShapeDtypeStruct(codes, jnp.int32),
            jax.ShapeDtypeStruct(rest, jnp.int32),
            jax.ShapeDtypeStruct(counts, jnp.int32),
            jax.ShapeDtypeStruct(columns, jnp.float32),
        ],
        scratch_shapes=[
            pltpu.VMEM((blocks * meta_layout(slots)[0], LANES), jnp.float32),
            pltpu.VMEM((blocks * first_rows, LANES), jnp.float32),
            pltpu.SMEM(codes, jnp.int32),
            pltpu.SMEM(counts, jnp.int32),
            pltpu.SemaphoreType.DMA((2,)),
        ],
        compiler_params=params,
        cost_estimate=pl.CostEstimate(flops=0, bytes_accessed=60_000_000, transcendentals=0),
        name="grid_first",
    )(moved_first)
    whole = pl.BlockSpec(memory_space=pltpu.VMEM)
    return pl.pallas_call(
        functools.partial(grid_last_kernel, dims),
        in_specs=[
            pl.BlockSpec(memory_space=pltpu.SMEM),
            pl.BlockSpec(memory_space=pltpu.SMEM),
            whole,
            pl.BlockSpec(memory_space=pl.ANY),
            pl.BlockSpec(memory_space=pl.ANY),
        ],
        out_specs=[pl.BlockSpec(memory_space=pl.ANY), whole, whole],
        out_shape=[
            jax.ShapeDtypeStruct((rows_tm, DAYS, LANES), jnp.bfloat16),
            pltpu.VMEM(half, jnp.float32),
            pltpu.VMEM(half, jnp.float32),
        ],
        scratch_shapes=[
            pltpu.VMEM(sums, jnp.float32),
            pltpu.VMEM((rows_tm * DAYS, LANES), jnp.float32),
            pltpu.VMEM((blocks, last_rows, LANES), jnp.bfloat16),
            pltpu.VMEM((blocks * last_rows, LANES), jnp.float32),
            pltpu.VMEM((rows_tm, DAYS, LANES), jnp.bfloat16),
            pltpu.VMEM((DAYS // LANES, RANK, LANES), jnp.float32),
            pltpu.SemaphoreType.DMA((STEPS,)),
            pltpu.SemaphoreType.DMA((blocks,)),
            pltpu.SemaphoreType.DMA,
        ],
        compiler_params=params,
        name="grid_last_and_gram",
    )(rest_code, count, column, moved_last, total)


def bf16_parts(x, count):
    found = []
    for _ in range(count):
        found.append(x.astype(jnp.bfloat16))
        x = x - found[-1].astype(jnp.float32)
    return found


def dot_f32(a, b, dims=(((1,), (0,)), ((), ()))):
    return lax.dot_general(a, b, dims, precision=lax.Precision.HIGHEST, preferred_element_type=jnp.float32)


def dot_three(a_parts, b_parts):
    a_high, a_low = a_parts
    b_high, b_low = b_parts
    a_all = jnp.concatenate([a_high, a_high, a_low], axis=1)
    b_all = jnp.concatenate([b_high, b_low, b_high], axis=0)
    half = a_all.shape[0] // 2
    rows = [jnp.dot(part, b_all, preferred_element_type=jnp.float32) for part in (a_all[:half], a_all[half:])]
    return jnp.concatenate(rows, axis=0)


def lower_inverse(a):
    n = a.shape[0]
    full = (8, n)
    tiles = [a[8 * i : 8 * i + 8, :] for i in range(n // 8)]
    lane = lax.broadcasted_iota(jnp.int32, full, 1)
    down = lax.broadcasted_iota(jnp.int32, full, 0)
    out = []
    for t in range(n // 8):
        k = 8 * t
        block = (lane >= k) & (lane < k + 8)
        panel = tiles[t]
        cols = [jnp.broadcast_to(panel[:, k + c : k + c + 1], full) for c in range(8)]
        e = {(i, c): jnp.broadcast_to(cols[c][i : i + 1, :], full) for c in range(8) for i in range(c, 8)}
        start = jnp.where(block, jnp.where(lane == k + down, 1.0, 0.0), panel)
        rows = [jnp.broadcast_to(start[i : i + 1, :], full) for i in range(8)]
        held = []
        for s in range(0, 8, 2):
            p, q, r = e[s, s], e[s + 1, s], e[s + 1, s + 1]
            det = p * r - q * q
            inv = pl.reciprocal(det, approx=True)
            factors = {}
            for i in range(s + 2, 8):
                x, y = e[i, s], e[i, s + 1]
                factors[i] = (r * x - q * y, p * y - q * x)
            for i in range(s + 2, 8):
                u, v = factors[i]
                for c in range(s + 2, i + 1):
                    e[i, c] = e[i, c] - (u * e[c, s] + v * e[c, s + 1]) * inv
                rows[i] = rows[i] - (u * rows[s] + v * rows[s + 1]) * inv
            held.append((p, q, r, det, inv, factors))
        done = jnp.zeros(full, jnp.float32)
        solved = [None] * 8
        for s in (6, 4, 2, 0):
            p, q, r, det, inv, factors = held[s // 2]
            root = lax.rsqrt(p)
            done = jnp.where(down == s, rows[s] * root, done)
            done = jnp.where(down == s + 1, (rows[s + 1] * p - q * rows[s]) * (root * lax.rsqrt(det)), done)
            first, second = r * rows[s] - q * rows[s + 1], p * rows[s + 1] - q * rows[s]
            for i in range(7, s + 1, -1):
                u, v = factors[i]
                first, second = first - u * solved[i], second - v * solved[i]
            solved[s], solved[s + 1] = first * inv, second * inv
        out.append(jnp.where(lane < k + 8, done, 0.0))
        for i in range(t + 1, n // 8):
            terms = [jnp.broadcast_to(tiles[i][:, k + c : k + c + 1], full) * solved[c] for c in range(8)]
            while len(terms) > 1:
                terms = [terms[j] + terms[j + 1] for j in range(0, len(terms), 2)]
            tiles[i] = jnp.where(block, 0.0, tiles[i]) - terms[0]
    return jnp.concatenate(out, axis=0)


def solve_kernel(scale, own_ref, other_ref, field_ref, basis_ref, prop_ref, gram_v, field_v, basis_v, sems):
    h = LANES
    pieces = DAYS // h
    rows_here = field_v.shape[0]
    load = pltpu.make_async_copy(field_ref.at[:, pl.ds(0, RANK), :], field_v, sems.at[0])
    load.start()
    odd = lax.axis_index("tm") % 2
    for c in range(pieces // 2):
        gram_v[odd * (pieces // 2) + c] = own_ref[c]
        gram_v[(1 - odd) * (pieces // 2) + c] = other_ref[c]

    gram = jnp.concatenate([gram_v[i] for i in range(pieces)], axis=1)
    eye = lax.broadcasted_iota(jnp.int32, (h, h), 0) == lax.broadcasted_iota(jnp.int32, (h, h), 1)
    a11, a12, a22 = gram_v[0, :h, :], gram_v[1, :h, :], gram_v[1, h:, :]
    size_col, size_row = [], []
    for part in (a11, a22):
        diag = jnp.where(eye, part, 0.0)
        size_col.append(lax.rsqrt(jnp.sum(diag, axis=1, keepdims=True)))
        size_row.append(lax.rsqrt(jnp.sum(diag, axis=0, keepdims=True)))
    top, low = gram[:h], gram[h:]
    x1 = lower_inverse(a11 * size_col[0] * size_row[0])
    r12 = dot_f32(x1, a12 * size_col[0] * size_row[1])
    x2 = lower_inverse(a22 * size_col[1] * size_row[1] - dot_f32(r12, r12, FIRST_FIRST))
    factor_top = dot_f32(x1, top * size_col[0])
    schur = low[:, h:] * size_col[1] - dot_f32(r12, factor_top[:, h:], FIRST_FIRST)
    mixed = -dot_f32(x2, dot_f32(r12, x1, FIRST_FIRST))
    factor_low = dot_f32(x2, schur)
    lower = jnp.concatenate(
        [
            jnp.concatenate([x1 * size_row[0], jnp.zeros((h, h), jnp.float32)], axis=1),
            jnp.concatenate([mixed * size_row[0], x2 * size_row[1]], axis=1),
        ],
        axis=0,
    )
    inverse = (scale * lower).astype(jnp.bfloat16)
    load.wait()

    def project(i):
        both = jnp.concatenate([field_v[2 * i], field_v[2 * i + 1]], axis=1)
        made = jnp.dot(inverse, both, preferred_element_type=jnp.float32).astype(jnp.bfloat16)
        basis_v[2 * i] = made[:, :h]
        basis_v[2 * i + 1] = made[:, h:]

    down = lax.broadcasted_iota(jnp.int32, (RANK, DAYS), 0)
    across = lax.broadcasted_iota(jnp.int32, (RANK, DAYS), 1)
    factor = jnp.concatenate(
        [factor_top, jnp.concatenate([jnp.zeros((h, h), jnp.float32), factor_low], axis=1)], axis=0
    )
    factor = jnp.where(across >= down, factor, 0.0)
    ahead = jnp.where(across < DAYS - 1, pltpu.roll(factor, DAYS - 1, 1), 0.0)
    cross = dot_three(bf16_parts(ahead, 2), [part.T for part in bf16_parts(factor, 2)])
    polar = cross * lax.rsqrt(jnp.sum(cross * cross) + 1e-06)
    todo = list(range(rows_here // 2))
    share = -(-len(todo) // (ITERS - 1))
    store = pltpu.make_async_copy(basis_v, basis_ref, sems.at[1])
    for n in range(ITERS):
        parts = bf16_parts(polar, 2)
        square = dot_three(parts, [part.T for part in parts])
        for i in todo[n * share : (n + 1) * share]:
            project(i)
        if n == ITERS - 2:
            store.start()
        polar = 1.5 * polar - 0.5 * dot_three(bf16_parts(square, 2), parts)
    prop_ref[...] = math.sqrt(RANK) * polar
    store.wait()


def solve(own, other, field, cell_total):
    rows_tm = field.shape[0]
    part = (rows_tm, RANK, LANES)
    whole = pl.BlockSpec(memory_space=pltpu.VMEM)
    own, other = (pltpu.with_memory_space_constraint(v, pltpu.VMEM) for v in (own, other))
    return pl.pallas_call(
        functools.partial(solve_kernel, math.sqrt(cell_total)),
        in_specs=[whole, whole, pl.BlockSpec(memory_space=pl.ANY)],
        out_specs=[pl.BlockSpec(memory_space=pl.ANY), whole],
        out_shape=[
            jax.ShapeDtypeStruct(part, jnp.bfloat16),
            jax.ShapeDtypeStruct((RANK, RANK), jnp.float32),
        ],
        scratch_shapes=[
            pltpu.VMEM((DAYS // LANES, RANK, LANES), jnp.float32),
            pltpu.VMEM(part, jnp.bfloat16),
            pltpu.VMEM(part, jnp.bfloat16),
            pltpu.SemaphoreType.DMA((2,)),
        ],
        compiler_params=pltpu.CompilerParams(vmem_limit_bytes=VMEM),
        name="factor_basis_and_polar",
    )(own, other, field)


def body(pixels, weights, tile_index, tile_row, granule_day):
    swath_rows = pixels.shape[0]
    width = pixels.shape[1]
    space_count = lax.axis_size("space")
    time_count = lax.axis_size("tm")
    dest_count = time_count * space_count
    rows_tm = GR_DEV // time_count
    slots = 2 * swath_rows // space_count // time_count
    axes = ("tm", "space")
    first, last = pack(pixels, weights, tile_index, tile_row, granule_day, time_count, space_count, rows_tm, slots)
    first = lax.all_to_all(first, axes, split_axis=0, concat_axis=0, tiled=True)
    last = lax.all_to_all(last, axes, split_axis=0, concat_axis=0, tiled=True)
    field, keep, give = grid_rows(first, last, time_count, space_count, rows_tm, slots)

    swap = [(t, t ^ 1) for t in range(time_count)]
    peers = [[t * space_count + s for t in range(core, time_count, 2) for s in range(space_count)] for core in (0, 1)]
    among = functools.partial(
        lax.all_to_all, axis_name=axes, split_axis=0, concat_axis=0, axis_index_groups=peers, tiled=True
    )
    pieces = (keep + lax.ppermute(give, "tm", swap)).reshape(dest_count // 2, -1, LANES)
    mine = jnp.sum(among(pieces), axis=0, keepdims=True)
    own = among(jnp.broadcast_to(mine, pieces.shape)).reshape(keep.shape)
    other = lax.ppermute(own, "tm", swap)
    cell_total = space_count * GR_DEV * width
    basis, propagator = solve(own, other, field, cell_total)
    return (field[None], basis[None], propagator)


def solution(mesh):
    placed = (
        P(("tm", "space"), None),
        P(("tm", "space")),
        P(("tm", "space")),
        P(("tm", "space")),
        P(("tm", "space")),
    )
    return jax.shard_map(
        body,
        mesh=mesh,
        in_specs=placed,
        out_specs=(P("space", "tm", None, None), P("space", "tm", None, None), P()),
        check_vma=False,
    )
```
